32 devices in a mesh: dp: 16 (over z, y, x), seq: 2 (over core).
Axes of the slice: x: 2, y: 2, z: 4, core: 2. Of those that a mesh axis runs over, the one named last changes fastest.
Arguments:
- tokens: bfloat16 [16, 256, 1152], P('dp', 'seq'), may hold values from -12 to 12
- cotangent: bfloat16 [16, 256, 1152], P('dp', 'seq'), may hold values from -12 to 12
- time_vec: bfloat16 [16, 1152], P('dp'), may hold values from -12 to 12
- labels: int32 [16], P('dp'), may hold values from 0 to 1023
- kept: int32 [16], P('dp'), may hold values from 0 to 256, as said below
- keep_index: int32 [16, 256], P('dp', 'seq'), may hold values from 0 to 255, each once within a row
- modulation_master: float32 [7962624], P('dp'), may hold values from -0.1875 to 0.1875
- modulation_first: float32 [7962624], P('dp'), may hold values from -0.0029296875 to 0.0029296875
- modulation_second: float32 [7962624], P('dp'), may hold values from 1.9933305e-08 to 3.1893288e-07
- attention_in_master: float32 [3981312], P('dp'), may hold values from -0.15320647 to 0.15320647
- attention_in_first: float32 [3981312], P('dp'), may hold values from -0.0029296875 to 0.0029296875
- attention_in_second: float32 [3981312], P('dp'), may hold values from 1.9933305e-08 to 3.1893288e-07
- attention_out_master: float32 [1327104], P('dp'), may hold values from -0.375 to 0.375
- attention_out_first: float32 [1327104], P('dp'), may hold values from -0.0029296875 to 0.0029296875
- attention_out_second: float32 [1327104], P('dp'), may hold values from 1.9933305e-08 to 3.1893288e-07
- expand_master: float32 [5308416], P('dp'), may hold values from -0.15320647 to 0.15320647
- expand_first: float32 [5308416], P('dp'), may hold values from -0.0012207031 to 0.0012207031
- expand_second: float32 [5308416], P('dp'), may hold values from 1.5946644e-09 to 2.551463e-08
- contract_master: float32 [5308416], P('dp'), may hold values from -0.09375 to 0.09375
- contract_first: float32 [5308416], P('dp'), may hold values from -0.0029296875 to 0.0029296875
- contract_second: float32 [5308416], P('dp'), may hold values from 1.9933305e-08 to 3.1893288e-07
- class_table_master: float32 [1179648], P('dp'), may hold values from -3 to 3
- class_table_first: float32 [1179648], P('dp'), may hold values from -0.00015258789 to 0.00015258789
- class_table_second: float32 [1179648], P('dp'), may hold values from 7.973322e-11 to 1.2757315e-09
- biases_master: float32 [16128], P('dp'), may hold values from -1.2 to 1.2
- biases_first: float32 [16128], P('dp'), may hold values from -0.0029296875 to 0.0029296875
- biases_second: float32 [16128], P('dp'), may hold values from 1.9933305e-08 to 3.1893288e-07
Outputs:
- block_out: bfloat16 [16, 256, 1152], P('dp', 'seq')
- tokens_grad: bfloat16 [16, 256, 1152], P('dp', 'seq')
- grad_norm: float32 [], replicated
- modulation_first_new: float32 [7962624], P('dp')
- modulation_second_new: float32 [7962624], P('dp')
- modulation_master_new: float32 [7962624], P('dp')
- attention_in_first_new: float32 [3981312], P('dp')
- attention_in_second_new: float32 [3981312], P('dp')
- attention_in_master_new: float32 [3981312], P('dp')
- attention_out_first_new: float32 [1327104], P('dp')
- attention_out_second_new: float32 [1327104], P('dp')
- attention_out_master_new: float32 [1327104], P('dp')
- expand_first_new: float32 [5308416], P('dp')
- expand_second_new: float32 [5308416], P('dp')
- expand_master_new: float32 [5308416], P('dp')
- contract_first_new: float32 [5308416], P('dp')
- contract_second_new: float32 [5308416], P('dp')
- contract_master_new: float32 [5308416], P('dp')
- class_table_first_new: float32 [1179648], P('dp')
- class_table_second_new: float32 [1179648], P('dp')
- class_table_master_new: float32 [1179648], P('dp')
- biases_first_new: float32 [16128], P('dp')
- biases_second_new: float32 [16128], P('dp')
- biases_master_new: float32 [16128], P('dp')
The draws below stay inside these ranges and needn't reach their ends.
Inputs may be any that keep to these rules, and one draw needn't show every extreme that they name: `kept`: each image slot keeps 0, 128 or 256 tokens; the first slot of every index of dp keeps 256. `keep_index`: each row is a permutation of the 256 grid positions.
All inputs are finite; a program needn't handle non-finite values.
Results may differ from the reference program's by a relative error of at most 0.04.
The reference program's roundings to bfloat16 on the way count: a program that leaves them out, or rounds other values in their place, can miss the bound.
Values may be sent and summed in bfloat16 or wider, within the bound.
A program may use at most 448 MiB of HBM per device.

```python
import math
import jax
import jax.numpy as jnp
from jax import lax

D = 1152
HEAD_DIM = 72
FF = 4608
SIDE = 16
GRID = 256
CLASSES = 1024
SLOTS = 1
STEP = 10
ROWS = 128
SLOTS_ALL = 16
BIASES = 16128
PARAMS = 25083648
N_SEQ = 2


def column_ramp(width, top):
    return 1.0 + (top - 1.0) * jnp.arange(width, dtype=jnp.float32) / (width - 1)


def with_columns(base, column_key, cols, share):
    common = jnp.clip(jax.random.normal(column_key, (1, cols), jnp.float32), -3.0, 3.0)
    return ((base + share * common) * D ** (-0.5)).reshape(-1)


def draw_tokens(key, part):
    key = jax.random.fold_in(key, 1)
    values = jnp.clip(jax.random.normal(key, (SLOTS_ALL, GRID, D), jnp.float32), -4.0, 4.0) * column_ramp(D, 3.0)
    return values.astype(jnp.bfloat16)


def draw_cotangent(key, part):
    key = jax.random.fold_in(key, 2)
    values = jnp.clip(jax.random.normal(key, (SLOTS_ALL, GRID, D), jnp.float32), -4.0, 4.0) * column_ramp(D, 3.0)
    return values.astype(jnp.bfloat16)


def draw_time_vec(key, part):
    key = jax.random.fold_in(key, 3)
    values = jnp.clip(jax.random.normal(key, (SLOTS_ALL, D), jnp.float32), -4.0, 4.0) * column_ramp(D, 3.0)
    return values.astype(jnp.bfloat16)


def draw_kept(key, part):
    key = jax.random.fold_in(key, 4)
    kinds = jax.random.randint(key, (SLOTS_ALL,), 0, 3)
    leading = jnp.arange(SLOTS_ALL) % SLOTS == 0
    kinds = jnp.where(leading, 2, kinds)
    counts = jnp.where(kinds == 2, GRID, jnp.where(kinds == 1, GRID // 2, 0))
    return counts.astype(jnp.int32)


def draw_attention_in_master(key, part):
    key = jax.random.fold_in(key, 5)
    base_key, column_key = jax.random.split(key)
    base = jnp.clip(jax.random.normal(base_key, (D, 3 * D), jnp.float32), -4.0, 4.0)
    return with_columns(base, column_key, 3 * D, 0.4)


def draw_expand_master(key, part):
    key = jax.random.fold_in(key, 6)
    base_key, column_key = jax.random.split(key)
    base = jnp.clip(jax.random.normal(base_key, (D, FF), jnp.float32), -4.0, 4.0)
    return with_columns(base, column_key, FF, 0.4)


def plant(values, own_key, least, high):
    extent = values.shape
    place = [jax.random.randint(jax.random.fold_in(own_key, axis), (), 0, extent[axis]) for axis in range(len(extent))]
    values = values.at[tuple(place)].set(least)
    longest = extent.index(max(extent))
    place[longest] = (place[longest] + 1) % extent[longest]
    return values.at[tuple(place)].set(high)


def shard_levels(own_key, extent, cuts, low, high):
    def one(dim, parts):
        draws = jax.random.uniform(jax.random.fold_in(jax.random.fold_in(own_key, 6), dim), (parts,), jnp.float32, low / len(cuts), high / len(cuts))
        return jnp.repeat(jnp.exp(draws), extent[dim] // parts).reshape((-1,) + (1,) * (len(extent) - dim - 1))

    level = one(*cuts[0])
    for cut in cuts[1:]:
        level = level * one(*cut)
    return level


def normal_values(key, extent, scale, most, cuts=(), kind=jnp.bfloat16):
    values = jax.random.normal(key, extent, jnp.float32) * scale
    if len(cuts) > 0:
        values = shard_levels(key, extent, cuts, -0.22, 0.18) * values
    return jnp.clip(values, min=-most, max=most).astype(kind)


def setup_inputs(seed: int = 0) -> dict:
    arg_keys = jax.random.split(jax.random.key(seed), 28)
    tokens = draw_tokens(jax.random.fold_in(arg_keys[27], 71), 0)
    cotangent = draw_cotangent(jax.random.fold_in(arg_keys[27], 71), 0)
    time_vec = draw_time_vec(jax.random.fold_in(arg_keys[27], 71), 0)
    labels = plant(jax.random.randint(arg_keys[3], (SLOTS_ALL,), 0, CLASSES), jax.random.fold_in(arg_keys[3], 1), 0, CLASSES - 1).astype(jnp.int32)
    kept = draw_kept(jax.random.fold_in(arg_keys[27], 71), 0)
    keep_index = jax.vmap(lambda own: jax.random.permutation(own, GRID))(jax.random.split(arg_keys[5], SLOTS_ALL)).reshape((SLOTS_ALL, GRID)).astype(jnp.int32)
    modulation_master = normal_values(arg_keys[6], (6 * D * D,), D ** -0.5, 0.1875, ((0, 16),), jnp.float32)
    modulation_first = normal_values(arg_keys[7], (6 * D * D,), (1.0 / PARAMS ** 0.5), 0.0029296875, ((0, 16),), jnp.float32)
    modulation_second = jnp.clip(jnp.exp(math.log(3.1893287655293534e-07) - 2.7725887 * jax.random.uniform(arg_keys[8], (6 * D * D,), jnp.float32) ** shard_levels(arg_keys[8], (6 * D * D,), ((0, 16),), -0.2, 0.2)), 1.993330478455846e-08, 3.1893287655293534e-07)
    attention_in_master = draw_attention_in_master(jax.random.fold_in(arg_keys[27], 71), 0)
    attention_in_first = normal_values(arg_keys[10], (3 * D * D,), (1.0 / PARAMS ** 0.5), 0.0029296875, ((0, 16),), jnp.float32)
    attention_in_second = jnp.clip(jnp.exp(math.log(3.1893287655293534e-07) - 2.7725887 * jax.random.uniform(arg_keys[11], (3 * D * D,), jnp.float32) ** shard_levels(arg_keys[11], (3 * D * D,), ((0, 16),), -0.2, 0.2)), 1.993330478455846e-08, 3.1893287655293534e-07)
    attention_out_master = normal_values(arg_keys[12], (D * D,), (D // 4) ** -0.5, 0.375, ((0, 16),), jnp.float32)
    attention_out_first = normal_values(arg_keys[13], (D * D,), (1.0 / PARAMS ** 0.5), 0.0029296875, ((0, 16),), jnp.float32)
    attention_out_second = jnp.clip(jnp.exp(math.log(3.1893287655293534e-07) - 2.7725887 * jax.random.uniform(arg_keys[14], (D * D,), jnp.float32) ** shard_levels(arg_keys[14], (D * D,), ((0, 16),), -0.2, 0.2)), 1.993330478455846e-08, 3.1893287655293534e-07)
    expand_master = draw_expand_master(jax.random.fold_in(arg_keys[27], 71), 0)
    expand_first = normal_values(arg_keys[16], (D * FF,), (0.4 / PARAMS ** 0.5), 0.0012207031, ((0, 16),), jnp.float32)
    expand_second = jnp.clip(jnp.exp(math.log(2.551463040845192e-08) - 2.7725887 * jax.random.uniform(arg_keys[17], (D * FF,), jnp.float32) ** shard_levels(arg_keys[17], (D * FF,), ((0, 16),), -0.2, 0.2)), 1.594664400528245e-09, 2.551463040845192e-08)
    contract_master = normal_values(arg_keys[18], (D * FF,), FF ** -0.5, 0.09375, ((0, 16),), jnp.float32)
    contract_first = normal_values(arg_keys[19], (D * FF,), (1.0 / PARAMS ** 0.5), 0.0029296875, ((0, 16),), jnp.float32)
    contract_second = jnp.clip(jnp.exp(math.log(3.1893287655293534e-07) - 2.7725887 * jax.random.uniform(arg_keys[20], (D * FF,), jnp.float32) ** shard_levels(arg_keys[20], (D * FF,), ((0, 16),), -0.2, 0.2)), 1.993330478455846e-08, 3.1893287655293534e-07)
    class_table_master = normal_values(arg_keys[21], (CLASSES * D,), 0.5, 3.0, ((0, 16),), jnp.float32)
    class_table_first = normal_values(arg_keys[22], (CLASSES * D,), (0.05 / PARAMS ** 0.5), 0.00015258789, ((0, 16),), jnp.float32)
    class_table_second = jnp.clip(jnp.exp(math.log(1.275731520422596e-09) - 2.7725887 * jax.random.uniform(arg_keys[23], (CLASSES * D,), jnp.float32) ** shard_levels(arg_keys[23], (CLASSES * D,), ((0, 16),), -0.2, 0.2)), 7.973322002641225e-11, 1.275731520422596e-09)
    biases_master = normal_values(arg_keys[24], (BIASES,), 0.2, 1.2, ((0, 16),), jnp.float32)
    biases_first = normal_values(arg_keys[25], (BIASES,), (1.0 / PARAMS ** 0.5), 0.0029296875, ((0, 16),), jnp.float32)
    biases_second = jnp.clip(jnp.exp(math.log(3.1893287655293534e-07) - 2.7725887 * jax.random.uniform(arg_keys[26], (BIASES,), jnp.float32) ** shard_levels(arg_keys[26], (BIASES,), ((0, 16),), -0.2, 0.2)), 1.993330478455846e-08, 3.1893287655293534e-07)
    return {"tokens": tokens, "cotangent": cotangent, "time_vec": time_vec, "labels": labels, "kept": kept, "keep_index": keep_index, "modulation_master": modulation_master, "modulation_first": modulation_first, "modulation_second": modulation_second, "attention_in_master": attention_in_master, "attention_in_first": attention_in_first, "attention_in_second": attention_in_second, "attention_out_master": attention_out_master, "attention_out_first": attention_out_first, "attention_out_second": attention_out_second, "expand_master": expand_master, "expand_first": expand_first, "expand_second": expand_second, "contract_master": contract_master, "contract_first": contract_first, "contract_second": contract_second, "class_table_master": class_table_master, "class_table_first": class_table_first, "class_table_second": class_table_second, "biases_master": biases_master, "biases_first": biases_first, "biases_second": biases_second}


LAYER_EPS = 1e-06
MASK_FILL = -1e+30
BETA_FIRST = 0.5
BETA_SECOND = 0.5
ADAM_EPS = 1e-08
WEIGHT_DECAY = 0.1
CLIP_LIMIT = 1.0
HIGHEST = lax.Precision.HIGHEST

@jax.custom_vjp
def low(v):
    return lax.optimization_barrier(v.astype(jnp.bfloat16)).astype(jnp.float32)

@jax.custom_vjp
def low_back(v):
    return v

def low_keep(v):
    return (low(v), None)

def low_pass(kept, grad):
    return (grad,)

def back_keep(v):
    return (v, None)

def back_low(kept, grad):
    return (low(grad),)
low.defvjp(low_keep, low_pass)
low_back.defvjp(back_keep, back_low)

def grid_embed(keep_index, width):
    quarter = width // 4
    freqs = 10000.0 ** (-jnp.arange(quarter).astype(jnp.float32) / quarter)
    across = (keep_index // SIDE).astype(jnp.float32)[..., None] * freqs
    along = (keep_index % SIDE).astype(jnp.float32)[..., None] * freqs
    return jnp.concatenate([jnp.sin(across), jnp.cos(across), jnp.sin(along), jnp.cos(along)], axis=-1)

def normalize(values):
    centre = values - lax.optimization_barrier(jnp.mean(values, axis=-1, keepdims=True))
    spread = lax.optimization_barrier(jnp.mean(centre * centre, axis=-1, keepdims=True))
    return centre * lax.rsqrt(spread + LAYER_EPS)

def modulated(values, shift, scale):
    return normalize(values) * (1.0 + scale) + shift

def forward(params, tokens, time_vec, labels, kept, keep_index):
    rounded = [low(item) for item in params]
    modulation = rounded[0].reshape(D, 6 * D)
    attention_in = rounded[1].reshape(D, 3 * D)
    attention_out = rounded[2].reshape(D, D)
    expand = rounded[3].reshape(D, FF)
    contract = rounded[4].reshape(D, FF)
    class_table = rounded[5].reshape(CLASSES, D)
    biases = rounded[6]
    bias_mod = biases[:6 * D]
    bias_query = biases[6 * D:7 * D]
    bias_value = biases[7 * D:8 * D]
    bias_out = biases[8 * D:9 * D]
    bias_expand = biases[9 * D:9 * D + FF]
    bias_contract = biases[9 * D + FF:]
    slots = tokens.shape[0]
    heads = D // HEAD_DIM
    cond = time_vec + class_table[labels]
    silu_cond = low(jax.nn.silu(cond))
    shifts = low_back(jnp.dot(silu_cond, modulation, precision=HIGHEST) + bias_mod)
    pieces = shifts.reshape(slots, 6, 1, D)
    inputs = tokens + grid_embed(keep_index, D)
    normed_in = low(modulated(inputs, pieces[:, 0], pieces[:, 1]))
    projected = jnp.einsum('srd,de->sre', normed_in, attention_in, precision=HIGHEST)
    queries = low_back(low(projected[..., :D] + bias_query))
    keys_all = low_back(low(projected[..., D:2 * D]))
    values_all = low_back(low(projected[..., 2 * D:] + bias_value))
    key_ok = (jnp.arange(GRID) % ROWS)[None, :] < (kept // N_SEQ)[:, None]
    query_heads = queries.reshape(slots, GRID, heads, HEAD_DIM)
    key_heads = keys_all.reshape(slots, GRID, heads, HEAD_DIM)
    value_heads = values_all.reshape(slots, GRID, heads, HEAD_DIM)
    logits = low_back(jnp.einsum('sqhe,skhe->shqk', query_heads, key_heads, precision=HIGHEST) * HEAD_DIM ** (-0.5))
    logits = jnp.where(key_ok[:, None, None, :], logits, MASK_FILL)
    largest = lax.optimization_barrier(jnp.max(logits, axis=-1, keepdims=True))
    expo = jnp.exp(logits - largest)
    weights = low(expo / lax.optimization_barrier(jnp.sum(expo, axis=-1, keepdims=True)))
    mixed = jnp.einsum('shqk,skhe->sqhe', weights, value_heads, precision=HIGHEST).reshape(slots, GRID, D)
    mixed = low_back(low(mixed))
    attended = low_back(jnp.einsum('sqi,oi->sqo', mixed, attention_out, precision=HIGHEST) + bias_out)
    middle = inputs + pieces[:, 2] * attended
    normed_mid = low(modulated(middle, pieces[:, 3], pieces[:, 4]))
    hidden = low_back(jnp.einsum('sqd,df->sqf', normed_mid, expand, precision=HIGHEST) + bias_expand)
    activated = low(jax.nn.gelu(hidden, approximate=True))
    branch = low_back(jnp.einsum('sqf,of->sqo', activated, contract, precision=HIGHEST) + bias_contract)
    return middle + pieces[:, 5] * branch

def adam_step(grad, master, first, second, rate):
    first_new = BETA_FIRST * first + (1.0 - BETA_FIRST) * grad
    second_new = BETA_SECOND * second + (1.0 - BETA_SECOND) * grad * grad
    first_hat = first_new / (1.0 - BETA_FIRST ** STEP)
    second_hat = second_new / (1.0 - BETA_SECOND ** STEP)
    master_new = master - rate * (first_hat / (jnp.sqrt(second_hat) + ADAM_EPS) + WEIGHT_DECAY * master)
    return (first_new, second_new, master_new)

def reference(tokens, cotangent, time_vec, labels, kept, keep_index, modulation_master, modulation_first, modulation_second, attention_in_master, attention_in_first, attention_in_second, attention_out_master, attention_out_first, attention_out_second, expand_master, expand_first, expand_second, contract_master, contract_first, contract_second, class_table_master, class_table_first, class_table_second, biases_master, biases_first, biases_second):
    masters = (modulation_master, attention_in_master, attention_out_master, expand_master, contract_master, class_table_master, biases_master)
    groups = SLOTS_ALL // SLOTS

    def regroup(array):
        return array.reshape((groups, SLOTS) + array.shape[1:])
    blocks = (regroup(tokens), regroup(cotangent), regroup(time_vec), regroup(labels), regroup(kept), regroup(keep_index))

    def one_group(totals, block):
        token_block, cot_block, time_block, label_block, kept_block, index_block = block
        row_ok = (jnp.arange(GRID) % ROWS)[None, :] < (kept_block // N_SEQ)[:, None]

        def run(params, token_values):
            return forward(params, token_values, time_block.astype(jnp.float32), label_block, kept_block, index_block)
        result, pullback = jax.vjp(run, masters, token_block.astype(jnp.float32))
        incoming = cot_block.astype(jnp.float32) * row_ok[..., None].astype(jnp.float32)
        param_grads, token_grads = pullback(incoming)
        totals = tuple((total + grad for total, grad in zip(totals, param_grads)))
        out_block = jnp.where(row_ok[..., None], result, 0.0).astype(jnp.bfloat16)
        return (totals, (out_block, token_grads.astype(jnp.bfloat16)))
    start = tuple((jnp.zeros_like(item) for item in masters))
    totals, stacked = lax.scan(one_group, start, blocks)
    block_out = stacked[0].reshape(SLOTS_ALL, GRID, D)
    tokens_grad = stacked[1].reshape(SLOTS_ALL, GRID, D)
    squares = totals[0] * 0.0
    squares = jnp.sum(squares)
    for grad in totals:
        squares = squares + jnp.sum(grad * grad)
    grad_norm = jnp.sqrt(squares)
    factor = jnp.minimum(1.0, CLIP_LIMIT / (grad_norm + 1e-06))
    rates = (D ** (-0.5), D ** (-0.5), (D // 4) ** (-0.5), D ** (-0.5), FF ** (-0.5), 0.5, 0.2)
    firsts = (modulation_first, attention_in_first, attention_out_first, expand_first, contract_first, class_table_first, biases_first)
    seconds = (modulation_second, attention_in_second, attention_out_second, expand_second, contract_second, class_table_second, biases_second)
    updated = [adam_step(grad * factor, master, first, second, rate) for grad, master, first, second, rate in zip(totals, masters, firsts, seconds, rates)]
    return (block_out, tokens_grad, grad_norm, updated[0][0], updated[0][1], updated[0][2], updated[1][0], updated[1][1], updated[1][2], updated[2][0], updated[2][1], updated[2][2], updated[3][0], updated[3][1], updated[3][2], updated[4][0], updated[4][1], updated[4][2], updated[5][0], updated[5][1], updated[5][2], updated[6][0], updated[6][1], updated[6][2])
```

```python
import functools
import jax
import jax.numpy as jnp
from jax import lax
from jax.experimental import pallas as pl
from jax.experimental.pallas import tpu as pltpu
from jax.sharding import PartitionSpec as P

HEAD_DIM = 72
FF = 4608
SIDE = 16
CLASSES = 1024
STEP = 10
LAYER_EPS = 1e-06
MASK_FILL = -1e30
BETA_FIRST = 0.5
BETA_SECOND = 0.5
ADAM_EPS = 1e-08
WEIGHT_DECAY = 0.1
CLIP_LIMIT = 1.0

MESH = pl.DeviceIdType.MESH
GROUPS = ((0, 768, 0, "x"), (768, 768, 0, "y"), (1536, 384, 1, "x"), (1920, 384, 1, "y"))


def when(cond, fn):
    pl.when(cond)(fn)


class Place:
    def __init__(self, line):
        self.line = line
        i = lax.axis_index("dp")
        self.c = lax.axis_index("seq")
        self.x, self.y, self.z = i % 2, (i // 2) % 2, i // 4

    def dev(self, z=None, y=None, x=None):
        z = self.z if z is None else z
        y = self.y if y is None else y
        x = self.x if x is None else x
        return (z * 4 + y * 2 + x, self.c)

    def peer(self, axis):
        return self.dev(x=1 - self.x) if axis == "x" else self.dev(y=1 - self.y)

    def barrier(self):
        bar = pltpu.get_barrier_semaphore()

        def sig(dev):
            pl.semaphore_signal(bar, inc=1, device_id=dev, device_id_type=MESH)

        sig(self.peer("x"))
        sig(self.peer("y"))
        when(self.z > 0, lambda: sig(self.dev(z=self.z - 1)))
        when(self.z < self.line - 1, lambda: sig(self.dev(z=self.z + 1)))
        pl.semaphore_wait(bar, 2 + (self.z > 0).astype(jnp.int32) + (self.z < self.line - 1).astype(jnp.int32))


def gather_kernel(line, src, out, own_sem, send_a, send_u, send_d, send_b, recv_a, recv_z, recv_b):
    me = Place(line)
    count = src.shape[0]
    x, y, z = me.x, me.y, me.z

    def single(m, g, zz, yy=None, xx=None):
        lo, width = GROUPS[g][:2]
        return out.at[m, zz, y if yy is None else yy, x if xx is None else xx, :, pl.ds(lo, width)]

    def pair(m, g, zz):
        lo, width, _, first = GROUPS[g]
        if first == "x":
            return out.at[m, zz, y, :, :, pl.ds(lo, width)]
        return out.at[m, zz, :, x, :, pl.ds(lo, width)]

    def remote(ref, send, recv, dev, source=None):
        return pltpu.make_async_remote_copy(
            src_ref=ref if source is None else source, dst_ref=ref, send_sem=send, recv_sem=recv,
            device_id=dev, device_id_type=MESH)

    def own(m, g):
        lo, width = GROUPS[g][:2]
        return src.at[m, :, pl.ds(lo, width)]

    def a_copy(m, g, zz, source=None):
        return remote(single(m, g, zz), send_a.at[m, g, zz], recv_a.at[m, g, zz], me.peer(GROUPS[g][3]), source)

    def z_ref(m, g, zz):
        return pair(m, g, zz) if GROUPS[g][2] == 0 else single(m, g, zz)

    def u_copy(m, g, zz, source=None):
        return remote(z_ref(m, g, zz), send_u.at[m, g, zz], recv_z.at[m, g, zz], me.dev(z=jnp.minimum(z + 1, line - 1)), source)

    def d_copy(m, g, zz, source=None):
        return remote(z_ref(m, g, zz), send_d.at[m, g, zz], recv_z.at[m, g, zz], me.dev(z=jnp.maximum(z - 1, 0)), source)

    def b_copy(m, g, zz):
        last = "y" if GROUPS[g][3] == "x" else "x"
        return remote(pair(m, g, zz), send_b.at[m, g, zz], recv_b.at[m, g, zz], me.peer(last))

    def keep(m):
        return pltpu.make_async_copy(src.at[m], out.at[m, z, y, x], own_sem.at[m])

    up, down = z < line - 1, z > 0

    @pl.loop(0, count)
    def _(m):
        keep(m).start()

    me.barrier()

    @pl.loop(0, count)
    def _(m):
        for g in range(4):
            a_copy(m, g, z, own(m, g)).start()
        for g in (2, 3):
            when(up, lambda g=g: u_copy(m, g, z, own(m, g)).start())
            when(down, lambda g=g: d_copy(m, g, z, own(m, g)).start())

    @pl.loop(0, count)
    def _(m):
        keep(m).wait()
        for g in (0, 1):
            a_copy(m, g, z).wait_recv()
            when(up, lambda g=g: u_copy(m, g, z).start())
            when(down, lambda g=g: d_copy(m, g, z).start())
            b_copy(m, g, z).start()

    def arrive(m, k, zz, onward, go):
        for g in range(4):
            copy = u_copy if go == "u" else d_copy
            copy(m, g, zz).wait_recv()
            when(onward, lambda g=g: copy(m, g, zz).start())
            if GROUPS[g][2] == 0:
                b_copy(m, g, zz).start()
            else:
                a_copy(m, g, zz).start()

    def crossed(m, zz):
        for g in (2, 3):
            a_copy(m, g, zz).wait_recv()
            b_copy(m, g, zz).start()

    @pl.loop(1, line + 1)
    def _(k):
        @pl.loop(0, count)
        def _(m):
            when(k <= z, lambda: arrive(m, k, jnp.maximum(z - k, 0), up, "u"))
            when(z + k < line, lambda: arrive(m, k, jnp.minimum(z + k, line - 1), down, "d"))
            when(k - 1 <= z, lambda: crossed(m, jnp.maximum(z - k + 1, 0)))
            when((k > 1) & (z + k - 1 < line), lambda: crossed(m, jnp.minimum(z + k - 1, line - 1)))

    @pl.loop(0, count)
    def _(m):
        @pl.loop(0, line)
        def _(zz):
            for g in range(4):
                b_copy(m, g, zz).wait()
                if GROUPS[g][2] == 1:
                    a_copy(m, g, zz).wait_send()
                when(up & (zz <= z), lambda g=g: u_copy(m, g, zz).wait_send())
                when(down & (zz >= z), lambda g=g: d_copy(m, g, zz).wait_send())
        for g in (0, 1):
            a_copy(m, g, z).wait_send()


def gather_weights(src, n, collective_id):
    count, rows, cols = src.shape
    line = n // 4
    dma = pltpu.SemaphoreType.DMA
    return pl.pallas_call(
        functools.partial(gather_kernel, line),
        out_shape=jax.ShapeDtypeStruct((count, line, 2, 2, rows, cols), src.dtype),
        in_specs=[pl.BlockSpec(memory_space=pltpu.HBM)],
        out_specs=pl.BlockSpec(memory_space=pltpu.HBM),
        scratch_shapes=[dma((count,))] + [dma((count, 4, line))] * 7,
        compiler_params=pltpu.CompilerParams(collective_id=collective_id, has_side_effects=True),
        cost_estimate=pl.CostEstimate(flops=0, bytes_accessed=2 * count * n * rows * cols * 2, transcendentals=0),
        name="gather_weights",
    )(src)


def reduce_kernel(line, *refs):
    count = len(refs) - 1 - 4 - 4 - 4 - 4 - 8
    grads = refs[:count]
    out = refs[count]
    s = count + 1
    acc = refs[s:s + 4]
    got_b = refs[s + 4:s + 8]
    got_z = refs[s + 8:s + 12]
    got_a = refs[s + 12:s + 16]
    load, send_b, send_z, send_a, recv_b, recv_z, recv_a, spare = refs[s + 16:]
    me = Place(line)
    x, y, z = me.x, me.y, me.z
    up, down = z < line - 1, z > 0

    def cols(g):
        return pl.ds(GROUPS[g][0], GROUPS[g][1])

    def last(g):
        return "y" if GROUPS[g][3] == "x" else "x"

    def half(m, g, zz, mine):
        if last(g) == "y":
            return grads[m].at[zz, y if mine else 1 - y, :, :, cols(g)]
        return grads[m].at[zz, :, x if mine else 1 - x, :, cols(g)]

    def first(g):
        return x if GROUPS[g][3] == "x" else y

    def loading(m, g, zz):
        return pltpu.make_async_copy(half(m, g, zz, True), acc[g].at[m, zz], load.at[m, g, zz])

    def remote(src, dst, send, recv, dev):
        return pltpu.make_async_remote_copy(src_ref=src, dst_ref=dst, send_sem=send, recv_sem=recv, device_id=dev, device_id_type=MESH)

    def b_copy(m, g, zz):
        return remote(half(m, g, zz, False), got_b[g].at[m, zz], send_b.at[m, g, zz], recv_b.at[m, g, zz], me.peer(last(g)))

    def a_copy(m, g, zz, slot):
        return remote(acc[g].at[m, zz, 1 - first(g)], got_a[g].at[m, slot], send_a.at[m, g, zz], recv_a.at[m, g, slot], me.peer(GROUPS[g][3]))

    def z_part(m, g, zz):
        return acc[g].at[m, zz] if GROUPS[g][2] == 0 else acc[g].at[m, zz, first(g)]

    def z_copy(m, g, zz, slot, dev):
        return remote(z_part(m, g, zz), got_z[g].at[m, slot], send_z.at[m, g, zz], recv_z.at[m, g, slot], dev)

    def z_recv(m, g, slot):
        z_copy(m, g, z, slot, me.dev(z=jnp.maximum(z - 1, 0))).wait_recv()

    above, below = me.dev(z=jnp.minimum(z + 1, line - 1)), me.dev(z=jnp.maximum(z - 1, 0))

    me.barrier()

    def start(m, zz):
        for g in range(4):
            b_copy(m, g, zz).start()
            loading(m, g, zz).start()

    def each(fn):
        @pl.loop(0, line)
        def _(j):
            k = line - 1 - j
            for m in range(count):
                when(z + k < line, lambda: fn(m, jnp.minimum(z + k, line - 1)))
                when((z >= k) & (k > 0), lambda: fn(m, jnp.maximum(z - k, 0)))

    each(start)

    def add_b(m, g, zz):
        loading(m, g, zz).wait()
        b_copy(m, g, zz).wait_recv()
        acc[g][m, zz] = acc[g][m, zz] + got_b[g][m, zz]

    def add_z(m, g, zz, slot):
        z_recv(m, g, slot)
        if GROUPS[g][2] == 0:
            acc[g][m, zz] = acc[g][m, zz] + got_z[g][m, slot]
        else:
            acc[g][m, zz, first(g)] = acc[g][m, zz, first(g)] + got_z[g][m, slot]

    def add_a(m, g, zz):
        a_copy(m, g, zz, zz).wait_recv()
        acc[g][m, zz, first(g)] = acc[g][m, zz, first(g)] + got_a[g][m, zz]

    def move_up(m, g, zz):
        when(down, lambda: add_z(m, g, zz, zz))
        z_copy(m, g, zz, zz, above).start()

    def move_down(m, g, zz, k):
        when(up, lambda: add_z(m, g, zz, zz))
        z_copy(m, g, zz, jnp.where(k == 1, line, zz), below).start()

    @pl.loop(0, line)
    def _(j):
        k = line - 1 - j

        def near(m, zz):
            for g in range(4):
                add_b(m, g, zz)
                if GROUPS[g][2] == 1:
                    a_copy(m, g, zz, zz).start()

        def go_up(m, gs, k):
            zz = jnp.minimum(z + k, line - 1)
            for g in gs:
                if GROUPS[g][2] == 1:
                    add_a(m, g, zz)
                move_up(m, g, zz)

        def go_down(m, gs, k):
            zz = jnp.maximum(z - k, 0)
            for g in gs:
                if GROUPS[g][2] == 1:
                    add_a(m, g, zz)
                move_down(m, g, zz, k)

        for m in range(count):
            when(z + k < line, lambda: near(m, jnp.minimum(z + k, line - 1)))
            when((z >= k) & (k > 0), lambda: near(m, jnp.maximum(z - k, 0)))
            when((k > 0) & (z + k < line), lambda: go_up(m, (0, 1), k))
            when((k > 0) & (z >= k), lambda: go_down(m, (0, 1), k))
            when((j > 0) & (z + k + 1 < line), lambda: go_up(m, (2, 3), k + 1))
            when((j > 0) & (z >= k + 1), lambda: go_down(m, (2, 3), k + 1))

    for m in range(count):
        for g in (0, 1):
            when(down, lambda: add_z(m, g, z, z))
            when(up, lambda: add_z(m, g, z, line))
            a_copy(m, g, z, z).start()
    for m in range(count):
        for g in (2, 3):
            add_a(m, g, z)
            when(down, lambda: add_z(m, g, z, z))
            when(up, lambda: add_z(m, g, z, line))
            out[m, :, cols(g)] = acc[g][m, z, first(g)]
        for g in (0, 1):
            a_copy(m, g, z, z).wait_recv()
            out[m, :, cols(g)] = acc[g][m, z, first(g)] + got_a[g][m, z]

    def finish(m, zz):
        for g in range(4):
            b_copy(m, g, zz).wait_send()
            if GROUPS[g][2] == 1:
                a_copy(m, g, zz, zz).wait_send()
            when(zz != z, lambda: z_copy(m, g, zz, zz, above).wait_send())

    each(finish)
    for m in range(count):
        for g in (0, 1):
            a_copy(m, g, z, z).wait_send()


def reduce_grads(grads, n, collective_id):
    line = n // 4
    count = len(grads)
    rows, cols = grads[0].shape[-2:]
    dt = grads[0].dtype
    dma = pltpu.SemaphoreType.DMA
    acc = [pltpu.VMEM((count, line, 2, rows, GROUPS[g][1]), dt) for g in range(4)]
    got_z = [pltpu.VMEM((count, line + 1) + ((2,) if GROUPS[g][2] == 0 else ()) + (rows, GROUPS[g][1]), dt) for g in range(4)]
    got_a = [pltpu.VMEM((count, line, rows, GROUPS[g][1]), dt) for g in range(4)]
    return pl.pallas_call(
        functools.partial(reduce_kernel, line),
        out_shape=jax.ShapeDtypeStruct((count, rows, cols), dt),
        in_specs=[pl.BlockSpec(memory_space=pltpu.HBM)] * count,
        out_specs=pl.BlockSpec(memory_space=pltpu.VMEM),
        scratch_shapes=acc + acc + got_z + got_a + [dma((count, 4, line))] * 5 + [dma((count, 4, line + 1))] + [dma((count, 4, line))] + [dma((1,))],
        compiler_params=pltpu.CompilerParams(collective_id=collective_id, has_side_effects=True, vmem_limit_bytes=48 * 2**20),
        cost_estimate=pl.CostEstimate(flops=0, bytes_accessed=2 * count * n * rows * cols * 2, transcendentals=0),
        name="reduce_grads",
    )(*grads)


def exchange_kernel(n, spread, *refs):
    count = len(spread)
    srcs, outs, (send, recv) = refs[:count], refs[count:2 * count], refs[2 * count:]
    me, c = lax.axis_index("dp"), lax.axis_index("seq")
    bar = pltpu.get_barrier_semaphore()

    @pl.loop(1, n)
    def _(j):
        pl.semaphore_signal(bar, inc=1, device_id=((me + j) % n, c), device_id_type=MESH)

    for a in range(count):
        outs[a][me] = srcs[a][me] if spread[a] else srcs[a][...]
    pl.semaphore_wait(bar, n - 1)

    def copy(a, j, there, slot):
        return pltpu.make_async_remote_copy(
            src_ref=srcs[a].at[there] if spread[a] else srcs[a], dst_ref=outs[a].at[slot],
            send_sem=send.at[a, j], recv_sem=recv.at[a, slot], device_id=(there, c), device_id_type=MESH)

    @pl.loop(1, n)
    def _(j):
        for a in range(count):
            copy(a, j, (me + j) % n, me).start()

    @pl.loop(1, n)
    def _(j):
        for a in range(count):
            copy(a, j, (me + j) % n, (me + n - j) % n).wait()


def exchange(blocks, spread, n, collective_id):
    count = len(blocks)
    parts = [b.shape[1:] if s else b.shape for b, s in zip(blocks, spread)]
    dma = pltpu.SemaphoreType.DMA
    return pl.pallas_call(
        functools.partial(exchange_kernel, n, spread),
        out_shape=[jax.ShapeDtypeStruct((n,) + p, b.dtype) for p, b in zip(parts, blocks)],
        in_specs=[pl.BlockSpec(memory_space=pltpu.VMEM)] * count,
        out_specs=[pl.BlockSpec(memory_space=pltpu.VMEM)] * count,
        scratch_shapes=[dma((count, n)), dma((count, n))],
        compiler_params=pltpu.CompilerParams(collective_id=collective_id, has_side_effects=True, vmem_limit_bytes=32 * 2**20),
        name="exchange",
    )(*blocks)


def grid_embed(keep_index, width):
    quarter = width // 4
    freqs = 10000.0 ** (-jnp.arange(quarter).astype(jnp.float32) / quarter)
    across = (keep_index // SIDE).astype(jnp.float32)[..., None] * freqs
    along = (keep_index % SIDE).astype(jnp.float32)[..., None] * freqs
    return jnp.concatenate(
        [jnp.sin(across), jnp.cos(across), jnp.sin(along), jnp.cos(along)], axis=-1
    )


def normalize(values):
    centre = values - jnp.mean(values, axis=-1, keepdims=True)
    spread = jnp.mean(centre * centre, axis=-1, keepdims=True)
    return centre * lax.rsqrt(spread + LAYER_EPS)


def modulated(values, shift, scale):
    return normalize(values) * (1.0 + scale) + shift


def gelu_tanh(values):
    return jax.nn.gelu(values, approximate=True)


def adam_step(grad, master, first, second, rate):
    first_new = BETA_FIRST * first + (1.0 - BETA_FIRST) * grad
    second_new = BETA_SECOND * second + (1.0 - BETA_SECOND) * grad * grad
    first_hat = first_new / (1.0 - BETA_FIRST**STEP)
    second_hat = second_new / (1.0 - BETA_SECOND**STEP)
    master_new = master - rate * (
        first_hat / (jnp.sqrt(second_hat) + ADAM_EPS) + WEIGHT_DECAY * master
    )
    return (first_new, second_new, master_new)


def per_device(
    tokens,
    cotangent,
    time_vec,
    labels,
    kept,
    keep_index,
    modulation_master,
    modulation_first,
    modulation_second,
    attention_in_master,
    attention_in_first,
    attention_in_second,
    attention_out_master,
    attention_out_first,
    attention_out_second,
    expand_master,
    expand_first,
    expand_second,
    contract_master,
    contract_first,
    contract_second,
    class_table_master,
    class_table_first,
    class_table_second,
    biases_master,
    biases_first,
    biases_second,
):
    rows, width = tokens.shape[1:]
    n, pairs = lax.axis_size("dp"), lax.axis_size("seq")
    me, c = lax.axis_index("dp"), lax.axis_index("seq")
    own_rows = width // n
    half_width, half_ff = width // pairs, FF // pairs
    low = jnp.bfloat16

    def flipped(values):
        return lax.ppermute(values, "seq", [(i, (i + 1) % pairs) for i in range(pairs)])

    def rows_all(values):
        return lax.all_gather(values, "seq", axis=0, tiled=True)

    def rows_own(partial):
        mine = lax.dynamic_slice_in_dim(partial, c * rows, rows, 0)
        return mine + flipped(lax.dynamic_slice_in_dim(partial, (1 - c) * rows, rows, 0))

    def my_half(values, parts):
        shaped = values.reshape(values.shape[0], parts, pairs, -1)
        return lax.dynamic_index_in_dim(shaped, c, 2, keepdims=False).reshape(values.shape[0], -1)

    def part_of(vector):
        return lax.dynamic_slice_in_dim(vector, c * (vector.shape[0] // pairs), vector.shape[0] // pairs, 0)

    own_attn = jnp.concatenate(
        [
            my_half(attention_in_master.reshape(own_rows, 3 * width), 3),
            my_half(attention_out_master.reshape(own_rows, width), 1),
        ],
        axis=1,
    )
    own_expand = my_half(expand_master.reshape(own_rows, FF), 1)
    own_contract = my_half(contract_master.reshape(own_rows, FF), 1)
    pieces_own = jnp.stack([own_attn, own_expand, own_contract]).astype(low)
    weights = gather_weights(pieces_own, n, 1).reshape(3, width, pieces_own.shape[2])
    weight_in = weights[0, :, : 3 * half_width]
    weight_out = weights[0, :, 3 * half_width :]
    weight_expand, weight_contract = weights[1], weights[2]

    bias_share = biases_master.shape[0]
    bias_block = jnp.pad(biases_master.astype(low).astype(jnp.float32), (0, 1024 - bias_share)).reshape(8, 128)
    label_block = jnp.broadcast_to(labels.astype(jnp.float32)[:, None], (8, 128))
    (got,) = exchange([jnp.concatenate([bias_block, label_block])], (False,), n, 3)
    biases = got[:, :8].reshape(n, 1024)[:, :bias_share].reshape(-1)
    labels_all = got[:, 8, 0].astype(jnp.int32)
    bias_mod = biases[: 6 * width]
    bias_query = biases[6 * width : 7 * width]
    bias_value = biases[7 * width : 8 * width]
    bias_out = biases[8 * width : 9 * width]
    bias_expand = biases[9 * width : 9 * width + FF]
    bias_contract = biases[9 * width + FF :]

    class_rows = CLASSES // n
    table = class_table_master.reshape(class_rows, width).astype(low)
    onehot = labels_all[:, None] == me * class_rows + jnp.arange(class_rows)[None, :]
    part = jnp.dot(onehot.astype(low), table, preferred_element_type=jnp.float32)
    part = part + jnp.where(jnp.arange(n)[:, None] == me, time_vec.astype(jnp.float32), 0.0)
    part = part.reshape(n, n, own_rows).transpose(1, 0, 2)
    part = jnp.pad(part, ((0, 0), (0, 0), (0, 128 - own_rows)))
    (got,) = exchange([part], (True,), n, 4)
    cond_own = jnp.sum(got, axis=0)[:, :own_rows]
    silu_own = jax.nn.silu(cond_own).astype(low)
    own_modulation = my_half(modulation_master.reshape(own_rows, 6 * width), 1).astype(low)
    part = jnp.dot(silu_own, own_modulation, preferred_element_type=jnp.float32).reshape(n, 3 * width // 128, 128)
    (got,) = exchange([jnp.pad(part, ((0, 0), (0, -part.shape[1] % 8), (0, 0)))], (True,), n, 5)
    mod_half = jnp.sum(got, axis=0)[: 3 * width // 128].reshape(-1) + part_of(bias_mod)
    pieces = lax.all_gather(mod_half.reshape(1, 3, width), "seq", axis=0, tiled=True).reshape(6, 1, width)

    inputs = tokens[0].astype(jnp.float32) + grid_embed(keep_index[0], width)
    half_kept = kept // pairs
    row_ok = jnp.arange(rows) < half_kept
    key_ok = (jnp.arange(rows * pairs) % rows) < half_kept
    normed_in = rows_all(modulated(inputs, pieces[0], pieces[1]).astype(low))
    projected = jnp.dot(normed_in, weight_in, preferred_element_type=jnp.float32)

    def split_heads(values):
        return values.reshape(values.shape[0], half_width // HEAD_DIM, HEAD_DIM)

    queries = split_heads((projected[:, :half_width] + part_of(bias_query)).astype(low))
    keys = split_heads(projected[:, half_width : 2 * half_width].astype(low))
    values = split_heads((projected[:, 2 * half_width :] + part_of(bias_value)).astype(low))
    scale = HEAD_DIM ** (-0.5)
    logits = jnp.einsum("rhe,ghe->hrg", queries, keys, preferred_element_type=jnp.float32) * scale
    logits = jnp.where(key_ok[None, None, :], logits, MASK_FILL)
    expo = jnp.exp(logits - jnp.max(logits, axis=-1, keepdims=True))
    probs = expo / jnp.sum(expo, axis=-1, keepdims=True)
    probs_low = probs.astype(low)
    mixed = jnp.einsum("hrg,ghe->rhe", probs_low, values, preferred_element_type=jnp.float32)
    mixed = mixed.reshape(rows * pairs, half_width).astype(low)

    def times_transposed(left, right):
        return lax.dot_general(left, right, (((1,), (1,)), ((), ())), preferred_element_type=jnp.float32)

    def contract_rows(left, right):
        return lax.dot_general(
            left, right, (((0,), (0,)), ((), ())), preferred_element_type=jnp.float32
        )

    attended = rows_own(times_transposed(mixed, weight_out)) + bias_out
    middle = inputs + pieces[2] * attended
    normed_mid = rows_all(modulated(middle, pieces[3], pieces[4]).astype(low))
    hidden = jnp.dot(normed_mid, weight_expand, preferred_element_type=jnp.float32) + part_of(bias_expand)
    activated = gelu_tanh(hidden).astype(low)
    branch = rows_own(times_transposed(activated, weight_contract)) + bias_contract
    result = middle + pieces[5] * branch
    block_out = jnp.where(row_ok[:, None], result, 0.0).astype(low)[None]

    grad_out = cotangent[0].astype(jnp.float32) * row_ok[:, None].astype(jnp.float32)
    d_branch = rows_all((pieces[5] * grad_out).astype(low))
    d_gate_mlp = jnp.sum(grad_out * branch, axis=0, keepdims=True)
    grad_contract = contract_rows(d_branch, activated).astype(low)
    grad_bias_contract = jnp.sum(d_branch.astype(jnp.float32), axis=0)
    d_activated = jnp.dot(d_branch, weight_contract, preferred_element_type=jnp.float32)
    d_hidden = jax.vjp(gelu_tanh, hidden)[1](d_activated)[0].astype(low)
    grad_expand = contract_rows(normed_mid, d_hidden).astype(low)
    grad_bias_expand = jnp.sum(d_hidden.astype(jnp.float32), axis=0)
    d_normed_mid = rows_own(times_transposed(d_hidden, weight_expand))
    d_middle, d_shift_mlp, d_scale_mlp = jax.vjp(modulated, middle, pieces[3], pieces[4])[1](d_normed_mid)
    d_middle = d_middle + grad_out
    d_attended = rows_all((pieces[2] * d_middle).astype(low))
    d_gate_attn = jnp.sum(d_middle * attended, axis=0, keepdims=True)
    grad_attention_out = contract_rows(d_attended, mixed)
    grad_bias_out = jnp.sum(d_attended.astype(jnp.float32), axis=0)
    d_mixed = split_heads(jnp.dot(d_attended, weight_out, preferred_element_type=jnp.float32).astype(low))
    d_probs = jnp.einsum("rhe,ghe->hrg", d_mixed, values, preferred_element_type=jnp.float32)
    inner = jnp.sum(probs * d_probs, axis=-1, keepdims=True)
    d_logits = (probs * (d_probs - inner)).astype(low)
    d_query = jnp.einsum("hrg,ghe->rhe", d_logits, keys, preferred_element_type=jnp.float32) * scale
    d_key = jnp.einsum("hrg,rhe->ghe", d_logits, queries, preferred_element_type=jnp.float32) * scale
    d_value = jnp.einsum("hrg,rhe->ghe", probs_low, d_mixed, preferred_element_type=jnp.float32)
    d_projected = jnp.concatenate(
        [item.reshape(rows * pairs, half_width) for item in (d_query, d_key, d_value)], axis=-1
    ).astype(low)
    grad_attention_in = contract_rows(normed_in, d_projected)
    bias_sums = jnp.sum(d_projected.astype(jnp.float32), axis=0)
    grad_attn = jnp.concatenate([grad_attention_in, grad_attention_out], axis=1).astype(low)
    d_normed_in = rows_own(times_transposed(d_projected, weight_in))
    d_inputs, d_shift_attn, d_scale_attn = jax.vjp(modulated, inputs, pieces[0], pieces[1])[1](d_normed_in)
    tokens_grad = (d_inputs + d_middle).astype(low)[None]

    shape = (n // 4, 2, 2, own_rows, pieces_own.shape[2])
    reduced = reduce_grads([g.reshape(shape) for g in (grad_attn, grad_expand, grad_contract)], n, 2)
    both = lax.all_gather(reduced, "seq", axis=0)

    d_pieces = jnp.concatenate(
        [d_shift_attn, d_scale_attn, d_gate_attn, d_shift_mlp, d_scale_mlp, d_gate_mlp], axis=0
    ).reshape(6 * width)
    d_mod = lax.psum(d_pieces, "seq").astype(low).astype(jnp.float32)

    def at_half(vector):
        whole = jnp.zeros((vector.shape[0] * pairs,), jnp.float32)
        return lax.dynamic_update_slice_in_dim(whole, vector, c * vector.shape[0], 0)

    once = (c == 0).astype(jnp.float32)
    grad_biases = jnp.concatenate(
        [
            d_mod * once,
            at_half(bias_sums[:half_width]),
            at_half(bias_sums[2 * half_width :]),
            grad_bias_out * once,
            at_half(grad_bias_expand),
            grad_bias_contract * once,
        ]
    )
    bias_parts = jnp.pad(grad_biases.reshape(n, bias_share), ((0, 0), (0, 1024 - bias_share))).reshape(n, 8, 128)
    d_mod_block = jnp.pad(d_mod.reshape(-1, 128), ((0, -(6 * width // 128) % 8), (0, 0)))
    d_mod_got, bias_got = exchange([d_mod_block, bias_parts], (False, True), n, 6)
    biases_shard = lax.psum(jnp.sum(bias_got, axis=0), "seq").reshape(1024)[:bias_share]
    d_mod_all = d_mod_got[:, : 6 * width // 128].reshape(n, 6 * width).astype(low)
    d_silu = times_transposed(
        lax.dynamic_slice_in_dim(d_mod_all, c * 3 * width, 3 * width, 1), own_modulation
    )
    d_silu = lax.psum(d_silu, "seq")
    d_cond_own = jax.vjp(jax.nn.silu, cond_own)[1](d_silu)[0]
    (got,) = exchange([jnp.pad(d_cond_own, ((0, 0), (0, 128 - own_rows)))], (False,), n, 7)
    d_cond = got[:, :, :own_rows].transpose(1, 0, 2).reshape(n, width)
    grad_table = jnp.dot(onehot.astype(jnp.float32).T, d_cond, precision=lax.Precision.HIGHEST)
    grad_modulation = contract_rows(silu_own, d_mod_all)

    in_shard = both[:, 0, :, : 3 * half_width].reshape(pairs, own_rows, 3, half_width).transpose(1, 2, 0, 3)
    out_shard = both[:, 0, :, 3 * half_width :].transpose(1, 0, 2)
    shards = (
        grad_modulation.reshape(-1),
        in_shard.astype(jnp.float32).reshape(-1),
        out_shard.astype(jnp.float32).reshape(-1),
        both[:, 1].transpose(1, 0, 2).astype(jnp.float32).reshape(-1),
        both[:, 2].transpose(1, 0, 2).astype(jnp.float32).reshape(-1),
        grad_table.reshape(-1),
        biases_shard,
    )
    squares = jnp.sum(shards[0] * shards[0])
    for shard in shards[1:]:
        squares = squares + jnp.sum(shard * shard)
    (got,) = exchange([jnp.broadcast_to(squares, (8, 128))], (False,), n, 8)
    grad_norm = jnp.sqrt(jnp.sum(got[:, 0, 0]))
    factor = jnp.minimum(1.0, CLIP_LIMIT / (grad_norm + 1e-06))
    rates = (
        width ** (-0.5),
        width ** (-0.5),
        (width // 4) ** (-0.5),
        width ** (-0.5),
        FF ** (-0.5),
        0.5,
        0.2,
    )
    masters = (
        modulation_master,
        attention_in_master,
        attention_out_master,
        expand_master,
        contract_master,
        class_table_master,
        biases_master,
    )
    firsts = (
        modulation_first,
        attention_in_first,
        attention_out_first,
        expand_first,
        contract_first,
        class_table_first,
        biases_first,
    )
    seconds = (
        modulation_second,
        attention_in_second,
        attention_out_second,
        expand_second,
        contract_second,
        class_table_second,
        biases_second,
    )
    updated = [
        adam_step(shard * factor, master, first, second, rate)
        for shard, master, first, second, rate in zip(shards, masters, firsts, seconds, rates)
    ]
    return (block_out, tokens_grad, grad_norm) + tuple(item for step in updated for item in step)


def solution(mesh):
    return jax.shard_map(
        per_device,
        mesh=mesh,
        in_specs=(
            P("dp", "seq", None),
            P("dp", "seq", None),
            P("dp", None),
            P("dp"),
            P("dp"),
            P("dp", "seq"),
            P("dp"),
            P("dp"),
            P("dp"),
            P("dp"),
            P("dp"),
            P("dp"),
            P("dp"),
            P("dp"),
            P("dp"),
            P("dp"),
            P("dp"),
            P("dp"),
            P("dp"),
            P("dp"),
            P("dp"),
            P("dp"),
            P("dp"),
            P("dp"),
            P("dp"),
            P("dp"),
            P("dp"),
        ),
        out_specs=(
            P("dp", "seq", None),
            P("dp", "seq", None),
            P(),
            P("dp"),
            P("dp"),
            P("dp"),
            P("dp"),
            P("dp"),
            P("dp"),
            P("dp"),
            P("dp"),
            P("dp"),
            P("dp"),
            P("dp"),
            P("dp"),
            P("dp"),
            P("dp"),
            P("dp"),
            P("dp"),
            P("dp"),
            P("dp"),
            P("dp"),
            P("dp"),
            P("dp"),
        ),
        check_vma=False,
    )
```

```python
import functools
import jax
import jax.numpy as jnp
from jax import lax
from jax.experimental import pallas as pl
from jax.experimental.pallas import tpu as pltpu
from jax.sharding import PartitionSpec as P

HEAD_DIM = 72
FF = 4608
SIDE = 16
CLASSES = 1024
STEP = 10
LAYER_EPS = 1e-06
MASK_FILL = -1e30
BETA_FIRST = 0.5
BETA_SECOND = 0.5
ADAM_EPS = 1e-08
WEIGHT_DECAY = 0.1
CLIP_LIMIT = 1.0

MESH = pl.DeviceIdType.MESH
GROUPS = ((0, 768, 0, "x"), (768, 768, 0, "y"), (1536, 384, 1, "x"), (1920, 384, 1, "y"))


def when(cond, fn):
    pl.when(cond)(fn)


class Place:
    def __init__(self, line):
        self.line = line
        i = lax.axis_index("dp")
        self.c = lax.axis_index("seq")
        self.x, self.y, self.z = i % 2, (i // 2) % 2, i // 4

    def dev(self, z=None, y=None, x=None):
        z = self.z if z is None else z
        y = self.y if y is None else y
        x = self.x if x is None else x
        return (z * 4 + y * 2 + x, self.c)

    def peer(self, axis):
        return self.dev(x=1 - self.x) if axis == "x" else self.dev(y=1 - self.y)

    def barrier(self):
        bar = pltpu.get_barrier_semaphore()

        def sig(dev):
            pl.semaphore_signal(bar, inc=1, device_id=dev, device_id_type=MESH)

        sig(self.peer("x"))
        sig(self.peer("y"))
        when(self.z > 0, lambda: sig(self.dev(z=self.z - 1)))
        when(self.z < self.line - 1, lambda: sig(self.dev(z=self.z + 1)))
        pl.semaphore_wait(bar, 2 + (self.z > 0).astype(jnp.int32) + (self.z < self.line - 1).astype(jnp.int32))


def gather_kernel(line, src, out, own_sem, send_a, send_u, send_d, send_b, recv_a, recv_z, recv_b):
    me = Place(line)
    count = src.shape[0]
    x, y, z = me.x, me.y, me.z

    def single(m, g, zz, yy=None, xx=None):
        lo, width = GROUPS[g][:2]
        return out.at[m, zz, y if yy is None else yy, x if xx is None else xx, :, pl.ds(lo, width)]

    def pair(m, g, zz):
        lo, width, _, first = GROUPS[g]
        if first == "x":
            return out.at[m, zz, y, :, :, pl.ds(lo, width)]
        return out.at[m, zz, :, x, :, pl.ds(lo, width)]

    def remote(ref, send, recv, dev, source=None):
        return pltpu.make_async_remote_copy(
            src_ref=ref if source is None else source, dst_ref=ref, send_sem=send, recv_sem=recv,
            device_id=dev, device_id_type=MESH)

    def own(m, g):
        lo, width = GROUPS[g][:2]
        return src.at[m, :, pl.ds(lo, width)]

    def a_copy(m, g, zz, source=None):
        return remote(single(m, g, zz), send_a.at[m, g, zz], recv_a.at[m, g, zz], me.peer(GROUPS[g][3]), source)

    def z_ref(m, g, zz):
        return pair(m, g, zz) if GROUPS[g][2] == 0 else single(m, g, zz)

    def u_copy(m, g, zz, source=None):
        return remote(z_ref(m, g, zz), send_u.at[m, g, zz], recv_z.at[m, g, zz], me.dev(z=jnp.minimum(z + 1, line - 1)), source)

    def d_copy(m, g, zz, source=None):
        return remote(z_ref(m, g, zz), send_d.at[m, g, zz], recv_z.at[m, g, zz], me.dev(z=jnp.maximum(z - 1, 0)), source)

    def b_copy(m, g, zz):
        last = "y" if GROUPS[g][3] == "x" else "x"
        return remote(pair(m, g, zz), send_b.at[m, g, zz], recv_b.at[m, g, zz], me.peer(last))

    def keep(m):
        return pltpu.make_async_copy(src.at[m], out.at[m, z, y, x], own_sem.at[m])

    up, down = z < line - 1, z > 0

    @pl.loop(0, count)
    def _(m):
        keep(m).start()

    me.barrier()

    @pl.loop(0, count)
    def _(m):
        for g in range(4):
            a_copy(m, g, z, own(m, g)).start()
        for g in (2, 3):
            when(up, lambda g=g: u_copy(m, g, z, own(m, g)).start())
            when(down, lambda g=g: d_copy(m, g, z, own(m, g)).start())

    @pl.loop(0, count)
    def _(m):
        keep(m).wait()
        for g in (0, 1):
            a_copy(m, g, z).wait_recv()
            when(up, lambda g=g: u_copy(m, g, z).start())
            when(down, lambda g=g: d_copy(m, g, z).start())
            b_copy(m, g, z).start()

    def arrive(m, k, zz, onward, go):
        for g in range(4):
            copy = u_copy if go == "u" else d_copy
            copy(m, g, zz).wait_recv()
            when(onward, lambda g=g: copy(m, g, zz).start())
            if GROUPS[g][2] == 0:
                b_copy(m, g, zz).start()
            else:
                a_copy(m, g, zz).start()

    def crossed(m, zz):
        for g in (2, 3):
            a_copy(m, g, zz).wait_recv()
            b_copy(m, g, zz).start()

    @pl.loop(1, line + 1)
    def _(k):
        @pl.loop(0, count)
        def _(m):
            when(k <= z, lambda: arrive(m, k, jnp.maximum(z - k, 0), up, "u"))
            when(z + k < line, lambda: arrive(m, k, jnp.minimum(z + k, line - 1), down, "d"))
            when(k - 1 <= z, lambda: crossed(m, jnp.maximum(z - k + 1, 0)))
            when((k > 1) & (z + k - 1 < line), lambda: crossed(m, jnp.minimum(z + k - 1, line - 1)))

    @pl.loop(0, count)
    def _(m):
        @pl.loop(0, line)
        def _(zz):
            for g in range(4):
                b_copy(m, g, zz).wait()
                if GROUPS[g][2] == 1:
                    a_copy(m, g, zz).wait_send()
                when(up & (zz <= z), lambda g=g: u_copy(m, g, zz).wait_send())
                when(down & (zz >= z), lambda g=g: d_copy(m, g, zz).wait_send())
        for g in (0, 1):
            a_copy(m, g, z).wait_send()


def gather_weights(src, n, collective_id):
    count, rows, cols = src.shape
    line = n // 4
    dma = pltpu.SemaphoreType.DMA
    return pl.pallas_call(
        functools.partial(gather_kernel, line),
        out_shape=jax.ShapeDtypeStruct((count, line, 2, 2, rows, cols), src.dtype),
        in_specs=[pl.BlockSpec(memory_space=pltpu.HBM)],
        out_specs=pl.BlockSpec(memory_space=pltpu.HBM),
        scratch_shapes=[dma((count,))] + [dma((count, 4, line))] * 7,
        compiler_params=pltpu.CompilerParams(collective_id=collective_id, has_side_effects=True),
        cost_estimate=pl.CostEstimate(flops=0, bytes_accessed=2 * count * n * rows * cols * 2, transcendentals=0),
        name="gather_weights",
    )(src)


def reduce_kernel(line, *refs):
    count = len(refs) - 1 - 16 - 7
    grads = refs[:count]
    out = refs[count]
    s = count + 1
    acc, got_b, got_z, got_a = (refs[s + 4 * i:s + 4 * i + 4] for i in range(4))
    load, send_b, send_z, send_a, recv_b, recv_z, recv_a = refs[s + 16:]
    me = Place(line)
    x, y, z = me.x, me.y, me.z
    up, down = z < line - 1, z > 0
    above, below = me.dev(z=jnp.minimum(z + 1, line - 1)), me.dev(z=jnp.maximum(z - 1, 0))

    def cols(g):
        return pl.ds(GROUPS[g][0], GROUPS[g][1])

    def last(g):
        return "y" if GROUPS[g][3] == "x" else "x"

    def half(grad, g, zz, mine):
        if last(g) == "y":
            return grad.at[zz, y if mine else 1 - y, :, :, cols(g)]
        return grad.at[zz, :, x if mine else 1 - x, :, cols(g)]

    def first(g):
        return x if GROUPS[g][3] == "x" else y

    def loading(m, g, zz, grad=grads[0]):
        return pltpu.make_async_copy(half(grad, g, zz, True), acc[g].at[m, zz], load.at[m, g, zz])

    def remote(src, dst, send, recv, dev):
        return pltpu.make_async_remote_copy(
            src_ref=src, dst_ref=dst, send_sem=send, recv_sem=recv, device_id=dev, device_id_type=MESH)

    def b_copy(m, g, zz, grad=grads[0]):
        return remote(half(grad, g, zz, False), got_b[g].at[m, zz], send_b.at[m, g, zz], recv_b.at[m, g, zz], me.peer(last(g)))

    def a_copy(m, g, zz):
        return remote(acc[g].at[m, zz, 1 - first(g)], got_a[g].at[m, zz], send_a.at[m, g, zz], recv_a.at[m, g, zz], me.peer(GROUPS[g][3]))

    def z_copy(m, g, zz, slot, dev):
        part = acc[g].at[m, zz] if GROUPS[g][2] == 0 else acc[g].at[m, zz, first(g)]
        return remote(part, got_z[g].at[m, slot], send_z.at[m, g, zz], recv_z.at[m, g, slot], dev)

    def add_b(m, g, zz):
        loading(m, g, zz).wait()
        b_copy(m, g, zz).wait_recv()
        acc[g][m, zz] = acc[g][m, zz] + got_b[g][m, zz]

    def add_z(m, g, zz, slot):
        z_copy(m, g, z, slot, below).wait_recv()
        if GROUPS[g][2] == 0:
            acc[g][m, zz] = acc[g][m, zz] + got_z[g][m, slot]
        else:
            acc[g][m, zz, first(g)] = acc[g][m, zz, first(g)] + got_z[g][m, slot]

    def add_a(m, g, zz):
        a_copy(m, g, zz).wait_recv()
        acc[g][m, zz, first(g)] = acc[g][m, zz, first(g)] + got_a[g][m, zz]

    def planes(k, fn):
        when(z + k < line, lambda: fn(jnp.minimum(z + k, line - 1), True))
        when((z >= k) & (k > 0), lambda: fn(jnp.maximum(z - k, 0), False))

    def begin(m, j):
        def one(grad, zz):
            for g in range(4):
                b_copy(m, g, zz, grad).start()
                loading(m, g, zz, grad).start()

        for index, grad in enumerate(grads):
            when(m == index, lambda: planes(line - 1 - j, lambda zz, upward: one(grad, zz)))

    def onward(m, g, zz, k, upward):
        if upward:
            when(down, lambda: add_z(m, g, zz, zz))
            z_copy(m, g, zz, zz, above).start()
        else:
            when(up, lambda: add_z(m, g, zz, zz))
            z_copy(m, g, zz, jnp.where(k == 1, line, zz), below).start()

    def near(m, j):
        k = line - 1 - j

        def one(zz, upward):
            for g in range(4):
                add_b(m, g, zz)
                if GROUPS[g][2] == 1:
                    a_copy(m, g, zz).start()
                else:
                    when(k > 0, lambda g=g: onward(m, g, zz, k, upward))

        planes(k, one)

    def far(m, j):
        k = line - j

        def one(zz, upward):
            for g in (2, 3):
                add_a(m, g, zz)
                onward(m, g, zz, k, upward)

        when((k > 0) & (k < line), lambda: planes(k, one))

    def close(m):
        for g in (0, 1):
            when(down, lambda g=g: add_z(m, g, z, z))
            when(up, lambda g=g: add_z(m, g, z, line))
            a_copy(m, g, z).start()

    def final(m):
        for g in (2, 3):
            add_a(m, g, z)
            when(down, lambda g=g: add_z(m, g, z, z))
            when(up, lambda g=g: add_z(m, g, z, line))
            out[m, :, cols(g)] = acc[g][m, z, first(g)]
        for g in (0, 1):
            a_copy(m, g, z).wait_recv()
            out[m, :, cols(g)] = acc[g][m, z, first(g)] + got_a[g][m, z]

    me.barrier()
    begin(0, 0)
    if line > 1:
        begin(0, 1)
    units = count * line

    @pl.loop(0, units)
    def _(u):
        m, j = u // line, u % line
        v = u + 2
        when(v < units, lambda: begin(jnp.minimum(v // line, count - 1), v % line))
        near(m, j)
        far(m, j)
        when(j == line - 1, lambda: close(m))
        when((j == 0) & (m > 0), lambda: final(jnp.maximum(m - 1, 0)))

    final(count - 1)

    @pl.loop(0, count)
    def _(m):
        @pl.loop(0, line)
        def _(zz):
            for g in range(4):
                b_copy(m, g, zz).wait_send()
                if GROUPS[g][2] == 1:
                    a_copy(m, g, zz).wait_send()
                when(zz != z, lambda g=g: z_copy(m, g, zz, zz, above).wait_send())
        for g in (0, 1):
            a_copy(m, g, z).wait_send()


def reduce_grads(grads, n, collective_id):
    line = n // 4
    count = len(grads)
    rows, cols = grads[0].shape[-2:]
    dt = grads[0].dtype
    dma = pltpu.SemaphoreType.DMA
    acc = [pltpu.VMEM((count, line, 2, rows, GROUPS[g][1]), dt) for g in range(4)]
    got_z = [pltpu.VMEM((count, line + 1) + ((2,) if GROUPS[g][2] == 0 else ()) + (rows, GROUPS[g][1]), dt) for g in range(4)]
    got_a = [pltpu.VMEM((count, line, rows, GROUPS[g][1]), dt) for g in range(4)]
    return pl.pallas_call(
        functools.partial(reduce_kernel, line),
        out_shape=jax.ShapeDtypeStruct((count, rows, cols), dt),
        in_specs=[pl.BlockSpec(memory_space=pltpu.HBM)] * count,
        out_specs=pl.BlockSpec(memory_space=pltpu.VMEM),
        scratch_shapes=acc + acc + got_z + got_a + [dma((count, 4, line))] * 5 + [dma((count, 4, line + 1))] + [dma((count, 4, line))],
        compiler_params=pltpu.CompilerParams(collective_id=collective_id, has_side_effects=True, vmem_limit_bytes=48 * 2**20),
        cost_estimate=pl.CostEstimate(flops=0, bytes_accessed=2 * count * n * rows * cols * 2, transcendentals=0),
        name="reduce_grads",
    )(*grads)


def exchange_kernel(n, spread, *refs):
    count = len(spread)
    srcs, outs, (send, recv) = refs[:count], refs[count:2 * count], refs[2 * count:]
    me, c = lax.axis_index("dp"), lax.axis_index("seq")
    bar = pltpu.get_barrier_semaphore()

    @pl.loop(1, n)
    def _(j):
        pl.semaphore_signal(bar, inc=1, device_id=((me + j) % n, c), device_id_type=MESH)

    for a in range(count):
        outs[a][me] = srcs[a][me] if spread[a] else srcs[a][...]
    pl.semaphore_wait(bar, n - 1)

    def copy(a, j, there, slot):
        return pltpu.make_async_remote_copy(
            src_ref=srcs[a].at[there] if spread[a] else srcs[a], dst_ref=outs[a].at[slot],
            send_sem=send.at[a, j], recv_sem=recv.at[a, slot], device_id=(there, c), device_id_type=MESH)

    @pl.loop(1, n)
    def _(j):
        for a in range(count):
            copy(a, j, (me + j) % n, me).start()

    @pl.loop(1, n)
    def _(j):
        for a in range(count):
            copy(a, j, (me + j) % n, (me + n - j) % n).wait()


def exchange(blocks, spread, n, collective_id):
    count = len(blocks)
    parts = [b.shape[1:] if s else b.shape for b, s in zip(blocks, spread)]
    dma = pltpu.SemaphoreType.DMA
    return pl.pallas_call(
        functools.partial(exchange_kernel, n, spread),
        out_shape=[jax.ShapeDtypeStruct((n,) + p, b.dtype) for p, b in zip(parts, blocks)],
        in_specs=[pl.BlockSpec(memory_space=pltpu.VMEM)] * count,
        out_specs=[pl.BlockSpec(memory_space=pltpu.VMEM)] * count,
        scratch_shapes=[dma((count, n)), dma((count, n))],
        compiler_params=pltpu.CompilerParams(collective_id=collective_id, has_side_effects=True, vmem_limit_bytes=32 * 2**20),
        name="exchange",
    )(*blocks)


def adam_step(grad, master, first, second, rate):
    first_new = BETA_FIRST * first + (1.0 - BETA_FIRST) * grad
    second_new = BETA_SECOND * second + (1.0 - BETA_SECOND) * grad * grad
    first_hat = first_new / (1.0 - BETA_FIRST**STEP)
    second_hat = second_new / (1.0 - BETA_SECOND**STEP)
    master_new = master - rate * (
        first_hat / (jnp.sqrt(second_hat) + ADAM_EPS) + WEIGHT_DECAY * master
    )
    return (first_new, second_new, master_new)


def chunk_rows(rows):
    sizes = [d for d in range(8, 257, 8) if rows % d == 0]
    return sizes[-1] if sizes else rows


def finish_kernel(n, rates, *refs):
    kinds = len(rates)
    reduced, silu, d_mod, d_cond, bias_grad, onehot, same = refs[:7]
    states = [refs[7 + 3 * a : 10 + 3 * a] for a in range(kinds)]
    at = 7 + 3 * kinds
    news = [refs[at + 3 * a : at + 3 * a + 3] for a in range(kinds)]
    at += 3 * kinds
    norm_out, at = refs[at], at + 1
    held = refs[at : at + kinds]
    flat = refs[at + kinds : at + 2 * kinds]
    both, wide, block, got, in_sem, out_sem, pair_send, pair_recv, send, recv = refs[at + 2 * kinds :]
    me, c = lax.axis_index("dp"), lax.axis_index("seq")
    rows = reduced.shape[1]
    half = reduced.shape[2]
    head = half // 4

    def loads(a, k):
        return pltpu.make_async_copy(states[a][k], held[a].at[k], in_sem.at[a, k])

    for a in range(kinds):
        for k in range(3):
            loads(a, k).start()

    bar = pltpu.get_barrier_semaphore()
    pl.semaphore_signal(bar, inc=1, device_id=(me, 1 - c), device_id_type=MESH)

    @pl.loop(1, n)
    def _(j):
        pl.semaphore_signal(bar, inc=1, device_id=((me + j) % n, c), device_id_type=MESH)

    both[c] = reduced[...]
    pl.semaphore_wait(bar, n)
    pair = pltpu.make_async_remote_copy(
        src_ref=reduced, dst_ref=both.at[c], send_sem=pair_send, recv_sem=pair_recv,
        device_id=(me, 1 - c), device_id_type=MESH)
    pair.start()

    def spread(a, width):
        total = None
        tiles = width // 128
        for t in range(tiles):
            part = wide[:, 128 * t : 128 * t + 128]
            flat[a][pl.ds(t, rows, stride=tiles), :] = part
            square = part * part
            total = square if total is None else total + square
        return jnp.sum(total)

    wide[...] = lax.dot_general(
        silu[...], d_mod[...], (((0,), (0,)), ((), ())), preferred_element_type=jnp.float32)
    squares = spread(0, wide.shape[1]) + jnp.sum(bias_grad[...] * bias_grad[...])
    pair.wait()
    for core in range(2):
        for part in range(3):
            lo = (2 * part + core) * head
            wide[:, lo : lo + head] = both[core, 0, :, part * head : (part + 1) * head].astype(jnp.float32)
    squares = squares + spread(1, 6 * head)
    for core in range(2):
        wide[:, core * head : (core + 1) * head] = both[core, 0, :, 3 * head :].astype(jnp.float32)
    squares = squares + spread(2, 2 * head)
    for a in (3, 4):
        for core in range(2):
            wide[:, core * half : (core + 1) * half] = both[core, a - 2].astype(jnp.float32)
        squares = squares + spread(a, 2 * half)

    slots = d_cond.shape[0]
    block[:slots] = d_cond[...]
    block[slots:] = jnp.full((8, 128), squares, jnp.float32)
    got[me] = block[...]

    def copy(j, there, slot):
        return pltpu.make_async_remote_copy(
            src_ref=block, dst_ref=got.at[slot], send_sem=send.at[j], recv_sem=recv.at[slot],
            device_id=(there, c), device_id_type=MESH)

    @pl.loop(1, n)
    def _(j):
        copy(j, (me + j) % n, me).start()

    @pl.loop(1, n)
    def _(j):
        copy(j, (me + j) % n, (me + n - j) % n).wait()

    total = jnp.sum(got[:, slots:], axis=0)[:1, :1]
    gram = jnp.zeros((slots, slots), jnp.float32)
    for i in range(n):
        part = got[i, :slots]
        gram = gram + lax.dot_general(
            part, part, (((1,), (1,)), ((), ())), preferred_element_type=jnp.float32, precision=lax.Precision.HIGHEST)
        wide[: onehot.shape[1], i * rows : (i + 1) * rows] = lax.dot_general(
            onehot[...], part, (((0,), (0,)), ((), ())), preferred_element_type=jnp.float32,
            precision=lax.Precision.HIGHEST)[:, :rows]
    total = total + jnp.sum(gram * same[...], keepdims=True)
    norm = jnp.sqrt(total)
    norm_out[...] = jnp.broadcast_to(norm, (8, 128))
    factor = jnp.minimum(1.0, CLIP_LIMIT / (norm + 1e-06))
    tiles = n * rows // 128
    for t in range(tiles):
        flat[5][pl.ds(t, onehot.shape[1], stride=tiles), :] = wide[: onehot.shape[1], 128 * t : 128 * t + 128]

    for a in range(kinds):
        for k in range(3):
            loads(a, k).wait()
        size = chunk_rows(flat[a].shape[0])

        @pl.loop(0, flat[a].shape[0] // size)
        def _(i, a=a, size=size):
            part = pl.ds(pl.multiple_of(i * size, size), size)
            grad = flat[a][part] * factor
            master, first, second = held[a][0, part], held[a][1, part], held[a][2, part]
            first, second, master = adam_step(grad, master, first, second, rates[a])
            held[a][0, part], held[a][1, part], held[a][2, part] = master, first, second
            for k in range(3):
                pltpu.make_async_copy(held[a].at[k, part], news[a][k].at[part], out_sem.at[a, k]).start()

    for a in range(kinds):
        for k in range(3):
            pltpu.make_async_copy(held[a].at[k], news[a][k], out_sem.at[a, k]).wait()


def finish(reduced, silu, d_mod, d_cond, bias_grad, onehot, same, states, rates, n, collective_id):
    vmem, hbm = pl.BlockSpec(memory_space=pltpu.VMEM), pl.BlockSpec(memory_space=pltpu.HBM)
    dma = pltpu.SemaphoreType.DMA
    kinds = len(states)
    rows = reduced.shape[1]
    flats = [jax.ShapeDtypeStruct(s[0].shape, jnp.float32) for s in states]
    block = d_cond.shape[0] + 8
    outs = pl.pallas_call(
        functools.partial(finish_kernel, n, rates),
        out_shape=[f for f in flats for _ in range(3)] + [jax.ShapeDtypeStruct((8, 128), jnp.float32)],
        in_specs=[vmem] * 7 + [hbm] * (3 * kinds),
        out_specs=[hbm] * (3 * kinds) + [vmem],
        scratch_shapes=[pltpu.VMEM((3,) + f.shape, jnp.float32) for f in flats]
        + [pltpu.VMEM(f.shape, jnp.float32) for f in flats]
        + [
            pltpu.VMEM((2,) + reduced.shape, reduced.dtype),
            pltpu.VMEM((rows, d_mod.shape[1]), jnp.float32),
            pltpu.VMEM((block, 128), jnp.float32),
            pltpu.VMEM((n, block, 128), jnp.float32),
            dma((kinds, 3)),
            dma((kinds, 3)),
            dma,
            dma,
            dma((n,)),
            dma((n,)),
        ],
        compiler_params=pltpu.CompilerParams(
            collective_id=collective_id, has_side_effects=True, vmem_limit_bytes=56 * 2**20),
        name="finish",
    )(reduced, silu, d_mod, d_cond, bias_grad, onehot, same, *[item for s in states for item in s])
    order = [3 * a + k for a in range(kinds) for k in (1, 2, 0)]
    return [outs[i] for i in order], outs[-1][0, 0]


def grid_embed(keep_index, width):
    quarter = width // 4
    freqs = 10000.0 ** (-jnp.arange(quarter).astype(jnp.float32) / quarter)
    across = (keep_index // SIDE).astype(jnp.float32)[..., None] * freqs
    along = (keep_index % SIDE).astype(jnp.float32)[..., None] * freqs
    return jnp.concatenate(
        [jnp.sin(across), jnp.cos(across), jnp.sin(along), jnp.cos(along)], axis=-1
    )


def normalize(values):
    centre = values - jnp.mean(values, axis=-1, keepdims=True)
    spread = jnp.mean(centre * centre, axis=-1, keepdims=True)
    return centre * lax.rsqrt(spread + LAYER_EPS)


def modulated(values, shift, scale):
    return normalize(values) * (1.0 + scale) + shift


def gelu_tanh(values):
    return jax.nn.gelu(values, approximate=True)


def per_device(
    tokens,
    cotangent,
    time_vec,
    labels,
    kept,
    keep_index,
    modulation_master,
    modulation_first,
    modulation_second,
    attention_in_master,
    attention_in_first,
    attention_in_second,
    attention_out_master,
    attention_out_first,
    attention_out_second,
    expand_master,
    expand_first,
    expand_second,
    contract_master,
    contract_first,
    contract_second,
    class_table_master,
    class_table_first,
    class_table_second,
    biases_master,
    biases_first,
    biases_second,
):
    rows, width = tokens.shape[1:]
    n, pairs = lax.axis_size("dp"), lax.axis_size("seq")
    me, c = lax.axis_index("dp"), lax.axis_index("seq")
    own_rows = width // n
    half_width, half_ff = width // pairs, FF // pairs
    low = jnp.bfloat16

    def flipped(values):
        return lax.ppermute(values, "seq", [(i, (i + 1) % pairs) for i in range(pairs)])

    def rows_all(values):
        return lax.all_gather(values, "seq", axis=0, tiled=True)

    def rows_own(partial):
        mine = lax.dynamic_slice_in_dim(partial, c * rows, rows, 0)
        return mine + flipped(lax.dynamic_slice_in_dim(partial, (1 - c) * rows, rows, 0))

    def my_half(values, parts):
        shaped = values.reshape(values.shape[0], parts, pairs, -1)
        return lax.dynamic_index_in_dim(shaped, c, 2, keepdims=False).reshape(values.shape[0], -1)

    def part_of(vector):
        return lax.dynamic_slice_in_dim(vector, c * (vector.shape[0] // pairs), vector.shape[0] // pairs, 0)

    own_attn = jnp.concatenate(
        [
            my_half(attention_in_master.reshape(own_rows, 3 * width), 3),
            my_half(attention_out_master.reshape(own_rows, width), 1),
        ],
        axis=1,
    )
    own_expand = my_half(expand_master.reshape(own_rows, FF), 1)
    own_contract = my_half(contract_master.reshape(own_rows, FF), 1)
    pieces_own = jnp.stack([own_attn, own_expand, own_contract]).astype(low)
    weights = gather_weights(pieces_own, n, 1).reshape(3, width, pieces_own.shape[2])
    weight_in = weights[0, :, : 3 * half_width]
    weight_out = weights[0, :, 3 * half_width :]
    weight_expand, weight_contract = weights[1], weights[2]

    bias_share = biases_master.shape[0]
    bias_block = jnp.pad(biases_master.astype(low).astype(jnp.float32), (0, 1024 - bias_share)).reshape(8, 128)
    label_block = jnp.broadcast_to(labels.astype(jnp.float32)[:, None], (8, 128))
    (got,) = exchange([jnp.concatenate([bias_block, label_block])], (False,), n, 3)
    biases = got[:, :8].reshape(n, 1024)[:, :bias_share].reshape(-1)
    labels_all = got[:, 8, 0].astype(jnp.int32)
    bias_mod = biases[: 6 * width]
    bias_query = biases[6 * width : 7 * width]
    bias_value = biases[7 * width : 8 * width]
    bias_out = biases[8 * width : 9 * width]
    bias_expand = biases[9 * width : 9 * width + FF]
    bias_contract = biases[9 * width + FF :]

    class_rows = CLASSES // n
    table = class_table_master.reshape(class_rows, width).astype(low)
    onehot = labels_all[:, None] == me * class_rows + jnp.arange(class_rows)[None, :]
    part = jnp.dot(onehot.astype(low), table, preferred_element_type=jnp.float32)
    part = part + jnp.where(jnp.arange(n)[:, None] == me, time_vec.astype(jnp.float32), 0.0)
    part = part.reshape(n, n, own_rows).transpose(1, 0, 2)
    part = jnp.pad(part, ((0, 0), (0, 0), (0, 128 - own_rows)))
    (got,) = exchange([part], (True,), n, 4)
    cond_own = jnp.sum(got, axis=0)[:, :own_rows]
    silu_own = jax.nn.silu(cond_own).astype(low)
    own_modulation = my_half(modulation_master.reshape(own_rows, 6 * width), 1).astype(low)
    part = jnp.dot(silu_own, own_modulation, preferred_element_type=jnp.float32).reshape(n, 3 * width // 128, 128)
    (got,) = exchange([jnp.pad(part, ((0, 0), (0, -part.shape[1] % 8), (0, 0)))], (True,), n, 5)
    mod_half = jnp.sum(got, axis=0)[: 3 * width // 128].reshape(-1) + part_of(bias_mod)
    pieces = lax.all_gather(mod_half.reshape(1, 3, width), "seq", axis=0, tiled=True).reshape(6, 1, width)

    inputs = tokens[0].astype(jnp.float32) + grid_embed(keep_index[0], width)
    half_kept = kept // pairs
    row_ok = jnp.arange(rows) < half_kept
    key_ok = (jnp.arange(rows * pairs) % rows) < half_kept
    normed_in = rows_all(modulated(inputs, pieces[0], pieces[1]).astype(low))
    projected = jnp.dot(normed_in, weight_in, preferred_element_type=jnp.float32)

    def split_heads(values):
        return values.reshape(values.shape[0], half_width // HEAD_DIM, HEAD_DIM)

    queries = split_heads((projected[:, :half_width] + part_of(bias_query)).astype(low))
    keys = split_heads(projected[:, half_width : 2 * half_width].astype(low))
    values = split_heads((projected[:, 2 * half_width :] + part_of(bias_value)).astype(low))
    scale = HEAD_DIM ** (-0.5)
    logits = jnp.einsum("rhe,ghe->hrg", queries, keys, preferred_element_type=jnp.float32) * scale
    logits = jnp.where(key_ok[None, None, :], logits, MASK_FILL)
    expo = jnp.exp(logits - jnp.max(logits, axis=-1, keepdims=True))
    probs = expo / jnp.sum(expo, axis=-1, keepdims=True)
    probs_low = probs.astype(low)
    mixed = jnp.einsum("hrg,ghe->rhe", probs_low, values, preferred_element_type=jnp.float32)
    mixed = mixed.reshape(rows * pairs, half_width).astype(low)

    def times_transposed(left, right):
        return lax.dot_general(left, right, (((1,), (1,)), ((), ())), preferred_element_type=jnp.float32)

    def contract_rows(left, right):
        return lax.dot_general(
            left, right, (((0,), (0,)), ((), ())), preferred_element_type=jnp.float32
        )

    attended = rows_own(times_transposed(mixed, weight_out)) + bias_out
    middle = inputs + pieces[2] * attended
    normed_mid = rows_all(modulated(middle, pieces[3], pieces[4]).astype(low))
    hidden = jnp.dot(normed_mid, weight_expand, preferred_element_type=jnp.float32) + part_of(bias_expand)
    activated = gelu_tanh(hidden).astype(low)
    branch = rows_own(times_transposed(activated, weight_contract)) + bias_contract
    result = middle + pieces[5] * branch
    block_out = jnp.where(row_ok[:, None], result, 0.0).astype(low)[None]

    grad_out = cotangent[0].astype(jnp.float32) * row_ok[:, None].astype(jnp.float32)
    d_branch = rows_all((pieces[5] * grad_out).astype(low))
    d_gate_mlp = jnp.sum(grad_out * branch, axis=0, keepdims=True)
    grad_contract = contract_rows(d_branch, activated).astype(low)
    grad_bias_contract = jnp.sum(d_branch.astype(jnp.float32), axis=0)
    d_activated = jnp.dot(d_branch, weight_contract, preferred_element_type=jnp.float32)
    d_hidden = jax.vjp(gelu_tanh, hidden)[1](d_activated)[0].astype(low)
    grad_expand = contract_rows(normed_mid, d_hidden).astype(low)
    grad_bias_expand = jnp.sum(d_hidden.astype(jnp.float32), axis=0)
    d_normed_mid = rows_own(times_transposed(d_hidden, weight_expand))
    d_middle, d_shift_mlp, d_scale_mlp = jax.vjp(modulated, middle, pieces[3], pieces[4])[1](d_normed_mid)
    d_middle = d_middle + grad_out
    d_attended = rows_all((pieces[2] * d_middle).astype(low))
    d_gate_attn = jnp.sum(d_middle * attended, axis=0, keepdims=True)
    grad_attention_out = contract_rows(d_attended, mixed)
    grad_bias_out = jnp.sum(d_attended.astype(jnp.float32), axis=0)
    d_mixed = split_heads(jnp.dot(d_attended, weight_out, preferred_element_type=jnp.float32).astype(low))
    d_probs = jnp.einsum("rhe,ghe->hrg", d_mixed, values, preferred_element_type=jnp.float32)
    inner = jnp.sum(probs * d_probs, axis=-1, keepdims=True)
    d_logits = (probs * (d_probs - inner)).astype(low)
    d_query = jnp.einsum("hrg,ghe->rhe", d_logits, keys, preferred_element_type=jnp.float32) * scale
    d_key = jnp.einsum("hrg,rhe->ghe", d_logits, queries, preferred_element_type=jnp.float32) * scale
    d_value = jnp.einsum("hrg,rhe->ghe", probs_low, d_mixed, preferred_element_type=jnp.float32)
    d_projected = jnp.concatenate(
        [item.reshape(rows * pairs, half_width) for item in (d_query, d_key, d_value)], axis=-1
    ).astype(low)
    grad_attention_in = contract_rows(normed_in, d_projected)
    bias_sums = jnp.sum(d_projected.astype(jnp.float32), axis=0)
    grad_attn = jnp.concatenate([grad_attention_in, grad_attention_out], axis=1).astype(low)
    d_normed_in = rows_own(times_transposed(d_projected, weight_in))
    d_inputs, d_shift_attn, d_scale_attn = jax.vjp(modulated, inputs, pieces[0], pieces[1])[1](d_normed_in)
    tokens_grad = (d_inputs + d_middle).astype(low)[None]

    shape = (n // 4, 2, 2, own_rows, pieces_own.shape[2])
    reduced = reduce_grads([g.reshape(shape) for g in (grad_attn, grad_expand, grad_contract)], n, 2)

    d_pieces = jnp.concatenate(
        [d_shift_attn, d_scale_attn, d_gate_attn, d_shift_mlp, d_scale_mlp, d_gate_mlp], axis=0
    ).reshape(6 * width)
    d_mod = lax.psum(d_pieces, "seq").astype(low).astype(jnp.float32)

    def at_half(vector):
        whole = jnp.zeros((vector.shape[0] * pairs,), jnp.float32)
        return lax.dynamic_update_slice_in_dim(whole, vector, c * vector.shape[0], 0)

    once = (c == 0).astype(jnp.float32)
    grad_biases = jnp.concatenate(
        [
            d_mod * once,
            at_half(bias_sums[:half_width]),
            at_half(bias_sums[2 * half_width :]),
            grad_bias_out * once,
            at_half(grad_bias_expand),
            grad_bias_contract * once,
        ]
    )
    bias_parts = jnp.pad(grad_biases.reshape(n, bias_share), ((0, 0), (0, 1024 - bias_share))).reshape(n, 8, 128)
    d_mod_block = jnp.pad(d_mod.reshape(-1, 128), ((0, -(6 * width // 128) % 8), (0, 0)))
    d_mod_got, bias_got = exchange([d_mod_block, bias_parts], (False, True), n, 6)
    biases_shard = lax.psum(jnp.sum(bias_got, axis=0), "seq")
    d_mod_all = d_mod_got[:, : 6 * width // 128].reshape(n, 6 * width).astype(low)
    d_silu = times_transposed(
        lax.dynamic_slice_in_dim(d_mod_all, c * 3 * width, 3 * width, 1), own_modulation
    )
    d_silu = lax.psum(d_silu, "seq")
    d_cond_own = jax.vjp(jax.nn.silu, cond_own)[1](d_silu)[0]
    d_cond_block = jnp.pad(d_cond_own, ((0, 0), (0, 128 - own_rows)))
    same = (labels_all[:, None] == labels_all[None, :]).astype(jnp.float32)
    rates = (
        width ** (-0.5),
        width ** (-0.5),
        (width // 4) ** (-0.5),
        width ** (-0.5),
        FF ** (-0.5),
        0.5,
        0.2,
    )
    masters = (
        modulation_master,
        attention_in_master,
        attention_out_master,
        expand_master,
        contract_master,
        class_table_master,
        biases_master,
    )
    firsts = (
        modulation_first,
        attention_in_first,
        attention_out_first,
        expand_first,
        contract_first,
        class_table_first,
        biases_first,
    )
    seconds = (
        modulation_second,
        attention_in_second,
        attention_out_second,
        expand_second,
        contract_second,
        class_table_second,
        biases_second,
    )
    states = list(zip(masters, firsts, seconds))
    updated, grad_norm = finish(
        reduced,
        silu_own,
        d_mod_all,
        d_cond_block,
        biases_shard,
        onehot.astype(jnp.float32),
        same,
        [tuple(item.reshape(-1, 128) for item in state) for state in states[:-1]],
        rates[:-1],
        n,
        8,
    )
    factor = jnp.minimum(1.0, CLIP_LIMIT / (grad_norm + 1e-06))
    bias_grad = biases_shard.reshape(1024)[:bias_share] * factor
    updated = [item.reshape(-1) for item in updated] + list(adam_step(bias_grad, *states[-1], rates[-1]))
    return (block_out, tokens_grad, grad_norm) + tuple(updated)


def solution(mesh):
    return jax.shard_map(
        per_device,
        mesh=mesh,
        in_specs=(
            P("dp", "seq", None),
            P("dp", "seq", None),
            P("dp", None),
            P("dp"),
            P("dp"),
            P("dp", "seq"),
            P("dp"),
            P("dp"),
            P("dp"),
            P("dp"),
            P("dp"),
            P("dp"),
            P("dp"),
            P("dp"),
            P("dp"),
            P("dp"),
            P("dp"),
            P("dp"),
            P("dp"),
            P("dp"),
            P("dp"),
            P("dp"),
            P("dp"),
            P("dp"),
            P("dp"),
            P("dp"),
            P("dp"),
        ),
        out_specs=(
            P("dp", "seq", None),
            P("dp", "seq", None),
            P(),
            P("dp"),
            P("dp"),
            P("dp"),
            P("dp"),
            P("dp"),
            P("dp"),
            P("dp"),
            P("dp"),
            P("dp"),
            P("dp"),
            P("dp"),
            P("dp"),
            P("dp"),
            P("dp"),
            P("dp"),
            P("dp"),
            P("dp"),
            P("dp"),
            P("dp"),
            P("dp"),
            P("dp"),
        ),
        check_vma=False,
    )
```

```python
import functools
import jax
import jax.numpy as jnp
from jax import lax
from jax.experimental import pallas as pl
from jax.experimental.pallas import tpu as pltpu
from jax.sharding import PartitionSpec as P

HEAD_DIM = 72
FF = 4608
SIDE = 16
CLASSES = 1024
STEP = 10
LAYER_EPS = 1e-06
MASK_FILL = -1e30
BETA_FIRST = 0.5
BETA_SECOND = 0.5
ADAM_EPS = 1e-08
WEIGHT_DECAY = 0.1
CLIP_LIMIT = 1.0

MESH = pl.DeviceIdType.MESH
GROUPS = ((0, 768, 0, "x"), (768, 768, 0, "y"), (1536, 384, 1, "x"), (1920, 384, 1, "y"))


def when(cond, fn):
    pl.when(cond)(fn)


class Place:
    def __init__(self, line):
        self.line = line
        i = lax.axis_index("dp")
        self.c = lax.axis_index("seq")
        self.x, self.y, self.z = i % 2, (i // 2) % 2, i // 4

    def dev(self, z=None, y=None, x=None):
        z = self.z if z is None else z
        y = self.y if y is None else y
        x = self.x if x is None else x
        return (z * 4 + y * 2 + x, self.c)

    def peer(self, axis):
        return self.dev(x=1 - self.x) if axis == "x" else self.dev(y=1 - self.y)

    def barrier(self):
        bar = pltpu.get_barrier_semaphore()

        def sig(dev):
            pl.semaphore_signal(bar, inc=1, device_id=dev, device_id_type=MESH)

        sig(self.peer("x"))
        sig(self.peer("y"))
        when(self.z > 0, lambda: sig(self.dev(z=self.z - 1)))
        when(self.z < self.line - 1, lambda: sig(self.dev(z=self.z + 1)))
        pl.semaphore_wait(bar, 2 + (self.z > 0).astype(jnp.int32) + (self.z < self.line - 1).astype(jnp.int32))


def gather_kernel(line, src, out, own_sem, send_a, send_u, send_d, send_b, recv_a, recv_z, recv_b):
    me = Place(line)
    count = src.shape[0]
    x, y, z = me.x, me.y, me.z

    def single(m, g, zz, yy=None, xx=None):
        lo, width = GROUPS[g][:2]
        return out.at[m, zz, y if yy is None else yy, x if xx is None else xx, :, pl.ds(lo, width)]

    def pair(m, g, zz):
        lo, width, _, first = GROUPS[g]
        if first == "x":
            return out.at[m, zz, y, :, :, pl.ds(lo, width)]
        return out.at[m, zz, :, x, :, pl.ds(lo, width)]

    def remote(ref, send, recv, dev, source=None):
        return pltpu.make_async_remote_copy(
            src_ref=ref if source is None else source, dst_ref=ref, send_sem=send, recv_sem=recv,
            device_id=dev, device_id_type=MESH)

    def own(m, g):
        lo, width = GROUPS[g][:2]
        return src.at[m, :, pl.ds(lo, width)]

    def a_copy(m, g, zz, source=None):
        return remote(single(m, g, zz), send_a.at[m, g, zz], recv_a.at[m, g, zz], me.peer(GROUPS[g][3]), source)

    def z_ref(m, g, zz):
        return pair(m, g, zz) if GROUPS[g][2] == 0 else single(m, g, zz)

    def u_copy(m, g, zz, source=None):
        return remote(z_ref(m, g, zz), send_u.at[m, g, zz], recv_z.at[m, g, zz], me.dev(z=jnp.minimum(z + 1, line - 1)), source)

    def d_copy(m, g, zz, source=None):
        return remote(z_ref(m, g, zz), send_d.at[m, g, zz], recv_z.at[m, g, zz], me.dev(z=jnp.maximum(z - 1, 0)), source)

    def b_copy(m, g, zz):
        last = "y" if GROUPS[g][3] == "x" else "x"
        return remote(pair(m, g, zz), send_b.at[m, g, zz], recv_b.at[m, g, zz], me.peer(last))

    def keep(m):
        return pltpu.make_async_copy(src.at[m], out.at[m, z, y, x], own_sem.at[m])

    up, down = z < line - 1, z > 0

    @pl.loop(0, count)
    def _(m):
        keep(m).start()

    me.barrier()

    @pl.loop(0, count)
    def _(m):
        for g in range(4):
            a_copy(m, g, z, own(m, g)).start()
        for g in (2, 3):
            when(up, lambda g=g: u_copy(m, g, z, own(m, g)).start())
            when(down, lambda g=g: d_copy(m, g, z, own(m, g)).start())

    @pl.loop(0, count)
    def _(m):
        keep(m).wait()
        for g in (0, 1):
            a_copy(m, g, z).wait_recv()
            when(up, lambda g=g: u_copy(m, g, z).start())
            when(down, lambda g=g: d_copy(m, g, z).start())
            b_copy(m, g, z).start()

    def arrive(m, k, zz, onward, go):
        for g in range(4):
            copy = u_copy if go == "u" else d_copy
            copy(m, g, zz).wait_recv()
            when(onward, lambda g=g: copy(m, g, zz).start())
            if GROUPS[g][2] == 0:
                b_copy(m, g, zz).start()
            else:
                a_copy(m, g, zz).start()

    def crossed(m, zz):
        for g in (2, 3):
            a_copy(m, g, zz).wait_recv()
            b_copy(m, g, zz).start()

    @pl.loop(1, line + 1)
    def _(k):
        @pl.loop(0, count)
        def _(m):
            when(k <= z, lambda: arrive(m, k, jnp.maximum(z - k, 0), up, "u"))
            when(z + k < line, lambda: arrive(m, k, jnp.minimum(z + k, line - 1), down, "d"))
            when(k - 1 <= z, lambda: crossed(m, jnp.maximum(z - k + 1, 0)))
            when((k > 1) & (z + k - 1 < line), lambda: crossed(m, jnp.minimum(z + k - 1, line - 1)))

    @pl.loop(0, count)
    def _(m):
        @pl.loop(0, line)
        def _(zz):
            for g in range(4):
                b_copy(m, g, zz).wait()
                if GROUPS[g][2] == 1:
                    a_copy(m, g, zz).wait_send()
                when(up & (zz <= z), lambda g=g: u_copy(m, g, zz).wait_send())
                when(down & (zz >= z), lambda g=g: d_copy(m, g, zz).wait_send())
        for g in (0, 1):
            a_copy(m, g, z).wait_send()


def gather_weights(src, n, collective_id):
    count, rows, cols = src.shape
    line = n // 4
    dma = pltpu.SemaphoreType.DMA
    return pl.pallas_call(
        functools.partial(gather_kernel, line),
        out_shape=jax.ShapeDtypeStruct((count, line, 2, 2, rows, cols), src.dtype),
        in_specs=[pl.BlockSpec(memory_space=pltpu.HBM)],
        out_specs=pl.BlockSpec(memory_space=pltpu.HBM),
        scratch_shapes=[dma((count,))] + [dma((count, 4, line))] * 7,
        compiler_params=pltpu.CompilerParams(collective_id=collective_id, has_side_effects=True),
        cost_estimate=pl.CostEstimate(flops=0, bytes_accessed=2 * count * n * rows * cols * 2, transcendentals=0),
        name="gather_weights",
    )(src)


class Reducer:
    def __init__(self, line, grads, out, own, got_b, got_z, got_a, sems):
        self.line, self.grads, self.out = line, grads, out
        self.own, self.acc, self.got_z, self.got_a = own, got_b, got_z, got_a
        self.load, self.send_b, self.send_z, self.send_a, self.recv_b, self.recv_z, self.recv_a = sems
        self.me = me = Place(line)
        self.up, self.down = me.z < line - 1, me.z > 0
        self.above, self.below = me.dev(z=jnp.minimum(me.z + 1, line - 1)), me.dev(z=jnp.maximum(me.z - 1, 0))
        self.units = len(grads) * line

    def last(self, g):
        return "y" if GROUPS[g][3] == "x" else "x"

    def first(self, g):
        return self.me.x if GROUPS[g][3] == "x" else self.me.y

    def half(self, grad, g, zz, mine):
        cols = pl.ds(GROUPS[g][0], GROUPS[g][1])
        if self.last(g) == "y":
            return grad.at[zz, self.me.y if mine else 1 - self.me.y, :, :, cols]
        return grad.at[zz, :, self.me.x if mine else 1 - self.me.x, :, cols]

    def loading(self, u, g, zz, side, grad=None):
        grad = self.grads[0] if grad is None else grad
        return pltpu.make_async_copy(
            self.half(grad, g, zz, True), self.own[g].at[u % 3, side], self.load.at[u % 3, g, side])

    def remote(self, src, dst, send, recv, dev):
        return pltpu.make_async_remote_copy(
            src_ref=src, dst_ref=dst, send_sem=send, recv_sem=recv, device_id=dev, device_id_type=MESH)

    def b_copy(self, m, g, zz, grad=None):
        grad = self.grads[0] if grad is None else grad
        return self.remote(
            self.half(grad, g, zz, False), self.acc[g].at[m, zz], self.send_b.at[m, g, zz], self.recv_b.at[m, g, zz],
            self.me.peer(self.last(g)))

    def slot_a(self, g, zz):
        return zz if GROUPS[g][2] == 1 else 0

    def a_copy(self, m, g, zz):
        return self.remote(
            self.acc[g].at[m, zz, 1 - self.first(g)], self.got_a[g].at[m, self.slot_a(g, zz)], self.send_a.at[m, g, zz],
            self.recv_a.at[m, g, zz], self.me.peer(GROUPS[g][3]))

    def z_copy(self, m, g, zz, slot, dev):
        part = self.acc[g].at[m, zz] if GROUPS[g][2] == 0 else self.acc[g].at[m, zz, self.first(g)]
        return self.remote(part, self.got_z[g].at[m, slot], self.send_z.at[m, g, zz], self.recv_z.at[m, g, slot], dev)

    def add_b(self, m, g, zz, u, side):
        self.loading(u, g, zz, side).wait()
        self.b_copy(m, g, zz).wait_recv()
        self.acc[g][m, zz] = self.acc[g][m, zz] + self.own[g][u % 3, side]

    def add_z(self, m, g, zz, slot):
        acc, got = self.acc[g], self.got_z[g]
        self.z_copy(m, g, self.me.z, slot, self.below).wait_recv()
        if GROUPS[g][2] == 0:
            acc[m, zz] = acc[m, zz] + got[m, slot]
        else:
            acc[m, zz, self.first(g)] = acc[m, zz, self.first(g)] + got[m, slot]

    def add_a(self, m, g, zz):
        self.a_copy(m, g, zz).wait_recv()
        acc, first = self.acc[g], self.first(g)
        acc[m, zz, first] = acc[m, zz, first] + self.got_a[g][m, self.slot_a(g, zz)]

    def planes(self, k, fn):
        z, line = self.me.z, self.line
        when(z + k < line, lambda: fn(jnp.minimum(z + k, line - 1), True))
        when((z >= k) & (k > 0), lambda: fn(jnp.maximum(z - k, 0), False))

    def begin(self, v):
        m, j = v // self.line, v % self.line

        def one(grad, zz, upward):
            for g in range(4):
                self.b_copy(m, g, zz, grad).start()
                self.loading(v, g, zz, 0 if upward else 1, grad).start()

        for index, grad in enumerate(self.grads):
            when(m == index, lambda: self.planes(self.line - 1 - j, lambda zz, upward: one(grad, zz, upward)))

    def onward(self, m, g, zz, k, upward):
        if upward:
            when(self.down, lambda: self.add_z(m, g, zz, zz))
            self.z_copy(m, g, zz, zz, self.above).start()
        else:
            when(self.up, lambda: self.add_z(m, g, zz, zz))
            self.z_copy(m, g, zz, jnp.where(k == 1, self.line, zz), self.below).start()

    def near(self, u, m, j):
        k = self.line - 1 - j

        def one(zz, upward):
            for g in range(4):
                self.add_b(m, g, zz, u, 0 if upward else 1)
                if GROUPS[g][2] == 1:
                    self.a_copy(m, g, zz).start()
                else:
                    when(k > 0, lambda g=g: self.onward(m, g, zz, k, upward))

        self.planes(k, one)

    def far(self, m, j):
        k = self.line - j

        def one(zz, upward):
            for g in (2, 3):
                self.add_a(m, g, zz)
                self.onward(m, g, zz, k, upward)

        when((k > 0) & (k < self.line), lambda: self.planes(k, one))

    def close(self, m):
        z = self.me.z
        for g in (0, 1):
            when(self.down, lambda g=g: self.add_z(m, g, z, z))
            when(self.up, lambda g=g: self.add_z(m, g, z, self.line))
            self.a_copy(m, g, z).start()

    def final(self, m):
        z = self.me.z
        for g in range(4):
            cols = pl.ds(GROUPS[g][0], GROUPS[g][1])
            self.add_a(m, g, z)
            if GROUPS[g][2] == 1:
                when(self.down, lambda g=g: self.add_z(m, g, z, z))
                when(self.up, lambda g=g: self.add_z(m, g, z, self.line))
            self.out[m, :, cols] = self.acc[g][m, z, self.first(g)]

    def unit(self, u):
        line = self.line
        m, j = u // line, u % line
        when(u + 2 < self.units, lambda: self.begin(jnp.minimum(u + 2, self.units - 1)))
        self.near(u, m, j)
        self.far(m, j)
        when(j == line - 1, lambda: self.close(m))
        when((j == 0) & (m > 0), lambda: self.final(jnp.maximum(m - 1, 0)))

    def drain(self):
        z = self.me.z

        @pl.loop(0, len(self.grads))
        def _(m):
            @pl.loop(0, self.line)
            def _(zz):
                for g in range(4):
                    self.b_copy(m, g, zz).wait_send()
                    if GROUPS[g][2] == 1:
                        self.a_copy(m, g, zz).wait_send()
                    when(zz != z, lambda g=g: self.z_copy(m, g, zz, zz, self.above).wait_send())
            for g in (0, 1):
                self.a_copy(m, g, z).wait_send()


def reducer_scratch(count, line, rows, dt):
    dma = pltpu.SemaphoreType.DMA
    own = [pltpu.VMEM((3, 2, 2, rows, GROUPS[g][1]), dt) for g in range(4)]
    got_b = [pltpu.VMEM((count, line, 2, rows, GROUPS[g][1]), dt) for g in range(4)]
    got_z = [pltpu.VMEM((count, line + 1) + ((2,) if GROUPS[g][2] == 0 else ()) + (rows, GROUPS[g][1]), dt) for g in range(4)]
    got_a = [pltpu.VMEM((count, line if GROUPS[g][2] == 1 else 1, rows, GROUPS[g][1]), dt) for g in range(4)]
    sems = [dma((3, 4, 2))] + [dma((count, 4, line))] * 4 + [dma((count, 4, line + 1))] + [dma((count, 4, line))]
    return own + got_b + got_z + got_a + sems


def make_reducer(line, grads, out, refs):
    return Reducer(line, grads, out, refs[:4], refs[4:8], refs[8:12], refs[12:16], refs[16:])


def dot(left, right, a=1, b=0):
    return lax.dot_general(left, right, (((a,), (b,)), ((), ())), preferred_element_type=jnp.float32)


def backward_kernel(line, *refs):
    (g_contract, g_expand, weight, pair_t, d_att, q, k, v, o, key_ok, x, d_mid, scale_a, d_pieces, v_rows, modulation, cond,
     out, tokens_grad, d_mod_all, d_cond, bias_sum) = refs[:22]
    (w, grads, rhs, d_o, d_q, d_k, d_v, d_h, d_h_got, dp, dp_got, msg, msg_got, vec, vec_got, d_silu, d_silu_got, chunk,
     w_sem, pair_send, pair_recv, msg_send, msg_recv, vec_send, vec_recv) = refs[22:47]
    n = line * 4
    low = jnp.bfloat16
    me, c = lax.axis_index("dp"), lax.axis_index("seq")
    red = make_reducer(line, (g_contract, g_expand, grads), out, refs[47:])
    rows, width = x.shape
    half = weight.shape[1] // 4
    heads = half // HEAD_DIM
    edge = 3 * half // 128 * 128
    partner = (me, 1 - c)

    def swap(i, src, dst):
        return pltpu.make_async_remote_copy(
            src_ref=src, dst_ref=dst, send_sem=pair_send.at[i], recv_sem=pair_recv.at[i], device_id=partner, device_id_type=MESH)

    def to_all(src, dst, send, recv, spread):
        def copy(j, there, slot):
            return pltpu.make_async_remote_copy(
                src_ref=src.at[there] if spread else src, dst_ref=dst.at[slot], send_sem=send.at[j], recv_sem=recv.at[slot],
                device_id=(there, c), device_id_type=MESH)

        def start():
            @pl.loop(1, n)
            def _(j):
                copy(j, (me + j) % n, me).start()

        def wait():
            @pl.loop(1, n)
            def _(j):
                copy(j, (me + j) % n, (me + n - j) % n).wait()

        return start, wait

    w_copy = pltpu.make_async_copy(weight, w, w_sem)
    w_copy.start()
    bar = pltpu.get_barrier_semaphore()
    pl.semaphore_signal(bar, inc=1, device_id=partner, device_id_type=MESH)

    @pl.loop(1, n)
    def _(j):
        pl.semaphore_signal(bar, inc=1, device_id=((me + j) % n, c), device_id_type=MESH)

    pl.semaphore_wait(bar, n)
    red.begin(0)
    red.begin(1)

    w_copy.wait()
    d_o[:, :half] = dot(d_att[...], w[:, edge:])[:, 3 * half - edge :].astype(low)
    d_o[:, half:] = jnp.zeros((2 * rows, d_o.shape[1] - half), low)
    for item in (d_q, d_k, d_v):
        item[...] = jnp.zeros_like(item)

    seen = jnp.broadcast_to(key_ok[...], (2 * rows, 2 * rows)) > 0.0

    def head(h):
        lo = pl.multiple_of(h * HEAD_DIM // 128 * 128, 128)
        win = pl.ds(lo, 256)
        lane = lax.broadcasted_iota(jnp.int32, (1, 256), 1) + lo - h * HEAD_DIM
        mine = ((lane >= 0) & (lane < HEAD_DIM)).astype(low)
        qh, kh, doh = q[:, win] * mine, k[:, win] * mine, d_o[:, win] * mine
        logits = jnp.where(seen, dot(qh, kh, 1, 1) * HEAD_DIM ** (-0.5), MASK_FILL)
        expo = jnp.exp(logits - jnp.max(logits, axis=-1, keepdims=True))
        probs = expo / jnp.sum(expo, axis=-1, keepdims=True)
        d_probs = dot(doh, v[:, win], 1, 1)
        inner = jnp.sum(probs * d_probs, axis=-1, keepdims=True)
        d_logits = (probs * (d_probs - inner)).astype(low)
        d_q[:, win] = d_q[:, win] + dot(d_logits, kh) * HEAD_DIM ** (-0.5)
        d_k[:, win] = d_k[:, win] + dot(d_logits, qh, 0, 0) * HEAD_DIM ** (-0.5)
        d_v[:, win] = d_v[:, win] + dot(probs.astype(low), doh, 0, 0)

    def weight_grads():
        for i, item in enumerate((d_q, d_k, d_v)):
            rhs[: 2 * rows, i * half : (i + 1) * half] = item[:, :half].astype(low)
        rhs[: 2 * rows, 3 * half :] = jnp.zeros((2 * rows, half), low)
        rhs[2 * rows :, edge : 3 * half] = jnp.zeros((2 * rows, 3 * half - edge), low)
        rhs[2 * rows :, 3 * half :] = o[:, :half]
        vec[0:1, :half] = jnp.sum(rhs[: 2 * rows, :half].astype(jnp.float32), axis=0, keepdims=True)
        vec[0:1, half:] = jnp.sum(rhs[: 2 * rows, 2 * half : 3 * half].astype(jnp.float32), axis=0, keepdims=True)
        vec[1:] = v_rows[1:]

        @pl.loop(0, n)
        def _(i):
            block = grads.at[i // 4, i // 2 % 2, i % 2]
            block[:, :edge] = dot(pair_t[i, :, : 2 * rows], rhs[: 2 * rows, :edge]).astype(low)
            block[:, edge:] = dot(pair_t[i], rhs[:, edge:]).astype(low)

    def input_grad():
        @pl.loop(0, width // 128)
        def _(t):
            cols = pl.ds(pl.multiple_of(t * 128, 128), 128)
            part = dot(rhs[: 2 * rows, : edge + 128], w[cols, : edge + 128], 1, 1)
            d_h[0, :, cols] = part[:rows]
            d_h[1, :, cols] = part[rows:]

        swap(0, d_h.at[1 - c], d_h_got).start()

    def norm_grad():
        swap(0, d_h.at[1 - c], d_h_got).wait()
        d_n = d_h[c] + d_h_got[...]
        centre = x[...] - jnp.mean(x[...], axis=-1, keepdims=True)
        inv = lax.rsqrt(jnp.mean(centre * centre, axis=-1, keepdims=True) + LAYER_EPS)
        normed = centre * inv
        e = d_n * (1.0 + scale_a[...])
        d_x = (e - jnp.mean(e, axis=-1, keepdims=True) - normed * jnp.mean(e * normed, axis=-1, keepdims=True)) * inv
        tokens_grad[...] = (d_x + d_mid[...]).astype(low)
        dp[...] = d_pieces[...]
        dp[0:1] = jnp.sum(d_n, axis=0, keepdims=True)
        dp[1:2] = jnp.sum(d_n * normed, axis=0, keepdims=True)
        swap(1, dp, dp_got).start()

    msg_start, msg_wait = to_all(msg, msg_got, msg_send, msg_recv, False)
    vec_start, vec_wait = to_all(chunk, vec_got, vec_send, vec_recv, True)
    per = chunk_tiles(n, width)

    def send_mod():
        swap(1, dp, dp_got).wait()
        d_mod = (dp[...] + dp_got[...]).astype(low).astype(jnp.float32)
        own = jnp.where(c == 0, d_mod[0:3], d_mod[3:6])
        for r in range(3):
            msg[r] = own[r : r + 1]
        msg_got[me] = msg[...]
        chunk[...] = jnp.zeros_like(chunk)
        tiles = width // 128
        for t in range(5 * tiles):
            chunk[t // per, t % per] = vec[t // tiles : t // tiles + 1, t % tiles * 128 : t % tiles * 128 + 128]
        vec_got[me] = chunk[me]
        msg_start()
        vec_start()

    def mod_grad():
        msg_wait()
        vec_wait()

        @pl.loop(0, n)
        def _(s):
            for r in range(3):
                d_mod_all[c, pl.ds(s, 1), r * width : (r + 1) * width] = msg_got[s, r]

        bias_sum[c] = jnp.zeros((8, 128), jnp.float32)
        for r in range(per):
            bias_sum[c, r : r + 1] = jnp.sum(vec_got[:, r], axis=0)
        d_silu[...] = dot(d_mod_all[c].astype(low), modulation[...], 1, 1)
        swap(2, d_silu, d_silu_got).start()
        swap(3, d_mod_all.at[c], d_mod_all.at[c]).start()
        swap(4, bias_sum.at[c], bias_sum.at[c]).start()

    def cond_grad():
        swap(2, d_silu, d_silu_got).wait()
        swap(3, d_mod_all.at[c], d_mod_all.at[c]).wait()
        swap(4, bias_sum.at[c], bias_sum.at[c]).wait()
        gate = 1.0 / (1.0 + jnp.exp(-cond[...]))
        d_cond[...] = (d_silu[...] + d_silu_got[...]) * (gate + cond[...] * gate * (1.0 - gate))

    steps = (weight_grads, input_grad, norm_grad, send_mod, mod_grad, cond_grad)

    @pl.loop(0, red.units)
    def _(u):
        @pl.loop(0, jnp.where(u < heads // 2, 2, 0))
        def _(i):
            head(2 * u + i)

        red.unit(u)
        for i, step in enumerate(steps):
            when(u == heads // 2 - 1 + i, step)

    red.final(2)
    red.drain()


def chunk_tiles(n, width):
    return -(-5 * (width // 128) // n)


def backward(hbm_args, vmem_args, n, collective_id):
    line = n // 4
    grad = hbm_args[0]
    rows, cols = grad.shape[-2:]
    pair_t, d_att, q = vmem_args[0], vmem_args[1], vmem_args[2]
    all_rows, width = d_att.shape
    low, f32 = jnp.bfloat16, jnp.float32
    dma = pltpu.SemaphoreType.DMA
    vmem, hbm = pl.BlockSpec(memory_space=pltpu.VMEM), pl.BlockSpec(memory_space=pltpu.HBM)
    wide = q.shape
    per = chunk_tiles(n, width)
    return pl.pallas_call(
        functools.partial(backward_kernel, line),
        out_shape=[
            jax.ShapeDtypeStruct((3, rows, cols), low),
            jax.ShapeDtypeStruct((all_rows // 2, width), low),
            jax.ShapeDtypeStruct((2, n, 3 * width), f32),
            jax.ShapeDtypeStruct((n, 128), f32),
            jax.ShapeDtypeStruct((2, 8, 128), f32),
        ],
        in_specs=[hbm] * len(hbm_args) + [vmem] * len(vmem_args),
        out_specs=[vmem] * 5,
        scratch_shapes=[
            pltpu.VMEM((width, cols), low),
            pltpu.VMEM((line, 2, 2, rows, cols), low),
            pltpu.VMEM((2 * all_rows, cols), low),
            pltpu.VMEM(wide, low),
            pltpu.VMEM(wide, f32),
            pltpu.VMEM(wide, f32),
            pltpu.VMEM(wide, f32),
            pltpu.VMEM((2, all_rows // 2, width), f32),
            pltpu.VMEM((all_rows // 2, width), f32),
            pltpu.VMEM((8, width), f32),
            pltpu.VMEM((8, width), f32),
            pltpu.VMEM((3, 1, width), f32),
            pltpu.VMEM((n, 3, 1, width), f32),
            pltpu.VMEM((8, width), f32),
            pltpu.VMEM((n, per, 1, 128), f32),
            pltpu.VMEM((n, 128), f32),
            pltpu.VMEM((n, 128), f32),
            pltpu.VMEM((n, per, 1, 128), f32),
            dma,
            dma((5,)),
            dma((5,)),
            dma((n,)),
            dma((n,)),
            dma((n,)),
            dma((n,)),
        ]
        + reducer_scratch(3, line, rows, low),
        compiler_params=pltpu.CompilerParams(
            collective_id=collective_id, has_side_effects=True, vmem_limit_bytes=63 * 2**20),
        name="backward",
    )(*hbm_args, *vmem_args)


def exchange_kernel(n, spread, *refs):
    count = len(spread)
    srcs, outs, (send, recv) = refs[:count], refs[count:2 * count], refs[2 * count:]
    me, c = lax.axis_index("dp"), lax.axis_index("seq")
    bar = pltpu.get_barrier_semaphore()

    @pl.loop(1, n)
    def _(j):
        pl.semaphore_signal(bar, inc=1, device_id=((me + j) % n, c), device_id_type=MESH)

    for a in range(count):
        outs[a][me] = srcs[a][me] if spread[a] else srcs[a][...]
    pl.semaphore_wait(bar, n - 1)

    def copy(a, j, there, slot):
        return pltpu.make_async_remote_copy(
            src_ref=srcs[a].at[there] if spread[a] else srcs[a], dst_ref=outs[a].at[slot],
            send_sem=send.at[a, j], recv_sem=recv.at[a, slot], device_id=(there, c), device_id_type=MESH)

    @pl.loop(1, n)
    def _(j):
        for a in range(count):
            copy(a, j, (me + j) % n, me).start()

    @pl.loop(1, n)
    def _(j):
        for a in range(count):
            copy(a, j, (me + j) % n, (me + n - j) % n).wait()


def exchange(blocks, spread, n, collective_id):
    count = len(blocks)
    parts = [b.shape[1:] if s else b.shape for b, s in zip(blocks, spread)]
    dma = pltpu.SemaphoreType.DMA
    return pl.pallas_call(
        functools.partial(exchange_kernel, n, spread),
        out_shape=[jax.ShapeDtypeStruct((n,) + p, b.dtype) for p, b in zip(parts, blocks)],
        in_specs=[pl.BlockSpec(memory_space=pltpu.VMEM)] * count,
        out_specs=[pl.BlockSpec(memory_space=pltpu.VMEM)] * count,
        scratch_shapes=[dma((count, n)), dma((count, n))],
        compiler_params=pltpu.CompilerParams(collective_id=collective_id, has_side_effects=True, vmem_limit_bytes=32 * 2**20),
        name="exchange",
    )(*blocks)


def adam_step(grad, master, first, second, rate):
    first_new = BETA_FIRST * first + (1.0 - BETA_FIRST) * grad
    second_new = BETA_SECOND * second + (1.0 - BETA_SECOND) * grad * grad
    first_hat = first_new / (1.0 - BETA_FIRST**STEP)
    second_hat = second_new / (1.0 - BETA_SECOND**STEP)
    master_new = master - rate * (
        first_hat / (jnp.sqrt(second_hat) + ADAM_EPS) + WEIGHT_DECAY * master
    )
    return (first_new, second_new, master_new)


def chunk_rows(rows):
    sizes = [d for d in range(8, 257, 8) if rows % d == 0]
    return sizes[-1] if sizes else rows


def norm_kernel(n, *refs):
    reduced, silu, d_mod, d_cond, bias_sum, onehot, same = refs[:7]
    flat, factor_out, norm_out, bias_out = refs[7:13], refs[13], refs[14], refs[15]
    both, wide, block, got, pair_send, pair_recv, send, recv = refs[16:]
    me, c = lax.axis_index("dp"), lax.axis_index("seq")
    rows = reduced.shape[1]
    half = reduced.shape[2]
    head = half // 4

    bar = pltpu.get_barrier_semaphore()
    pl.semaphore_signal(bar, inc=1, device_id=(me, 1 - c), device_id_type=MESH)

    @pl.loop(1, n)
    def _(j):
        pl.semaphore_signal(bar, inc=1, device_id=((me + j) % n, c), device_id_type=MESH)

    both[c] = reduced[...]
    pl.semaphore_wait(bar, n)
    pair = pltpu.make_async_remote_copy(
        src_ref=reduced, dst_ref=both.at[c], send_sem=pair_send, recv_sem=pair_recv,
        device_id=(me, 1 - c), device_id_type=MESH)
    pair.start()

    def spread(a, width):
        total = None
        tiles = width // 128
        for t in range(tiles):
            part = wide[:, 128 * t : 128 * t + 128]
            flat[a][pl.ds(t, rows, stride=tiles), :] = part
            square = part * part
            total = square if total is None else total + square
        return jnp.sum(total)

    part_mod = d_mod.shape[2]
    for core in range(2):
        wide[:, core * part_mod : (core + 1) * part_mod] = dot(silu[...], d_mod[core].astype(silu.dtype), 0, 0)
    squares = spread(0, wide.shape[1])
    mod_sums = jnp.sum(d_mod[...], axis=1)
    squares = squares + jnp.where(me == 0, jnp.sum(mod_sums * mod_sums), 0.0)
    width = n * rows
    tile = chunk_tiles(n, width) * me + lax.broadcasted_iota(jnp.int32, (8, 128), 0)
    squares = squares + jnp.sum(bias_sum[0] * bias_sum[0])
    squares = squares + jnp.sum(jnp.where(tile < 3 * (width // 128), bias_sum[1] * bias_sum[1], 0.0))
    pair.wait()
    for core in range(2):
        for part in range(3):
            lo = (2 * part + core) * head
            wide[:, lo : lo + head] = both[core, 2, :, part * head : (part + 1) * head].astype(jnp.float32)
    squares = squares + spread(1, 6 * head)
    for core in range(2):
        wide[:, core * head : (core + 1) * head] = both[core, 2, :, 3 * head :].astype(jnp.float32)
    squares = squares + spread(2, 2 * head)
    for a in (3, 4):
        for core in range(2):
            wide[:, core * half : (core + 1) * half] = both[core, 4 - a].astype(jnp.float32)
        squares = squares + spread(a, 2 * half)

    slots = d_cond.shape[0]
    block[:slots] = d_cond[...]
    block[slots : slots + 8] = jnp.full((8, 128), squares, jnp.float32)
    block[slots + 8 : slots + 16] = bias_sum[0]
    block[slots + 16 :] = bias_sum[1]
    got[me] = block[...]

    def copy(j, there, slot):
        return pltpu.make_async_remote_copy(
            src_ref=block, dst_ref=got.at[slot], send_sem=send.at[j], recv_sem=recv.at[slot],
            device_id=(there, c), device_id_type=MESH)

    @pl.loop(1, n)
    def _(j):
        copy(j, (me + j) % n, me).start()

    @pl.loop(1, n)
    def _(j):
        copy(j, (me + j) % n, (me + n - j) % n).wait()

    bias_out[...] = got[:, slots + 8 :]
    total = jnp.sum(got[:, slots : slots + 8], axis=0)[:1, :1]
    gram = jnp.zeros((slots, slots), jnp.float32)
    for i in range(n):
        part = got[i, :slots]
        gram = gram + lax.dot_general(
            part, part, (((1,), (1,)), ((), ())), preferred_element_type=jnp.float32, precision=lax.Precision.HIGHEST)
        wide[: onehot.shape[1], i * rows : (i + 1) * rows] = lax.dot_general(
            onehot[...], part, (((0,), (0,)), ((), ())), preferred_element_type=jnp.float32,
            precision=lax.Precision.HIGHEST)[:, :rows]
    total = total + jnp.sum(gram * same[...], keepdims=True)
    norm = jnp.sqrt(total)
    norm_out[...] = jnp.broadcast_to(norm, (8, 128))
    factor_out[...] = jnp.broadcast_to(jnp.minimum(1.0, CLIP_LIMIT / (norm + 1e-06)), (8, 128))
    tiles = n * rows // 128
    for t in range(tiles):
        flat[5][pl.ds(t, onehot.shape[1], stride=tiles), :] = wide[: onehot.shape[1], 128 * t : 128 * t + 128]


def adam_kernel(rates, *refs):
    kinds = len(rates)
    factor_ref, flat = refs[0], refs[1 : 1 + kinds]
    at = 1 + kinds
    states = [refs[at + 3 * a : at + 3 * a + 3] for a in range(kinds)]
    at += 3 * kinds
    news = [refs[at + 3 * a : at + 3 * a + 3] for a in range(kinds)]
    at += 3 * kinds
    held = refs[at : at + kinds]
    in_sem, out_sem = refs[at + kinds :]

    def loads(a):
        return [pltpu.make_async_copy(states[a][k], held[a].at[k], in_sem.at[a, k]) for k in range(3)]

    for a in range(kinds):
        for copy in loads(a):
            copy.start()
    factor = factor_ref[:1, :]
    for a in range(kinds):
        for copy in loads(a):
            copy.wait()
        size = chunk_rows(flat[a].shape[0])

        @pl.loop(0, flat[a].shape[0] // size)
        def _(i, a=a, size=size):
            part = pl.ds(pl.multiple_of(i * size, size), size)
            grad = flat[a][part] * factor
            master, first, second = held[a][0, part], held[a][1, part], held[a][2, part]
            first, second, master = adam_step(grad, master, first, second, rates[a])
            held[a][0, part], held[a][1, part], held[a][2, part] = master, first, second
            for k in range(3):
                pltpu.make_async_copy(held[a].at[k, part], news[a][k].at[part], out_sem.at[a, k]).start()

    for a in range(kinds):
        for k in range(3):
            pltpu.make_async_copy(held[a].at[k], news[a][k], out_sem.at[a, k]).wait()


def finish(reduced, silu, d_mod, d_cond, bias_sum, onehot, same, states, rates, n, collective_id):
    vmem, hbm = pl.BlockSpec(memory_space=pltpu.VMEM), pl.BlockSpec(memory_space=pltpu.HBM)
    dma = pltpu.SemaphoreType.DMA
    kinds = len(states)
    rows = reduced.shape[1]
    flats = [jax.ShapeDtypeStruct(s[0].shape, jnp.float32) for s in states]
    small = jax.ShapeDtypeStruct((8, 128), jnp.float32)
    block = d_cond.shape[0] + 24
    outs = pl.pallas_call(
        functools.partial(norm_kernel, n),
        out_shape=flats + [small, small, jax.ShapeDtypeStruct((n, 16, 128), jnp.float32)],
        in_specs=[vmem] * 7,
        out_specs=[vmem] * (kinds + 3),
        scratch_shapes=[
            pltpu.VMEM((2,) + reduced.shape, reduced.dtype),
            pltpu.VMEM((rows, 2 * d_mod.shape[2]), jnp.float32),
            pltpu.VMEM((block, 128), jnp.float32),
            pltpu.VMEM((n, block, 128), jnp.float32),
            dma,
            dma,
            dma((n,)),
            dma((n,)),
        ],
        compiler_params=pltpu.CompilerParams(
            collective_id=collective_id, has_side_effects=True, vmem_limit_bytes=40 * 2**20),
        name="norm",
    )(reduced, silu, d_mod, d_cond, bias_sum, onehot, same)
    grads, factor, norm = outs[:kinds], outs[kinds], outs[kinds + 1]
    news = pl.pallas_call(
        functools.partial(adam_kernel, rates),
        out_shape=[f for f in flats for _ in range(3)],
        in_specs=[vmem] * (1 + kinds) + [hbm] * (3 * kinds),
        out_specs=[hbm] * (3 * kinds),
        scratch_shapes=[pltpu.VMEM((3,) + f.shape, jnp.float32) for f in flats]
        + [dma((kinds, 3)), dma((kinds, 3))],
        compiler_params=pltpu.CompilerParams(vmem_limit_bytes=56 * 2**20),
        name="adam",
    )(factor, *grads, *[item for s in states for item in s])
    order = [3 * a + k for a in range(kinds) for k in (1, 2, 0)]
    return [news[i] for i in order], norm[0, 0], outs[kinds + 2]


def grid_embed(keep_index, width):
    quarter = width // 4
    freqs = 10000.0 ** (-jnp.arange(quarter).astype(jnp.float32) / quarter)
    across = (keep_index // SIDE).astype(jnp.float32)[..., None] * freqs
    along = (keep_index % SIDE).astype(jnp.float32)[..., None] * freqs
    return jnp.concatenate(
        [jnp.sin(across), jnp.cos(across), jnp.sin(along), jnp.cos(along)], axis=-1
    )


def normalize(values):
    centre = values - jnp.mean(values, axis=-1, keepdims=True)
    spread = jnp.mean(centre * centre, axis=-1, keepdims=True)
    return centre * lax.rsqrt(spread + LAYER_EPS)


def modulated(values, shift, scale):
    return normalize(values) * (1.0 + scale) + shift


def gelu_tanh(values):
    return jax.nn.gelu(values, approximate=True)


def per_device(
    tokens,
    cotangent,
    time_vec,
    labels,
    kept,
    keep_index,
    modulation_master,
    modulation_first,
    modulation_second,
    attention_in_master,
    attention_in_first,
    attention_in_second,
    attention_out_master,
    attention_out_first,
    attention_out_second,
    expand_master,
    expand_first,
    expand_second,
    contract_master,
    contract_first,
    contract_second,
    class_table_master,
    class_table_first,
    class_table_second,
    biases_master,
    biases_first,
    biases_second,
):
    rows, width = tokens.shape[1:]
    n, pairs = lax.axis_size("dp"), lax.axis_size("seq")
    me, c = lax.axis_index("dp"), lax.axis_index("seq")
    own_rows = width // n
    half_width, half_ff = width // pairs, FF // pairs
    low = jnp.bfloat16

    def flipped(values):
        return lax.ppermute(values, "seq", [(i, (i + 1) % pairs) for i in range(pairs)])

    def rows_all(values):
        return lax.all_gather(values, "seq", axis=0, tiled=True)

    def rows_own(partial):
        mine = lax.dynamic_slice_in_dim(partial, c * rows, rows, 0)
        return mine + flipped(lax.dynamic_slice_in_dim(partial, (1 - c) * rows, rows, 0))

    def my_half(values, parts):
        shaped = values.reshape(values.shape[0], parts, pairs, -1)
        return lax.dynamic_index_in_dim(shaped, c, 2, keepdims=False).reshape(values.shape[0], -1)

    def part_of(vector):
        return lax.dynamic_slice_in_dim(vector, c * (vector.shape[0] // pairs), vector.shape[0] // pairs, 0)

    own_attn = jnp.concatenate(
        [
            my_half(attention_in_master.reshape(own_rows, 3 * width), 3),
            my_half(attention_out_master.reshape(own_rows, width), 1),
        ],
        axis=1,
    )
    own_expand = my_half(expand_master.reshape(own_rows, FF), 1)
    own_contract = my_half(contract_master.reshape(own_rows, FF), 1)
    pieces_own = jnp.stack([own_attn, own_expand, own_contract]).astype(low)
    weights = gather_weights(pieces_own, n, 1).reshape(3, width, pieces_own.shape[2])
    weight_in = weights[0, :, : 3 * half_width]
    weight_out = weights[0, :, 3 * half_width :]
    weight_expand, weight_contract = weights[1], weights[2]

    bias_share = biases_master.shape[0]
    bias_block = jnp.pad(biases_master.astype(low).astype(jnp.float32), (0, 1024 - bias_share)).reshape(8, 128)
    label_block = jnp.broadcast_to(labels.astype(jnp.float32)[:, None], (8, 128))
    (got,) = exchange([jnp.concatenate([bias_block, label_block])], (False,), n, 3)
    biases = got[:, :8].reshape(n, 1024)[:, :bias_share].reshape(-1)
    labels_all = got[:, 8, 0].astype(jnp.int32)
    bias_mod = biases[: 6 * width]
    bias_query = biases[6 * width : 7 * width]
    bias_value = biases[7 * width : 8 * width]
    bias_out = biases[8 * width : 9 * width]
    bias_expand = biases[9 * width : 9 * width + FF]
    bias_contract = biases[9 * width + FF :]

    class_rows = CLASSES // n
    table = class_table_master.reshape(class_rows, width).astype(low)
    onehot = labels_all[:, None] == me * class_rows + jnp.arange(class_rows)[None, :]
    part = jnp.dot(onehot.astype(low), table, preferred_element_type=jnp.float32)
    part = part + jnp.where(jnp.arange(n)[:, None] == me, time_vec.astype(jnp.float32), 0.0)
    part = part.reshape(n, n, own_rows).transpose(1, 0, 2)
    part = jnp.pad(part, ((0, 0), (0, 0), (0, 128 - own_rows)))
    (got,) = exchange([part], (True,), n, 4)
    cond_own = jnp.sum(got, axis=0)[:, :own_rows]
    silu_own = jax.nn.silu(cond_own).astype(low)
    own_modulation = my_half(modulation_master.reshape(own_rows, 6 * width), 1).astype(low)
    part = jnp.dot(silu_own, own_modulation, preferred_element_type=jnp.float32).reshape(n, 3 * width // 128, 128)
    (got,) = exchange([jnp.pad(part, ((0, 0), (0, -part.shape[1] % 8), (0, 0)))], (True,), n, 5)
    mod_half = jnp.sum(got, axis=0)[: 3 * width // 128].reshape(-1) + part_of(bias_mod)
    pieces = lax.all_gather(mod_half.reshape(1, 3, width), "seq", axis=0, tiled=True).reshape(6, 1, width)

    inputs = tokens[0].astype(jnp.float32) + grid_embed(keep_index[0], width)
    half_kept = kept // pairs
    row_ok = jnp.arange(rows) < half_kept
    key_ok = (jnp.arange(rows * pairs) % rows) < half_kept
    normed_in = rows_all(modulated(inputs, pieces[0], pieces[1]).astype(low))
    projected = jnp.dot(normed_in, weight_in, preferred_element_type=jnp.float32)

    def split_heads(values):
        return values.reshape(values.shape[0], half_width // HEAD_DIM, HEAD_DIM)

    flat_query = (projected[:, :half_width] + part_of(bias_query)).astype(low)
    flat_key = projected[:, half_width : 2 * half_width].astype(low)
    flat_value = (projected[:, 2 * half_width :] + part_of(bias_value)).astype(low)
    queries, keys, values = split_heads(flat_query), split_heads(flat_key), split_heads(flat_value)
    scale = HEAD_DIM ** (-0.5)
    logits = jnp.einsum("rhe,ghe->hrg", queries, keys, preferred_element_type=jnp.float32) * scale
    logits = jnp.where(key_ok[None, None, :], logits, MASK_FILL)
    expo = jnp.exp(logits - jnp.max(logits, axis=-1, keepdims=True))
    probs = expo / jnp.sum(expo, axis=-1, keepdims=True)
    probs_low = probs.astype(low)
    mixed = jnp.einsum("hrg,ghe->rhe", probs_low, values, preferred_element_type=jnp.float32)
    mixed = mixed.reshape(rows * pairs, half_width).astype(low)

    def times_transposed(left, right):
        return lax.dot_general(left, right, (((1,), (1,)), ((), ())), preferred_element_type=jnp.float32)

    def contract_rows(left, right):
        return lax.dot_general(
            left, right, (((0,), (0,)), ((), ())), preferred_element_type=jnp.float32
        )

    attended = rows_own(times_transposed(mixed, weight_out)) + bias_out
    middle = inputs + pieces[2] * attended
    normed_mid = rows_all(modulated(middle, pieces[3], pieces[4]).astype(low))
    hidden = jnp.dot(normed_mid, weight_expand, preferred_element_type=jnp.float32) + part_of(bias_expand)
    activated = gelu_tanh(hidden).astype(low)
    branch = rows_own(times_transposed(activated, weight_contract)) + bias_contract
    result = middle + pieces[5] * branch
    block_out = jnp.where(row_ok[:, None], result, 0.0).astype(low)[None]

    grad_out = cotangent[0].astype(jnp.float32) * row_ok[:, None].astype(jnp.float32)
    d_branch = rows_all((pieces[5] * grad_out).astype(low))
    d_gate_mlp = jnp.sum(grad_out * branch, axis=0, keepdims=True)
    grad_contract = contract_rows(d_branch, activated).astype(low)
    grad_bias_contract = jnp.sum(d_branch.astype(jnp.float32), axis=0)
    d_activated = jnp.dot(d_branch, weight_contract, preferred_element_type=jnp.float32)
    d_hidden = jax.vjp(gelu_tanh, hidden)[1](d_activated)[0].astype(low)
    grad_expand = contract_rows(normed_mid, d_hidden).astype(low)
    grad_bias_expand = jnp.sum(d_hidden.astype(jnp.float32), axis=0)
    d_normed_mid = rows_own(times_transposed(d_hidden, weight_expand))
    d_middle, d_shift_mlp, d_scale_mlp = jax.vjp(modulated, middle, pieces[3], pieces[4])[1](d_normed_mid)
    d_middle = d_middle + grad_out
    d_attended = rows_all((pieces[2] * d_middle).astype(low))
    d_gate_attn = jnp.sum(d_middle * attended, axis=0, keepdims=True)
    grad_bias_out = jnp.sum(d_attended.astype(jnp.float32), axis=0)

    def to_tiles(values):
        return jnp.pad(values, ((0, 0), (0, -values.shape[1] % 128)))

    pair_t = jnp.concatenate([normed_in.T, d_attended.T], axis=1).reshape(n, own_rows, 2 * pairs * rows)
    zero_row = jnp.zeros((1, width), jnp.float32)
    d_pieces = jnp.concatenate(
        [zero_row, zero_row, d_gate_attn, d_shift_mlp, d_scale_mlp, d_gate_mlp, zero_row, zero_row]
    )
    v_rows = jnp.concatenate(
        [
            zero_row,
            grad_bias_expand.reshape(2, width),
            grad_bias_out[None],
            grad_bias_contract[None],
            zero_row,
            zero_row,
            zero_row,
        ]
    )
    shape = (n // 4, 2, 2, own_rows, pieces_own.shape[2])
    reduced, tokens_grad, d_mod_all, d_cond, bias_sum = backward(
        (grad_contract.reshape(shape), grad_expand.reshape(shape), weights[0]),
        (
            pair_t,
            d_attended,
            to_tiles(flat_query),
            to_tiles(flat_key),
            to_tiles(flat_value),
            to_tiles(mixed),
            key_ok.astype(jnp.float32)[None],
            inputs,
            d_middle,
            pieces[1],
            d_pieces,
            v_rows,
            jnp.pad(own_modulation, ((0, 128 - own_rows), (0, 0))),
            jnp.pad(cond_own, ((0, 0), (0, 128 - own_rows))),
        ),
        n,
        2,
    )
    tokens_grad = tokens_grad[None]
    same = (labels_all[:, None] == labels_all[None, :]).astype(jnp.float32)
    rates = (
        width ** (-0.5),
        width ** (-0.5),
        (width // 4) ** (-0.5),
        width ** (-0.5),
        FF ** (-0.5),
        0.5,
        0.2,
    )
    masters = (
        modulation_master,
        attention_in_master,
        attention_out_master,
        expand_master,
        contract_master,
        class_table_master,
        biases_master,
    )
    firsts = (
        modulation_first,
        attention_in_first,
        attention_out_first,
        expand_first,
        contract_first,
        class_table_first,
        biases_first,
    )
    seconds = (
        modulation_second,
        attention_in_second,
        attention_out_second,
        expand_second,
        contract_second,
        class_table_second,
        biases_second,
    )
    states = list(zip(masters, firsts, seconds))
    updated, grad_norm, bias_parts = finish(
        reduced,
        silu_own,
        d_mod_all,
        d_cond,
        bias_sum,
        onehot.astype(jnp.float32),
        same,
        [tuple(item.reshape(-1, 128) for item in state) for state in states[:-1]],
        rates[:-1],
        n,
        8,
    )
    factor = jnp.minimum(1.0, CLIP_LIMIT / (grad_norm + 1e-06))
    bias_parts = bias_parts.reshape(n, pairs, 8, 128)[:, :, : chunk_tiles(n, width)].transpose(1, 0, 2, 3)
    bias_parts = bias_parts.reshape(pairs, -1)[:, : 5 * width].reshape(pairs, 5, width)
    grad_biases = jnp.concatenate(
        [
            jnp.sum(d_mod_all, axis=1).reshape(-1),
            bias_parts[:, 0, :half_width].reshape(-1),
            bias_parts[:, 0, half_width:].reshape(-1),
            bias_parts[0, 3],
            bias_parts[:, 1:3].reshape(-1),
            bias_parts[0, 4],
        ]
    )
    bias_grad = lax.dynamic_slice_in_dim(grad_biases, me * bias_share, bias_share, 0) * factor
    updated = [item.reshape(-1) for item in updated] + list(adam_step(bias_grad, *states[-1], rates[-1]))
    return (block_out, tokens_grad, grad_norm) + tuple(updated)


def solution(mesh):
    return jax.shard_map(
        per_device,
        mesh=mesh,
        in_specs=(
            P("dp", "seq", None),
            P("dp", "seq", None),
            P("dp", None),
            P("dp"),
            P("dp"),
            P("dp", "seq"),
            P("dp"),
            P("dp"),
            P("dp"),
            P("dp"),
            P("dp"),
            P("dp"),
            P("dp"),
            P("dp"),
            P("dp"),
            P("dp"),
            P("dp"),
            P("dp"),
            P("dp"),
            P("dp"),
            P("dp"),
            P("dp"),
            P("dp"),
            P("dp"),
            P("dp"),
            P("dp"),
            P("dp"),
        ),
        out_specs=(
            P("dp", "seq", None),
            P("dp", "seq", None),
            P(),
            P("dp"),
            P("dp"),
            P("dp"),
            P("dp"),
            P("dp"),
            P("dp"),
            P("dp"),
            P("dp"),
            P("dp"),
            P("dp"),
            P("dp"),
            P("dp"),
            P("dp"),
            P("dp"),
            P("dp"),
            P("dp"),
            P("dp"),
            P("dp"),
            P("dp"),
            P("dp"),
            P("dp"),
        ),
        check_vma=False,
    )
```

```python
import functools
import jax
import jax.numpy as jnp
from jax import lax
from jax.experimental import pallas as pl
from jax.experimental.pallas import tpu as pltpu
from jax.sharding import PartitionSpec as P

HEAD_DIM = 72
FF = 4608
SIDE = 16
CLASSES = 1024
STEP = 10
LAYER_EPS = 1e-06
MASK_FILL = -1e30
BETA_FIRST = 0.5
BETA_SECOND = 0.5
ADAM_EPS = 1e-08
WEIGHT_DECAY = 0.1
CLIP_LIMIT = 1.0

MESH = pl.DeviceIdType.MESH
GROUPS = ((0, 768, 0, "x"), (768, 768, 0, "y"), (1536, 384, 1, "x"), (1920, 384, 1, "y"))


def when(cond, fn):
    pl.when(cond)(fn)


class Place:
    def __init__(self, line):
        self.line = line
        i = lax.axis_index("dp")
        self.c = lax.axis_index("seq")
        self.x, self.y, self.z = i % 2, (i // 2) % 2, i // 4

    def dev(self, z=None, y=None, x=None):
        z = self.z if z is None else z
        y = self.y if y is None else y
        x = self.x if x is None else x
        return (z * 4 + y * 2 + x, self.c)

    def peer(self, axis):
        return self.dev(x=1 - self.x) if axis == "x" else self.dev(y=1 - self.y)

    def barrier(self):
        bar = pltpu.get_barrier_semaphore()

        def sig(dev):
            pl.semaphore_signal(bar, inc=1, device_id=dev, device_id_type=MESH)

        sig(self.peer("x"))
        sig(self.peer("y"))
        when(self.z > 0, lambda: sig(self.dev(z=self.z - 1)))
        when(self.z < self.line - 1, lambda: sig(self.dev(z=self.z + 1)))
        pl.semaphore_wait(bar, 2 + (self.z > 0).astype(jnp.int32) + (self.z < self.line - 1).astype(jnp.int32))


class Gatherer:
    def __init__(self, line, own, out, keep_sem, sems):
        self.line, self.own, self.out, self.keep_sem = line, own, out, keep_sem
        self.send_a, self.send_u, self.send_d, self.send_b, self.recv_a, self.recv_z, self.recv_b = sems
        self.me = Place(line)
        self.up, self.down = self.me.z < line - 1, self.me.z > 0

    def single(self, m, g, zz):
        lo, width = GROUPS[g][:2]
        return self.out.at[m, zz, self.me.y, self.me.x, :, pl.ds(lo, width)]

    def pair(self, m, g, zz):
        lo, width, _, first = GROUPS[g]
        if first == "x":
            return self.out.at[m, zz, self.me.y, :, :, pl.ds(lo, width)]
        return self.out.at[m, zz, :, self.me.x, :, pl.ds(lo, width)]

    def remote(self, ref, send, recv, dev, source):
        return pltpu.make_async_remote_copy(
            src_ref=ref if source is None else source, dst_ref=ref, send_sem=send, recv_sem=recv,
            device_id=dev, device_id_type=MESH)

    def source(self, m, g):
        lo, width = GROUPS[g][:2]
        return self.own.at[m, :, pl.ds(lo, width)]

    def a_copy(self, m, g, zz, source=None):
        return self.remote(
            self.single(m, g, zz), self.send_a.at[m, g, zz], self.recv_a.at[m, g, zz], self.me.peer(GROUPS[g][3]), source)

    def z_ref(self, m, g, zz):
        return self.pair(m, g, zz) if GROUPS[g][2] == 0 else self.single(m, g, zz)

    def u_copy(self, m, g, zz, source=None):
        dev = self.me.dev(z=jnp.minimum(self.me.z + 1, self.line - 1))
        return self.remote(self.z_ref(m, g, zz), self.send_u.at[m, g, zz], self.recv_z.at[m, g, zz], dev, source)

    def d_copy(self, m, g, zz, source=None):
        dev = self.me.dev(z=jnp.maximum(self.me.z - 1, 0))
        return self.remote(self.z_ref(m, g, zz), self.send_d.at[m, g, zz], self.recv_z.at[m, g, zz], dev, source)

    def b_copy(self, m, g, zz):
        last = "y" if GROUPS[g][3] == "x" else "x"
        return self.remote(self.pair(m, g, zz), self.send_b.at[m, g, zz], self.recv_b.at[m, g, zz], self.me.peer(last), None)

    def keep(self, m):
        me = self.me
        return pltpu.make_async_copy(self.own.at[m], self.out.at[m, me.z, me.y, me.x], self.keep_sem.at[m])

    def begin(self, m):
        z = self.me.z
        self.keep(m).start()
        for g in range(4):
            self.a_copy(m, g, z, self.source(m, g)).start()
        for g in (2, 3):
            when(self.up, lambda g=g: self.u_copy(m, g, z, self.source(m, g)).start())
            when(self.down, lambda g=g: self.d_copy(m, g, z, self.source(m, g)).start())

    def paired(self, m):
        z = self.me.z
        self.keep(m).wait()
        for g in (0, 1):
            self.a_copy(m, g, z).wait_recv()
            when(self.up, lambda g=g: self.u_copy(m, g, z).start())
            when(self.down, lambda g=g: self.d_copy(m, g, z).start())
            self.b_copy(m, g, z).start()

    def arrive(self, m, zz, upward):
        for g in range(4):
            copy = self.u_copy if upward else self.d_copy
            copy(m, g, zz).wait_recv()
            when(self.up if upward else self.down, lambda g=g: copy(m, g, zz).start())
            if GROUPS[g][2] == 0:
                self.b_copy(m, g, zz).start()
            else:
                self.a_copy(m, g, zz).start()

    def crossed(self, m, zz):
        for g in (2, 3):
            self.a_copy(m, g, zz).wait_recv()
            self.b_copy(m, g, zz).start()

    def step(self, m, k):
        z, line = self.me.z, self.line
        when(k <= z, lambda: self.arrive(m, jnp.maximum(z - k, 0), True))
        when(z + k < line, lambda: self.arrive(m, jnp.minimum(z + k, line - 1), False))
        when(k - 1 <= z, lambda: self.crossed(m, jnp.maximum(z - k + 1, 0)))
        when((k > 1) & (z + k - 1 < line), lambda: self.crossed(m, jnp.minimum(z + k - 1, line - 1)))

    def complete(self, m):
        @pl.loop(0, self.line)
        def _(zz):
            for g in range(4):
                self.b_copy(m, g, zz).wait_recv()

    def drain(self, m):
        z = self.me.z

        @pl.loop(0, self.line)
        def _(zz):
            for g in range(4):
                self.b_copy(m, g, zz).wait_send()
                if GROUPS[g][2] == 1:
                    self.a_copy(m, g, zz).wait_send()
                when(self.up & (zz <= z), lambda g=g: self.u_copy(m, g, zz).wait_send())
                when(self.down & (zz >= z), lambda g=g: self.d_copy(m, g, zz).wait_send())

        for g in (0, 1):
            self.a_copy(m, g, z).wait_send()


def dot(left, right, a=1, b=0):
    return lax.dot_general(left, right, (((a,), (b,)), ((), ())), preferred_element_type=jnp.float32)


def normal(values):
    centre = values - jnp.mean(values, axis=-1, keepdims=True)
    return centre * lax.rsqrt(jnp.mean(centre * centre, axis=-1, keepdims=True) + LAYER_EPS)


def all_peers(n, src, dst, send, recv, spread):
    me, c = lax.axis_index("dp"), lax.axis_index("seq")

    def copy(j, there, slot):
        return pltpu.make_async_remote_copy(
            src_ref=src.at[there] if spread else src, dst_ref=dst.at[slot], send_sem=send.at[j], recv_sem=recv.at[slot],
            device_id=(there, c), device_id_type=MESH)

    def start():
        @pl.loop(1, n)
        def _(j):
            copy(j, (me + j) % n, me).start()

    def wait():
        @pl.loop(1, n)
        def _(j):
            copy(j, (me + j) % n, (me + n - j) % n).wait()

    return start, wait


def greet_all(n):
    me, c = lax.axis_index("dp"), lax.axis_index("seq")
    bar = pltpu.get_barrier_semaphore()
    pl.semaphore_signal(bar, inc=1, device_id=(me, 1 - c), device_id_type=MESH)

    @pl.loop(1, n)
    def _(j):
        pl.semaphore_signal(bar, inc=1, device_id=((me + j) % n, c), device_id_type=MESH)

    return bar


def head_window(h):
    lo = pl.multiple_of(h * HEAD_DIM // 128 * 128, 128)
    lane = lax.broadcasted_iota(jnp.int32, (1, 256), 1) + lo - h * HEAD_DIM
    return pl.ds(lo, 256), ((lane >= 0) & (lane < HEAD_DIM)).astype(jnp.bfloat16)


def head_probs(qh, kh, seen):
    logits = jnp.where(seen, dot(qh, kh, 1, 1) * HEAD_DIM ** (-0.5), MASK_FILL)
    expo = jnp.exp(logits - jnp.max(logits, axis=-1, keepdims=True))
    return expo / jnp.sum(expo, axis=-1, keepdims=True)


def forward_kernel(line, *refs):
    (m_in, m_out, m_expand, m_contract, m_table, m_mod, onehot, time_vec, x, key_ok, b_mod, b_query, b_value, b_out,
     weights, weight, h1, q, k, v, o, attended, middle, h2, pieces, cond, silu, mod_half) = refs[:28]
    (f_in, f_out, f_expand, f_contract, f_table, f_mod, own, table, cond_part, cond_got, mods, mod_part, mod_got, blocks, w,
     proj, mix, wide, partial, partial_got, in_sem, w_sem, pair_send, pair_recv, cond_send, cond_recv, mod_send, mod_recv,
     keep_sem) = refs[28:57]
    n = line * 4
    low, f32 = jnp.bfloat16, jnp.float32
    me, c = lax.axis_index("dp"), lax.axis_index("seq")
    gat = Gatherer(line, own, weights, keep_sem, refs[57:])
    rows, width = x.shape
    own_rows, half = own.shape[1], own.shape[2] // 4
    edge = 3 * half // 128 * 128
    tiles = width // 128
    sources, flats = (m_in, m_out, m_table, m_mod, m_expand, m_contract), (f_in, f_out, f_table, f_mod, f_expand, f_contract)

    def load(i):
        return pltpu.make_async_copy(sources[i], flats[i], in_sem.at[i])

    for i in range(6):
        load(i).start()
    bar = greet_all(n)

    def swap(i, src, dst):
        return pltpu.make_async_remote_copy(
            src_ref=src, dst_ref=dst, send_sem=pair_send.at[i], recv_sem=pair_recv.at[i], device_id=(me, 1 - c),
            device_id_type=MESH)

    def tile(flat, t, count, per_row):
        return flat[pl.ds(t, count, stride=per_row), :]

    def cut_heads(flat, part, per_row):
        start = part * tiles + c * (tiles // 2)
        found = jnp.concatenate([tile(flat, start + j, own_rows, per_row) for j in range(tiles // 2 + 1)], axis=1)
        return jnp.where(c == 0, found[:, :half], found[:, found.shape[1] - half :]).astype(low)

    def cut(flat, target, count):
        for j in range(count):
            target[:own_rows, 128 * j : 128 * j + 128] = tile(flat, c * count + j, own_rows, 2 * count).astype(low)

    load(0).wait()
    load(1).wait()
    for part in range(3):
        own[0, :, part * half : (part + 1) * half] = cut_heads(f_in, part, 3 * tiles)
    own[0, :, 3 * half :] = cut_heads(f_out, 0, tiles)
    load(2).wait()
    class_rows = table.shape[0]
    for t in range(tiles):
        table[:, 128 * t : 128 * t + 128] = tile(f_table, t, class_rows, tiles).astype(low)
    found = dot(onehot[...], table[...])
    mine = lax.broadcasted_iota(jnp.int32, (n, width), 0) == me
    found = found + jnp.where(mine, jnp.broadcast_to(time_vec[...].astype(f32), (n, width)), 0.0)
    cond_part[...] = jnp.zeros_like(cond_part)
    for i in range(n):
        cond_part[i, :, :own_rows] = found[:, i * own_rows : (i + 1) * own_rows]
    cond_got[me] = cond_part[me]

    pl.semaphore_wait(bar, n)
    cond_start, cond_wait = all_peers(n, cond_part, cond_got, cond_send, cond_recv, True)
    mod_start, mod_wait = all_peers(n, mod_part, mod_got, mod_send, mod_recv, True)
    cond_start()
    gat.begin(0)
    load(3).wait()
    mod_half[own_rows:] = jnp.zeros((mod_half.shape[0] - own_rows, mod_half.shape[1]), low)
    cut(f_mod, mod_half, 3 * tiles)
    load(4).wait()
    cut(f_expand, own.at[1], 4 * half // 128)

    cond_wait()
    value = jnp.sum(cond_got[...], axis=0)
    cond[...] = value
    silu[...] = (value / (1.0 + jnp.exp(-value))).astype(low)
    mods[...] = dot(silu[...], mod_half[...])

    @pl.loop(0, n)
    def _(s):
        mod_part[s] = mods[pl.ds(s, 1), :]

    mod_got[me] = mod_part[me]
    mod_start()
    gat.paired(0)
    gat.begin(1)
    load(5).wait()
    cut(f_contract, own.at[2], 4 * half // 128)
    mod_wait()
    pieces[c] = jnp.sum(mod_got[...], axis=0) + b_mod[...]
    swap(0, pieces.at[c], pieces.at[c]).start()
    gat.step(0, 1)
    gat.begin(2)
    swap(0, pieces.at[c], pieces.at[c]).wait()
    shift, scale, gate = (pieces[0, :, i * width : (i + 1) * width] for i in range(3))
    h1[c] = (normal(x[...]) * (1.0 + scale) + shift).astype(low)
    swap(1, h1.at[c], h1.at[c]).start()

    @pl.loop(2, line + 1)
    def _(k):
        gat.step(0, k)

    gat.paired(1)
    gat.complete(0)

    def fetch():
        return pltpu.make_async_copy(weights.at[0], blocks, w_sem.at[0])

    fetch().start()
    gat.paired(2)
    swap(1, h1.at[c], h1.at[c]).wait()
    fetch().wait()
    for i in range(n):
        w[i * own_rows : (i + 1) * own_rows, :] = blocks[i // 4, i // 2 % 2, i % 2]
    keep_w = pltpu.make_async_copy(w, weight, w_sem.at[1])
    keep_w.start()
    both = jnp.concatenate([h1[0], h1[1]], axis=0)

    @pl.loop(0, proj.shape[1] // 256)
    def _(t):
        cols = pl.ds(pl.multiple_of(t * 256, 256), 256)
        proj[:, cols] = dot(both, w[:, cols])

    spare = q.shape[1] - half
    for item, value in (
        (q, proj[:, :half] + b_query[...]),
        (k, proj[:, half : 2 * half]),
        (v, proj[:, 2 * half : 3 * half] + b_value[...]),
    ):
        item[:, :half] = value.astype(low)
        item[:, half:] = jnp.zeros((2 * rows, spare), low)
    mix[...] = jnp.zeros_like(mix)
    seen = jnp.broadcast_to(key_ok[...], (2 * rows, 2 * rows)) > 0.0
    heads = half // HEAD_DIM

    def head(h):
        win, lanes = head_window(h)
        probs = head_probs(q[:, win] * lanes, k[:, win], seen)
        mix[:, win] = mix[:, win] + dot(probs.astype(low), v[:, win] * lanes)

    @pl.loop(0, max(heads, 2 * line))
    def _(t):
        when(t < heads, lambda: head(t))
        when(t < 2 * line, lambda: gat.step(1 + t % 2, t // 2 + 1))

    o[...] = mix[...].astype(low)
    wide[:, : 3 * half - edge] = jnp.zeros((2 * rows, 3 * half - edge), low)
    wide[:, 3 * half - edge :] = mix[:, :half].astype(low)

    @pl.loop(0, tiles)
    def _(t):
        cols = pl.ds(pl.multiple_of(t * 128, 128), 128)
        part = dot(wide[...], w[cols, edge:], 1, 1)
        partial[0, :, cols] = part[:rows]
        partial[1, :, cols] = part[rows:]

    swap(2, partial.at[1 - c], partial_got).start()
    swap(2, partial.at[1 - c], partial_got).wait()
    attended[...] = partial[c] + partial_got[...] + b_out[...]
    middle[...] = x[...] + gate * attended[...]
    shift, scale = (pieces[1, :, i * width : (i + 1) * width] for i in range(2))
    h2[c] = (normal(middle[...]) * (1.0 + scale) + shift).astype(low)
    swap(3, h2.at[c], h2.at[c]).start()
    gat.complete(1)
    gat.complete(2)
    swap(3, h2.at[c], h2.at[c]).wait()
    keep_w.wait()

    @pl.loop(0, 3)
    def _(m):
        gat.drain(m)


def forward(hbm_args, vmem_args, n, collective_id):
    line = n // 4
    onehot, time_vec, x = vmem_args[:3]
    rows, width = x.shape
    own_rows, half = width // n, width // 2
    low, f32 = jnp.bfloat16, jnp.float32
    dma = pltpu.SemaphoreType.DMA
    vmem, hbm = pl.BlockSpec(memory_space=pltpu.VMEM), pl.BlockSpec(memory_space=pltpu.HBM)
    heads = (2 * rows, -(-half // 128) * 128)
    edge = 3 * half // 128 * 128

    def shape(dims, kind):
        return jax.ShapeDtypeStruct(dims, kind)

    def scratch(dims, kind):
        return pltpu.VMEM(dims, kind)

    return pl.pallas_call(
        functools.partial(forward_kernel, line),
        out_shape=[
            shape((3, line, 2, 2, own_rows, 4 * half), low),
            shape((width, 4 * half), low),
            shape((2, rows, width), low),
            shape(heads, low),
            shape(heads, low),
            shape(heads, low),
            shape(heads, low),
            shape((rows, width), f32),
            shape((rows, width), f32),
            shape((2, rows, width), low),
            shape((2, 1, 3 * width), f32),
            shape((n, 128), f32),
            shape((n, 128), low),
            shape((128, 3 * width), low),
        ],
        in_specs=[hbm] * len(hbm_args) + [vmem] * len(vmem_args),
        out_specs=[hbm] * 2 + [vmem] * 12,
        scratch_shapes=[scratch(item.shape, f32) for item in hbm_args]
        + [
            scratch((3, own_rows, 4 * half), low),
            scratch((onehot.shape[1], width), low),
            scratch((n, n, 128), f32),
            scratch((n, n, 128), f32),
            scratch((n, 3 * width), f32),
            scratch((n, 1, 3 * width), f32),
            scratch((n, 1, 3 * width), f32),
            scratch((line, 2, 2, own_rows, 4 * half), low),
            scratch((width, 4 * half), low),
            scratch((2 * rows, edge + 128), f32),
            scratch(heads, f32),
            scratch(heads, low),
            scratch((2, rows, width), f32),
            scratch((rows, width), f32),
            dma((6,)),
            dma((2,)),
            dma((4,)),
            dma((4,)),
            dma((n,)),
            dma((n,)),
            dma((n,)),
            dma((n,)),
            dma((3,)),
        ]
        + [dma((3, 4, line))] * 7,
        compiler_params=pltpu.CompilerParams(
            collective_id=collective_id, has_side_effects=True, vmem_limit_bytes=60 * 2**20),
        name="forward",
    )(*hbm_args, *vmem_args)


class Reducer:
    def __init__(self, line, grads, out, own, got_b, got_z, got_a, sems):
        self.line, self.grads, self.out = line, grads, out
        self.own, self.acc, self.got_z, self.got_a = own, got_b, got_z, got_a
        self.load, self.send_b, self.send_z, self.send_a, self.recv_b, self.recv_z, self.recv_a = sems
        self.me = me = Place(line)
        self.up, self.down = me.z < line - 1, me.z > 0
        self.above, self.below = me.dev(z=jnp.minimum(me.z + 1, line - 1)), me.dev(z=jnp.maximum(me.z - 1, 0))
        self.units = len(grads) * line

    def last(self, g):
        return "y" if GROUPS[g][3] == "x" else "x"

    def first(self, g):
        return self.me.x if GROUPS[g][3] == "x" else self.me.y

    def half(self, grad, g, zz, mine):
        cols = pl.ds(GROUPS[g][0], GROUPS[g][1])
        if self.last(g) == "y":
            return grad.at[zz, self.me.y if mine else 1 - self.me.y, :, :, cols]
        return grad.at[zz, :, self.me.x if mine else 1 - self.me.x, :, cols]

    def loading(self, u, g, zz, side, grad=None):
        grad = self.grads[0] if grad is None else grad
        return pltpu.make_async_copy(
            self.half(grad, g, zz, True), self.own[g].at[u % 3, side], self.load.at[u % 3, g, side])

    def remote(self, src, dst, send, recv, dev):
        return pltpu.make_async_remote_copy(
            src_ref=src, dst_ref=dst, send_sem=send, recv_sem=recv, device_id=dev, device_id_type=MESH)

    def b_copy(self, m, g, zz, grad=None):
        grad = self.grads[0] if grad is None else grad
        return self.remote(
            self.half(grad, g, zz, False), self.acc[g].at[m, zz], self.send_b.at[m, g, zz], self.recv_b.at[m, g, zz],
            self.me.peer(self.last(g)))

    def slot_a(self, g, zz):
        return zz if GROUPS[g][2] == 1 else 0

    def a_copy(self, m, g, zz):
        return self.remote(
            self.acc[g].at[m, zz, 1 - self.first(g)], self.got_a[g].at[m, self.slot_a(g, zz)], self.send_a.at[m, g, zz],
            self.recv_a.at[m, g, zz], self.me.peer(GROUPS[g][3]))

    def z_copy(self, m, g, zz, slot, dev):
        part = self.acc[g].at[m, zz] if GROUPS[g][2] == 0 else self.acc[g].at[m, zz, self.first(g)]
        return self.remote(part, self.got_z[g].at[m, slot], self.send_z.at[m, g, zz], self.recv_z.at[m, g, slot], dev)

    def add_b(self, m, g, zz, u, side):
        self.loading(u, g, zz, side).wait()
        self.b_copy(m, g, zz).wait_recv()
        self.acc[g][m, zz] = self.acc[g][m, zz] + self.own[g][u % 3, side]

    def add_z(self, m, g, zz, slot):
        acc, got = self.acc[g], self.got_z[g]
        self.z_copy(m, g, self.me.z, slot, self.below).wait_recv()
        if GROUPS[g][2] == 0:
            acc[m, zz] = acc[m, zz] + got[m, slot]
        else:
            acc[m, zz, self.first(g)] = acc[m, zz, self.first(g)] + got[m, slot]

    def add_a(self, m, g, zz):
        self.a_copy(m, g, zz).wait_recv()
        acc, first = self.acc[g], self.first(g)
        acc[m, zz, first] = acc[m, zz, first] + self.got_a[g][m, self.slot_a(g, zz)]

    def planes(self, k, fn):
        z, line = self.me.z, self.line
        when(z + k < line, lambda: fn(jnp.minimum(z + k, line - 1), True))
        when((z >= k) & (k > 0), lambda: fn(jnp.maximum(z - k, 0), False))

    def begin(self, v):
        m, j = v // self.line, v % self.line

        def one(grad, zz, upward):
            for g in range(4):
                self.b_copy(m, g, zz, grad).start()
                self.loading(v, g, zz, 0 if upward else 1, grad).start()

        for index, grad in enumerate(self.grads):
            when(m == index, lambda: self.planes(self.line - 1 - j, lambda zz, upward: one(grad, zz, upward)))

    def onward(self, m, g, zz, k, upward):
        if upward:
            when(self.down, lambda: self.add_z(m, g, zz, zz))
            self.z_copy(m, g, zz, zz, self.above).start()
        else:
            when(self.up, lambda: self.add_z(m, g, zz, zz))
            self.z_copy(m, g, zz, jnp.where(k == 1, self.line, zz), self.below).start()

    def near(self, u, m, j):
        k = self.line - 1 - j

        def one(zz, upward):
            for g in range(4):
                self.add_b(m, g, zz, u, 0 if upward else 1)
                if GROUPS[g][2] == 1:
                    self.a_copy(m, g, zz).start()
                else:
                    when(k > 0, lambda g=g: self.onward(m, g, zz, k, upward))

        self.planes(k, one)

    def far(self, m, j):
        k = self.line - j

        def one(zz, upward):
            for g in (2, 3):
                self.add_a(m, g, zz)
                self.onward(m, g, zz, k, upward)

        when((k > 0) & (k < self.line), lambda: self.planes(k, one))

    def close(self, m):
        z = self.me.z
        for g in (0, 1):
            when(self.down, lambda g=g: self.add_z(m, g, z, z))
            when(self.up, lambda g=g: self.add_z(m, g, z, self.line))
            self.a_copy(m, g, z).start()

    def final(self, m):
        z = self.me.z
        for g in range(4):
            cols = pl.ds(GROUPS[g][0], GROUPS[g][1])
            self.add_a(m, g, z)
            if GROUPS[g][2] == 1:
                when(self.down, lambda g=g: self.add_z(m, g, z, z))
                when(self.up, lambda g=g: self.add_z(m, g, z, self.line))
            self.out[m, :, cols] = self.acc[g][m, z, self.first(g)]

    def unit(self, u):
        line = self.line
        m, j = u // line, u % line
        when(u + 2 < self.units, lambda: self.begin(jnp.minimum(u + 2, self.units - 1)))
        self.near(u, m, j)
        self.far(m, j)
        when(j == line - 1, lambda: self.close(m))
        when((j == 0) & (m > 0), lambda: self.final(jnp.maximum(m - 1, 0)))

    def drain(self):
        z = self.me.z

        @pl.loop(0, len(self.grads))
        def _(m):
            @pl.loop(0, self.line)
            def _(zz):
                for g in range(4):
                    self.b_copy(m, g, zz).wait_send()
                    if GROUPS[g][2] == 1:
                        self.a_copy(m, g, zz).wait_send()
                    when(zz != z, lambda g=g: self.z_copy(m, g, zz, zz, self.above).wait_send())
            for g in (0, 1):
                self.a_copy(m, g, z).wait_send()


def reducer_scratch(count, line, rows, dt):
    dma = pltpu.SemaphoreType.DMA
    own = [pltpu.VMEM((3, 2, 2, rows, GROUPS[g][1]), dt) for g in range(4)]
    got_b = [pltpu.VMEM((count, line, 2, rows, GROUPS[g][1]), dt) for g in range(4)]
    got_z = [pltpu.VMEM((count, line + 1) + ((2,) if GROUPS[g][2] == 0 else ()) + (rows, GROUPS[g][1]), dt) for g in range(4)]
    got_a = [pltpu.VMEM((count, line if GROUPS[g][2] == 1 else 1, rows, GROUPS[g][1]), dt) for g in range(4)]
    sems = [dma((3, 4, 2))] + [dma((count, 4, line))] * 4 + [dma((count, 4, line + 1))] + [dma((count, 4, line))]
    return own + got_b + got_z + got_a + sems


def make_reducer(line, grads, out, refs):
    return Reducer(line, grads, out, refs[:4], refs[4:8], refs[8:12], refs[12:16], refs[16:])


def backward_kernel(line, *refs):
    (g_contract, g_expand, weight, pair_t, d_att, q, k, v, o, key_ok, x, d_mid, scale_a, d_pieces, v_rows, modulation, cond,
     out, tokens_grad, d_mod_all, d_cond, bias_sum) = refs[:22]
    (w, grads, rhs, d_o, d_q, d_k, d_v, d_h, d_h_got, dp, dp_got, msg, msg_got, vec, vec_got, d_silu, d_silu_got, chunk,
     w_sem, pair_send, pair_recv, msg_send, msg_recv, vec_send, vec_recv) = refs[22:47]
    n = line * 4
    low = jnp.bfloat16
    me, c = lax.axis_index("dp"), lax.axis_index("seq")
    red = make_reducer(line, (g_contract, g_expand, grads), out, refs[47:])
    rows, width = x.shape
    half = weight.shape[1] // 4
    heads = half // HEAD_DIM
    edge = 3 * half // 128 * 128
    partner = (me, 1 - c)

    def swap(i, src, dst):
        return pltpu.make_async_remote_copy(
            src_ref=src, dst_ref=dst, send_sem=pair_send.at[i], recv_sem=pair_recv.at[i], device_id=partner, device_id_type=MESH)

    w_copy = pltpu.make_async_copy(weight, w, w_sem)
    w_copy.start()
    bar = greet_all(n)
    pl.semaphore_wait(bar, n)
    red.begin(0)
    red.begin(1)

    w_copy.wait()
    d_o[:, :half] = dot(d_att[...], w[:, edge:])[:, 3 * half - edge :].astype(low)
    d_o[:, half:] = jnp.zeros((2 * rows, d_o.shape[1] - half), low)
    for item in (d_q, d_k, d_v):
        item[...] = jnp.zeros_like(item)

    seen = jnp.broadcast_to(key_ok[...], (2 * rows, 2 * rows)) > 0.0

    def head(h):
        win, lanes = head_window(h)
        qh, kh, doh = q[:, win] * lanes, k[:, win] * lanes, d_o[:, win] * lanes
        probs = head_probs(qh, kh, seen)
        d_probs = dot(doh, v[:, win], 1, 1)
        inner = jnp.sum(probs * d_probs, axis=-1, keepdims=True)
        d_logits = (probs * (d_probs - inner)).astype(low)
        d_q[:, win] = d_q[:, win] + dot(d_logits, kh) * HEAD_DIM ** (-0.5)
        d_k[:, win] = d_k[:, win] + dot(d_logits, qh, 0, 0) * HEAD_DIM ** (-0.5)
        d_v[:, win] = d_v[:, win] + dot(probs.astype(low), doh, 0, 0)

    def weight_grads():
        for i, item in enumerate((d_q, d_k, d_v)):
            rhs[: 2 * rows, i * half : (i + 1) * half] = item[:, :half].astype(low)
        rhs[: 2 * rows, 3 * half :] = jnp.zeros((2 * rows, half), low)
        rhs[2 * rows :, edge : 3 * half] = jnp.zeros((2 * rows, 3 * half - edge), low)
        rhs[2 * rows :, 3 * half :] = o[:, :half]
        vec[0:1, :half] = jnp.sum(rhs[: 2 * rows, :half].astype(jnp.float32), axis=0, keepdims=True)
        vec[0:1, half:] = jnp.sum(rhs[: 2 * rows, 2 * half : 3 * half].astype(jnp.float32), axis=0, keepdims=True)
        vec[1:] = v_rows[1:]

        @pl.loop(0, n)
        def _(i):
            block = grads.at[i // 4, i // 2 % 2, i % 2]
            block[:, :edge] = dot(pair_t[i, :, : 2 * rows], rhs[: 2 * rows, :edge]).astype(low)
            block[:, edge:] = dot(pair_t[i], rhs[:, edge:]).astype(low)

    def input_grad():
        @pl.loop(0, width // 128)
        def _(t):
            cols = pl.ds(pl.multiple_of(t * 128, 128), 128)
            part = dot(rhs[: 2 * rows, : edge + 128], w[cols, : edge + 128], 1, 1)
            d_h[0, :, cols] = part[:rows]
            d_h[1, :, cols] = part[rows:]

        swap(0, d_h.at[1 - c], d_h_got).start()

    def norm_grad():
        swap(0, d_h.at[1 - c], d_h_got).wait()
        d_n = d_h[c] + d_h_got[...]
        centre = x[...] - jnp.mean(x[...], axis=-1, keepdims=True)
        inv = lax.rsqrt(jnp.mean(centre * centre, axis=-1, keepdims=True) + LAYER_EPS)
        normed = centre * inv
        e = d_n * (1.0 + scale_a[...])
        d_x = (e - jnp.mean(e, axis=-1, keepdims=True) - normed * jnp.mean(e * normed, axis=-1, keepdims=True)) * inv
        tokens_grad[...] = (d_x + d_mid[...]).astype(low)
        dp[...] = d_pieces[...]
        dp[0:1] = jnp.sum(d_n, axis=0, keepdims=True)
        dp[1:2] = jnp.sum(d_n * normed, axis=0, keepdims=True)
        swap(1, dp, dp_got).start()

    msg_start, msg_wait = all_peers(n, msg, msg_got, msg_send, msg_recv, False)
    vec_start, vec_wait = all_peers(n, chunk, vec_got, vec_send, vec_recv, True)
    per = chunk_tiles(n, width)

    def send_mod():
        swap(1, dp, dp_got).wait()
        d_mod = (dp[...] + dp_got[...]).astype(low).astype(jnp.float32)
        own = jnp.where(c == 0, d_mod[0:3], d_mod[3:6])
        for r in range(3):
            msg[r] = own[r : r + 1]
        msg_got[me] = msg[...]
        chunk[...] = jnp.zeros_like(chunk)
        tiles = width // 128
        for t in range(5 * tiles):
            chunk[t // per, t % per] = vec[t // tiles : t // tiles + 1, t % tiles * 128 : t % tiles * 128 + 128]
        vec_got[me] = chunk[me]
        msg_start()
        vec_start()

    def mod_grad():
        msg_wait()
        vec_wait()

        @pl.loop(0, n)
        def _(s):
            for r in range(3):
                d_mod_all[c, pl.ds(s, 1), r * width : (r + 1) * width] = msg_got[s, r]

        bias_sum[c] = jnp.zeros((8, 128), jnp.float32)
        for r in range(per):
            bias_sum[c, r : r + 1] = jnp.sum(vec_got[:, r], axis=0)
        d_silu[...] = dot(d_mod_all[c].astype(low), modulation[...], 1, 1)
        swap(2, d_silu, d_silu_got).start()
        swap(3, d_mod_all.at[c], d_mod_all.at[c]).start()
        swap(4, bias_sum.at[c], bias_sum.at[c]).start()

    def cond_grad():
        swap(2, d_silu, d_silu_got).wait()
        swap(3, d_mod_all.at[c], d_mod_all.at[c]).wait()
        swap(4, bias_sum.at[c], bias_sum.at[c]).wait()
        gate = 1.0 / (1.0 + jnp.exp(-cond[...]))
        d_cond[...] = (d_silu[...] + d_silu_got[...]) * (gate + cond[...] * gate * (1.0 - gate))

    steps = (weight_grads, input_grad, norm_grad, send_mod, mod_grad, cond_grad)

    @pl.loop(0, red.units)
    def _(u):
        @pl.loop(0, jnp.where(u < heads // 2, 2, 0))
        def _(i):
            head(2 * u + i)

        red.unit(u)
        for i, step in enumerate(steps):
            when(u == heads // 2 - 1 + i, step)

    red.final(2)
    red.drain()


def chunk_tiles(n, width):
    return -(-5 * (width // 128) // n)


def backward(hbm_args, vmem_args, n, collective_id):
    line = n // 4
    grad = hbm_args[0]
    rows, cols = grad.shape[-2:]
    pair_t, d_att, q = vmem_args[0], vmem_args[1], vmem_args[2]
    all_rows, width = d_att.shape
    low, f32 = jnp.bfloat16, jnp.float32
    dma = pltpu.SemaphoreType.DMA
    vmem, hbm = pl.BlockSpec(memory_space=pltpu.VMEM), pl.BlockSpec(memory_space=pltpu.HBM)
    wide = q.shape
    per = chunk_tiles(n, width)
    return pl.pallas_call(
        functools.partial(backward_kernel, line),
        out_shape=[
            jax.ShapeDtypeStruct((3, rows, cols), low),
            jax.ShapeDtypeStruct((all_rows // 2, width), low),
            jax.ShapeDtypeStruct((2, n, 3 * width), f32),
            jax.ShapeDtypeStruct((n, 128), f32),
            jax.ShapeDtypeStruct((2, 8, 128), f32),
        ],
        in_specs=[hbm] * len(hbm_args) + [vmem] * len(vmem_args),
        out_specs=[vmem] * 5,
        scratch_shapes=[
            pltpu.VMEM((width, cols), low),
            pltpu.VMEM((line, 2, 2, rows, cols), low),
            pltpu.VMEM((2 * all_rows, cols), low),
            pltpu.VMEM(wide, low),
            pltpu.VMEM(wide, f32),
            pltpu.VMEM(wide, f32),
            pltpu.VMEM(wide, f32),
            pltpu.VMEM((2, all_rows // 2, width), f32),
            pltpu.VMEM((all_rows // 2, width), f32),
            pltpu.VMEM((8, width), f32),
            pltpu.VMEM((8, width), f32),
            pltpu.VMEM((3, 1, width), f32),
            pltpu.VMEM((n, 3, 1, width), f32),
            pltpu.VMEM((8, width), f32),
            pltpu.VMEM((n, per, 1, 128), f32),
            pltpu.VMEM((n, 128), f32),
            pltpu.VMEM((n, 128), f32),
            pltpu.VMEM((n, per, 1, 128), f32),
            dma,
            dma((5,)),
            dma((5,)),
            dma((n,)),
            dma((n,)),
            dma((n,)),
            dma((n,)),
        ]
        + reducer_scratch(3, line, rows, low),
        compiler_params=pltpu.CompilerParams(
            collective_id=collective_id, has_side_effects=True, vmem_limit_bytes=63 * 2**20),
        name="backward",
    )(*hbm_args, *vmem_args)


def exchange_kernel(n, spread, *refs):
    count = len(spread)
    srcs, outs, (send, recv) = refs[:count], refs[count:2 * count], refs[2 * count:]
    me, c = lax.axis_index("dp"), lax.axis_index("seq")
    bar = pltpu.get_barrier_semaphore()

    @pl.loop(1, n)
    def _(j):
        pl.semaphore_signal(bar, inc=1, device_id=((me + j) % n, c), device_id_type=MESH)

    for a in range(count):
        outs[a][me] = srcs[a][me] if spread[a] else srcs[a][...]
    pl.semaphore_wait(bar, n - 1)

    def copy(a, j, there, slot):
        return pltpu.make_async_remote_copy(
            src_ref=srcs[a].at[there] if spread[a] else srcs[a], dst_ref=outs[a].at[slot],
            send_sem=send.at[a, j], recv_sem=recv.at[a, slot], device_id=(there, c), device_id_type=MESH)

    @pl.loop(1, n)
    def _(j):
        for a in range(count):
            copy(a, j, (me + j) % n, me).start()

    @pl.loop(1, n)
    def _(j):
        for a in range(count):
            copy(a, j, (me + j) % n, (me + n - j) % n).wait()


def exchange(blocks, spread, n, collective_id):
    count = len(blocks)
    parts = [b.shape[1:] if s else b.shape for b, s in zip(blocks, spread)]
    dma = pltpu.SemaphoreType.DMA
    return pl.pallas_call(
        functools.partial(exchange_kernel, n, spread),
        out_shape=[jax.ShapeDtypeStruct((n,) + p, b.dtype) for p, b in zip(parts, blocks)],
        in_specs=[pl.BlockSpec(memory_space=pltpu.VMEM)] * count,
        out_specs=[pl.BlockSpec(memory_space=pltpu.VMEM)] * count,
        scratch_shapes=[dma((count, n)), dma((count, n))],
        compiler_params=pltpu.CompilerParams(collective_id=collective_id, has_side_effects=True, vmem_limit_bytes=32 * 2**20),
        name="exchange",
    )(*blocks)


def adam_step(grad, master, first, second, rate):
    first_new = BETA_FIRST * first + (1.0 - BETA_FIRST) * grad
    second_new = BETA_SECOND * second + (1.0 - BETA_SECOND) * grad * grad
    first_hat = first_new / (1.0 - BETA_FIRST**STEP)
    second_hat = second_new / (1.0 - BETA_SECOND**STEP)
    master_new = master - rate * (
        first_hat / (jnp.sqrt(second_hat) + ADAM_EPS) + WEIGHT_DECAY * master
    )
    return (first_new, second_new, master_new)


def chunk_rows(rows):
    sizes = [d for d in range(8, 257, 8) if rows % d == 0]
    return sizes[-1] if sizes else rows


def norm_kernel(n, *refs):
    reduced, silu, d_mod, d_cond, bias_sum, onehot, same = refs[:7]
    flat, factor_out, norm_out, bias_out = refs[7:13], refs[13], refs[14], refs[15]
    both, wide, block, got, pair_send, pair_recv, send, recv = refs[16:]
    me, c = lax.axis_index("dp"), lax.axis_index("seq")
    rows = reduced.shape[1]
    half = reduced.shape[2]
    head = half // 4

    bar = pltpu.get_barrier_semaphore()
    pl.semaphore_signal(bar, inc=1, device_id=(me, 1 - c), device_id_type=MESH)

    @pl.loop(1, n)
    def _(j):
        pl.semaphore_signal(bar, inc=1, device_id=((me + j) % n, c), device_id_type=MESH)

    both[c] = reduced[...]
    pl.semaphore_wait(bar, n)
    pair = pltpu.make_async_remote_copy(
        src_ref=reduced, dst_ref=both.at[c], send_sem=pair_send, recv_sem=pair_recv,
        device_id=(me, 1 - c), device_id_type=MESH)
    pair.start()

    def spread(a, width):
        total = None
        tiles = width // 128
        for t in range(tiles):
            part = wide[:, 128 * t : 128 * t + 128]
            flat[a][pl.ds(t, rows, stride=tiles), :] = part
            square = part * part
            total = square if total is None else total + square
        return jnp.sum(total)

    part_mod = d_mod.shape[2]
    for core in range(2):
        wide[:, core * part_mod : (core + 1) * part_mod] = dot(silu[...], d_mod[core].astype(silu.dtype), 0, 0)
    squares = spread(0, wide.shape[1])
    mod_sums = jnp.sum(d_mod[...], axis=1)
    squares = squares + jnp.where(me == 0, jnp.sum(mod_sums * mod_sums), 0.0)
    width = n * rows
    tile = chunk_tiles(n, width) * me + lax.broadcasted_iota(jnp.int32, (8, 128), 0)
    squares = squares + jnp.sum(bias_sum[0] * bias_sum[0])
    squares = squares + jnp.sum(jnp.where(tile < 3 * (width // 128), bias_sum[1] * bias_sum[1], 0.0))
    pair.wait()
    for core in range(2):
        for part in range(3):
            lo = (2 * part + core) * head
            wide[:, lo : lo + head] = both[core, 2, :, part * head : (part + 1) * head].astype(jnp.float32)
    squares = squares + spread(1, 6 * head)
    for core in range(2):
        wide[:, core * head : (core + 1) * head] = both[core, 2, :, 3 * head :].astype(jnp.float32)
    squares = squares + spread(2, 2 * head)
    for a in (3, 4):
        for core in range(2):
            wide[:, core * half : (core + 1) * half] = both[core, 4 - a].astype(jnp.float32)
        squares = squares + spread(a, 2 * half)

    slots = d_cond.shape[0]
    block[:slots] = d_cond[...]
    block[slots : slots + 8] = jnp.full((8, 128), squares, jnp.float32)
    block[slots + 8 : slots + 16] = bias_sum[0]
    block[slots + 16 :] = bias_sum[1]
    got[me] = block[...]

    def copy(j, there, slot):
        return pltpu.make_async_remote_copy(
            src_ref=block, dst_ref=got.at[slot], send_sem=send.at[j], recv_sem=recv.at[slot],
            device_id=(there, c), device_id_type=MESH)

    @pl.loop(1, n)
    def _(j):
        copy(j, (me + j) % n, me).start()

    @pl.loop(1, n)
    def _(j):
        copy(j, (me + j) % n, (me + n - j) % n).wait()

    bias_out[...] = got[:, slots + 8 :]
    total = jnp.sum(got[:, slots : slots + 8], axis=0)[:1, :1]
    gram = jnp.zeros((slots, slots), jnp.float32)
    for i in range(n):
        part = got[i, :slots]
        gram = gram + lax.dot_general(
            part, part, (((1,), (1,)), ((), ())), preferred_element_type=jnp.float32, precision=lax.Precision.HIGHEST)
        wide[: onehot.shape[1], i * rows : (i + 1) * rows] = lax.dot_general(
            onehot[...], part, (((0,), (0,)), ((), ())), preferred_element_type=jnp.float32,
            precision=lax.Precision.HIGHEST)[:, :rows]
    total = total + jnp.sum(gram * same[...], keepdims=True)
    norm = jnp.sqrt(total)
    norm_out[...] = jnp.broadcast_to(norm, (8, 128))
    factor_out[...] = jnp.broadcast_to(jnp.minimum(1.0, CLIP_LIMIT / (norm + 1e-06)), (8, 128))
    tiles = n * rows // 128
    for t in range(tiles):
        flat[5][pl.ds(t, onehot.shape[1], stride=tiles), :] = wide[: onehot.shape[1], 128 * t : 128 * t + 128]


def adam_kernel(rates, *refs):
    kinds = len(rates)
    factor_ref, flat = refs[0], refs[1 : 1 + kinds]
    at = 1 + kinds
    states = [refs[at + 3 * a : at + 3 * a + 3] for a in range(kinds)]
    at += 3 * kinds
    news = [refs[at + 3 * a : at + 3 * a + 3] for a in range(kinds)]
    at += 3 * kinds
    held = refs[at : at + kinds]
    in_sem, out_sem = refs[at + kinds :]

    def loads(a):
        return [pltpu.make_async_copy(states[a][k], held[a].at[k], in_sem.at[a, k]) for k in range(3)]

    for a in range(kinds):
        for copy in loads(a):
            copy.start()
    factor = factor_ref[:1, :]
    for a in range(kinds):
        for copy in loads(a):
            copy.wait()
        size = chunk_rows(flat[a].shape[0])

        @pl.loop(0, flat[a].shape[0] // size)
        def _(i, a=a, size=size):
            part = pl.ds(pl.multiple_of(i * size, size), size)
            grad = flat[a][part] * factor
            master, first, second = held[a][0, part], held[a][1, part], held[a][2, part]
            first, second, master = adam_step(grad, master, first, second, rates[a])
            held[a][0, part], held[a][1, part], held[a][2, part] = master, first, second
            for k in range(3):
                pltpu.make_async_copy(held[a].at[k, part], news[a][k].at[part], out_sem.at[a, k]).start()

    for a in range(kinds):
        for k in range(3):
            pltpu.make_async_copy(held[a].at[k], news[a][k], out_sem.at[a, k]).wait()


def finish(reduced, silu, d_mod, d_cond, bias_sum, onehot, same, states, rates, n, collective_id):
    vmem, hbm = pl.BlockSpec(memory_space=pltpu.VMEM), pl.BlockSpec(memory_space=pltpu.HBM)
    dma = pltpu.SemaphoreType.DMA
    kinds = len(states)
    rows = reduced.shape[1]
    flats = [jax.ShapeDtypeStruct(s[0].shape, jnp.float32) for s in states]
    small = jax.ShapeDtypeStruct((8, 128), jnp.float32)
    block = d_cond.shape[0] + 24
    outs = pl.pallas_call(
        functools.partial(norm_kernel, n),
        out_shape=flats + [small, small, jax.ShapeDtypeStruct((n, 16, 128), jnp.float32)],
        in_specs=[vmem] * 7,
        out_specs=[vmem] * (kinds + 3),
        scratch_shapes=[
            pltpu.VMEM((2,) + reduced.shape, reduced.dtype),
            pltpu.VMEM((rows, 2 * d_mod.shape[2]), jnp.float32),
            pltpu.VMEM((block, 128), jnp.float32),
            pltpu.VMEM((n, block, 128), jnp.float32),
            dma,
            dma,
            dma((n,)),
            dma((n,)),
        ],
        compiler_params=pltpu.CompilerParams(
            collective_id=collective_id, has_side_effects=True, vmem_limit_bytes=40 * 2**20),
        name="norm",
    )(reduced, silu, d_mod, d_cond, bias_sum, onehot, same)
    grads, factor, norm = outs[:kinds], outs[kinds], outs[kinds + 1]
    news = pl.pallas_call(
        functools.partial(adam_kernel, rates),
        out_shape=[f for f in flats for _ in range(3)],
        in_specs=[vmem] * (1 + kinds) + [hbm] * (3 * kinds),
        out_specs=[hbm] * (3 * kinds),
        scratch_shapes=[pltpu.VMEM((3,) + f.shape, jnp.float32) for f in flats]
        + [dma((kinds, 3)), dma((kinds, 3))],
        compiler_params=pltpu.CompilerParams(vmem_limit_bytes=56 * 2**20),
        name="adam",
    )(factor, *grads, *[item for s in states for item in s])
    order = [3 * a + k for a in range(kinds) for k in (1, 2, 0)]
    return [news[i] for i in order], norm[0, 0], outs[kinds + 2]


def grid_embed(keep_index, width):
    quarter = width // 4
    freqs = 10000.0 ** (-jnp.arange(quarter).astype(jnp.float32) / quarter)
    across = (keep_index // SIDE).astype(jnp.float32)[..., None] * freqs
    along = (keep_index % SIDE).astype(jnp.float32)[..., None] * freqs
    return jnp.concatenate(
        [jnp.sin(across), jnp.cos(across), jnp.sin(along), jnp.cos(along)], axis=-1
    )


def normalize(values):
    centre = values - jnp.mean(values, axis=-1, keepdims=True)
    spread = jnp.mean(centre * centre, axis=-1, keepdims=True)
    return centre * lax.rsqrt(spread + LAYER_EPS)


def modulated(values, shift, scale):
    return normalize(values) * (1.0 + scale) + shift


def gelu_tanh(values):
    return jax.nn.gelu(values, approximate=True)


def per_device(
    tokens,
    cotangent,
    time_vec,
    labels,
    kept,
    keep_index,
    modulation_master,
    modulation_first,
    modulation_second,
    attention_in_master,
    attention_in_first,
    attention_in_second,
    attention_out_master,
    attention_out_first,
    attention_out_second,
    expand_master,
    expand_first,
    expand_second,
    contract_master,
    contract_first,
    contract_second,
    class_table_master,
    class_table_first,
    class_table_second,
    biases_master,
    biases_first,
    biases_second,
):
    rows, width = tokens.shape[1:]
    n, pairs = lax.axis_size("dp"), lax.axis_size("seq")
    me, c = lax.axis_index("dp"), lax.axis_index("seq")
    own_rows = width // n
    half_width, half_ff = width // pairs, FF // pairs
    low = jnp.bfloat16

    def flipped(values):
        return lax.ppermute(values, "seq", [(i, (i + 1) % pairs) for i in range(pairs)])

    def rows_all(values):
        return lax.all_gather(values, "seq", axis=0, tiled=True)

    def rows_own(partial):
        mine = lax.dynamic_slice_in_dim(partial, c * rows, rows, 0)
        return mine + flipped(lax.dynamic_slice_in_dim(partial, (1 - c) * rows, rows, 0))

    def part_of(vector):
        return lax.dynamic_slice_in_dim(vector, c * (vector.shape[0] // pairs), vector.shape[0] // pairs, 0)

    bias_share = biases_master.shape[0]
    bias_block = jnp.pad(biases_master.astype(low).astype(jnp.float32), (0, 1024 - bias_share)).reshape(8, 128)
    label_block = jnp.broadcast_to(labels.astype(jnp.float32)[:, None], (8, 128))
    (got,) = exchange([jnp.concatenate([bias_block, label_block])], (False,), n, 3)
    biases = got[:, :8].reshape(n, 1024)[:, :bias_share].reshape(-1)
    labels_all = got[:, 8, 0].astype(jnp.int32)
    bias_mod = biases[: 6 * width]
    bias_query = biases[6 * width : 7 * width]
    bias_value = biases[7 * width : 8 * width]
    bias_out = biases[8 * width : 9 * width]
    bias_expand = biases[9 * width : 9 * width + FF]
    bias_contract = biases[9 * width + FF :]

    class_rows = CLASSES // n
    onehot = labels_all[:, None] == me * class_rows + jnp.arange(class_rows)[None, :]
    inputs = tokens[0].astype(jnp.float32) + grid_embed(keep_index[0], width)
    half_kept = kept // pairs
    row_ok = jnp.arange(rows) < half_kept
    key_ok = ((jnp.arange(rows * pairs) % rows) < half_kept).astype(jnp.float32)[None]
    (weights, weight_attn, normed_in, flat_query, flat_key, flat_value, mixed, attended, middle, normed_mid, pieces, cond_own,
     silu_own, own_modulation) = forward(
        [
            item.reshape(-1, 128)
            for item in (
                attention_in_master,
                attention_out_master,
                expand_master,
                contract_master,
                class_table_master,
                modulation_master,
            )
        ],
        [
            onehot.astype(low),
            time_vec,
            inputs,
            key_ok,
            part_of(bias_mod)[None],
            part_of(bias_query)[None],
            part_of(bias_value)[None],
            bias_out[None],
        ],
        n,
        1,
    )
    weights = weights.reshape(3, width, 4 * half_width)
    weight_expand, weight_contract = weights[1], weights[2]
    pieces = pieces.reshape(6, 1, width)
    normed_in, normed_mid = normed_in.reshape(-1, width), normed_mid.reshape(-1, width)

    def times_transposed(left, right):
        return lax.dot_general(left, right, (((1,), (1,)), ((), ())), preferred_element_type=jnp.float32)

    def contract_rows(left, right):
        return lax.dot_general(
            left, right, (((0,), (0,)), ((), ())), preferred_element_type=jnp.float32
        )

    hidden = jnp.dot(normed_mid, weight_expand, preferred_element_type=jnp.float32) + part_of(bias_expand)
    activated = gelu_tanh(hidden).astype(low)
    branch = rows_own(times_transposed(activated, weight_contract)) + bias_contract
    result = middle + pieces[5] * branch
    block_out = jnp.where(row_ok[:, None], result, 0.0).astype(low)[None]

    grad_out = cotangent[0].astype(jnp.float32) * row_ok[:, None].astype(jnp.float32)
    d_branch = rows_all((pieces[5] * grad_out).astype(low))
    d_gate_mlp = jnp.sum(grad_out * branch, axis=0, keepdims=True)
    grad_contract = contract_rows(d_branch, activated).astype(low)
    grad_bias_contract = jnp.sum(d_branch.astype(jnp.float32), axis=0)
    d_activated = jnp.dot(d_branch, weight_contract, preferred_element_type=jnp.float32)
    d_hidden = jax.vjp(gelu_tanh, hidden)[1](d_activated)[0].astype(low)
    grad_expand = contract_rows(normed_mid, d_hidden).astype(low)
    grad_bias_expand = jnp.sum(d_hidden.astype(jnp.float32), axis=0)
    d_normed_mid = rows_own(times_transposed(d_hidden, weight_expand))
    d_middle, d_shift_mlp, d_scale_mlp = jax.vjp(modulated, middle, pieces[3], pieces[4])[1](d_normed_mid)
    d_middle = d_middle + grad_out
    d_attended = rows_all((pieces[2] * d_middle).astype(low))
    d_gate_attn = jnp.sum(d_middle * attended, axis=0, keepdims=True)
    grad_bias_out = jnp.sum(d_attended.astype(jnp.float32), axis=0)

    pair_t = jnp.concatenate([normed_in.T, d_attended.T], axis=1).reshape(n, own_rows, 2 * pairs * rows)
    zero_row = jnp.zeros((1, width), jnp.float32)
    d_pieces = jnp.concatenate(
        [zero_row, zero_row, d_gate_attn, d_shift_mlp, d_scale_mlp, d_gate_mlp, zero_row, zero_row]
    )
    v_rows = jnp.concatenate(
        [
            zero_row,
            grad_bias_expand.reshape(2, width),
            grad_bias_out[None],
            grad_bias_contract[None],
            zero_row,
            zero_row,
            zero_row,
        ]
    )
    shape = (n // 4, 2, 2, own_rows, 4 * half_width)
    reduced, tokens_grad, d_mod_all, d_cond, bias_sum = backward(
        (grad_contract.reshape(shape), grad_expand.reshape(shape), weight_attn),
        (
            pair_t,
            d_attended,
            flat_query,
            flat_key,
            flat_value,
            mixed,
            key_ok,
            inputs,
            d_middle,
            pieces[1],
            d_pieces,
            v_rows,
            own_modulation,
            cond_own,
        ),
        n,
        2,
    )
    tokens_grad = tokens_grad[None]
    same = (labels_all[:, None] == labels_all[None, :]).astype(jnp.float32)
    rates = (
        width ** (-0.5),
        width ** (-0.5),
        (width // 4) ** (-0.5),
        width ** (-0.5),
        FF ** (-0.5),
        0.5,
        0.2,
    )
    masters = (
        modulation_master,
        attention_in_master,
        attention_out_master,
        expand_master,
        contract_master,
        class_table_master,
        biases_master,
    )
    firsts = (
        modulation_first,
        attention_in_first,
        attention_out_first,
        expand_first,
        contract_first,
        class_table_first,
        biases_first,
    )
    seconds = (
        modulation_second,
        attention_in_second,
        attention_out_second,
        expand_second,
        contract_second,
        class_table_second,
        biases_second,
    )
    states = list(zip(masters, firsts, seconds))
    updated, grad_norm, bias_parts = finish(
        reduced,
        silu_own[:, :own_rows],
        d_mod_all,
        d_cond,
        bias_sum,
        onehot.astype(jnp.float32),
        same,
        [tuple(item.reshape(-1, 128) for item in state) for state in states[:-1]],
        rates[:-1],
        n,
        8,
    )
    factor = jnp.minimum(1.0, CLIP_LIMIT / (grad_norm + 1e-06))
    bias_parts = bias_parts.reshape(n, pairs, 8, 128)[:, :, : chunk_tiles(n, width)].transpose(1, 0, 2, 3)
    bias_parts = bias_parts.reshape(pairs, -1)[:, : 5 * width].reshape(pairs, 5, width)
    grad_biases = jnp.concatenate(
        [
            jnp.sum(d_mod_all, axis=1).reshape(-1),
            bias_parts[:, 0, :half_width].reshape(-1),
            bias_parts[:, 0, half_width:].reshape(-1),
            bias_parts[0, 3],
            bias_parts[:, 1:3].reshape(-1),
            bias_parts[0, 4],
        ]
    )
    bias_grad = lax.dynamic_slice_in_dim(grad_biases, me * bias_share, bias_share, 0) * factor
    updated = [item.reshape(-1) for item in updated] + list(adam_step(bias_grad, *states[-1], rates[-1]))
    return (block_out, tokens_grad, grad_norm) + tuple(updated)


def solution(mesh):
    return jax.shard_map(
        per_device,
        mesh=mesh,
        in_specs=(
            P("dp", "seq", None),
            P("dp", "seq", None),
            P("dp", None),
            P("dp"),
            P("dp"),
            P("dp", "seq"),
            P("dp"),
            P("dp"),
            P("dp"),
            P("dp"),
            P("dp"),
            P("dp"),
            P("dp"),
            P("dp"),
            P("dp"),
            P("dp"),
            P("dp"),
            P("dp"),
            P("dp"),
            P("dp"),
            P("dp"),
            P("dp"),
            P("dp"),
            P("dp"),
            P("dp"),
            P("dp"),
            P("dp"),
        ),
        out_specs=(
            P("dp", "seq", None),
            P("dp", "seq", None),
            P(),
            P("dp"),
            P("dp"),
            P("dp"),
            P("dp"),
            P("dp"),
            P("dp"),
            P("dp"),
            P("dp"),
            P("dp"),
            P("dp"),
            P("dp"),
            P("dp"),
            P("dp"),
            P("dp"),
            P("dp"),
            P("dp"),
            P("dp"),
            P("dp"),
            P("dp"),
            P("dp"),
            P("dp"),
        ),
        check_vma=False,
    )
```

```python
import functools
import jax
import jax.numpy as jnp
from jax import lax
from jax.experimental import pallas as pl
from jax.experimental.pallas import tpu as pltpu
from jax.sharding import PartitionSpec as P

HEAD_DIM = 72
FF = 4608
SIDE = 16
CLASSES = 1024
STEP = 10
LAYER_EPS = 1e-06
MASK_FILL = -1e30
BETA_FIRST = 0.5
BETA_SECOND = 0.5
ADAM_EPS = 1e-08
WEIGHT_DECAY = 0.1
CLIP_LIMIT = 1.0

MESH = pl.DeviceIdType.MESH
GELU_A = (2.0 / 3.141592653589793) ** 0.5
GELU_B = 0.044715
GROUPS = ((0, 768, 0, "x"), (768, 768, 0, "y"), (1536, 384, 1, "x"), (1920, 384, 1, "y"))


def when(cond, fn):
    pl.when(cond)(fn)


class Place:
    def __init__(self, line):
        self.line = line
        i = lax.axis_index("dp")
        self.c = lax.axis_index("seq")
        self.x, self.y, self.z = i % 2, (i // 2) % 2, i // 4

    def dev(self, z=None, y=None, x=None):
        z = self.z if z is None else z
        y = self.y if y is None else y
        x = self.x if x is None else x
        return (z * 4 + y * 2 + x, self.c)

    def peer(self, axis):
        return self.dev(x=1 - self.x) if axis == "x" else self.dev(y=1 - self.y)

    def barrier(self):
        bar = pltpu.get_barrier_semaphore()

        def sig(dev):
            pl.semaphore_signal(bar, inc=1, device_id=dev, device_id_type=MESH)

        sig(self.peer("x"))
        sig(self.peer("y"))
        when(self.z > 0, lambda: sig(self.dev(z=self.z - 1)))
        when(self.z < self.line - 1, lambda: sig(self.dev(z=self.z + 1)))
        pl.semaphore_wait(bar, 2 + (self.z > 0).astype(jnp.int32) + (self.z < self.line - 1).astype(jnp.int32))


class Gatherer:
    def __init__(self, line, own, out, keep_sem, sems):
        self.line, self.own, self.out, self.keep_sem = line, own, out, keep_sem
        self.send_a, self.send_u, self.send_d, self.send_b, self.recv_a, self.recv_z, self.recv_b = sems
        self.me = Place(line)
        self.up, self.down = self.me.z < line - 1, self.me.z > 0

    def single(self, m, g, zz):
        lo, width = GROUPS[g][:2]
        return self.out.at[m, zz, self.me.y, self.me.x, :, pl.ds(lo, width)]

    def pair(self, m, g, zz):
        lo, width, _, first = GROUPS[g]
        if first == "x":
            return self.out.at[m, zz, self.me.y, :, :, pl.ds(lo, width)]
        return self.out.at[m, zz, :, self.me.x, :, pl.ds(lo, width)]

    def remote(self, ref, send, recv, dev, source):
        return pltpu.make_async_remote_copy(
            src_ref=ref if source is None else source, dst_ref=ref, send_sem=send, recv_sem=recv,
            device_id=dev, device_id_type=MESH)

    def source(self, m, g):
        lo, width = GROUPS[g][:2]
        return self.own.at[m, :, pl.ds(lo, width)]

    def a_copy(self, m, g, zz, source=None):
        return self.remote(
            self.single(m, g, zz), self.send_a.at[m, g, zz], self.recv_a.at[m, g, zz], self.me.peer(GROUPS[g][3]), source)

    def z_ref(self, m, g, zz):
        return self.pair(m, g, zz) if GROUPS[g][2] == 0 else self.single(m, g, zz)

    def u_copy(self, m, g, zz, source=None):
        dev = self.me.dev(z=jnp.minimum(self.me.z + 1, self.line - 1))
        return self.remote(self.z_ref(m, g, zz), self.send_u.at[m, g, zz], self.recv_z.at[m, g, zz], dev, source)

    def d_copy(self, m, g, zz, source=None):
        dev = self.me.dev(z=jnp.maximum(self.me.z - 1, 0))
        return self.remote(self.z_ref(m, g, zz), self.send_d.at[m, g, zz], self.recv_z.at[m, g, zz], dev, source)

    def b_copy(self, m, g, zz):
        last = "y" if GROUPS[g][3] == "x" else "x"
        return self.remote(self.pair(m, g, zz), self.send_b.at[m, g, zz], self.recv_b.at[m, g, zz], self.me.peer(last), None)

    def keep(self, m):
        me = self.me
        return pltpu.make_async_copy(self.own.at[m], self.out.at[m, me.z, me.y, me.x], self.keep_sem.at[m])

    def begin(self, m):
        z = self.me.z
        self.keep(m).start()
        for g in range(4):
            self.a_copy(m, g, z, self.source(m, g)).start()
        for g in (2, 3):
            when(self.up, lambda g=g: self.u_copy(m, g, z, self.source(m, g)).start())
            when(self.down, lambda g=g: self.d_copy(m, g, z, self.source(m, g)).start())

    def paired(self, m):
        z = self.me.z
        self.keep(m).wait()
        for g in (0, 1):
            self.a_copy(m, g, z).wait_recv()
            when(self.up, lambda g=g: self.u_copy(m, g, z).start())
            when(self.down, lambda g=g: self.d_copy(m, g, z).start())
            self.b_copy(m, g, z).start()

    def arrive(self, m, zz, upward):
        for g in range(4):
            copy = self.u_copy if upward else self.d_copy
            copy(m, g, zz).wait_recv()
            when(self.up if upward else self.down, lambda g=g: copy(m, g, zz).start())
            if GROUPS[g][2] == 0:
                self.b_copy(m, g, zz).start()
            else:
                self.a_copy(m, g, zz).start()

    def crossed(self, m, zz):
        for g in (2, 3):
            self.a_copy(m, g, zz).wait_recv()
            self.b_copy(m, g, zz).start()

    def step(self, m, k):
        z, line = self.me.z, self.line
        when(k <= z, lambda: self.arrive(m, jnp.maximum(z - k, 0), True))
        when(z + k < line, lambda: self.arrive(m, jnp.minimum(z + k, line - 1), False))
        when(k - 1 <= z, lambda: self.crossed(m, jnp.maximum(z - k + 1, 0)))
        when((k > 1) & (z + k - 1 < line), lambda: self.crossed(m, jnp.minimum(z + k - 1, line - 1)))

    def complete(self, m):
        @pl.loop(0, self.line)
        def _(zz):
            for g in range(4):
                self.b_copy(m, g, zz).wait_recv()

    def drain(self, m):
        z = self.me.z

        @pl.loop(0, self.line)
        def _(zz):
            for g in range(4):
                self.b_copy(m, g, zz).wait_send()
                if GROUPS[g][2] == 1:
                    self.a_copy(m, g, zz).wait_send()
                when(self.up & (zz <= z), lambda g=g: self.u_copy(m, g, zz).wait_send())
                when(self.down & (zz >= z), lambda g=g: self.d_copy(m, g, zz).wait_send())

        for g in (0, 1):
            self.a_copy(m, g, z).wait_send()


def dot(left, right, a=1, b=0):
    return lax.dot_general(left, right, (((a,), (b,)), ((), ())), preferred_element_type=jnp.float32)


def normal(values):
    centre = values - jnp.mean(values, axis=-1, keepdims=True)
    return centre * lax.rsqrt(jnp.mean(centre * centre, axis=-1, keepdims=True) + LAYER_EPS)


def all_peers(n, src, dst, send, recv, spread):
    me, c = lax.axis_index("dp"), lax.axis_index("seq")

    def copy(j, there, slot):
        return pltpu.make_async_remote_copy(
            src_ref=src.at[there] if spread else src, dst_ref=dst.at[slot], send_sem=send.at[j], recv_sem=recv.at[slot],
            device_id=(there, c), device_id_type=MESH)

    def start():
        @pl.loop(1, n)
        def _(j):
            copy(j, (me + j) % n, me).start()

    def wait():
        @pl.loop(1, n)
        def _(j):
            copy(j, (me + j) % n, (me + n - j) % n).wait()

    return start, wait


def greet_all(n):
    me, c = lax.axis_index("dp"), lax.axis_index("seq")
    bar = pltpu.get_barrier_semaphore()
    pl.semaphore_signal(bar, inc=1, device_id=(me, 1 - c), device_id_type=MESH)

    @pl.loop(1, n)
    def _(j):
        pl.semaphore_signal(bar, inc=1, device_id=((me + j) % n, c), device_id_type=MESH)

    return bar


def head_window(h):
    lo = pl.multiple_of(h * HEAD_DIM // 128 * 128, 128)
    lane = lax.broadcasted_iota(jnp.int32, (1, 256), 1) + lo - h * HEAD_DIM
    return pl.ds(lo, 256), ((lane >= 0) & (lane < HEAD_DIM)).astype(jnp.bfloat16)


def head_probs(qh, kh, seen):
    logits = jnp.where(seen, dot(qh, kh, 1, 1) * HEAD_DIM ** (-0.5), MASK_FILL)
    expo = jnp.exp(logits - jnp.max(logits, axis=-1, keepdims=True))
    return expo / jnp.sum(expo, axis=-1, keepdims=True)


def to_blocks(values, ref):
    count, size = ref.shape[:2]
    turned = values.T
    for i in range(count):
        ref[i] = turned[i * size : (i + 1) * size]


def write_blocks(n, target, stage, sem, block):
    def copy(i):
        return pltpu.make_async_copy(stage.at[i % 2], target.at[i // 4, i // 2 % 2, i % 2], sem.at[i % 2])

    @pl.loop(0, n)
    def _(i):
        when(i >= 2, lambda: copy(i).wait())
        stage[i % 2] = block(i).astype(stage.dtype)
        copy(i).start()

    copy(0).wait()
    copy(1).wait()


def forward_kernel(line, *refs):
    (m_in, m_out, m_expand, m_contract, m_table, m_mod, onehot, time_vec, x, key_ok, b_mod, b_query, b_value, b_out,
     b_expand, cot, row_ok) = refs[:17]
    (weights, g_contract, h1_t, h2_t, q, k, v, o, attended, middle, act, slope, d_branch, pieces, cond, silu,
     mod_half) = refs[17:34]
    (f_in, f_out, f_expand, f_contract, f_table, f_mod, own, table, cond_part, cond_got, mods, mod_part, mod_got, blocks, w,
     proj, mix, wide, partial, partial_got, h1, h2, d_branch_t, stage, in_sem, w_sem, pair_send, pair_recv, cond_send,
     cond_recv, mod_send, mod_recv, keep_sem, stage_sem) = refs[34:68]
    n = line * 4
    low, f32 = jnp.bfloat16, jnp.float32
    me, c = lax.axis_index("dp"), lax.axis_index("seq")
    gat = Gatherer(line, own, weights, keep_sem, refs[68:])
    rows, width = x.shape
    own_rows, half = own.shape[1], own.shape[2] // 4
    edge = 3 * half // 128 * 128
    tiles = width // 128
    sources, flats = (m_in, m_out, m_table, m_mod, m_expand, m_contract), (f_in, f_out, f_table, f_mod, f_expand, f_contract)

    def load(i):
        return pltpu.make_async_copy(sources[i], flats[i], in_sem.at[i])

    for i in range(6):
        load(i).start()
    bar = greet_all(n)

    def swap(i, src, dst):
        return pltpu.make_async_remote_copy(
            src_ref=src, dst_ref=dst, send_sem=pair_send.at[i], recv_sem=pair_recv.at[i], device_id=(me, 1 - c),
            device_id_type=MESH)

    def tile(flat, t, count, per_row):
        return flat[pl.ds(t, count, stride=per_row), :]

    def cut_heads(flat, part, per_row):
        start = part * tiles + c * (tiles // 2)
        found = jnp.concatenate([tile(flat, start + j, own_rows, per_row) for j in range(tiles // 2 + 1)], axis=1)
        return jnp.where(c == 0, found[:, :half], found[:, found.shape[1] - half :]).astype(low)

    def cut(flat, target, count):
        for j in range(count):
            target[:own_rows, 128 * j : 128 * j + 128] = tile(flat, c * count + j, own_rows, 2 * count).astype(low)

    load(0).wait()
    load(1).wait()
    for part in range(3):
        own[0, :, part * half : (part + 1) * half] = cut_heads(f_in, part, 3 * tiles)
    own[0, :, 3 * half :] = cut_heads(f_out, 0, tiles)
    load(2).wait()
    class_rows = table.shape[0]
    for t in range(tiles):
        table[:, 128 * t : 128 * t + 128] = tile(f_table, t, class_rows, tiles).astype(low)
    found = dot(onehot[...], table[...])
    mine = lax.broadcasted_iota(jnp.int32, (n, width), 0) == me
    found = found + jnp.where(mine, jnp.broadcast_to(time_vec[...].astype(f32), (n, width)), 0.0)
    cond_part[...] = jnp.zeros_like(cond_part)
    for i in range(n):
        cond_part[i, :, :own_rows] = found[:, i * own_rows : (i + 1) * own_rows]
    cond_got[me] = cond_part[me]

    pl.semaphore_wait(bar, n)
    cond_start, cond_wait = all_peers(n, cond_part, cond_got, cond_send, cond_recv, True)
    mod_start, mod_wait = all_peers(n, mod_part, mod_got, mod_send, mod_recv, True)
    cond_start()
    gat.begin(0)
    load(3).wait()
    mod_half[own_rows:] = jnp.zeros((mod_half.shape[0] - own_rows, mod_half.shape[1]), low)
    cut(f_mod, mod_half, 3 * tiles)
    load(4).wait()
    cut(f_expand, own.at[1], 4 * half // 128)

    cond_wait()
    value = jnp.sum(cond_got[...], axis=0)
    cond[...] = value
    silu[...] = (value / (1.0 + jnp.exp(-value))).astype(low)
    mods[...] = dot(silu[...], mod_half[...])

    @pl.loop(0, n)
    def _(s):
        mod_part[s] = mods[pl.ds(s, 1), :]

    mod_got[me] = mod_part[me]
    mod_start()
    gat.paired(0)
    gat.begin(1)
    load(5).wait()
    cut(f_contract, own.at[2], 4 * half // 128)
    mod_wait()
    pieces[c] = jnp.sum(mod_got[...], axis=0) + b_mod[...]
    swap(0, pieces.at[c], pieces.at[c]).start()
    gat.step(0, 1)
    gat.begin(2)
    swap(0, pieces.at[c], pieces.at[c]).wait()
    shift, scale, gate = (pieces[0, :, i * width : (i + 1) * width] for i in range(3))
    h1[c] = (normal(x[...]) * (1.0 + scale) + shift).astype(low)
    swap(1, h1.at[c], h1.at[c]).start()
    d_branch[c] = (pieces[1, :, 2 * width :] * (cot[...].astype(f32) * row_ok[...])).astype(low)
    swap(4, d_branch.at[c], d_branch.at[c]).start()

    @pl.loop(2, line + 1)
    def _(k):
        gat.step(0, k)

    gat.paired(1)
    gat.complete(0)

    def fetch(m):
        return pltpu.make_async_copy(weights.at[m], blocks, w_sem.at[m])

    def unpack():
        for i in range(n):
            w[i * own_rows : (i + 1) * own_rows, :] = blocks[i // 4, i // 2 % 2, i % 2]

    fetch(0).start()
    gat.paired(2)
    swap(1, h1.at[c], h1.at[c]).wait()
    fetch(0).wait()
    unpack()
    both = jnp.concatenate([h1[0], h1[1]], axis=0)
    to_blocks(both, h1_t)

    @pl.loop(0, proj.shape[1] // 256)
    def _(t):
        cols = pl.ds(pl.multiple_of(t * 256, 256), 256)
        proj[:, cols] = dot(both, w[:, cols])

    spare = q.shape[1] - half
    for item, value in (
        (q, proj[:, :half] + b_query[...]),
        (k, proj[:, half : 2 * half]),
        (v, proj[:, 2 * half : 3 * half] + b_value[...]),
    ):
        item[:, :half] = value.astype(low)
        item[:, half:] = jnp.zeros((2 * rows, spare), low)
    mix[...] = jnp.zeros_like(mix)
    seen = jnp.broadcast_to(key_ok[...], (2 * rows, 2 * rows)) > 0.0
    heads = half // HEAD_DIM

    def head(h):
        win, lanes = head_window(h)
        probs = head_probs(q[:, win] * lanes, k[:, win], seen)
        mix[:, win] = mix[:, win] + dot(probs.astype(low), v[:, win] * lanes)

    @pl.loop(0, max(heads, 2 * line))
    def _(t):
        when(t < heads, lambda: head(t))
        when((t % 2 == 1) & (t < 2 * line), lambda: gat.step(1, t // 2 + 1))

    o[...] = mix[...].astype(low)
    wide[:, : 3 * half - edge] = jnp.zeros((2 * rows, 3 * half - edge), low)
    wide[:, 3 * half - edge :] = mix[:, :half].astype(low)

    @pl.loop(0, tiles)
    def _(t):
        cols = pl.ds(pl.multiple_of(t * 128, 128), 128)
        part = dot(wide[...], w[cols, edge:], 1, 1)
        partial[0, :, cols] = part[:rows]
        partial[1, :, cols] = part[rows:]

    swap(2, partial.at[1 - c], partial_got).start()
    gat.step(2, 1)
    swap(2, partial.at[1 - c], partial_got).wait()
    attended[...] = partial[c] + partial_got[...] + b_out[...]
    middle[...] = x[...] + gate * attended[...]
    shift, scale = (pieces[1, :, i * width : (i + 1) * width] for i in range(2))
    h2[c] = (normal(middle[...]) * (1.0 + scale) + shift).astype(low)
    swap(3, h2.at[c], h2.at[c]).start()
    gat.complete(1)
    fetch(1).start()
    swap(4, d_branch.at[c], d_branch.at[c]).wait()
    to_blocks(jnp.concatenate([d_branch[0], d_branch[1]], axis=0), d_branch_t)
    gat.step(2, 2)
    swap(3, h2.at[c], h2.at[c]).wait()
    both = jnp.concatenate([h2[0], h2[1]], axis=0)
    to_blocks(both, h2_t)
    fetch(1).wait()
    unpack()

    @pl.loop(0, act.shape[1] // 256)
    def _(t):
        cols = pl.ds(pl.multiple_of(t * 256, 256), 256)
        z = dot(both, w[:, cols]) + b_expand[:, cols]
        bend = jnp.tanh(GELU_A * (z + GELU_B * z * z * z))
        act[:, cols] = (0.5 * z * (1.0 + bend)).astype(low)
        slope[:, cols] = 0.5 * (1.0 + bend) + 0.5 * z * (1.0 - bend * bend) * (GELU_A * (1.0 + 3.0 * GELU_B * z * z))

    gat.step(2, 3)
    write_blocks(n, g_contract, stage, stage_sem, lambda i: dot(d_branch_t[i], act[...]))

    @pl.loop(4, line + 1)
    def _(k):
        gat.step(2, k)

    gat.complete(2)

    @pl.loop(0, 3)
    def _(m):
        gat.drain(m)


def forward(hbm_args, vmem_args, n, collective_id):
    line = n // 4
    onehot, time_vec, x = vmem_args[:3]
    rows, width = x.shape
    own_rows, half = width // n, width // 2
    low, f32 = jnp.bfloat16, jnp.float32
    dma = pltpu.SemaphoreType.DMA
    vmem, hbm = pl.BlockSpec(memory_space=pltpu.VMEM), pl.BlockSpec(memory_space=pltpu.HBM)
    heads = (2 * rows, -(-half // 128) * 128)
    edge = 3 * half // 128 * 128

    def shape(dims, kind):
        return jax.ShapeDtypeStruct(dims, kind)

    def scratch(dims, kind):
        return pltpu.VMEM(dims, kind)

    return pl.pallas_call(
        functools.partial(forward_kernel, line),
        out_shape=[
            shape((3, line, 2, 2, own_rows, 4 * half), low),
            shape((line, 2, 2, own_rows, 4 * half), low),
            shape((n, own_rows, 2 * rows), low),
            shape((n, own_rows, 2 * rows), low),
            shape(heads, low),
            shape(heads, low),
            shape(heads, low),
            shape(heads, low),
            shape((rows, width), f32),
            shape((rows, width), f32),
            shape((2 * rows, 4 * half), low),
            shape((2 * rows, 4 * half), f32),
            shape((2, rows, width), low),
            shape((2, 1, 3 * width), f32),
            shape((n, 128), f32),
            shape((n, 128), low),
            shape((128, 3 * width), low),
        ],
        in_specs=[hbm] * len(hbm_args) + [vmem] * len(vmem_args),
        out_specs=[hbm] * 2 + [vmem] * 15,
        scratch_shapes=[scratch(item.shape, f32) for item in hbm_args]
        + [
            scratch((3, own_rows, 4 * half), low),
            scratch((onehot.shape[1], width), low),
            scratch((n, n, 128), f32),
            scratch((n, n, 128), f32),
            scratch((n, 3 * width), f32),
            scratch((n, 1, 3 * width), f32),
            scratch((n, 1, 3 * width), f32),
            scratch((line, 2, 2, own_rows, 4 * half), low),
            scratch((width, 4 * half), low),
            scratch((2 * rows, edge + 128), f32),
            scratch(heads, f32),
            scratch(heads, low),
            scratch((2, rows, width), f32),
            scratch((rows, width), f32),
            scratch((2, rows, width), low),
            scratch((2, rows, width), low),
            scratch((n, own_rows, 2 * rows), low),
            scratch((2, own_rows, 4 * half), low),
            dma((6,)),
            dma((2,)),
            dma((5,)),
            dma((5,)),
            dma((n,)),
            dma((n,)),
            dma((n,)),
            dma((n,)),
            dma((3,)),
            dma((2,)),
        ]
        + [dma((3, 4, line))] * 7,
        compiler_params=pltpu.CompilerParams(
            collective_id=collective_id, has_side_effects=True, vmem_limit_bytes=63 * 2**20),
        name="forward",
    )(*hbm_args, *vmem_args)


class Reducer:
    def __init__(self, line, grads, out, own, got_b, got_z, got_a, sems):
        self.line, self.grads, self.out = line, grads, out
        self.own, self.acc, self.got_z, self.got_a = own, got_b, got_z, got_a
        self.load, self.send_b, self.send_z, self.send_a, self.recv_b, self.recv_z, self.recv_a = sems
        self.me = me = Place(line)
        self.up, self.down = me.z < line - 1, me.z > 0
        self.above, self.below = me.dev(z=jnp.minimum(me.z + 1, line - 1)), me.dev(z=jnp.maximum(me.z - 1, 0))
        self.units = len(grads) * line

    def last(self, g):
        return "y" if GROUPS[g][3] == "x" else "x"

    def first(self, g):
        return self.me.x if GROUPS[g][3] == "x" else self.me.y

    def half(self, grad, g, zz, mine):
        cols = pl.ds(GROUPS[g][0], GROUPS[g][1])
        if self.last(g) == "y":
            return grad.at[zz, self.me.y if mine else 1 - self.me.y, :, :, cols]
        return grad.at[zz, :, self.me.x if mine else 1 - self.me.x, :, cols]

    def loading(self, u, g, zz, side, grad=None):
        grad = self.grads[0] if grad is None else grad
        return pltpu.make_async_copy(
            self.half(grad, g, zz, True), self.own[g].at[u % 3, side], self.load.at[u % 3, g, side])

    def remote(self, src, dst, send, recv, dev):
        return pltpu.make_async_remote_copy(
            src_ref=src, dst_ref=dst, send_sem=send, recv_sem=recv, device_id=dev, device_id_type=MESH)

    def b_copy(self, m, g, zz, grad=None):
        grad = self.grads[0] if grad is None else grad
        return self.remote(
            self.half(grad, g, zz, False), self.acc[g].at[m, zz], self.send_b.at[m, g, zz], self.recv_b.at[m, g, zz],
            self.me.peer(self.last(g)))

    def slot_a(self, g, zz):
        return zz if GROUPS[g][2] == 1 else 0

    def a_copy(self, m, g, zz):
        return self.remote(
            self.acc[g].at[m, zz, 1 - self.first(g)], self.got_a[g].at[m, self.slot_a(g, zz)], self.send_a.at[m, g, zz],
            self.recv_a.at[m, g, zz], self.me.peer(GROUPS[g][3]))

    def z_copy(self, m, g, zz, slot, dev):
        part = self.acc[g].at[m, zz] if GROUPS[g][2] == 0 else self.acc[g].at[m, zz, self.first(g)]
        return self.remote(part, self.got_z[g].at[m, slot], self.send_z.at[m, g, zz], self.recv_z.at[m, g, slot], dev)

    def add_b(self, m, g, zz, u, side):
        self.loading(u, g, zz, side).wait()
        self.b_copy(m, g, zz).wait_recv()
        self.acc[g][m, zz] = self.acc[g][m, zz] + self.own[g][u % 3, side]

    def add_z(self, m, g, zz, slot):
        acc, got = self.acc[g], self.got_z[g]
        self.z_copy(m, g, self.me.z, slot, self.below).wait_recv()
        if GROUPS[g][2] == 0:
            acc[m, zz] = acc[m, zz] + got[m, slot]
        else:
            acc[m, zz, self.first(g)] = acc[m, zz, self.first(g)] + got[m, slot]

    def add_a(self, m, g, zz):
        self.a_copy(m, g, zz).wait_recv()
        acc, first = self.acc[g], self.first(g)
        acc[m, zz, first] = acc[m, zz, first] + self.got_a[g][m, self.slot_a(g, zz)]

    def planes(self, k, fn):
        z, line = self.me.z, self.line
        when(z + k < line, lambda: fn(jnp.minimum(z + k, line - 1), True))
        when((z >= k) & (k > 0), lambda: fn(jnp.maximum(z - k, 0), False))

    def begin(self, v):
        m, j = v // self.line, v % self.line

        def one(grad, zz, upward):
            for g in range(4):
                self.b_copy(m, g, zz, grad).start()
                self.loading(v, g, zz, 0 if upward else 1, grad).start()

        for index, grad in enumerate(self.grads):
            when(m == index, lambda: self.planes(self.line - 1 - j, lambda zz, upward: one(grad, zz, upward)))

    def onward(self, m, g, zz, k, upward):
        if upward:
            when(self.down, lambda: self.add_z(m, g, zz, zz))
            self.z_copy(m, g, zz, zz, self.above).start()
        else:
            when(self.up, lambda: self.add_z(m, g, zz, zz))
            self.z_copy(m, g, zz, jnp.where(k == 1, self.line, zz), self.below).start()

    def near(self, u, m, j):
        k = self.line - 1 - j

        def one(zz, upward):
            for g in range(4):
                self.add_b(m, g, zz, u, 0 if upward else 1)
                if GROUPS[g][2] == 1:
                    self.a_copy(m, g, zz).start()
                else:
                    when(k > 0, lambda g=g: self.onward(m, g, zz, k, upward))

        self.planes(k, one)

    def far(self, m, j):
        k = self.line - j

        def one(zz, upward):
            for g in (2, 3):
                self.add_a(m, g, zz)
                self.onward(m, g, zz, k, upward)

        when((k > 0) & (k < self.line), lambda: self.planes(k, one))

    def close(self, m):
        z = self.me.z
        for g in (0, 1):
            when(self.down, lambda g=g: self.add_z(m, g, z, z))
            when(self.up, lambda g=g: self.add_z(m, g, z, self.line))
            self.a_copy(m, g, z).start()

    def final(self, m):
        z = self.me.z
        for g in range(4):
            cols = pl.ds(GROUPS[g][0], GROUPS[g][1])
            self.add_a(m, g, z)
            if GROUPS[g][2] == 1:
                when(self.down, lambda g=g: self.add_z(m, g, z, z))
                when(self.up, lambda g=g: self.add_z(m, g, z, self.line))
            self.out[m, :, cols] = self.acc[g][m, z, self.first(g)]

    def unit(self, u):
        line = self.line
        m, j = u // line, u % line
        when(u + 2 < self.units, lambda: self.begin(jnp.minimum(u + 2, self.units - 1)))
        self.near(u, m, j)
        self.far(m, j)
        when(j == line - 1, lambda: self.close(m))
        when((j == 0) & (m > 0), lambda: self.final(jnp.maximum(m - 1, 0)))

    def drain(self):
        z = self.me.z

        @pl.loop(0, len(self.grads))
        def _(m):
            @pl.loop(0, self.line)
            def _(zz):
                for g in range(4):
                    self.b_copy(m, g, zz).wait_send()
                    if GROUPS[g][2] == 1:
                        self.a_copy(m, g, zz).wait_send()
                    when(zz != z, lambda g=g: self.z_copy(m, g, zz, zz, self.above).wait_send())
            for g in (0, 1):
                self.a_copy(m, g, z).wait_send()


def reducer_scratch(count, line, rows, dt):
    dma = pltpu.SemaphoreType.DMA
    own = [pltpu.VMEM((3, 2, 2, rows, GROUPS[g][1]), dt) for g in range(4)]
    got_b = [pltpu.VMEM((count, line, 2, rows, GROUPS[g][1]), dt) for g in range(4)]
    got_z = [pltpu.VMEM((count, line + 1) + ((2,) if GROUPS[g][2] == 0 else ()) + (rows, GROUPS[g][1]), dt) for g in range(4)]
    got_a = [pltpu.VMEM((count, line if GROUPS[g][2] == 1 else 1, rows, GROUPS[g][1]), dt) for g in range(4)]
    sems = [dma((3, 4, 2))] + [dma((count, 4, line))] * 4 + [dma((count, 4, line + 1))] + [dma((count, 4, line))]
    return own + got_b + got_z + got_a + sems


def make_reducer(line, grads, out, refs):
    return Reducer(line, grads, out, refs[:4], refs[4:8], refs[8:12], refs[12:16], refs[16:])


def backward_kernel(line, *refs):
    (weights, g_contract, h1_t, h2_t, act, slope, d_branch, q, k, v, o, key_ok, x, middle, attended, cot, row_ok, pieces,
     b_contract, modulation, cond) = refs[:21]
    (g_expand, g_attn, d_mod_all, out, block_out, tokens_grad, d_cond, bias_sum) = refs[21:29]
    (w, rhs, d_o, d_q, d_k, d_v, d_h, d_h_got, branch_got, d_mid, d_att, d_att_t, stage, dp, dp_got, msg, msg_got, d_mod, vec,
     vec_got, d_silu, d_silu_got, chunk, w_sem, mod_sem, stage_sem, pair_send, pair_recv, msg_send, msg_recv, vec_send,
     vec_recv) = refs[29:61]
    n = line * 4
    low, f32 = jnp.bfloat16, jnp.float32
    me, c = lax.axis_index("dp"), lax.axis_index("seq")
    red = make_reducer(line, (g_contract, g_expand, g_attn), out, refs[61:])
    rows, width = x.shape
    half = weights.shape[2] // 4
    heads = half // HEAD_DIM
    edge = 3 * half // 128 * 128
    tiles = width // 128
    d_z = rhs.at[2 * rows :]

    def swap(i, src, dst):
        return pltpu.make_async_remote_copy(
            src_ref=src, dst_ref=dst, send_sem=pair_send.at[i], recv_sem=pair_recv.at[i], device_id=(me, 1 - c),
            device_id_type=MESH)

    def fetch(i):
        return pltpu.make_async_copy(weights.at[(2, 1, 0, 2)[i]], w, w_sem.at[i])

    def back(values, lanes):
        @pl.loop(0, tiles)
        def _(t):
            cols = pl.ds(pl.multiple_of(t * 128, 128), 128)
            part = dot(values[...], w[cols, :lanes], 1, 1)
            d_h[0, :, cols] = part[:rows]
            d_h[1, :, cols] = part[rows:]

    def column_sums(values):
        return jnp.sum(values.astype(f32), axis=0, keepdims=True)

    def norm_back(values, scale, d_n):
        centre = values - jnp.mean(values, axis=-1, keepdims=True)
        inv = lax.rsqrt(jnp.mean(centre * centre, axis=-1, keepdims=True) + LAYER_EPS)
        normed = centre * inv
        e = d_n * (1.0 + scale)
        d_x = (e - jnp.mean(e, axis=-1, keepdims=True) - normed * jnp.mean(e * normed, axis=-1, keepdims=True)) * inv
        return d_x, jnp.sum(d_n, axis=0, keepdims=True), jnp.sum(d_n * normed, axis=0, keepdims=True)

    def piece(i):
        return pieces[i // 3, :, i % 3 * width : (i % 3 + 1) * width]

    fetch(0).start()
    bar = greet_all(n)
    for item in (d_q, d_k, d_v):
        item[...] = jnp.zeros_like(item)
    dp[...] = jnp.zeros_like(dp)
    vec[...] = jnp.zeros_like(vec)
    vec[4:5] = column_sums(d_branch[0]) + column_sums(d_branch[1])
    pl.semaphore_wait(bar, n)
    red.begin(0)
    red.begin(1)

    fetch(0).wait()
    d_out = jnp.concatenate([d_branch[0], d_branch[1]], axis=0)

    @pl.loop(0, act.shape[1] // 256)
    def _(t):
        cols = pl.ds(pl.multiple_of(t * 256, 256), 256)
        d_z[:, cols] = (dot(d_out, w[:, cols]) * slope[:, cols]).astype(low)

    fetch(1).start()

    def expand_grads():
        write_blocks(n, g_expand, stage, stage_sem, lambda i: dot(h2_t[i], d_z[...]))
        sums = column_sums(d_z[...])
        vec[1:2] = sums[:, :width]
        vec[2:3] = sums[:, width:]

    def hidden_back():
        fetch(1).wait()
        back(d_z, 4 * half)
        swap(0, d_h.at[1 - c], d_h_got).start()
        fetch(2).start()

    def middle_back():
        swap(0, d_h.at[1 - c], d_h_got).wait()
        d_x, shift, scale = norm_back(middle[...], piece(4), d_h[c] + d_h_got[...])
        d_mid[...] = d_x + cot[...].astype(f32) * row_ok[...]
        dp[2:3] = jnp.sum(d_mid[...] * attended[...], axis=0, keepdims=True)
        dp[3:4] = shift
        dp[4:5] = scale
        d_att[c] = (piece(2) * d_mid[...]).astype(low)
        swap(1, d_att.at[c], d_att.at[c]).start()

    def mixed_back():
        swap(1, d_att.at[c], d_att.at[c]).wait()
        d_all = jnp.concatenate([d_att[0], d_att[1]], axis=0)
        to_blocks(d_all, d_att_t)
        vec[3:4] = column_sums(d_att[0]) + column_sums(d_att[1])
        fetch(2).wait()
        d_o[:, :half] = dot(d_all, w[:, edge:])[:, 3 * half - edge :].astype(low)
        d_o[:, half:] = jnp.zeros((2 * rows, d_o.shape[1] - half), low)

    seen = jnp.broadcast_to(key_ok[...], (2 * rows, 2 * rows)) > 0.0

    def head(h):
        win, lanes = head_window(h)
        qh, kh, doh = q[:, win] * lanes, k[:, win] * lanes, d_o[:, win] * lanes
        probs = head_probs(qh, kh, seen)
        d_probs = dot(doh, v[:, win], 1, 1)
        inner = jnp.sum(probs * d_probs, axis=-1, keepdims=True)
        d_logits = (probs * (d_probs - inner)).astype(low)
        d_q[:, win] = d_q[:, win] + dot(d_logits, kh) * HEAD_DIM ** (-0.5)
        d_k[:, win] = d_k[:, win] + dot(d_logits, qh, 0, 0) * HEAD_DIM ** (-0.5)
        d_v[:, win] = d_v[:, win] + dot(probs.astype(low), doh, 0, 0)

    def attention_grads():
        for i, item in enumerate((d_q, d_k, d_v)):
            rhs[: 2 * rows, i * half : (i + 1) * half] = item[:, :half].astype(low)
        rhs[: 2 * rows, 3 * half :] = jnp.zeros((2 * rows, half), low)
        rhs[2 * rows :, edge : 3 * half] = jnp.zeros((2 * rows, 3 * half - edge), low)
        rhs[2 * rows :, 3 * half :] = o[:, :half]
        sums = column_sums(rhs[: 2 * rows, : 3 * half])
        vec[0:1, :half] = sums[:, :half]
        vec[0:1, half:] = sums[:, 2 * half :]

        def block(i):
            left = dot(h1_t[i], rhs[: 2 * rows, :edge])
            right = dot(h1_t[i], rhs[: 2 * rows, edge:]) + dot(d_att_t[i], rhs[2 * rows :, edge:])
            return jnp.concatenate([left, right], axis=1)

        write_blocks(n, g_attn, stage, stage_sem, block)

    def input_back():
        back(rhs.at[: 2 * rows, : edge + 128], edge + 128)
        swap(2, d_h.at[1 - c], d_h_got).start()
        fetch(3).start()

    def first_back():
        swap(2, d_h.at[1 - c], d_h_got).wait()
        d_x, shift, scale = norm_back(x[...], piece(1), d_h[c] + d_h_got[...])
        tokens_grad[...] = (d_x + d_mid[...]).astype(low)
        dp[0:1] = shift
        dp[1:2] = scale
        fetch(3).wait()
        back(act, 4 * half)
        swap(3, d_h.at[1 - c], branch_got).start()

    def branch_out():
        swap(3, d_h.at[1 - c], branch_got).wait()
        branch = d_h[c] + branch_got[...] + b_contract[...]
        result = middle[...] + piece(5) * branch
        block_out[...] = jnp.where(jnp.broadcast_to(row_ok[...], result.shape) > 0.0, result, 0.0).astype(low)
        dp[5:6] = jnp.sum(cot[...].astype(f32) * row_ok[...] * branch, axis=0, keepdims=True)
        swap(4, dp, dp_got).start()

    msg_start, msg_wait = all_peers(n, msg, msg_got, msg_send, msg_recv, False)
    vec_start, vec_wait = all_peers(n, chunk, vec_got, vec_send, vec_recv, True)
    per = chunk_tiles(n, width)

    def send_mod():
        swap(4, dp, dp_got).wait()
        total = (dp[...] + dp_got[...]).astype(low).astype(f32)
        own = jnp.where(c == 0, total[0:3], total[3:6])
        for r in range(3):
            msg[r] = own[r : r + 1]
        msg_got[me] = msg[...]
        chunk[...] = jnp.zeros_like(chunk)
        for t in range(5 * tiles):
            chunk[t // per, t % per] = vec[t // tiles : t // tiles + 1, t % tiles * 128 : t % tiles * 128 + 128]
        vec_got[me] = chunk[me]
        msg_start()
        vec_start()

    keep_mod = pltpu.make_async_copy(d_mod, d_mod_all.at[c], mod_sem)

    def mod_grad():
        msg_wait()
        vec_wait()

        @pl.loop(0, n)
        def _(s):
            for r in range(3):
                d_mod[pl.ds(s, 1), r * width : (r + 1) * width] = msg_got[s, r]

        bias_sum[c] = jnp.zeros((8, 128), f32)
        for r in range(per):
            bias_sum[c, r : r + 1] = jnp.sum(vec_got[:, r], axis=0)
        d_silu[...] = dot(d_mod[...].astype(low), modulation[...], 1, 1)
        swap(5, d_silu, d_silu_got).start()
        swap(6, d_mod, d_mod_all.at[c]).start()
        swap(7, bias_sum.at[c], bias_sum.at[c]).start()
        keep_mod.start()

    def cond_grad():
        swap(5, d_silu, d_silu_got).wait()
        swap(6, d_mod, d_mod_all.at[c]).wait()
        swap(7, bias_sum.at[c], bias_sum.at[c]).wait()
        keep_mod.wait()
        gate = 1.0 / (1.0 + jnp.exp(-cond[...]))
        d_cond[...] = (d_silu[...] + d_silu_got[...]) * (gate + cond[...] * gate * (1.0 - gate))

    def heads_at(first, count):
        @pl.loop(first, first + count)
        def _(h):
            head(h)

    third = -(-heads // 3)

    def first_heads():
        mixed_back()
        heads_at(0, third)

    def last_heads():
        heads_at(2 * third, heads - 2 * third)
        attention_grads()

    steps = (
        expand_grads,
        hidden_back,
        middle_back,
        first_heads,
        lambda: heads_at(third, third),
        last_heads,
        input_back,
        first_back,
        branch_out,
        send_mod,
        mod_grad,
        cond_grad,
    )

    @pl.loop(0, red.units)
    def _(u):
        red.unit(u)
        for i, step in enumerate(steps):
            when(u == i, step)

    red.final(2)
    red.drain()


def chunk_tiles(n, width):
    return -(-5 * (width // 128) // n)


def backward(hbm_args, vmem_args, n, collective_id):
    line = n // 4
    grad = hbm_args[1]
    rows, cols = grad.shape[-2:]
    two, own, width = vmem_args[4].shape
    all_rows = two * own
    heads = vmem_args[5].shape
    low, f32 = jnp.bfloat16, jnp.float32
    dma = pltpu.SemaphoreType.DMA
    vmem, hbm = pl.BlockSpec(memory_space=pltpu.VMEM), pl.BlockSpec(memory_space=pltpu.HBM)
    per = chunk_tiles(n, width)
    return pl.pallas_call(
        functools.partial(backward_kernel, line),
        out_shape=[
            jax.ShapeDtypeStruct(grad.shape, low),
            jax.ShapeDtypeStruct(grad.shape, low),
            jax.ShapeDtypeStruct((2, n, 3 * width), f32),
            jax.ShapeDtypeStruct((3, rows, cols), low),
            jax.ShapeDtypeStruct((own, width), low),
            jax.ShapeDtypeStruct((own, width), low),
            jax.ShapeDtypeStruct((n, 128), f32),
            jax.ShapeDtypeStruct((2, 8, 128), f32),
        ],
        in_specs=[hbm] * len(hbm_args) + [vmem] * len(vmem_args),
        out_specs=[hbm] * 3 + [vmem] * 5,
        scratch_shapes=[
            pltpu.VMEM((width, cols), low),
            pltpu.VMEM((2 * all_rows, cols), low),
            pltpu.VMEM(heads, low),
            pltpu.VMEM(heads, f32),
            pltpu.VMEM(heads, f32),
            pltpu.VMEM(heads, f32),
            pltpu.VMEM((2, own, width), f32),
            pltpu.VMEM((own, width), f32),
            pltpu.VMEM((own, width), f32),
            pltpu.VMEM((own, width), f32),
            pltpu.VMEM((2, own, width), low),
            pltpu.VMEM((n, rows, all_rows), low),
            pltpu.VMEM((2, rows, cols), low),
            pltpu.VMEM((8, width), f32),
            pltpu.VMEM((8, width), f32),
            pltpu.VMEM((3, 1, width), f32),
            pltpu.VMEM((n, 3, 1, width), f32),
            pltpu.VMEM((n, 3 * width), f32),
            pltpu.VMEM((8, width), f32),
            pltpu.VMEM((n, per, 1, 128), f32),
            pltpu.VMEM((n, 128), f32),
            pltpu.VMEM((n, 128), f32),
            pltpu.VMEM((n, per, 1, 128), f32),
            dma((4,)),
            dma,
            dma((2,)),
            dma((8,)),
            dma((8,)),
            dma((n,)),
            dma((n,)),
            dma((n,)),
            dma((n,)),
        ]
        + reducer_scratch(3, line, rows, low),
        compiler_params=pltpu.CompilerParams(
            collective_id=collective_id, has_side_effects=True, vmem_limit_bytes=63 * 2**20),
        name="backward",
    )(*hbm_args, *vmem_args)


def exchange_kernel(n, spread, *refs):
    count = len(spread)
    srcs, outs, (send, recv) = refs[:count], refs[count:2 * count], refs[2 * count:]
    me, c = lax.axis_index("dp"), lax.axis_index("seq")
    bar = pltpu.get_barrier_semaphore()

    @pl.loop(1, n)
    def _(j):
        pl.semaphore_signal(bar, inc=1, device_id=((me + j) % n, c), device_id_type=MESH)

    for a in range(count):
        outs[a][me] = srcs[a][me] if spread[a] else srcs[a][...]
    pl.semaphore_wait(bar, n - 1)

    def copy(a, j, there, slot):
        return pltpu.make_async_remote_copy(
            src_ref=srcs[a].at[there] if spread[a] else srcs[a], dst_ref=outs[a].at[slot],
            send_sem=send.at[a, j], recv_sem=recv.at[a, slot], device_id=(there, c), device_id_type=MESH)

    @pl.loop(1, n)
    def _(j):
        for a in range(count):
            copy(a, j, (me + j) % n, me).start()

    @pl.loop(1, n)
    def _(j):
        for a in range(count):
            copy(a, j, (me + j) % n, (me + n - j) % n).wait()


def exchange(blocks, spread, n, collective_id):
    count = len(blocks)
    parts = [b.shape[1:] if s else b.shape for b, s in zip(blocks, spread)]
    dma = pltpu.SemaphoreType.DMA
    return pl.pallas_call(
        functools.partial(exchange_kernel, n, spread),
        out_shape=[jax.ShapeDtypeStruct((n,) + p, b.dtype) for p, b in zip(parts, blocks)],
        in_specs=[pl.BlockSpec(memory_space=pltpu.VMEM)] * count,
        out_specs=[pl.BlockSpec(memory_space=pltpu.VMEM)] * count,
        scratch_shapes=[dma((count, n)), dma((count, n))],
        compiler_params=pltpu.CompilerParams(collective_id=collective_id, has_side_effects=True, vmem_limit_bytes=32 * 2**20),
        name="exchange",
    )(*blocks)


def adam_step(grad, master, first, second, rate):
    first_new = BETA_FIRST * first + (1.0 - BETA_FIRST) * grad
    second_new = BETA_SECOND * second + (1.0 - BETA_SECOND) * grad * grad
    first_hat = first_new / (1.0 - BETA_FIRST**STEP)
    second_hat = second_new / (1.0 - BETA_SECOND**STEP)
    master_new = master - rate * (
        first_hat / (jnp.sqrt(second_hat) + ADAM_EPS) + WEIGHT_DECAY * master
    )
    return (first_new, second_new, master_new)


def chunk_rows(rows):
    sizes = [d for d in range(8, 257, 8) if rows % d == 0]
    return sizes[-1] if sizes else rows


def norm_kernel(n, *refs):
    reduced, silu, d_mod, d_cond, bias_sum, onehot, same = refs[:7]
    flat, factor_out, norm_out, bias_out = refs[7:13], refs[13], refs[14], refs[15]
    both, wide, block, got, pair_send, pair_recv, send, recv = refs[16:]
    me, c = lax.axis_index("dp"), lax.axis_index("seq")
    rows = reduced.shape[1]
    half = reduced.shape[2]
    head = half // 4

    bar = pltpu.get_barrier_semaphore()
    pl.semaphore_signal(bar, inc=1, device_id=(me, 1 - c), device_id_type=MESH)

    @pl.loop(1, n)
    def _(j):
        pl.semaphore_signal(bar, inc=1, device_id=((me + j) % n, c), device_id_type=MESH)

    both[c] = reduced[...]
    pl.semaphore_wait(bar, n)
    pair = pltpu.make_async_remote_copy(
        src_ref=reduced, dst_ref=both.at[c], send_sem=pair_send, recv_sem=pair_recv,
        device_id=(me, 1 - c), device_id_type=MESH)
    pair.start()

    def spread(a, width):
        total = None
        tiles = width // 128
        for t in range(tiles):
            part = wide[:, 128 * t : 128 * t + 128]
            flat[a][pl.ds(t, rows, stride=tiles), :] = part
            square = part * part
            total = square if total is None else total + square
        return jnp.sum(total)

    part_mod = d_mod.shape[2]
    for core in range(2):
        wide[:, core * part_mod : (core + 1) * part_mod] = dot(silu[...], d_mod[core].astype(silu.dtype), 0, 0)
    squares = spread(0, wide.shape[1])
    mod_sums = jnp.sum(d_mod[...], axis=1)
    squares = squares + jnp.where(me == 0, jnp.sum(mod_sums * mod_sums), 0.0)
    width = n * rows
    tile = chunk_tiles(n, width) * me + lax.broadcasted_iota(jnp.int32, (8, 128), 0)
    squares = squares + jnp.sum(bias_sum[0] * bias_sum[0])
    squares = squares + jnp.sum(jnp.where(tile < 3 * (width // 128), bias_sum[1] * bias_sum[1], 0.0))
    pair.wait()
    for core in range(2):
        for part in range(3):
            lo = (2 * part + core) * head
            wide[:, lo : lo + head] = both[core, 2, :, part * head : (part + 1) * head].astype(jnp.float32)
    squares = squares + spread(1, 6 * head)
    for core in range(2):
        wide[:, core * head : (core + 1) * head] = both[core, 2, :, 3 * head :].astype(jnp.float32)
    squares = squares + spread(2, 2 * head)
    for a in (3, 4):
        for core in range(2):
            wide[:, core * half : (core + 1) * half] = both[core, 4 - a].astype(jnp.float32)
        squares = squares + spread(a, 2 * half)

    slots = d_cond.shape[0]
    block[:slots] = d_cond[...]
    block[slots : slots + 8] = jnp.full((8, 128), squares, jnp.float32)
    block[slots + 8 : slots + 16] = bias_sum[0]
    block[slots + 16 :] = bias_sum[1]
    got[me] = block[...]

    def copy(j, there, slot):
        return pltpu.make_async_remote_copy(
            src_ref=block, dst_ref=got.at[slot], send_sem=send.at[j], recv_sem=recv.at[slot],
            device_id=(there, c), device_id_type=MESH)

    @pl.loop(1, n)
    def _(j):
        copy(j, (me + j) % n, me).start()

    @pl.loop(1, n)
    def _(j):
        copy(j, (me + j) % n, (me + n - j) % n).wait()

    bias_out[...] = got[:, slots + 8 :]
    total = jnp.sum(got[:, slots : slots + 8], axis=0)[:1, :1]
    gram = jnp.zeros((slots, slots), jnp.float32)
    for i in range(n):
        part = got[i, :slots]
        gram = gram + lax.dot_general(
            part, part, (((1,), (1,)), ((), ())), preferred_element_type=jnp.float32, precision=lax.Precision.HIGHEST)
        wide[: onehot.shape[1], i * rows : (i + 1) * rows] = lax.dot_general(
            onehot[...], part, (((0,), (0,)), ((), ())), preferred_element_type=jnp.float32,
            precision=lax.Precision.HIGHEST)[:, :rows]
    total = total + jnp.sum(gram * same[...], keepdims=True)
    norm = jnp.sqrt(total)
    norm_out[...] = jnp.broadcast_to(norm, (8, 128))
    factor_out[...] = jnp.broadcast_to(jnp.minimum(1.0, CLIP_LIMIT / (norm + 1e-06)), (8, 128))
    tiles = n * rows // 128
    for t in range(tiles):
        flat[5][pl.ds(t, onehot.shape[1], stride=tiles), :] = wide[: onehot.shape[1], 128 * t : 128 * t + 128]


def adam_kernel(rates, *refs):
    kinds = len(rates)
    factor_ref, flat = refs[0], refs[1 : 1 + kinds]
    at = 1 + kinds
    states = [refs[at + 3 * a : at + 3 * a + 3] for a in range(kinds)]
    at += 3 * kinds
    news = [refs[at + 3 * a : at + 3 * a + 3] for a in range(kinds)]
    at += 3 * kinds
    held = refs[at : at + kinds]
    in_sem, out_sem = refs[at + kinds :]

    def loads(a):
        return [pltpu.make_async_copy(states[a][k], held[a].at[k], in_sem.at[a, k]) for k in range(3)]

    for a in range(kinds):
        for copy in loads(a):
            copy.start()
    factor = factor_ref[:1, :]
    for a in range(kinds):
        for copy in loads(a):
            copy.wait()
        size = chunk_rows(flat[a].shape[0])

        @pl.loop(0, flat[a].shape[0] // size)
        def _(i, a=a, size=size):
            part = pl.ds(pl.multiple_of(i * size, size), size)
            grad = flat[a][part] * factor
            master, first, second = held[a][0, part], held[a][1, part], held[a][2, part]
            first, second, master = adam_step(grad, master, first, second, rates[a])
            held[a][0, part], held[a][1, part], held[a][2, part] = master, first, second
            for k in range(3):
                pltpu.make_async_copy(held[a].at[k, part], news[a][k].at[part], out_sem.at[a, k]).start()

    for a in range(kinds):
        for k in range(3):
            pltpu.make_async_copy(held[a].at[k], news[a][k], out_sem.at[a, k]).wait()


def finish(reduced, silu, d_mod, d_cond, bias_sum, onehot, same, states, rates, n, collective_id):
    vmem, hbm = pl.BlockSpec(memory_space=pltpu.VMEM), pl.BlockSpec(memory_space=pltpu.HBM)
    dma = pltpu.SemaphoreType.DMA
    kinds = len(states)
    rows = reduced.shape[1]
    flats = [jax.ShapeDtypeStruct(s[0].shape, jnp.float32) for s in states]
    small = jax.ShapeDtypeStruct((8, 128), jnp.float32)
    block = d_cond.shape[0] + 24
    outs = pl.pallas_call(
        functools.partial(norm_kernel, n),
        out_shape=flats + [small, small, jax.ShapeDtypeStruct((n, 16, 128), jnp.float32)],
        in_specs=[vmem] * 7,
        out_specs=[vmem] * (kinds + 3),
        scratch_shapes=[
            pltpu.VMEM((2,) + reduced.shape, reduced.dtype),
            pltpu.VMEM((rows, 2 * d_mod.shape[2]), jnp.float32),
            pltpu.VMEM((block, 128), jnp.float32),
            pltpu.VMEM((n, block, 128), jnp.float32),
            dma,
            dma,
            dma((n,)),
            dma((n,)),
        ],
        compiler_params=pltpu.CompilerParams(
            collective_id=collective_id, has_side_effects=True, vmem_limit_bytes=40 * 2**20),
        name="norm",
    )(reduced, silu, d_mod, d_cond, bias_sum, onehot, same)
    grads, factor, norm = outs[:kinds], outs[kinds], outs[kinds + 1]
    news = pl.pallas_call(
        functools.partial(adam_kernel, rates),
        out_shape=[f for f in flats for _ in range(3)],
        in_specs=[vmem] * (1 + kinds) + [hbm] * (3 * kinds),
        out_specs=[hbm] * (3 * kinds),
        scratch_shapes=[pltpu.VMEM((3,) + f.shape, jnp.float32) for f in flats]
        + [dma((kinds, 3)), dma((kinds, 3))],
        compiler_params=pltpu.CompilerParams(vmem_limit_bytes=56 * 2**20),
        name="adam",
    )(factor, *grads, *[item for s in states for item in s])
    order = [3 * a + k for a in range(kinds) for k in (1, 2, 0)]
    return [news[i] for i in order], norm[0, 0], outs[kinds + 2]


def grid_embed(keep_index, width):
    quarter = width // 4
    freqs = 10000.0 ** (-jnp.arange(quarter).astype(jnp.float32) / quarter)
    across = (keep_index // SIDE).astype(jnp.float32)[..., None] * freqs
    along = (keep_index % SIDE).astype(jnp.float32)[..., None] * freqs
    return jnp.concatenate(
        [jnp.sin(across), jnp.cos(across), jnp.sin(along), jnp.cos(along)], axis=-1
    )


def per_device(
    tokens,
    cotangent,
    time_vec,
    labels,
    kept,
    keep_index,
    modulation_master,
    modulation_first,
    modulation_second,
    attention_in_master,
    attention_in_first,
    attention_in_second,
    attention_out_master,
    attention_out_first,
    attention_out_second,
    expand_master,
    expand_first,
    expand_second,
    contract_master,
    contract_first,
    contract_second,
    class_table_master,
    class_table_first,
    class_table_second,
    biases_master,
    biases_first,
    biases_second,
):
    rows, width = tokens.shape[1:]
    n, pairs = lax.axis_size("dp"), lax.axis_size("seq")
    me, c = lax.axis_index("dp"), lax.axis_index("seq")
    own_rows = width // n
    half_width, half_ff = width // pairs, FF // pairs
    low = jnp.bfloat16

    def part_of(vector):
        return lax.dynamic_slice_in_dim(vector, c * (vector.shape[0] // pairs), vector.shape[0] // pairs, 0)

    bias_share = biases_master.shape[0]
    bias_block = jnp.pad(biases_master.astype(low).astype(jnp.float32), (0, 1024 - bias_share)).reshape(8, 128)
    label_block = jnp.broadcast_to(labels.astype(jnp.float32)[:, None], (8, 128))
    (got,) = exchange([jnp.concatenate([bias_block, label_block])], (False,), n, 3)
    biases = got[:, :8].reshape(n, 1024)[:, :bias_share].reshape(-1)
    labels_all = got[:, 8, 0].astype(jnp.int32)
    bias_mod = biases[: 6 * width]
    bias_query = biases[6 * width : 7 * width]
    bias_value = biases[7 * width : 8 * width]
    bias_out = biases[8 * width : 9 * width]
    bias_expand = biases[9 * width : 9 * width + FF]
    bias_contract = biases[9 * width + FF :]

    class_rows = CLASSES // n
    onehot = labels_all[:, None] == me * class_rows + jnp.arange(class_rows)[None, :]
    inputs = tokens[0].astype(jnp.float32) + grid_embed(keep_index[0], width)
    half_kept = kept // pairs
    row_ok = jnp.arange(rows) < half_kept
    key_ok = ((jnp.arange(rows * pairs) % rows) < half_kept).astype(jnp.float32)[None]
    row_ok = row_ok.astype(jnp.float32)[:, None]
    (weights, grad_contract, normed_in, normed_mid, queries, keys, values, mixed, attended, middle, activated, slope, d_branch,
     pieces, cond_own, silu_own, own_modulation) = forward(
        [
            item.reshape(-1, 128)
            for item in (
                attention_in_master,
                attention_out_master,
                expand_master,
                contract_master,
                class_table_master,
                modulation_master,
            )
        ],
        [
            onehot.astype(low),
            time_vec,
            inputs,
            key_ok,
            part_of(bias_mod)[None],
            part_of(bias_query)[None],
            part_of(bias_value)[None],
            bias_out[None],
            part_of(bias_expand)[None],
            cotangent[0],
            row_ok,
        ],
        n,
        1,
    )
    _, _, d_mod_all, reduced, block_out, tokens_grad, d_cond, bias_sum = backward(
        [weights.reshape(3, width, 4 * half_width), grad_contract],
        [
            normed_in,
            normed_mid,
            activated,
            slope,
            d_branch,
            queries,
            keys,
            values,
            mixed,
            key_ok,
            inputs,
            middle,
            attended,
            cotangent[0],
            row_ok,
            pieces,
            bias_contract[None],
            own_modulation,
            cond_own,
        ],
        n,
        2,
    )
    block_out, tokens_grad = block_out[None], tokens_grad[None]
    same = (labels_all[:, None] == labels_all[None, :]).astype(jnp.float32)
    rates = (
        width ** (-0.5),
        width ** (-0.5),
        (width // 4) ** (-0.5),
        width ** (-0.5),
        FF ** (-0.5),
        0.5,
        0.2,
    )
    masters = (
        modulation_master,
        attention_in_master,
        attention_out_master,
        expand_master,
        contract_master,
        class_table_master,
        biases_master,
    )
    firsts = (
        modulation_first,
        attention_in_first,
        attention_out_first,
        expand_first,
        contract_first,
        class_table_first,
        biases_first,
    )
    seconds = (
        modulation_second,
        attention_in_second,
        attention_out_second,
        expand_second,
        contract_second,
        class_table_second,
        biases_second,
    )
    states = list(zip(masters, firsts, seconds))
    updated, grad_norm, bias_parts = finish(
        reduced,
        silu_own[:, :own_rows],
        d_mod_all,
        d_cond,
        bias_sum,
        onehot.astype(jnp.float32),
        same,
        [tuple(item.reshape(-1, 128) for item in state) for state in states[:-1]],
        rates[:-1],
        n,
        8,
    )
    factor = jnp.minimum(1.0, CLIP_LIMIT / (grad_norm + 1e-06))
    bias_parts = bias_parts.reshape(n, pairs, 8, 128)[:, :, : chunk_tiles(n, width)].transpose(1, 0, 2, 3)
    bias_parts = bias_parts.reshape(pairs, -1)[:, : 5 * width].reshape(pairs, 5, width)
    grad_biases = jnp.concatenate(
        [
            jnp.sum(d_mod_all, axis=1).reshape(-1),
            bias_parts[:, 0, :half_width].reshape(-1),
            bias_parts[:, 0, half_width:].reshape(-1),
            bias_parts[0, 3],
            bias_parts[:, 1:3].reshape(-1),
            bias_parts[0, 4],
        ]
    )
    bias_grad = lax.dynamic_slice_in_dim(grad_biases, me * bias_share, bias_share, 0) * factor
    updated = [item.reshape(-1) for item in updated] + list(adam_step(bias_grad, *states[-1], rates[-1]))
    return (block_out, tokens_grad, grad_norm) + tuple(updated)


def solution(mesh):
    return jax.shard_map(
        per_device,
        mesh=mesh,
        in_specs=(
            P("dp", "seq", None),
            P("dp", "seq", None),
            P("dp", None),
            P("dp"),
            P("dp"),
            P("dp", "seq"),
            P("dp"),
            P("dp"),
            P("dp"),
            P("dp"),
            P("dp"),
            P("dp"),
            P("dp"),
            P("dp"),
            P("dp"),
            P("dp"),
            P("dp"),
            P("dp"),
            P("dp"),
            P("dp"),
            P("dp"),
            P("dp"),
            P("dp"),
            P("dp"),
            P("dp"),
            P("dp"),
            P("dp"),
        ),
        out_specs=(
            P("dp", "seq", None),
            P("dp", "seq", None),
            P(),
            P("dp"),
            P("dp"),
            P("dp"),
            P("dp"),
            P("dp"),
            P("dp"),
            P("dp"),
            P("dp"),
            P("dp"),
            P("dp"),
            P("dp"),
            P("dp"),
            P("dp"),
            P("dp"),
            P("dp"),
            P("dp"),
            P("dp"),
            P("dp"),
            P("dp"),
            P("dp"),
            P("dp"),
        ),
        check_vma=False,
    )
```

```python
import functools
import jax
import jax.numpy as jnp
from jax import lax
from jax.experimental import pallas as pl
from jax.experimental.pallas import tpu as pltpu
from jax.sharding import PartitionSpec as P

HEAD_DIM = 72
FF = 4608
SIDE = 16
CLASSES = 1024
STEP = 10
LAYER_EPS = 1e-06
MASK_FILL = -1e30
BETA_FIRST = 0.5
BETA_SECOND = 0.5
ADAM_EPS = 1e-08
WEIGHT_DECAY = 0.1
CLIP_LIMIT = 1.0

MESH = pl.DeviceIdType.MESH
GELU_A = (2.0 / 3.141592653589793) ** 0.5
GELU_B = 0.044715
UNIT_PLACES = ((0, 1, 2, 4, 6, 7, 9, 12, 14, 14, 16, 17), (1, 2, 4, 6, 7, 10, 13, 15, 16, 16, 17, 20))
GROUPS = ((0, 768, 0, "x"), (768, 768, 0, "y"), (1536, 384, 1, "x"), (1920, 384, 1, "y"))


def when(cond, fn):
    pl.when(cond)(fn)


class Place:
    def __init__(self, line):
        self.line = line
        i = lax.axis_index("dp")
        self.c = lax.axis_index("seq")
        self.x, self.y, self.z = i % 2, (i // 2) % 2, i // 4

    def dev(self, z=None, y=None, x=None):
        z = self.z if z is None else z
        y = self.y if y is None else y
        x = self.x if x is None else x
        return (z * 4 + y * 2 + x, self.c)

    def peer(self, axis):
        return self.dev(x=1 - self.x) if axis == "x" else self.dev(y=1 - self.y)

    def barrier(self):
        bar = pltpu.get_barrier_semaphore()

        def sig(dev):
            pl.semaphore_signal(bar, inc=1, device_id=dev, device_id_type=MESH)

        sig(self.peer("x"))
        sig(self.peer("y"))
        when(self.z > 0, lambda: sig(self.dev(z=self.z - 1)))
        when(self.z < self.line - 1, lambda: sig(self.dev(z=self.z + 1)))
        pl.semaphore_wait(bar, 2 + (self.z > 0).astype(jnp.int32) + (self.z < self.line - 1).astype(jnp.int32))


class Gatherer:
    def __init__(self, line, own, out, keep_sem, sems):
        self.line, self.own, self.out, self.keep_sem = line, own, out, keep_sem
        self.send_a, self.send_u, self.send_d, self.send_b, self.recv_a, self.recv_z, self.recv_b = sems
        self.me = Place(line)
        self.up, self.down = self.me.z < line - 1, self.me.z > 0

    def single(self, m, g, zz):
        lo, width = GROUPS[g][:2]
        return self.out.at[m, zz, self.me.y, self.me.x, :, pl.ds(lo, width)]

    def pair(self, m, g, zz):
        lo, width, _, first = GROUPS[g]
        if first == "x":
            return self.out.at[m, zz, self.me.y, :, :, pl.ds(lo, width)]
        return self.out.at[m, zz, :, self.me.x, :, pl.ds(lo, width)]

    def remote(self, ref, send, recv, dev, source):
        return pltpu.make_async_remote_copy(
            src_ref=ref if source is None else source, dst_ref=ref, send_sem=send, recv_sem=recv,
            device_id=dev, device_id_type=MESH)

    def source(self, m, g):
        lo, width = GROUPS[g][:2]
        return self.own.at[m, :, pl.ds(lo, width)]

    def a_copy(self, m, g, zz, source=None):
        return self.remote(
            self.single(m, g, zz), self.send_a.at[m, g, zz], self.recv_a.at[m, g, zz], self.me.peer(GROUPS[g][3]), source)

    def z_ref(self, m, g, zz):
        return self.pair(m, g, zz) if GROUPS[g][2] == 0 else self.single(m, g, zz)

    def u_copy(self, m, g, zz, source=None):
        dev = self.me.dev(z=jnp.minimum(self.me.z + 1, self.line - 1))
        return self.remote(self.z_ref(m, g, zz), self.send_u.at[m, g, zz], self.recv_z.at[m, g, zz], dev, source)

    def d_copy(self, m, g, zz, source=None):
        dev = self.me.dev(z=jnp.maximum(self.me.z - 1, 0))
        return self.remote(self.z_ref(m, g, zz), self.send_d.at[m, g, zz], self.recv_z.at[m, g, zz], dev, source)

    def b_copy(self, m, g, zz):
        last = "y" if GROUPS[g][3] == "x" else "x"
        return self.remote(self.pair(m, g, zz), self.send_b.at[m, g, zz], self.recv_b.at[m, g, zz], self.me.peer(last), None)

    def keep(self, m):
        me = self.me
        return pltpu.make_async_copy(self.own.at[m], self.out.at[m, me.z, me.y, me.x], self.keep_sem.at[m])

    def begin(self, m):
        z = self.me.z
        self.keep(m).start()
        for g in range(4):
            self.a_copy(m, g, z, self.source(m, g)).start()
        for g in (2, 3):
            when(self.up, lambda g=g: self.u_copy(m, g, z, self.source(m, g)).start())
            when(self.down, lambda g=g: self.d_copy(m, g, z, self.source(m, g)).start())

    def paired(self, m):
        z = self.me.z
        self.keep(m).wait()
        for g in (0, 1):
            self.a_copy(m, g, z).wait_recv()
            when(self.up, lambda g=g: self.u_copy(m, g, z).start())
            when(self.down, lambda g=g: self.d_copy(m, g, z).start())
            self.b_copy(m, g, z).start()

    def arrive(self, m, zz, upward):
        for g in range(4):
            copy = self.u_copy if upward else self.d_copy
            copy(m, g, zz).wait_recv()
            when(self.up if upward else self.down, lambda g=g: copy(m, g, zz).start())
            if GROUPS[g][2] == 0:
                self.b_copy(m, g, zz).start()
            else:
                self.a_copy(m, g, zz).start()

    def crossed(self, m, zz):
        for g in (2, 3):
            self.a_copy(m, g, zz).wait_recv()
            self.b_copy(m, g, zz).start()

    def step(self, m, k):
        z, line = self.me.z, self.line
        when(k <= z, lambda: self.arrive(m, jnp.maximum(z - k, 0), True))
        when(z + k < line, lambda: self.arrive(m, jnp.minimum(z + k, line - 1), False))
        when(k - 1 <= z, lambda: self.crossed(m, jnp.maximum(z - k + 1, 0)))
        when((k > 1) & (z + k - 1 < line), lambda: self.crossed(m, jnp.minimum(z + k - 1, line - 1)))

    def steps(self, m, first, last):
        @pl.loop(first, last + 1)
        def _(k):
            self.step(m, k)

    def complete(self, m):
        @pl.loop(0, self.line)
        def _(zz):
            for g in range(4):
                self.b_copy(m, g, zz).wait_recv()

    def drain(self, m):
        z = self.me.z

        @pl.loop(0, self.line)
        def _(zz):
            for g in range(4):
                self.b_copy(m, g, zz).wait_send()
                if GROUPS[g][2] == 1:
                    self.a_copy(m, g, zz).wait_send()
                when(self.up & (zz <= z), lambda g=g: self.u_copy(m, g, zz).wait_send())
                when(self.down & (zz >= z), lambda g=g: self.d_copy(m, g, zz).wait_send())

        for g in (0, 1):
            self.a_copy(m, g, z).wait_send()


def dot(left, right, a=1, b=0):
    return lax.dot_general(left, right, (((a,), (b,)), ((), ())), preferred_element_type=jnp.float32)


def normal(values):
    centre = values - jnp.mean(values, axis=-1, keepdims=True)
    return centre * lax.rsqrt(jnp.mean(centre * centre, axis=-1, keepdims=True) + LAYER_EPS)


def all_peers(n, src, dst, send, recv, spread):
    me, c = lax.axis_index("dp"), lax.axis_index("seq")

    def copy(j, there, slot):
        return pltpu.make_async_remote_copy(
            src_ref=src.at[there] if spread else src, dst_ref=dst.at[slot], send_sem=send.at[j], recv_sem=recv.at[slot],
            device_id=(there, c), device_id_type=MESH)

    def start():
        @pl.loop(1, n)
        def _(j):
            copy(j, (me + j) % n, me).start()

    def wait():
        @pl.loop(1, n)
        def _(j):
            copy(j, (me + j) % n, (me + n - j) % n).wait()

    return start, wait


def greet_all(n):
    me, c = lax.axis_index("dp"), lax.axis_index("seq")
    bar = pltpu.get_barrier_semaphore()
    pl.semaphore_signal(bar, inc=1, device_id=(me, 1 - c), device_id_type=MESH)

    @pl.loop(1, n)
    def _(j):
        pl.semaphore_signal(bar, inc=1, device_id=((me + j) % n, c), device_id_type=MESH)

    return bar


def head_window(h):
    lo = pl.multiple_of(h * HEAD_DIM // 128 * 128, 128)
    lane = lax.broadcasted_iota(jnp.int32, (1, 256), 1) + lo - h * HEAD_DIM
    return pl.ds(lo, 256), ((lane >= 0) & (lane < HEAD_DIM)).astype(jnp.bfloat16)


def head_probs(qh, kh, seen):
    logits = jnp.where(seen, dot(qh, kh, 1, 1) * HEAD_DIM ** (-0.5), MASK_FILL)
    expo = jnp.exp(logits - jnp.max(logits, axis=-1, keepdims=True))
    return expo / jnp.sum(expo, axis=-1, keepdims=True)


def to_blocks(values, ref):
    count, size = ref.shape[:2]
    turned = values.T
    for i in range(count):
        ref[i] = turned[i * size : (i + 1) * size]


def write_blocks(n, target, stage, sem, block):
    def copy(i):
        return pltpu.make_async_copy(stage.at[i % 2], target.at[i // 4, i // 2 % 2, i % 2], sem.at[i % 2])

    @pl.loop(0, n)
    def _(i):
        when(i >= 2, lambda: copy(i).wait())
        stage[i % 2] = block(i).astype(stage.dtype)
        copy(i).start()

    copy(0).wait()
    copy(1).wait()


def forward_kernel(line, *refs):
    (m_in, m_out, m_expand, m_contract, m_table, m_mod, block, time_vec, tokens, cells, freqs, kept, cot) = refs[:13]
    (weights, g_contract, h1_t, h2_t, q, k, v, o, attended, middle, act, slope, d_branch, pieces, cond, silu,
     mod_half, x, key_ok, row_ok, onehot, same, biases) = refs[13:36]
    (f_in, f_out, f_expand, f_contract, f_table, f_mod, own, table, cond_part, cond_got, mods, mod_part, mod_got, blocks, w,
     proj, mix, wide, partial, partial_got, h1, h2, d_branch_t, stage, block_got, wide_bias, in_sem, w_sem, pair_send, pair_recv,
     block_send, block_recv, cond_send, cond_recv, mod_send, mod_recv, keep_sem, stage_sem) = refs[36:74]
    n = line * 4
    low, f32 = jnp.bfloat16, jnp.float32
    me, c = lax.axis_index("dp"), lax.axis_index("seq")
    gat = Gatherer(line, own, weights, keep_sem, refs[74:])
    rows, width = x.shape
    own_rows, half = own.shape[1], own.shape[2] // 4
    edge = 3 * half // 128 * 128
    tiles = width // 128
    sources, flats = (m_in, m_out, m_table, m_mod, m_expand, m_contract), (f_in, f_out, f_table, f_mod, f_expand, f_contract)

    def load(i):
        return pltpu.make_async_copy(sources[i], flats[i], in_sem.at[i])

    for i in range(6):
        load(i).start()
    bar = greet_all(n)

    def swap(i, src, dst):
        return pltpu.make_async_remote_copy(
            src_ref=src, dst_ref=dst, send_sem=pair_send.at[i], recv_sem=pair_recv.at[i], device_id=(me, 1 - c),
            device_id_type=MESH)

    def tile(flat, t, count, per_row):
        return flat[pl.ds(t, count, stride=per_row), :]

    def cut_heads(flat, part, per_row):
        start = part * tiles + c * (tiles // 2)
        found = jnp.concatenate([tile(flat, start + j, own_rows, per_row) for j in range(tiles // 2 + 1)], axis=1)
        return jnp.where(c == 0, found[:, :half], found[:, found.shape[1] - half :]).astype(low)

    def cut(flat, target, count):
        for j in range(count):
            target[:own_rows, 128 * j : 128 * j + 128] = tile(flat, c * count + j, own_rows, 2 * count).astype(low)

    block_start, block_wait = all_peers(n, block, block_got, block_send, block_recv, False)
    cond_start, cond_wait = all_peers(n, cond_part, cond_got, cond_send, cond_recv, True)
    mod_start, mod_wait = all_peers(n, mod_part, mod_got, mod_send, mod_recv, True)
    block_got[me] = block[...]
    load(0).wait()
    load(1).wait()
    for part in range(3):
        own[0, :, part * half : (part + 1) * half] = cut_heads(f_in, part, 3 * tiles)
    own[0, :, 3 * half :] = cut_heads(f_out, 0, tiles)
    pl.semaphore_wait(bar, n)
    block_start()
    gat.begin(0)
    load(5).wait()
    cut(f_contract, own.at[2], 4 * half // 128)
    load(2).wait()
    class_rows = table.shape[0]
    for t in range(tiles):
        table[:, 128 * t : 128 * t + 128] = tile(f_table, t, class_rows, tiles).astype(low)

    block_wait()
    labels = block_got[:, 8, :]
    hot = (labels[:, :class_rows] - (me * class_rows).astype(f32)
           == lax.broadcasted_iota(jnp.int32, (n, class_rows), 1).astype(f32)).astype(f32)
    onehot[...] = hot
    row = jnp.concatenate([block_got[s, 8:9, :1] for s in range(n)], axis=1)
    same[...] = (labels[:, :1] == row).astype(f32)
    found = dot(hot.astype(low), table[...])
    mine = lax.broadcasted_iota(jnp.int32, (n, width), 0) == me
    found = found + jnp.where(mine, jnp.broadcast_to(time_vec[...].astype(f32), (n, width)), 0.0)
    cond_part[...] = jnp.zeros_like(cond_part)
    for i in range(n):
        cond_part[i, :, :own_rows] = found[:, i * own_rows : (i + 1) * own_rows]
    cond_got[me] = cond_part[me]
    cond_start()
    gat.begin(2)
    load(3).wait()
    mod_half[own_rows:] = jnp.zeros((mod_half.shape[0] - own_rows, mod_half.shape[1]), low)
    cut(f_mod, mod_half, 3 * tiles)
    gat.paired(0)
    load(4).wait()
    cut(f_expand, own.at[1], 4 * half // 128)
    gat.begin(1)

    share = biases.shape[1] // n
    for i in range(n):
        for r in range(-(-share // 128)):
            size = min(128, share - 128 * r)
            biases[:, i * share + 128 * r : i * share + 128 * r + size] = block_got[i, r : r + 1, :size]

    def bias(start, size):
        return biases[:, start : start + size]

    def bias_half(start, size):
        return jnp.where(c == 0, bias(start, size // 2), bias(start + size // 2, size // 2))

    half_kept = jnp.floor(kept[...] * 0.5)
    rows_at = lax.broadcasted_iota(jnp.int32, (rows, 1), 0).astype(f32)
    row_ok[...] = (rows_at < half_kept).astype(f32)
    lanes_at = lax.broadcasted_iota(jnp.int32, (1, 2 * rows), 1)
    lanes_at = jnp.where(lanes_at < rows, lanes_at, lanes_at - rows).astype(f32)
    key_ok[...] = (lanes_at < half_kept).astype(f32)
    quarter = width // 4
    for i, place in enumerate((cells[:, :1], cells[:, 1:2])):
        angle = place * freqs[...]
        for j, wave in enumerate((jnp.sin(angle), jnp.cos(angle))):
            cols = slice((2 * i + j) * quarter, (2 * i + j + 1) * quarter)
            x[:, cols] = tokens[:, cols].astype(f32) + wave

    cond_wait()
    value = jnp.sum(cond_got[...], axis=0)
    cond[...] = value
    silu[...] = (value / (1.0 + jnp.exp(-value))).astype(low)
    mods[...] = dot(silu[...], mod_half[...])

    @pl.loop(0, n)
    def _(s):
        mod_part[s] = mods[pl.ds(s, 1), :]

    mod_got[me] = mod_part[me]
    mod_start()
    gat.steps(0, 1, 2)
    mod_wait()
    pieces[c] = jnp.sum(mod_got[...], axis=0) + bias_half(0, 6 * width)
    swap(0, pieces.at[c], pieces.at[c]).start()
    gat.paired(1)
    swap(0, pieces.at[c], pieces.at[c]).wait()
    shift, scale, gate = (pieces[0, :, i * width : (i + 1) * width] for i in range(3))
    h1[c] = (normal(x[...]) * (1.0 + scale) + shift).astype(low)
    swap(1, h1.at[c], h1.at[c]).start()
    d_branch[c] = (pieces[1, :, 2 * width :] * (cot[...].astype(f32) * row_ok[...])).astype(low)
    swap(4, d_branch.at[c], d_branch.at[c]).start()
    gat.steps(0, 3, line)
    gat.steps(1, 1, 1)
    gat.complete(0)

    def fetch(m):
        return pltpu.make_async_copy(weights.at[m], blocks, w_sem.at[m])

    def unpack():
        for i in range(n):
            w[i * own_rows : (i + 1) * own_rows, :] = blocks[i // 4, i // 2 % 2, i % 2]

    fetch(0).start()
    swap(1, h1.at[c], h1.at[c]).wait()
    both = jnp.concatenate([h1[0], h1[1]], axis=0)
    to_blocks(both, h1_t)
    fetch(0).wait()
    unpack()
    gat.steps(1, 2, 2)

    @pl.loop(0, proj.shape[1] // 256)
    def _(t):
        cols = pl.ds(pl.multiple_of(t * 256, 256), 256)
        proj[:, cols] = dot(both, w[:, cols])

    spare = q.shape[1] - half
    for item, value in (
        (q, proj[:, :half] + bias_half(6 * width, width)),
        (k, proj[:, half : 2 * half]),
        (v, proj[:, 2 * half : 3 * half] + bias_half(7 * width, width)),
    ):
        item[:, :half] = value.astype(low)
        item[:, half:] = jnp.zeros((2 * rows, spare), low)
    mix[...] = jnp.zeros_like(mix)
    seen = jnp.broadcast_to(key_ok[...], (2 * rows, 2 * rows)) > 0.0
    heads = half // HEAD_DIM

    def head(h):
        win, lanes = head_window(h)
        probs = head_probs(q[:, win] * lanes, k[:, win], seen)
        mix[:, win] = mix[:, win] + dot(probs.astype(low), v[:, win] * lanes)

    @pl.loop(0, heads)
    def _(t):
        head(t)
        when(t == 0, lambda: gat.paired(2))
        when(t == 3, lambda: gat.steps(1, 3, 3))
        when(t == 5, lambda: gat.steps(1, 4, line))
        when(t == heads - 1, lambda: gat.steps(2, 1, 1))

    o[...] = mix[...].astype(low)
    wide[:, : 3 * half - edge] = jnp.zeros((2 * rows, 3 * half - edge), low)
    wide[:, 3 * half - edge :] = mix[:, :half].astype(low)

    @pl.loop(0, tiles)
    def _(t):
        cols = pl.ds(pl.multiple_of(t * 128, 128), 128)
        part = dot(wide[...], w[cols, edge:], 1, 1)
        partial[0, :, cols] = part[:rows]
        partial[1, :, cols] = part[rows:]

    swap(2, partial.at[1 - c], partial_got).start()
    swap(2, partial.at[1 - c], partial_got).wait()
    attended[...] = partial[c] + partial_got[...] + bias(8 * width, width)
    middle[...] = x[...] + gate * attended[...]
    shift, scale = (pieces[1, :, i * width : (i + 1) * width] for i in range(2))
    h2[c] = (normal(middle[...]) * (1.0 + scale) + shift).astype(low)
    swap(3, h2.at[c], h2.at[c]).start()
    gat.complete(1)
    fetch(1).start()
    swap(4, d_branch.at[c], d_branch.at[c]).wait()
    to_blocks(jnp.concatenate([d_branch[0], d_branch[1]], axis=0), d_branch_t)
    swap(3, h2.at[c], h2.at[c]).wait()
    both = jnp.concatenate([h2[0], h2[1]], axis=0)
    to_blocks(both, h2_t)
    fetch(1).wait()
    unpack()
    gat.steps(2, 2, 2)

    wide_bias[...] = bias_half(9 * width, 8 * half)

    @pl.loop(0, act.shape[1] // 256)
    def _(t):
        cols = pl.ds(pl.multiple_of(t * 256, 256), 256)
        z = dot(both, w[:, cols]) + wide_bias[:, cols]
        bend = jnp.tanh(GELU_A * (z + GELU_B * z * z * z))
        act[:, cols] = (0.5 * z * (1.0 + bend)).astype(low)
        slope[:, cols] = 0.5 * (1.0 + bend) + 0.5 * z * (1.0 - bend * bend) * (GELU_A * (1.0 + 3.0 * GELU_B * z * z))

    gat.steps(2, 3, 3)

    def contract_block(i):
        when(i == n // 4, lambda: gat.steps(2, 4, line))
        return dot(d_branch_t[i], act[...])

    write_blocks(n, g_contract, stage, stage_sem, contract_block)
    gat.complete(2)

    @pl.loop(0, 3)
    def _(m):
        gat.drain(m)


def forward(hbm_args, vmem_args, bias_size, n, collective_id):
    line = n // 4
    block, time_vec, tokens = vmem_args[:3]
    rows, width = tokens.shape
    class_rows = hbm_args[4].size // width
    own_rows, half = width // n, width // 2
    low, f32 = jnp.bfloat16, jnp.float32
    dma = pltpu.SemaphoreType.DMA
    vmem, hbm = pl.BlockSpec(memory_space=pltpu.VMEM), pl.BlockSpec(memory_space=pltpu.HBM)
    heads = (2 * rows, -(-half // 128) * 128)
    edge = 3 * half // 128 * 128

    def shape(dims, kind):
        return jax.ShapeDtypeStruct(dims, kind)

    def scratch(dims, kind):
        return pltpu.VMEM(dims, kind)

    return pl.pallas_call(
        functools.partial(forward_kernel, line),
        out_shape=[
            shape((3, line, 2, 2, own_rows, 4 * half), low),
            shape((line, 2, 2, own_rows, 4 * half), low),
            shape((n, own_rows, 2 * rows), low),
            shape((n, own_rows, 2 * rows), low),
            shape(heads, low),
            shape(heads, low),
            shape(heads, low),
            shape(heads, low),
            shape((rows, width), f32),
            shape((rows, width), f32),
            shape((2 * rows, 4 * half), low),
            shape((2 * rows, 4 * half), f32),
            shape((2, rows, width), low),
            shape((2, 1, 3 * width), f32),
            shape((n, 128), f32),
            shape((n, 128), low),
            shape((128, 3 * width), low),
            shape((rows, width), f32),
            shape((1, 2 * rows), f32),
            shape((rows, 1), f32),
            shape((n, class_rows), f32),
            shape((n, n), f32),
            shape((1, bias_size), f32),
        ],
        in_specs=[hbm] * len(hbm_args) + [vmem] * len(vmem_args),
        out_specs=[hbm] * 2 + [vmem] * 21,
        scratch_shapes=[scratch(item.shape, f32) for item in hbm_args]
        + [
            scratch((3, own_rows, 4 * half), low),
            scratch((class_rows, width), low),
            scratch((n, n, 128), f32),
            scratch((n, n, 128), f32),
            scratch((n, 3 * width), f32),
            scratch((n, 1, 3 * width), f32),
            scratch((n, 1, 3 * width), f32),
            scratch((line, 2, 2, own_rows, 4 * half), low),
            scratch((width, 4 * half), low),
            scratch((2 * rows, edge + 128), f32),
            scratch(heads, f32),
            scratch(heads, low),
            scratch((2, rows, width), f32),
            scratch((rows, width), f32),
            scratch((2, rows, width), low),
            scratch((2, rows, width), low),
            scratch((n, own_rows, 2 * rows), low),
            scratch((2, own_rows, 4 * half), low),
            scratch((n,) + block.shape, f32),
            scratch((1, 4 * half), f32),
            dma((6,)),
            dma((2,)),
            dma((5,)),
            dma((5,)),
            dma((n,)),
            dma((n,)),
            dma((n,)),
            dma((n,)),
            dma((n,)),
            dma((n,)),
            dma((3,)),
            dma((2,)),
        ]
        + [dma((3, 4, line))] * 7,
        compiler_params=pltpu.CompilerParams(
            collective_id=collective_id, has_side_effects=True, vmem_limit_bytes=63 * 2**20),
        name="forward",
    )(*hbm_args, *vmem_args)


class Reducer:
    def __init__(self, line, grads, out, own, got_b, got_z, got_a, sems):
        self.line, self.grads, self.out = line, grads, out
        self.own, self.acc, self.got_z, self.got_a = own, got_b, got_z, got_a
        self.load, self.send_b, self.send_z, self.send_a, self.recv_b, self.recv_z, self.recv_a = sems
        self.me = me = Place(line)
        self.up, self.down = me.z < line - 1, me.z > 0
        self.above, self.below = me.dev(z=jnp.minimum(me.z + 1, line - 1)), me.dev(z=jnp.maximum(me.z - 1, 0))
        self.units = len(grads) * line

    def last(self, g):
        return "y" if GROUPS[g][3] == "x" else "x"

    def first(self, g):
        return self.me.x if GROUPS[g][3] == "x" else self.me.y

    def half(self, grad, g, zz, mine):
        cols = pl.ds(GROUPS[g][0], GROUPS[g][1])
        if self.last(g) == "y":
            return grad.at[zz, self.me.y if mine else 1 - self.me.y, :, :, cols]
        return grad.at[zz, :, self.me.x if mine else 1 - self.me.x, :, cols]

    def loading(self, u, g, zz, side, grad=None):
        grad = self.grads[0] if grad is None else grad
        return pltpu.make_async_copy(
            self.half(grad, g, zz, True), self.own[g].at[u % 3, side], self.load.at[u % 3, g, side])

    def remote(self, src, dst, send, recv, dev):
        return pltpu.make_async_remote_copy(
            src_ref=src, dst_ref=dst, send_sem=send, recv_sem=recv, device_id=dev, device_id_type=MESH)

    def b_copy(self, m, g, zz, grad=None):
        grad = self.grads[0] if grad is None else grad
        return self.remote(
            self.half(grad, g, zz, False), self.acc[g].at[m, zz], self.send_b.at[m, g, zz], self.recv_b.at[m, g, zz],
            self.me.peer(self.last(g)))

    def slot_a(self, g, zz):
        return zz if GROUPS[g][2] == 1 else 0

    def a_copy(self, m, g, zz):
        return self.remote(
            self.acc[g].at[m, zz, 1 - self.first(g)], self.got_a[g].at[m, self.slot_a(g, zz)], self.send_a.at[m, g, zz],
            self.recv_a.at[m, g, zz], self.me.peer(GROUPS[g][3]))

    def z_copy(self, m, g, zz, slot, dev):
        part = self.acc[g].at[m, zz] if GROUPS[g][2] == 0 else self.acc[g].at[m, zz, self.first(g)]
        return self.remote(part, self.got_z[g].at[m, slot], self.send_z.at[m, g, zz], self.recv_z.at[m, g, slot], dev)

    def add_b(self, m, g, zz, u, side):
        self.loading(u, g, zz, side).wait()
        self.b_copy(m, g, zz).wait_recv()
        self.acc[g][m, zz] = self.acc[g][m, zz] + self.own[g][u % 3, side]

    def add_z(self, m, g, zz, slot):
        acc, got = self.acc[g], self.got_z[g]
        self.z_copy(m, g, self.me.z, slot, self.below).wait_recv()
        if GROUPS[g][2] == 0:
            acc[m, zz] = acc[m, zz] + got[m, slot]
        else:
            acc[m, zz, self.first(g)] = acc[m, zz, self.first(g)] + got[m, slot]

    def add_a(self, m, g, zz):
        self.a_copy(m, g, zz).wait_recv()
        acc, first = self.acc[g], self.first(g)
        acc[m, zz, first] = acc[m, zz, first] + self.got_a[g][m, self.slot_a(g, zz)]

    def planes(self, k, fn):
        z, line = self.me.z, self.line
        when(z + k < line, lambda: fn(jnp.minimum(z + k, line - 1), True))
        when((z >= k) & (k > 0), lambda: fn(jnp.maximum(z - k, 0), False))

    def begin(self, v):
        m, j = v // self.line, v % self.line

        def one(grad, zz, upward):
            for g in range(4):
                self.b_copy(m, g, zz, grad).start()
                self.loading(v, g, zz, 0 if upward else 1, grad).start()

        for index, grad in enumerate(self.grads):
            when(m == index, lambda: self.planes(self.line - 1 - j, lambda zz, upward: one(grad, zz, upward)))

    def onward(self, m, g, zz, k, upward):
        if upward:
            when(self.down, lambda: self.add_z(m, g, zz, zz))
            self.z_copy(m, g, zz, zz, self.above).start()
        else:
            when(self.up, lambda: self.add_z(m, g, zz, zz))
            self.z_copy(m, g, zz, jnp.where(k == 1, self.line, zz), self.below).start()

    def near(self, u, m, j):
        k = self.line - 1 - j

        def one(zz, upward):
            for g in range(4):
                self.add_b(m, g, zz, u, 0 if upward else 1)
                if GROUPS[g][2] == 1:
                    self.a_copy(m, g, zz).start()
                else:
                    when(k > 0, lambda g=g: self.onward(m, g, zz, k, upward))

        self.planes(k, one)

    def far(self, m, j):
        k = self.line - j

        def one(zz, upward):
            for g in (2, 3):
                self.add_a(m, g, zz)
                self.onward(m, g, zz, k, upward)

        when((k > 0) & (k < self.line), lambda: self.planes(k, one))

    def close(self, m):
        z = self.me.z
        for g in (0, 1):
            when(self.down, lambda g=g: self.add_z(m, g, z, z))
            when(self.up, lambda g=g: self.add_z(m, g, z, self.line))
            self.a_copy(m, g, z).start()

    def final(self, m):
        z = self.me.z
        for g in range(4):
            cols = pl.ds(GROUPS[g][0], GROUPS[g][1])
            self.add_a(m, g, z)
            if GROUPS[g][2] == 1:
                when(self.down, lambda g=g: self.add_z(m, g, z, z))
                when(self.up, lambda g=g: self.add_z(m, g, z, self.line))
            self.out[m, :, cols] = self.acc[g][m, z, self.first(g)]

    def unit(self, u):
        line = self.line
        m, j = u // line, u % line
        self.near(u, m, j)
        self.far(m, j)
        when(j == line - 1, lambda: self.close(m))
        when((j == 0) & (m > 0), lambda: self.final(jnp.maximum(m - 1, 0)))

    def drain(self):
        z = self.me.z

        @pl.loop(0, len(self.grads))
        def _(m):
            @pl.loop(0, self.line)
            def _(zz):
                for g in range(4):
                    self.b_copy(m, g, zz).wait_send()
                    if GROUPS[g][2] == 1:
                        self.a_copy(m, g, zz).wait_send()
                    when(zz != z, lambda g=g: self.z_copy(m, g, zz, zz, self.above).wait_send())
            for g in (0, 1):
                self.a_copy(m, g, z).wait_send()


def reducer_scratch(count, line, rows, dt):
    dma = pltpu.SemaphoreType.DMA
    own = [pltpu.VMEM((3, 2, 2, rows, GROUPS[g][1]), dt) for g in range(4)]
    got_b = [pltpu.VMEM((count, line, 2, rows, GROUPS[g][1]), dt) for g in range(4)]
    got_z = [pltpu.VMEM((count, line + 1) + ((2,) if GROUPS[g][2] == 0 else ()) + (rows, GROUPS[g][1]), dt) for g in range(4)]
    got_a = [pltpu.VMEM((count, line if GROUPS[g][2] == 1 else 1, rows, GROUPS[g][1]), dt) for g in range(4)]
    sems = [dma((3, 4, 2))] + [dma((count, 4, line))] * 4 + [dma((count, 4, line + 1))] + [dma((count, 4, line))]
    return own + got_b + got_z + got_a + sems


def make_reducer(line, grads, out, refs):
    return Reducer(line, grads, out, refs[:4], refs[4:8], refs[8:12], refs[12:16], refs[16:])


def backward_kernel(line, *refs):
    (weights, g_contract, h1_t, h2_t, act, slope, d_branch, q, k, v, o, key_ok, x, middle, attended, cot, row_ok, pieces,
     b_contract, modulation, cond, silu, same) = refs[:23]
    (g_expand, g_attn, d_mod_all, cond_all, both, block_out, tokens_grad, bias_all, norm_out, factor_out) = refs[23:33]
    (w, rhs, d_o, d_q, d_k, d_v, d_h, d_h_got, branch_got, d_mid, d_att, d_att_t, stage, dp, dp_got, msg, msg_got, d_mod, vec,
     vec_got, d_silu, d_silu_got, chunk, out, bias_sum, d_cond, squares, squares_got, table_squares, squares_pair, cond_some, w_sem,
     mod_sem, stage_sem, pair_send, pair_recv, msg_send, msg_recv, vec_send, vec_recv, cond_send, cond_recv, bias_send, bias_recv, square_send,
     square_recv) = refs[33:79]
    n = line * 4
    low, f32 = jnp.bfloat16, jnp.float32
    me, c = lax.axis_index("dp"), lax.axis_index("seq")
    red = make_reducer(line, (g_contract, g_expand, g_attn), out, refs[79:])
    rows, width = x.shape
    half = weights.shape[2] // 4
    heads = half // HEAD_DIM
    edge = 3 * half // 128 * 128
    tiles = width // 128
    d_z = rhs.at[2 * rows :]

    def swap(i, src, dst):
        return pltpu.make_async_remote_copy(
            src_ref=src, dst_ref=dst, send_sem=pair_send.at[i], recv_sem=pair_recv.at[i], device_id=(me, 1 - c),
            device_id_type=MESH)

    def fetch(i):
        return pltpu.make_async_copy(weights.at[(2, 1, 0, 2)[i]], w, w_sem.at[i])

    def back(values, lanes):
        @pl.loop(0, tiles)
        def _(t):
            cols = pl.ds(pl.multiple_of(t * 128, 128), 128)
            part = dot(values[...], w[cols, :lanes], 1, 1)
            d_h[0, :, cols] = part[:rows]
            d_h[1, :, cols] = part[rows:]

    def column_sums(values):
        return jnp.sum(values.astype(f32), axis=0, keepdims=True)

    def norm_back(values, scale, d_n):
        centre = values - jnp.mean(values, axis=-1, keepdims=True)
        inv = lax.rsqrt(jnp.mean(centre * centre, axis=-1, keepdims=True) + LAYER_EPS)
        normed = centre * inv
        e = d_n * (1.0 + scale)
        d_x = (e - jnp.mean(e, axis=-1, keepdims=True) - normed * jnp.mean(e * normed, axis=-1, keepdims=True)) * inv
        return d_x, jnp.sum(d_n, axis=0, keepdims=True), jnp.sum(d_n * normed, axis=0, keepdims=True)

    def piece(i):
        return pieces[i // 3, :, i % 3 * width : (i % 3 + 1) * width]

    fetch(0).start()
    bar = greet_all(n)
    for item in (d_q, d_k, d_v):
        item[...] = jnp.zeros_like(item)
    dp[...] = jnp.zeros_like(dp)
    vec[...] = jnp.zeros_like(vec)
    vec[4:5] = column_sums(d_branch[0]) + column_sums(d_branch[1])
    pl.semaphore_wait(bar, n)

    def hidden_grad():
        fetch(0).wait()
        d_out = jnp.concatenate([d_branch[0], d_branch[1]], axis=0)

        @pl.loop(0, act.shape[1] // 256)
        def _(t):
            cols = pl.ds(pl.multiple_of(t * 256, 256), 256)
            d_z[:, cols] = (dot(d_out, w[:, cols]) * slope[:, cols]).astype(low)

        fetch(1).start()

    def expand_grads():
        write_blocks(n, g_expand, stage, stage_sem, lambda i: dot(h2_t[i], d_z[...]))
        sums = column_sums(d_z[...])
        vec[1:2] = sums[:, :width]
        vec[2:3] = sums[:, width:]

    def hidden_back():
        fetch(1).wait()
        back(d_z, 4 * half)
        swap(0, d_h.at[1 - c], d_h_got).start()
        fetch(2).start()

    def middle_back():
        swap(0, d_h.at[1 - c], d_h_got).wait()
        d_x, shift, scale = norm_back(middle[...], piece(4), d_h[c] + d_h_got[...])
        d_mid[...] = d_x + cot[...].astype(f32) * row_ok[...]
        dp[2:3] = jnp.sum(d_mid[...] * attended[...], axis=0, keepdims=True)
        dp[3:4] = shift
        dp[4:5] = scale
        d_att[c] = (piece(2) * d_mid[...]).astype(low)
        swap(1, d_att.at[c], d_att.at[c]).start()

    def mixed_back():
        swap(1, d_att.at[c], d_att.at[c]).wait()
        d_all = jnp.concatenate([d_att[0], d_att[1]], axis=0)
        to_blocks(d_all, d_att_t)
        vec[3:4] = column_sums(d_att[0]) + column_sums(d_att[1])
        fetch(2).wait()
        d_o[:, :half] = dot(d_all, w[:, edge:])[:, 3 * half - edge :].astype(low)
        d_o[:, half:] = jnp.zeros((2 * rows, d_o.shape[1] - half), low)

    seen = jnp.broadcast_to(key_ok[...], (2 * rows, 2 * rows)) > 0.0

    def head(h):
        win, lanes = head_window(h)
        qh, kh, doh = q[:, win] * lanes, k[:, win] * lanes, d_o[:, win] * lanes
        probs = head_probs(qh, kh, seen)
        d_probs = dot(doh, v[:, win], 1, 1)
        inner = jnp.sum(probs * d_probs, axis=-1, keepdims=True)
        d_logits = (probs * (d_probs - inner)).astype(low)
        d_q[:, win] = d_q[:, win] + dot(d_logits, kh) * HEAD_DIM ** (-0.5)
        d_k[:, win] = d_k[:, win] + dot(d_logits, qh, 0, 0) * HEAD_DIM ** (-0.5)
        d_v[:, win] = d_v[:, win] + dot(probs.astype(low), doh, 0, 0)

    def attention_grads():
        for i, item in enumerate((d_q, d_k, d_v)):
            rhs[: 2 * rows, i * half : (i + 1) * half] = item[:, :half].astype(low)
        rhs[: 2 * rows, 3 * half :] = jnp.zeros((2 * rows, half), low)
        rhs[2 * rows :, edge : 3 * half] = jnp.zeros((2 * rows, 3 * half - edge), low)
        rhs[2 * rows :, 3 * half :] = o[:, :half]
        sums = column_sums(rhs[: 2 * rows, : 3 * half])
        vec[0:1, :half] = sums[:, :half]
        vec[0:1, half:] = sums[:, 2 * half :]

        def block(i):
            left = dot(h1_t[i], rhs[: 2 * rows, :edge])
            right = dot(h1_t[i], rhs[: 2 * rows, edge:]) + dot(d_att_t[i], rhs[2 * rows :, edge:])
            return jnp.concatenate([left, right], axis=1)

        write_blocks(n, g_attn, stage, stage_sem, block)

    def input_back():
        back(rhs.at[: 2 * rows, : edge + 128], edge + 128)
        swap(2, d_h.at[1 - c], d_h_got).start()
        fetch(3).start()

    def first_back():
        swap(2, d_h.at[1 - c], d_h_got).wait()
        d_x, shift, scale = norm_back(x[...], piece(1), d_h[c] + d_h_got[...])
        tokens_grad[...] = (d_x + d_mid[...]).astype(low)
        dp[0:1] = shift
        dp[1:2] = scale
        fetch(3).wait()
        back(act, 4 * half)
        swap(3, d_h.at[1 - c], branch_got).start()

    def branch_out():
        swap(3, d_h.at[1 - c], branch_got).wait()
        branch = d_h[c] + branch_got[...] + b_contract[...]
        result = middle[...] + piece(5) * branch
        block_out[...] = jnp.where(jnp.broadcast_to(row_ok[...], result.shape) > 0.0, result, 0.0).astype(low)
        dp[5:6] = jnp.sum(cot[...].astype(f32) * row_ok[...] * branch, axis=0, keepdims=True)
        swap(4, dp, dp_got).start()

    msg_start, msg_wait = all_peers(n, msg, msg_got, msg_send, msg_recv, False)
    vec_start, vec_wait = all_peers(n, chunk, vec_got, vec_send, vec_recv, True)
    per = chunk_tiles(n, width)

    def send_mod():
        swap(4, dp, dp_got).wait()
        total = (dp[...] + dp_got[...]).astype(low).astype(f32)
        own = jnp.where(c == 0, total[0:3], total[3:6])
        for r in range(3):
            msg[r] = own[r : r + 1]
        msg_got[me] = msg[...]
        chunk[...] = jnp.zeros_like(chunk)
        for t in range(5 * tiles):
            chunk[t // per, t % per] = vec[t // tiles : t // tiles + 1, t % tiles * 128 : t % tiles * 128 + 128]
        vec_got[me] = chunk[me]
        msg_start()
        vec_start()

    keep_mod = pltpu.make_async_copy(d_mod, d_mod_all.at[c], mod_sem.at[0])
    keep_cond = pltpu.make_async_copy(d_cond, cond_all.at[me], mod_sem.at[2])

    def mod_grad():
        msg_wait()
        vec_wait()

        @pl.loop(0, n)
        def _(s):
            for r in range(3):
                d_mod[pl.ds(s, 1), r * width : (r + 1) * width] = msg_got[s, r]

        bias_sum[c] = jnp.zeros((8, 128), f32)
        for r in range(per):
            bias_sum[c, r : r + 1] = jnp.sum(vec_got[:, r], axis=0)
        d_silu[...] = dot(d_mod[...].astype(low), modulation[...], 1, 1)
        swap(5, d_silu, d_silu_got).start()
        swap(6, d_mod, d_mod_all.at[c]).start()
        swap(7, bias_sum.at[c], bias_sum.at[c]).start()
        keep_mod.start()

    cond_start, cond_wait = all_peers(n, d_cond, cond_all, cond_send, cond_recv, False)
    bias_start, bias_wait = all_peers(n, bias_sum, bias_all, bias_send, bias_recv, False)
    square_start, square_wait = all_peers(n, squares, squares_got, square_send, square_recv, False)

    def cond_grad():
        swap(5, d_silu, d_silu_got).wait()
        swap(6, d_mod, d_mod_all.at[c]).wait()
        swap(7, bias_sum.at[c], bias_sum.at[c]).wait()
        keep_mod.wait()
        gate = 1.0 / (1.0 + jnp.exp(-cond[...]))
        d_cond[...] = (d_silu[...] + d_silu_got[...]) * (gate + cond[...] * gate * (1.0 - gate))
        keep_cond.start()
        bias_all[me] = bias_sum[...]
        cond_start()
        bias_start()
        d_low = d_mod[...].astype(low)
        grad = dot(silu[...], d_low, 0, 0)[: out.shape[1]]
        sums = jnp.sum(d_mod[...], axis=0, keepdims=True)
        tile = per * me + lax.broadcasted_iota(jnp.int32, (8, 128), 0)
        counted = (tile < 3 * tiles) | (c == 0)
        total = jnp.sum(grad * grad) + jnp.where(me == 0, jnp.sum(sums * sums), 0.0)
        total = total + jnp.sum(jnp.where(counted, bias_sum[c] * bias_sum[c], 0.0))
        squares[...] = jnp.full((8, 128), total, f32)

    def table_norm():
        cond_wait()
        bias_wait()
        keep_cond.wait()
        table_squares[...] = jnp.zeros((8, 128), f32)
        size = cond_some.shape[0]

        @pl.loop(0, n // size)
        def _(j):
            some = pltpu.make_async_copy(cond_all.at[pl.ds(j * size, size)], cond_some, mod_sem.at[1])
            some.start()
            some.wait()
            gram = jnp.zeros((n, n), f32)
            for i in range(size):
                part = cond_some[i]
                gram = gram + lax.dot_general(
                    part, part, (((1,), (1,)), ((), ())), preferred_element_type=f32, precision=lax.Precision.HIGHEST)
            table_squares[...] = table_squares[...] + jnp.sum(gram * same[...])

    def reduced(m):
        value = out[m].astype(f32)
        squares[...] = squares[...] + jnp.sum(value * value)
        both[c, m] = out[m]
        swap(8 + m, out.at[m], both.at[c, m]).start()

    parts = (hidden_grad, expand_grads, hidden_back, middle_back, mixed_back) + (None,) * heads
    parts += (attention_grads, input_back, first_back, branch_out, send_mod, mod_grad, cond_grad, table_norm)
    first_head = parts.index(None)
    begun, carried = ([places[u // line * 4 + u % line * 4 // line] for u in range(red.units)] for places in UNIT_PLACES)

    def upto(places, s):
        total = jnp.int32(0)
        for place in places:
            total = total + (place <= s).astype(jnp.int32)
        return total

    @pl.loop(0, len(parts) + 1)
    def _(s):
        @pl.loop(upto(begun, s - 1), upto(begun, s))
        def _(v):
            red.begin(v)

        @pl.loop(upto(carried, s - 1), upto(carried, s))
        def _(u):
            red.unit(u)

        when((s >= first_head) & (s < first_head + heads), lambda: head(s - first_head))
        for i, part in enumerate(parts):
            if part is not None:
                when(s == i, part)

    reduced(0)
    reduced(1)
    red.final(2)
    reduced(2)
    squares_got[me] = squares[...]
    square_start()
    red.drain()
    square_wait()
    squares[...] = jnp.sum(squares_got[...], axis=0)
    swap(11, squares, squares_pair).start()
    for m in range(3):
        swap(8 + m, out.at[m], both.at[c, m]).wait()
    swap(11, squares, squares_pair).wait()
    norm = jnp.sqrt(squares[...] + squares_pair[...] + table_squares[...])
    norm_out[...] = norm
    factor_out[...] = jnp.minimum(1.0, CLIP_LIMIT / (norm + 1e-06))


def chunk_tiles(n, width):
    return -(-5 * (width // 128) // n)


def backward(hbm_args, vmem_args, n, collective_id):
    line = n // 4
    grad = hbm_args[1]
    rows, cols = grad.shape[-2:]
    two, own, width = vmem_args[4].shape
    all_rows = two * own
    heads = vmem_args[5].shape
    low, f32 = jnp.bfloat16, jnp.float32
    dma = pltpu.SemaphoreType.DMA
    vmem, hbm = pl.BlockSpec(memory_space=pltpu.VMEM), pl.BlockSpec(memory_space=pltpu.HBM)
    per = chunk_tiles(n, width)
    return pl.pallas_call(
        functools.partial(backward_kernel, line),
        out_shape=[
            jax.ShapeDtypeStruct(grad.shape, low),
            jax.ShapeDtypeStruct(grad.shape, low),
            jax.ShapeDtypeStruct((2, n, 3 * width), f32),
            jax.ShapeDtypeStruct((n, n, 128), f32),
            jax.ShapeDtypeStruct((2, 3, rows, cols), low),
            jax.ShapeDtypeStruct((own, width), low),
            jax.ShapeDtypeStruct((own, width), low),
            jax.ShapeDtypeStruct((n, 2, 8, 128), f32),
            jax.ShapeDtypeStruct((8, 128), f32),
            jax.ShapeDtypeStruct((8, 128), f32),
        ],
        in_specs=[hbm] * len(hbm_args) + [vmem] * len(vmem_args),
        out_specs=[hbm] * 4 + [vmem] * 6,
        scratch_shapes=[
            pltpu.VMEM((width, cols), low),
            pltpu.VMEM((2 * all_rows, cols), low),
            pltpu.VMEM(heads, low),
            pltpu.VMEM(heads, f32),
            pltpu.VMEM(heads, f32),
            pltpu.VMEM(heads, f32),
            pltpu.VMEM((2, own, width), f32),
            pltpu.VMEM((own, width), f32),
            pltpu.VMEM((own, width), f32),
            pltpu.VMEM((own, width), f32),
            pltpu.VMEM((2, own, width), low),
            pltpu.VMEM((n, rows, all_rows), low),
            pltpu.VMEM((2, rows, cols), low),
            pltpu.VMEM((8, width), f32),
            pltpu.VMEM((8, width), f32),
            pltpu.VMEM((3, 1, width), f32),
            pltpu.VMEM((n, 3, 1, width), f32),
            pltpu.VMEM((n, 3 * width), f32),
            pltpu.VMEM((8, width), f32),
            pltpu.VMEM((n, per, 1, 128), f32),
            pltpu.VMEM((n, 128), f32),
            pltpu.VMEM((n, 128), f32),
            pltpu.VMEM((n, per, 1, 128), f32),
            pltpu.VMEM((3, rows, cols), low),
            pltpu.VMEM((2, 8, 128), f32),
            pltpu.VMEM((n, 128), f32),
            pltpu.VMEM((8, 128), f32),
            pltpu.VMEM((n, 8, 128), f32),
            pltpu.VMEM((8, 128), f32),
            pltpu.VMEM((8, 128), f32),
            pltpu.VMEM((min(n, 16), n, 128), f32),
            dma((4,)),
            dma((3,)),
            dma((2,)),
            dma((12,)),
            dma((12,)),
        ]
        + [dma((n,))] * 10
        + reducer_scratch(3, line, rows, low),
        compiler_params=pltpu.CompilerParams(
            collective_id=collective_id, has_side_effects=True, vmem_limit_bytes=63 * 2**20),
        name="backward",
    )(*hbm_args, *vmem_args)


def adam_step(grad, master, first, second, rate):
    first_new = BETA_FIRST * first + (1.0 - BETA_FIRST) * grad
    second_new = BETA_SECOND * second + (1.0 - BETA_SECOND) * grad * grad
    first_hat = first_new / (1.0 - BETA_FIRST**STEP)
    second_hat = second_new / (1.0 - BETA_SECOND**STEP)
    master_new = master - rate * (
        first_hat / (jnp.sqrt(second_hat) + ADAM_EPS) + WEIGHT_DECAY * master
    )
    return (first_new, second_new, master_new)


def chunk_rows(rows):
    sizes = [d for d in range(8, 257, 8) if rows % d == 0]
    return sizes[-1] if sizes else rows


def adam_kernel(n, rates, *refs):
    kinds = len(rates)
    factor_ref, both, silu, d_mod, cond_all, onehot = refs[:6]
    at = 6
    states = [refs[at + 3 * a : at + 3 * a + 3] for a in range(kinds)]
    at += 3 * kinds
    news = [refs[at + 3 * a : at + 3 * a + 3] for a in range(kinds)]
    at += 3 * kinds
    held, flat = refs[at : at + kinds], refs[at + kinds : at + 2 * kinds]
    wide, in_sem, out_sem = refs[at + 2 * kinds :]
    rows, half = both.shape[2:]
    head = half // 4
    order = (3, 4, 0, 1, 2, 5)

    def loads(a):
        return [pltpu.make_async_copy(states[a][k], held[a].at[k], in_sem.at[a, k]) for k in range(3)]

    for a in order:
        for copy in loads(a):
            copy.start()

    def spread(a, width, count=rows):
        tiles = width // 128
        for t in range(tiles):
            flat[a][pl.ds(t, count, stride=tiles), :] = wide[:count, 128 * t : 128 * t + 128]

    def gradient(a):
        if a == 0:
            part = d_mod.shape[2]
            for core in range(2):
                grad = dot(silu[...], d_mod[core].astype(silu.dtype), 0, 0)
                wide[:, core * part : (core + 1) * part] = grad[:rows]
            spread(a, 2 * part)
        elif a == 1:
            for core in range(2):
                for part in range(3):
                    lo = (2 * part + core) * head
                    wide[:, lo : lo + head] = both[core, 2, :, part * head : (part + 1) * head].astype(jnp.float32)
            spread(a, 6 * head)
        elif a == 2:
            for core in range(2):
                wide[:, core * head : (core + 1) * head] = both[core, 2, :, 3 * head :].astype(jnp.float32)
            spread(a, 2 * head)
        elif a == 5:
            count = onehot.shape[1]
            for i in range(n):
                wide[:count, i * rows : (i + 1) * rows] = lax.dot_general(
                    onehot[...], cond_all[i], (((0,), (0,)), ((), ())), preferred_element_type=jnp.float32,
                    precision=lax.Precision.HIGHEST)[:, :rows]
            spread(a, n * rows, count)
        else:
            for core in range(2):
                wide[:, core * half : (core + 1) * half] = both[core, 4 - a].astype(jnp.float32)
            spread(a, 2 * half)

    factor = factor_ref[:1, :]
    for a in order:
        gradient(a)
        for copy in loads(a):
            copy.wait()
        size = chunk_rows(flat[a].shape[0])

        @pl.loop(0, flat[a].shape[0] // size)
        def _(i, a=a, size=size):
            part = pl.ds(pl.multiple_of(i * size, size), size)
            grad = flat[a][part] * factor
            master, first, second = held[a][0, part], held[a][1, part], held[a][2, part]
            first, second, master = adam_step(grad, master, first, second, rates[a])
            held[a][0, part], held[a][1, part], held[a][2, part] = master, first, second
            for k in range(3):
                pltpu.make_async_copy(held[a].at[k, part], news[a][k].at[part], out_sem.at[a, k]).start()

    for a in range(kinds):
        for k in range(3):
            pltpu.make_async_copy(held[a].at[k], news[a][k], out_sem.at[a, k]).wait()


def adam(factor, both, silu, d_mod, cond_all, onehot, states, rates, n):
    vmem, hbm = pl.BlockSpec(memory_space=pltpu.VMEM), pl.BlockSpec(memory_space=pltpu.HBM)
    dma = pltpu.SemaphoreType.DMA
    kinds = len(states)
    flats = [jax.ShapeDtypeStruct(s[0].shape, jnp.float32) for s in states]
    news = pl.pallas_call(
        functools.partial(adam_kernel, n, rates),
        out_shape=[f for f in flats for _ in range(3)],
        in_specs=[vmem] * 6 + [hbm] * (3 * kinds),
        out_specs=[hbm] * (3 * kinds),
        scratch_shapes=[pltpu.VMEM((3,) + f.shape, jnp.float32) for f in flats]
        + [pltpu.VMEM(f.shape, jnp.float32) for f in flats]
        + [pltpu.VMEM((both.shape[2], 2 * d_mod.shape[2]), jnp.float32), dma((kinds, 3)), dma((kinds, 3))],
        compiler_params=pltpu.CompilerParams(vmem_limit_bytes=56 * 2**20),
        name="adam",
    )(factor, both, silu, d_mod, cond_all, onehot, *[item for s in states for item in s])
    order = [3 * a + k for a in range(kinds) for k in (1, 2, 0)]
    return [news[i] for i in order]


def per_device(
    tokens,
    cotangent,
    time_vec,
    labels,
    kept,
    keep_index,
    modulation_master,
    modulation_first,
    modulation_second,
    attention_in_master,
    attention_in_first,
    attention_in_second,
    attention_out_master,
    attention_out_first,
    attention_out_second,
    expand_master,
    expand_first,
    expand_second,
    contract_master,
    contract_first,
    contract_second,
    class_table_master,
    class_table_first,
    class_table_second,
    biases_master,
    biases_first,
    biases_second,
):
    rows, width = tokens.shape[1:]
    n, pairs = lax.axis_size("dp"), lax.axis_size("seq")
    me = lax.axis_index("dp")
    half_width = width // pairs
    low = jnp.bfloat16

    bias_share = biases_master.shape[0]
    bias_block = jnp.pad(biases_master.astype(low).astype(jnp.float32), (0, 1024 - bias_share)).reshape(8, 128)
    label_block = jnp.broadcast_to(labels.astype(jnp.float32)[:, None], (8, 128))
    place = keep_index[0]
    cells = jnp.stack([place // SIDE, place % SIDE], axis=1).astype(jnp.float32)
    quarter = width // 4
    freqs = 10000.0 ** (-jnp.arange(quarter).astype(jnp.float32) / quarter)
    (weights, grad_contract, normed_in, normed_mid, queries, keys, values, mixed, attended, middle, activated, slope, d_branch,
     pieces, cond_own, silu_own, own_modulation, inputs, key_ok, row_ok, onehot, same, biases) = forward(
        [
            item.reshape(-1, 128)
            for item in (
                attention_in_master,
                attention_out_master,
                expand_master,
                contract_master,
                class_table_master,
                modulation_master,
            )
        ],
        [
            jnp.concatenate([bias_block, label_block]),
            time_vec,
            tokens[0],
            cells,
            freqs[None],
            kept.astype(jnp.float32)[None],
            cotangent[0],
        ],
        bias_share * n,
        n,
        1,
    )
    _, _, d_mod_all, cond_all, reduced, block_out, tokens_grad, bias_parts, norm, clip = backward(
        [weights.reshape(3, width, 4 * half_width), grad_contract],
        [
            normed_in,
            normed_mid,
            activated,
            slope,
            d_branch,
            queries,
            keys,
            values,
            mixed,
            key_ok,
            inputs,
            middle,
            attended,
            cotangent[0],
            row_ok,
            pieces,
            biases[:, 9 * width + FF :],
            own_modulation,
            cond_own,
            silu_own,
            same,
        ],
        n,
        2,
    )
    block_out, tokens_grad, grad_norm = block_out[None], tokens_grad[None], norm[0, 0]
    rates = (
        width ** (-0.5),
        width ** (-0.5),
        (width // 4) ** (-0.5),
        width ** (-0.5),
        FF ** (-0.5),
        0.5,
        0.2,
    )
    masters = (
        modulation_master,
        attention_in_master,
        attention_out_master,
        expand_master,
        contract_master,
        class_table_master,
        biases_master,
    )
    firsts = (
        modulation_first,
        attention_in_first,
        attention_out_first,
        expand_first,
        contract_first,
        class_table_first,
        biases_first,
    )
    seconds = (
        modulation_second,
        attention_in_second,
        attention_out_second,
        expand_second,
        contract_second,
        class_table_second,
        biases_second,
    )
    states = list(zip(masters, firsts, seconds))
    updated = adam(
        clip,
        reduced,
        silu_own,
        d_mod_all,
        cond_all,
        onehot,
        [tuple(item.reshape(-1, 128) for item in state) for state in states[:-1]],
        rates[:-1],
        n,
    )
    bias_parts = bias_parts.reshape(n, pairs, 8, 128)[:, :, : chunk_tiles(n, width)].transpose(1, 0, 2, 3)
    bias_parts = bias_parts.reshape(pairs, -1)[:, : 5 * width].reshape(pairs, 5, width)
    grad_biases = jnp.concatenate(
        [
            jnp.sum(d_mod_all, axis=1).reshape(-1),
            bias_parts[:, 0, :half_width].reshape(-1),
            bias_parts[:, 0, half_width:].reshape(-1),
            bias_parts[0, 3],
            bias_parts[:, 1:3].reshape(-1),
            bias_parts[0, 4],
        ]
    )
    bias_grad = lax.dynamic_slice_in_dim(grad_biases, me * bias_share, bias_share, 0) * clip[0, 0]
    updated = [item.reshape(-1) for item in updated] + list(adam_step(bias_grad, *states[-1], rates[-1]))
    return (block_out, tokens_grad, grad_norm) + tuple(updated)


def solution(mesh):
    return jax.shard_map(
        per_device,
        mesh=mesh,
        in_specs=(
            P("dp", "seq", None),
            P("dp", "seq", None),
            P("dp", None),
            P("dp"),
            P("dp"),
            P("dp", "seq"),
            P("dp"),
            P("dp"),
            P("dp"),
            P("dp"),
            P("dp"),
            P("dp"),
            P("dp"),
            P("dp"),
            P("dp"),
            P("dp"),
            P("dp"),
            P("dp"),
            P("dp"),
            P("dp"),
            P("dp"),
            P("dp"),
            P("dp"),
            P("dp"),
            P("dp"),
            P("dp"),
            P("dp"),
        ),
        out_specs=(
            P("dp", "seq", None),
            P("dp", "seq", None),
            P(),
            P("dp"),
            P("dp"),
            P("dp"),
            P("dp"),
            P("dp"),
            P("dp"),
            P("dp"),
            P("dp"),
            P("dp"),
            P("dp"),
            P("dp"),
            P("dp"),
            P("dp"),
            P("dp"),
            P("dp"),
            P("dp"),
            P("dp"),
            P("dp"),
            P("dp"),
            P("dp"),
            P("dp"),
        ),
        check_vma=False,
    )
```

```python
import functools
import jax
import jax.numpy as jnp
from jax import lax
from jax.experimental import pallas as pl
from jax.experimental.pallas import tpu as pltpu
from jax.sharding import PartitionSpec as P

HEAD_DIM = 72
FF = 4608
SIDE = 16
CLASSES = 1024
STEP = 10
LAYER_EPS = 1e-06
MASK_FILL = -1e30
BETA_FIRST = 0.5
BETA_SECOND = 0.5
ADAM_EPS = 1e-08
WEIGHT_DECAY = 0.1
CLIP_LIMIT = 1.0

MESH = pl.DeviceIdType.MESH
GELU_A = (2.0 / 3.141592653589793) ** 0.5
GELU_B = 0.044715
UNIT_PLACES = ((0, 0, 2, 10, 12, 13, 13, 15), (1, 3, 11, 12, 13, 14, 15, 18))
GROUPS = ((0, 640, 0, "x"), (640, 640, 0, "y"), (1280, 512, 1, "x"), (1792, 512, 1, "y"))


def when(cond, fn):
    pl.when(cond)(fn)


class Place:
    def __init__(self, line):
        self.line = line
        i = lax.axis_index("dp")
        self.c = lax.axis_index("seq")
        self.x, self.y, self.z = i % 2, (i // 2) % 2, i // 4

    def dev(self, z=None, y=None, x=None):
        z = self.z if z is None else z
        y = self.y if y is None else y
        x = self.x if x is None else x
        return (z * 4 + y * 2 + x, self.c)

    def peer(self, axis):
        return self.dev(x=1 - self.x) if axis == "x" else self.dev(y=1 - self.y)

    def barrier(self):
        bar = pltpu.get_barrier_semaphore()

        def sig(dev):
            pl.semaphore_signal(bar, inc=1, device_id=dev, device_id_type=MESH)

        sig(self.peer("x"))
        sig(self.peer("y"))
        when(self.z > 0, lambda: sig(self.dev(z=self.z - 1)))
        when(self.z < self.line - 1, lambda: sig(self.dev(z=self.z + 1)))
        pl.semaphore_wait(bar, 2 + (self.z > 0).astype(jnp.int32) + (self.z < self.line - 1).astype(jnp.int32))


class Gatherer:
    def __init__(self, line, own, out, keep_sem, sems):
        self.line, self.own, self.out, self.keep_sem = line, own, out, keep_sem
        self.send_a, self.send_z, self.send_b, self.recv_a, self.recv_z, self.recv_b = sems
        self.me = Place(line)
        self.up, self.down = self.me.z < line - 1, self.me.z > 0

    def single(self, m, g, zz):
        lo, width = GROUPS[g][:2]
        return self.out.at[m, zz, self.me.y, self.me.x, :, pl.ds(lo, width)]

    def pair(self, m, g, zz):
        lo, width, _, first = GROUPS[g]
        if first == "x":
            return self.out.at[m, zz, self.me.y, :, :, pl.ds(lo, width)]
        return self.out.at[m, zz, :, self.me.x, :, pl.ds(lo, width)]

    def remote(self, ref, send, recv, dev, source):
        return pltpu.make_async_remote_copy(
            src_ref=ref if source is None else source, dst_ref=ref, send_sem=send, recv_sem=recv,
            device_id=dev, device_id_type=MESH)

    def source(self, m, g):
        lo, width = GROUPS[g][:2]
        return self.own.at[m, :, pl.ds(lo, width)]

    def a_copy(self, m, g, zz, source=None):
        return self.remote(
            self.single(m, g, zz), self.send_a.at[m, g, zz], self.recv_a.at[m, g, zz], self.me.peer(GROUPS[g][3]), source)

    def z_ref(self, m, g, zz):
        return self.pair(m, g, zz) if GROUPS[g][2] == 0 else self.single(m, g, zz)

    def u_copy(self, m, g, zz, source=None):
        dev = self.me.dev(z=jnp.minimum(self.me.z + 1, self.line - 1))
        return self.remote(self.z_ref(m, g, zz), self.send_z.at[m, g, zz], self.recv_z.at[m, g, zz], dev, source)

    def d_copy(self, m, g, zz, source=None):
        dev = self.me.dev(z=jnp.maximum(self.me.z - 1, 0))
        sem = self.send_z.at[m, g, jnp.where(zz == self.me.z, self.line, zz)]
        return self.remote(self.z_ref(m, g, zz), sem, self.recv_z.at[m, g, zz], dev, source)

    def b_copy(self, m, g, zz):
        last = "y" if GROUPS[g][3] == "x" else "x"
        return self.remote(self.pair(m, g, zz), self.send_b.at[m, g, zz], self.recv_b.at[m, g, zz], self.me.peer(last), None)

    def keep(self, m):
        me = self.me
        return pltpu.make_async_copy(self.own.at[m], self.out.at[m, me.z, me.y, me.x], self.keep_sem.at[m])

    def begin(self, m):
        z = self.me.z
        self.keep(m).start()
        for g in range(4):
            self.a_copy(m, g, z, self.source(m, g)).start()
        for g in (2, 3):
            when(self.up, lambda g=g: self.u_copy(m, g, z, self.source(m, g)).start())
            when(self.down, lambda g=g: self.d_copy(m, g, z, self.source(m, g)).start())

    def paired(self, m):
        z = self.me.z
        self.keep(m).wait()
        for g in (0, 1):
            self.a_copy(m, g, z).wait_recv()
            when(self.up, lambda g=g: self.u_copy(m, g, z).start())
            when(self.down, lambda g=g: self.d_copy(m, g, z).start())
            self.b_copy(m, g, z).start()

    def arrive(self, m, zz, upward):
        for g in range(4):
            copy = self.u_copy if upward else self.d_copy
            copy(m, g, zz).wait_recv()
            when(self.up if upward else self.down, lambda g=g: copy(m, g, zz).start())
            if GROUPS[g][2] == 0:
                self.b_copy(m, g, zz).start()
            else:
                self.a_copy(m, g, zz).start()

    def crossed(self, m, zz):
        for g in (2, 3):
            self.a_copy(m, g, zz).wait_recv()
            self.b_copy(m, g, zz).start()

    def step(self, m, k):
        z, line = self.me.z, self.line
        when(k <= z, lambda: self.arrive(m, jnp.maximum(z - k, 0), True))
        when(z + k < line, lambda: self.arrive(m, jnp.minimum(z + k, line - 1), False))
        when(k - 1 <= z, lambda: self.crossed(m, jnp.maximum(z - k + 1, 0)))
        when((k > 1) & (z + k - 1 < line), lambda: self.crossed(m, jnp.minimum(z + k - 1, line - 1)))

    def steps(self, m, first, last):
        @pl.loop(first, last + 1)
        def _(k):
            self.step(m, k)

    def complete(self, m):
        @pl.loop(0, self.line)
        def _(zz):
            for g in range(4):
                self.b_copy(m, g, zz).wait_recv()

    def drain(self, m):
        z = self.me.z

        @pl.loop(0, self.line)
        def _(zz):
            for g in range(4):
                self.b_copy(m, g, zz).wait_send()
                if GROUPS[g][2] == 1:
                    self.a_copy(m, g, zz).wait_send()
                when(self.up & (zz <= z), lambda g=g: self.u_copy(m, g, zz).wait_send())
                when(self.down & (zz >= z), lambda g=g: self.d_copy(m, g, zz).wait_send())

        for g in (0, 1):
            self.a_copy(m, g, z).wait_send()


def dot(left, right, a=1, b=0):
    return lax.dot_general(left, right, (((a,), (b,)), ((), ())), preferred_element_type=jnp.float32)


def normal(values):
    centre = values - jnp.mean(values, axis=-1, keepdims=True)
    return centre * lax.rsqrt(jnp.mean(centre * centre, axis=-1, keepdims=True) + LAYER_EPS)


def all_peers(n, src, dst, send, recv, spread):
    me, c = lax.axis_index("dp"), lax.axis_index("seq")

    def copy(j, there, slot):
        return pltpu.make_async_remote_copy(
            src_ref=src.at[there] if spread else src, dst_ref=dst.at[slot], send_sem=send.at[j], recv_sem=recv.at[slot],
            device_id=(there, c), device_id_type=MESH)

    def start():
        @pl.loop(1, n)
        def _(j):
            copy(j, (me + j) % n, me).start()

    def wait():
        @pl.loop(1, n)
        def _(j):
            copy(j, (me + j) % n, (me + n - j) % n).wait()

    return start, wait


def greet_all(n):
    me, c = lax.axis_index("dp"), lax.axis_index("seq")
    bar = pltpu.get_barrier_semaphore()
    pl.semaphore_signal(bar, inc=1, device_id=(me, 1 - c), device_id_type=MESH)

    @pl.loop(1, n)
    def _(j):
        pl.semaphore_signal(bar, inc=1, device_id=((me + j) % n, c), device_id_type=MESH)

    return bar


def head_window(h):
    lo = pl.multiple_of(h * HEAD_DIM // 128 * 128, 128)
    lane = lax.broadcasted_iota(jnp.int32, (1, 256), 1) + lo - h * HEAD_DIM
    return pl.ds(lo, 256), ((lane >= 0) & (lane < HEAD_DIM)).astype(jnp.bfloat16)


def head_probs(qh, kh, seen):
    logits = jnp.where(seen, dot(qh, kh, 1, 1) * HEAD_DIM ** (-0.5), MASK_FILL)
    expo = jnp.exp(logits - jnp.max(logits, axis=-1, keepdims=True))
    return expo / jnp.sum(expo, axis=-1, keepdims=True)


def to_blocks(values, ref):
    count, size = ref.shape[:2]
    turned = values.T
    for i in range(count):
        ref[i] = turned[i * size : (i + 1) * size]


def write_blocks(n, target, stage, sem, block):
    def copy(i):
        return pltpu.make_async_copy(stage.at[i % 2], target.at[i // 4, i // 2 % 2, i % 2], sem.at[i % 2])

    @pl.loop(0, n)
    def _(i):
        when(i >= 2, lambda: copy(i).wait())
        stage[i % 2] = block(i).astype(stage.dtype)
        copy(i).start()

    copy(0).wait()
    copy(1).wait()


def forward_kernel(line, *refs):
    (m_in, m_out, m_expand, m_contract, m_table, m_mod, block, time_vec, tokens, cells, freqs, kept, cot) = refs[:13]
    (weights, g_contract, g_expand, cond_got, h1_t, q, k, v, o, attended, middle, act, d_z, sums, out, pieces, cond, silu,
     mod_half, x, key_ok, row_ok, onehot, same, biases) = refs[13:38]
    (f_in, f_out, f_expand, f_contract, f_table, f_mod, own, table, cond_part, cond_some, mods, mod_part, mod_got, blocks, w,
     proj, mix, wide, partial, partial_got, h1, h2, h2_t, slope, d_branch, d_branch_t, stage, block_got, wide_bias, in_sem,
     w_sem, pair_send, pair_recv, peer_send, block_recv, cond_recv, mod_recv, keep_sem, stage_sem, cond_sem) = refs[38:78]
    n = line * 4
    low, f32 = jnp.bfloat16, jnp.float32
    me, c = lax.axis_index("dp"), lax.axis_index("seq")
    gat = Gatherer(line, own, weights, keep_sem, refs[78:84])
    red = make_reducer(line, (g_contract,), out, refs[84:])
    rows, width = x.shape
    own_rows, half = own.shape[1], own.shape[2] // 4
    edge = 3 * half // 128 * 128
    tiles = width // 128
    sources, flats = (m_in, m_out, m_table, m_mod, m_expand, m_contract), (f_in, f_out, f_table, f_mod, f_expand, f_contract)

    def load(i):
        return pltpu.make_async_copy(sources[i], flats[i], in_sem.at[i])

    for i in range(6):
        load(i).start()
    bar = greet_all(n)

    def swap(i, src, dst):
        return pltpu.make_async_remote_copy(
            src_ref=src, dst_ref=dst, send_sem=pair_send.at[i], recv_sem=pair_recv.at[i], device_id=(me, 1 - c),
            device_id_type=MESH)

    def tile(flat, t, count, per_row):
        return flat[pl.ds(t, count, stride=per_row), :]

    def cut_heads(flat, part, per_row):
        start = part * tiles + c * (tiles // 2)
        found = jnp.concatenate([tile(flat, start + j, own_rows, per_row) for j in range(tiles // 2 + 1)], axis=1)
        return jnp.where(c == 0, found[:, :half], found[:, found.shape[1] - half :]).astype(low)

    def cut(flat, target, count):
        for j in range(count):
            target[:own_rows, 128 * j : 128 * j + 128] = tile(flat, c * count + j, own_rows, 2 * count).astype(low)

    block_start, block_wait = all_peers(n, block, block_got, peer_send, block_recv, False)
    cond_start, cond_wait = all_peers(n, cond_part, cond_got, peer_send, cond_recv, True)
    mod_start, mod_wait = all_peers(n, mod_part, mod_got, peer_send, mod_recv, True)
    block_got[me] = block[...]
    load(0).wait()
    load(1).wait()
    for part in range(3):
        own[0, :, part * half : (part + 1) * half] = cut_heads(f_in, part, 3 * tiles)
    own[0, :, 3 * half :] = cut_heads(f_out, 0, tiles)
    pl.semaphore_wait(bar, n)
    block_start()
    gat.begin(0)
    load(5).wait()
    cut(f_contract, own.at[2], 4 * half // 128)
    load(2).wait()
    class_rows = table.shape[0]
    for t in range(tiles):
        table[:, 128 * t : 128 * t + 128] = tile(f_table, t, class_rows, tiles).astype(low)

    block_wait()
    labels = block_got[:, 8, :]
    hot = (labels[:, :class_rows] - (me * class_rows).astype(f32)
           == lax.broadcasted_iota(jnp.int32, (n, class_rows), 1).astype(f32)).astype(f32)
    onehot[...] = hot
    row = jnp.concatenate([block_got[s, 8:9, :1] for s in range(n)], axis=1)
    same[...] = (labels[:, :1] == row).astype(f32)
    found = dot(hot.astype(low), table[...])
    mine = lax.broadcasted_iota(jnp.int32, (n, width), 0) == me
    found = found + jnp.where(mine, jnp.broadcast_to(time_vec[...].astype(f32), (n, width)), 0.0)
    cond_part[...] = jnp.zeros_like(cond_part)
    for i in range(n):
        cond_part[i, :, :own_rows] = found[:, i * own_rows : (i + 1) * own_rows]
    keep_cond = pltpu.make_async_copy(cond_part.at[me], cond_got.at[me], cond_sem.at[0])
    keep_cond.start()
    cond_start()
    gat.begin(2)
    gat.paired(0)
    load(3).wait()
    mod_half[own_rows:] = jnp.zeros((mod_half.shape[0] - own_rows, mod_half.shape[1]), low)
    cut(f_mod, mod_half, 3 * tiles)
    load(4).wait()
    cut(f_expand, own.at[1], 4 * half // 128)
    gat.begin(1)

    share = biases.shape[1] // n
    for i in range(n):
        for r in range(-(-share // 128)):
            size = min(128, share - 128 * r)
            biases[:, i * share + 128 * r : i * share + 128 * r + size] = block_got[i, r : r + 1, :size]

    def bias(start, size):
        return biases[:, start : start + size]

    def bias_half(start, size):
        return jnp.where(c == 0, bias(start, size // 2), bias(start + size // 2, size // 2))

    half_kept = jnp.floor(kept[...] * 0.5)
    rows_at = lax.broadcasted_iota(jnp.int32, (rows, 1), 0).astype(f32)
    row_ok[...] = (rows_at < half_kept).astype(f32)
    lanes_at = lax.broadcasted_iota(jnp.int32, (1, 2 * rows), 1)
    lanes_at = jnp.where(lanes_at < rows, lanes_at, lanes_at - rows).astype(f32)
    key_ok[...] = (lanes_at < half_kept).astype(f32)
    quarter = width // 4
    for i, place in enumerate((cells[:, :1], cells[:, 1:2])):
        angle = place * freqs[...]
        for j, wave in enumerate((jnp.sin(angle), jnp.cos(angle))):
            cols = slice((2 * i + j) * quarter, (2 * i + j + 1) * quarter)
            x[:, cols] = tokens[:, cols].astype(f32) + wave

    gat.steps(0, 1, 1)
    cond_wait()
    keep_cond.wait()
    cond[...] = jnp.zeros_like(cond)
    some = cond_some.shape[0]

    @pl.loop(0, n // some)
    def _(j):
        copy = pltpu.make_async_copy(cond_got.at[pl.ds(j * some, some)], cond_some, cond_sem.at[1])
        copy.start()
        copy.wait()
        cond[...] = cond[...] + jnp.sum(cond_some[...], axis=0)

    value = cond[...]
    silu[...] = (value / (1.0 + jnp.exp(-value))).astype(low)
    mods[...] = dot(silu[...], mod_half[...])

    @pl.loop(0, n)
    def _(s):
        mod_part[s] = mods[pl.ds(s, 1), :]

    mod_got[me] = mod_part[me]
    mod_start()
    gat.steps(0, 2, 2)
    gat.paired(1)
    gat.steps(0, 3, line)
    gat.steps(1, 1, 1)
    mod_wait()
    pieces[c] = jnp.sum(mod_got[...], axis=0) + bias_half(0, 6 * width)
    swap(0, pieces.at[c], pieces.at[c]).start()
    def fetch(m):
        return pltpu.make_async_copy(weights.at[m], blocks, w_sem.at[m])

    def unpack():
        for i in range(n):
            w[i * own_rows : (i + 1) * own_rows, :] = blocks[i // 4, i // 2 % 2, i % 2]

    gat.complete(0)
    fetch(0).start()
    swap(0, pieces.at[c], pieces.at[c]).wait()
    shift, scale, gate = (pieces[0, :, i * width : (i + 1) * width] for i in range(3))
    h1[c] = (normal(x[...]) * (1.0 + scale) + shift).astype(low)
    swap(1, h1.at[c], h1.at[c]).start()
    d_branch[c] = (pieces[1, :, 2 * width :] * (cot[...].astype(f32) * row_ok[...])).astype(low)
    swap(4, d_branch.at[c], d_branch.at[c]).start()
    fetch(0).wait()
    unpack()
    swap(1, h1.at[c], h1.at[c]).wait()
    both = jnp.concatenate([h1[0], h1[1]], axis=0)
    to_blocks(both, h1_t)

    @pl.loop(0, proj.shape[1] // 256)
    def _(t):
        cols = pl.ds(pl.multiple_of(t * 256, 256), 256)
        proj[:, cols] = dot(both, w[:, cols])

    spare = q.shape[1] - half
    for item, value in (
        (q, proj[:, :half] + bias_half(6 * width, width)),
        (k, proj[:, half : 2 * half]),
        (v, proj[:, 2 * half : 3 * half] + bias_half(7 * width, width)),
    ):
        item[:, :half] = value.astype(low)
        item[:, half:] = jnp.zeros((2 * rows, spare), low)
    mix[...] = jnp.zeros_like(mix)
    seen = jnp.broadcast_to(key_ok[...], (2 * rows, 2 * rows)) > 0.0
    heads = half // HEAD_DIM

    def head(h):
        win, lanes = head_window(h)
        probs = head_probs(q[:, win] * lanes, k[:, win], seen)
        mix[:, win] = mix[:, win] + dot(probs.astype(low), v[:, win] * lanes)

    @pl.loop(0, heads)
    def _(t):
        head(t)
        when(t == 1, lambda: gat.steps(1, 2, 2))
        when(t == 3, lambda: gat.paired(2))
        when(t == heads - 1, lambda: gat.steps(1, 3, 3))

    o[...] = mix[...].astype(low)
    wide[:, : 3 * half - edge] = jnp.zeros((2 * rows, 3 * half - edge), low)
    wide[:, 3 * half - edge :] = mix[:, :half].astype(low)

    @pl.loop(0, tiles)
    def _(t):
        cols = pl.ds(pl.multiple_of(t * 128, 128), 128)
        part = dot(wide[...], w[cols, edge:], 1, 1)
        partial[0, :, cols] = part[:rows]
        partial[1, :, cols] = part[rows:]

    swap(2, partial.at[1 - c], partial_got).start()
    gat.steps(1, 4, line)
    swap(2, partial.at[1 - c], partial_got).wait()
    attended[...] = partial[c] + partial_got[...] + bias(8 * width, width)
    middle[...] = x[...] + gate * attended[...]
    shift, scale = (pieces[1, :, i * width : (i + 1) * width] for i in range(2))
    h2[c] = (normal(middle[...]) * (1.0 + scale) + shift).astype(low)
    swap(3, h2.at[c], h2.at[c]).start()
    gat.complete(1)
    fetch(1).start()
    gat.steps(2, 1, 1)
    swap(4, d_branch.at[c], d_branch.at[c]).wait()
    to_blocks(jnp.concatenate([d_branch[0], d_branch[1]], axis=0), d_branch_t)
    swap(3, h2.at[c], h2.at[c]).wait()
    both = jnp.concatenate([h2[0], h2[1]], axis=0)
    to_blocks(both, h2_t)
    fetch(1).wait()
    unpack()
    gat.steps(2, 2, 2)

    wide_bias[...] = bias_half(9 * width, 8 * half)

    @pl.loop(0, act.shape[1] // 256)
    def _(t):
        cols = pl.ds(pl.multiple_of(t * 256, 256), 256)
        z = dot(both, w[:, cols]) + wide_bias[:, cols]
        bend = jnp.tanh(GELU_A * (z + GELU_B * z * z * z))
        act[:, cols] = (0.5 * z * (1.0 + bend)).astype(low)
        slope[:, cols] = 0.5 * (1.0 + bend) + 0.5 * z * (1.0 - bend * bend) * (GELU_A * (1.0 + 3.0 * GELU_B * z * z))

    def contract_block(i):
        when(i == n // 4, lambda: gat.steps(2, 3, 3))
        when(i == n // 2, lambda: gat.steps(2, 4, line))
        return dot(d_branch_t[i], act[...])

    write_blocks(n, g_contract, stage, stage_sem, contract_block)
    quarter = line // 4
    red.begin_some(0, 2 * quarter)
    gat.complete(2)
    fetch(2).start()
    sums[...] = jnp.zeros_like(sums)
    sums[4:5] = jnp.sum(d_branch[...].astype(f32), axis=(0, 1))[None]
    fetch(2).wait()
    unpack()
    red.unit_some(0, quarter)
    d_out = jnp.concatenate([d_branch[0], d_branch[1]], axis=0)

    @pl.loop(0, act.shape[1] // 256)
    def _(t):
        cols = pl.ds(pl.multiple_of(t * 256, 256), 256)
        d_z[:, cols] = (dot(d_out, w[:, cols]) * slope[:, cols]).astype(low)

    red.begin_some(2 * quarter, 3 * quarter)
    red.unit_some(quarter, 2 * quarter)
    totals = jnp.sum(d_z[...].astype(f32), axis=0, keepdims=True)
    sums[1:2] = totals[:, :width]
    sums[2:3] = totals[:, width:]

    def expand_block(i):
        when(i == n // 4, lambda: red.begin_some(3 * quarter, line))
        when(i == n // 2, lambda: red.unit_some(2 * quarter, 3 * quarter))
        return dot(h2_t[i], d_z[...])

    write_blocks(n, g_expand, stage, stage_sem, expand_block)
    red.unit_some(3 * quarter, line)
    red.final(0)
    red.drain()

    @pl.loop(0, 3)
    def _(m):
        gat.drain(m)


def forward(hbm_args, vmem_args, bias_size, n, collective_id):
    line = n // 4
    block, time_vec, tokens = vmem_args[:3]
    rows, width = tokens.shape
    class_rows = hbm_args[4].size // width
    own_rows, half = width // n, width // 2
    low, f32 = jnp.bfloat16, jnp.float32
    dma = pltpu.SemaphoreType.DMA
    vmem, hbm = pl.BlockSpec(memory_space=pltpu.VMEM), pl.BlockSpec(memory_space=pltpu.HBM)
    heads = (2 * rows, -(-half // 128) * 128)
    edge = 3 * half // 128 * 128

    def shape(dims, kind):
        return jax.ShapeDtypeStruct(dims, kind)

    def scratch(dims, kind):
        return pltpu.VMEM(dims, kind)

    return pl.pallas_call(
        functools.partial(forward_kernel, line),
        out_shape=[
            shape((3, line, 2, 2, own_rows, 4 * half), low),
            shape((line, 2, 2, own_rows, 4 * half), low),
            shape((line, 2, 2, own_rows, 4 * half), low),
            shape((n, n, 128), f32),
            shape((n, own_rows, 2 * rows), low),
            shape(heads, low),
            shape(heads, low),
            shape(heads, low),
            shape(heads, low),
            shape((rows, width), f32),
            shape((rows, width), f32),
            shape((2 * rows, 4 * half), low),
            shape((2 * rows, 4 * half), low),
            shape((8, width), f32),
            shape((1, own_rows, 4 * half), low),
            shape((2, 1, 3 * width), f32),
            shape((n, 128), f32),
            shape((n, 128), low),
            shape((128, 3 * width), low),
            shape((rows, width), f32),
            shape((1, 2 * rows), f32),
            shape((rows, 1), f32),
            shape((n, class_rows), f32),
            shape((n, n), f32),
            shape((1, bias_size), f32),
        ],
        in_specs=[hbm] * len(hbm_args) + [vmem] * len(vmem_args),
        out_specs=[hbm] * 4 + [vmem] * 21,
        scratch_shapes=[scratch(item.shape, f32) for item in hbm_args]
        + [
            scratch((3, own_rows, 4 * half), low),
            scratch((class_rows, width), low),
            scratch((n, n, 128), f32),
            scratch((min(n, 16), n, 128), f32),
            scratch((n, 3 * width), f32),
            scratch((n, 1, 3 * width), f32),
            scratch((n, 1, 3 * width), f32),
            scratch((line, 2, 2, own_rows, 4 * half), low),
            scratch((width, 4 * half), low),
            scratch((2 * rows, edge + 128), f32),
            scratch(heads, f32),
            scratch(heads, low),
            scratch((2, rows, width), f32),
            scratch((rows, width), f32),
            scratch((2, rows, width), low),
            scratch((2, rows, width), low),
            scratch((n, own_rows, 2 * rows), low),
            scratch((2 * rows, 4 * half), f32),
            scratch((2, rows, width), low),
            scratch((n, own_rows, 2 * rows), low),
            scratch((2, own_rows, 4 * half), low),
            scratch((n,) + block.shape, f32),
            scratch((1, 4 * half), f32),
            dma((6,)),
            dma((3,)),
            dma((5,)),
            dma((5,)),
            dma((n,)),
            dma((n,)),
            dma((n,)),
            dma((n,)),
            dma((3,)),
            dma((2,)),
            dma((2,)),
        ]
        + [dma((3, 4, line)), dma((3, 4, line + 1))] + [dma((3, 4, line))] * 4
        + reducer_scratch(1, line, own_rows, low),
        compiler_params=pltpu.CompilerParams(
            collective_id=collective_id, has_side_effects=True, vmem_limit_bytes=63 * 2**20),
        name="forward",
    )(*hbm_args, *vmem_args)


class Reducer:
    def __init__(self, line, grads, out, own, got_b, got_z, got_a, sems):
        self.line, self.grads, self.out = line, grads, out
        self.own, self.acc, self.got_z, self.got_a = own, got_b, got_z, got_a
        self.load, self.send_b, self.send_z, self.send_a, self.recv_b, self.recv_z, self.recv_a = sems
        self.me = me = Place(line)
        self.up, self.down = me.z < line - 1, me.z > 0
        self.above, self.below = me.dev(z=jnp.minimum(me.z + 1, line - 1)), me.dev(z=jnp.maximum(me.z - 1, 0))
        self.units = len(grads) * line

    def last(self, g):
        return "y" if GROUPS[g][3] == "x" else "x"

    def first(self, g):
        return self.me.x if GROUPS[g][3] == "x" else self.me.y

    def half(self, grad, g, zz, mine):
        cols = pl.ds(GROUPS[g][0], GROUPS[g][1])
        if self.last(g) == "y":
            return grad.at[zz, self.me.y if mine else 1 - self.me.y, :, :, cols]
        return grad.at[zz, :, self.me.x if mine else 1 - self.me.x, :, cols]

    def loading(self, u, g, zz, side, grad=None):
        grad = self.grads[0] if grad is None else grad
        return pltpu.make_async_copy(
            self.half(grad, g, zz, True), self.own[g].at[u % 3, side], self.load.at[u % 3, g, side])

    def remote(self, src, dst, send, recv, dev):
        return pltpu.make_async_remote_copy(
            src_ref=src, dst_ref=dst, send_sem=send, recv_sem=recv, device_id=dev, device_id_type=MESH)

    def b_copy(self, m, g, zz, grad=None):
        grad = self.grads[0] if grad is None else grad
        return self.remote(
            self.half(grad, g, zz, False), self.acc[g].at[m, zz], self.send_b.at[m, g, zz], self.recv_b.at[m, g, zz],
            self.me.peer(self.last(g)))

    def slot_a(self, g, zz):
        return zz if GROUPS[g][2] == 1 else 0

    def a_copy(self, m, g, zz):
        return self.remote(
            self.acc[g].at[m, zz, 1 - self.first(g)], self.got_a[g].at[m, self.slot_a(g, zz)], self.send_a.at[m, g, zz],
            self.recv_a.at[m, g, zz], self.me.peer(GROUPS[g][3]))

    def z_copy(self, m, g, zz, slot, dev):
        part = self.acc[g].at[m, zz] if GROUPS[g][2] == 0 else self.acc[g].at[m, zz, self.first(g)]
        return self.remote(part, self.got_z[g].at[m, slot], self.send_z.at[m, g, zz], self.recv_z.at[m, g, slot], dev)

    def add_b(self, m, g, zz, u, side):
        self.loading(u, g, zz, side).wait()
        self.b_copy(m, g, zz).wait_recv()
        self.acc[g][m, zz] = self.acc[g][m, zz] + self.own[g][u % 3, side]

    def add_z(self, m, g, zz, slot):
        acc, got = self.acc[g], self.got_z[g]
        self.z_copy(m, g, self.me.z, slot, self.below).wait_recv()
        if GROUPS[g][2] == 0:
            acc[m, zz] = acc[m, zz] + got[m, slot]
        else:
            acc[m, zz, self.first(g)] = acc[m, zz, self.first(g)] + got[m, slot]

    def add_a(self, m, g, zz):
        self.a_copy(m, g, zz).wait_recv()
        acc, first = self.acc[g], self.first(g)
        acc[m, zz, first] = acc[m, zz, first] + self.got_a[g][m, self.slot_a(g, zz)]

    def planes(self, k, fn):
        z, line = self.me.z, self.line
        when(z + k < line, lambda: fn(jnp.minimum(z + k, line - 1), True))
        when((z >= k) & (k > 0), lambda: fn(jnp.maximum(z - k, 0), False))

    def begin(self, v):
        m, j = v // self.line, v % self.line

        def one(grad, zz, upward):
            for g in range(4):
                self.b_copy(m, g, zz, grad).start()
                self.loading(v, g, zz, 0 if upward else 1, grad).start()

        for index, grad in enumerate(self.grads):
            when(m == index, lambda: self.planes(self.line - 1 - j, lambda zz, upward: one(grad, zz, upward)))

    def onward(self, m, g, zz, k, upward):
        if upward:
            when(self.down, lambda: self.add_z(m, g, zz, zz))
            self.z_copy(m, g, zz, zz, self.above).start()
        else:
            when(self.up, lambda: self.add_z(m, g, zz, zz))
            self.z_copy(m, g, zz, jnp.where(k == 1, self.line, zz), self.below).start()

    def near(self, u, m, j):
        k = self.line - 1 - j

        def one(zz, upward):
            for g in range(4):
                self.add_b(m, g, zz, u, 0 if upward else 1)
                if GROUPS[g][2] == 1:
                    self.a_copy(m, g, zz).start()
                else:
                    when(k > 0, lambda g=g: self.onward(m, g, zz, k, upward))

        self.planes(k, one)

    def far(self, m, j):
        k = self.line - j

        def one(zz, upward):
            for g in (2, 3):
                self.add_a(m, g, zz)
                self.onward(m, g, zz, k, upward)

        when((k > 0) & (k < self.line), lambda: self.planes(k, one))

    def close(self, m):
        z = self.me.z
        for g in (0, 1):
            when(self.down, lambda g=g: self.add_z(m, g, z, z))
            when(self.up, lambda g=g: self.add_z(m, g, z, self.line))
            self.a_copy(m, g, z).start()

    def final(self, m):
        z = self.me.z
        for g in range(4):
            cols = pl.ds(GROUPS[g][0], GROUPS[g][1])
            self.add_a(m, g, z)
            if GROUPS[g][2] == 1:
                when(self.down, lambda g=g: self.add_z(m, g, z, z))
                when(self.up, lambda g=g: self.add_z(m, g, z, self.line))
            self.out[m, :, cols] = self.acc[g][m, z, self.first(g)]

    def unit(self, u):
        line = self.line
        m, j = u // line, u % line
        self.near(u, m, j)
        self.far(m, j)
        when(j == line - 1, lambda: self.close(m))
        if len(self.grads) > 1:
            when((j == 0) & (m > 0), lambda: self.final(jnp.maximum(m - 1, 0)))

    def begin_some(self, first, last):
        @pl.loop(first, last)
        def _(v):
            self.begin(v)

    def unit_some(self, first, last):
        @pl.loop(first, last)
        def _(u):
            self.unit(u)

    def drain(self):
        z = self.me.z

        @pl.loop(0, len(self.grads))
        def _(m):
            @pl.loop(0, self.line)
            def _(zz):
                for g in range(4):
                    self.b_copy(m, g, zz).wait_send()
                    if GROUPS[g][2] == 1:
                        self.a_copy(m, g, zz).wait_send()
                    when(zz != z, lambda g=g: self.z_copy(m, g, zz, zz, self.above).wait_send())
            for g in (0, 1):
                self.a_copy(m, g, z).wait_send()


def reducer_scratch(count, line, rows, dt):
    dma = pltpu.SemaphoreType.DMA
    own = [pltpu.VMEM((3, 2, 2, rows, GROUPS[g][1]), dt) for g in range(4)]
    got_b = [pltpu.VMEM((count, line, 2, rows, GROUPS[g][1]), dt) for g in range(4)]
    got_z = [pltpu.VMEM((count, line + 1) + ((2,) if GROUPS[g][2] == 0 else ()) + (rows, GROUPS[g][1]), dt) for g in range(4)]
    got_a = [pltpu.VMEM((count, line if GROUPS[g][2] == 1 else 1, rows, GROUPS[g][1]), dt) for g in range(4)]
    sems = [dma((3, 4, 2))] + [dma((count, 4, line))] * 4 + [dma((count, 4, line + 1))] + [dma((count, 4, line))]
    return own + got_b + got_z + got_a + sems


def make_reducer(line, grads, out, refs):
    return Reducer(line, grads, out, refs[:4], refs[4:8], refs[8:12], refs[12:16], refs[16:])


def backward_kernel(line, *refs):
    (weights, g_expand, h1_t, act, d_z, sums, out_contract, q, k, v, o, key_ok, x, middle, attended, cot, row_ok, pieces,
     b_contract, modulation, cond, silu, same) = refs[:23]
    (g_attn, d_mod_all, cond_all, both, block_out, tokens_grad, bias_all, norm_out, factor_out) = refs[23:32]
    (w, rhs, d_o, d_q, d_k, d_v, d_h, d_h_got, branch_got, d_mid, d_att, d_att_t, stage, dp, dp_got, msg, msg_got, d_mod, vec,
     vec_got, d_silu, d_silu_got, chunk, out, bias_sum, d_cond, squares, squares_got, table_squares, squares_pair, cond_some, w_sem,
     mod_sem, stage_sem, pair_send, pair_recv, msg_send, msg_recv, vec_send, vec_recv, cond_send, cond_recv, bias_send, bias_recv, square_send,
     square_recv) = refs[32:78]
    n = line * 4
    low, f32 = jnp.bfloat16, jnp.float32
    me, c = lax.axis_index("dp"), lax.axis_index("seq")
    red = make_reducer(line, (g_expand, g_attn), out, refs[78:])
    rows, width = x.shape
    half = weights.shape[2] // 4
    heads = half // HEAD_DIM
    edge = 3 * half // 128 * 128
    tiles = width // 128

    def swap(i, src, dst):
        return pltpu.make_async_remote_copy(
            src_ref=src, dst_ref=dst, send_sem=pair_send.at[i], recv_sem=pair_recv.at[i], device_id=(me, 1 - c),
            device_id_type=MESH)

    def fetch(i):
        return pltpu.make_async_copy(weights.at[(1, 0, 2)[i]], w, w_sem.at[i])

    def back(values, lanes):
        @pl.loop(0, tiles)
        def _(t):
            cols = pl.ds(pl.multiple_of(t * 128, 128), 128)
            part = dot(values[...], w[cols, :lanes], 1, 1)
            d_h[0, :, cols] = part[:rows]
            d_h[1, :, cols] = part[rows:]

    def column_sums(values):
        return jnp.sum(values.astype(f32), axis=0, keepdims=True)

    def norm_back(values, scale, d_n):
        centre = values - jnp.mean(values, axis=-1, keepdims=True)
        inv = lax.rsqrt(jnp.mean(centre * centre, axis=-1, keepdims=True) + LAYER_EPS)
        normed = centre * inv
        e = d_n * (1.0 + scale)
        d_x = (e - jnp.mean(e, axis=-1, keepdims=True) - normed * jnp.mean(e * normed, axis=-1, keepdims=True)) * inv
        return d_x, jnp.sum(d_n, axis=0, keepdims=True), jnp.sum(d_n * normed, axis=0, keepdims=True)

    def piece(i):
        return pieces[i // 3, :, i % 3 * width : (i % 3 + 1) * width]

    fetch(0).start()
    bar = greet_all(n)
    for item in (d_q, d_k, d_v):
        item[...] = jnp.zeros_like(item)
    dp[...] = jnp.zeros_like(dp)
    vec[...] = sums[...]
    pl.semaphore_wait(bar, n)

    def hidden_back():
        fetch(0).wait()
        back(d_z, 4 * half)
        swap(0, d_h.at[1 - c], d_h_got).start()
        fetch(1).start()

    def middle_back():
        swap(0, d_h.at[1 - c], d_h_got).wait()
        d_x, shift, scale = norm_back(middle[...], piece(4), d_h[c] + d_h_got[...])
        d_mid[...] = d_x + cot[...].astype(f32) * row_ok[...]
        dp[2:3] = jnp.sum(d_mid[...] * attended[...], axis=0, keepdims=True)
        dp[3:4] = shift
        dp[4:5] = scale
        d_att[c] = (piece(2) * d_mid[...]).astype(low)
        swap(1, d_att.at[c], d_att.at[c]).start()

    def mixed_back():
        swap(1, d_att.at[c], d_att.at[c]).wait()
        d_all = jnp.concatenate([d_att[0], d_att[1]], axis=0)
        to_blocks(d_all, d_att_t)
        vec[3:4] = column_sums(d_att[0]) + column_sums(d_att[1])
        fetch(1).wait()
        d_o[:, :half] = dot(d_all, w[:, edge:])[:, 3 * half - edge :].astype(low)
        d_o[:, half:] = jnp.zeros((2 * rows, d_o.shape[1] - half), low)

    seen = jnp.broadcast_to(key_ok[...], (2 * rows, 2 * rows)) > 0.0

    def head(h):
        win, lanes = head_window(h)
        qh, kh, doh = q[:, win] * lanes, k[:, win] * lanes, d_o[:, win] * lanes
        probs = head_probs(qh, kh, seen)
        d_probs = dot(doh, v[:, win], 1, 1)
        inner = jnp.sum(probs * d_probs, axis=-1, keepdims=True)
        d_logits = (probs * (d_probs - inner)).astype(low)
        d_q[:, win] = d_q[:, win] + dot(d_logits, kh) * HEAD_DIM ** (-0.5)
        d_k[:, win] = d_k[:, win] + dot(d_logits, qh, 0, 0) * HEAD_DIM ** (-0.5)
        d_v[:, win] = d_v[:, win] + dot(probs.astype(low), doh, 0, 0)

    def attention_grads():
        for i, item in enumerate((d_q, d_k, d_v)):
            rhs[: 2 * rows, i * half : (i + 1) * half] = item[:, :half].astype(low)
        rhs[: 2 * rows, 3 * half :] = jnp.zeros((2 * rows, half), low)
        rhs[2 * rows :, edge : 3 * half] = jnp.zeros((2 * rows, 3 * half - edge), low)
        rhs[2 * rows :, 3 * half :] = o[:, :half]
        sums = column_sums(rhs[: 2 * rows, : 3 * half])
        vec[0:1, :half] = sums[:, :half]
        vec[0:1, half:] = sums[:, 2 * half :]

        def block(i):
            left = dot(h1_t[i], rhs[: 2 * rows, :edge])
            right = dot(h1_t[i], rhs[: 2 * rows, edge:]) + dot(d_att_t[i], rhs[2 * rows :, edge:])
            return jnp.concatenate([left, right], axis=1)

        write_blocks(n, g_attn, stage, stage_sem, block)

    def input_back():
        back(rhs.at[: 2 * rows, : edge + 128], edge + 128)
        swap(2, d_h.at[1 - c], d_h_got).start()
        fetch(2).start()

    def first_back():
        swap(2, d_h.at[1 - c], d_h_got).wait()
        d_x, shift, scale = norm_back(x[...], piece(1), d_h[c] + d_h_got[...])
        tokens_grad[...] = (d_x + d_mid[...]).astype(low)
        dp[0:1] = shift
        dp[1:2] = scale
        fetch(2).wait()
        back(act, 4 * half)
        swap(3, d_h.at[1 - c], branch_got).start()

    def branch_out():
        swap(3, d_h.at[1 - c], branch_got).wait()
        branch = d_h[c] + branch_got[...] + b_contract[...]
        result = middle[...] + piece(5) * branch
        block_out[...] = jnp.where(jnp.broadcast_to(row_ok[...], result.shape) > 0.0, result, 0.0).astype(low)
        dp[5:6] = jnp.sum(cot[...].astype(f32) * row_ok[...] * branch, axis=0, keepdims=True)
        swap(4, dp, dp_got).start()

    msg_start, msg_wait = all_peers(n, msg, msg_got, msg_send, msg_recv, False)
    vec_start, vec_wait = all_peers(n, chunk, vec_got, vec_send, vec_recv, True)
    per = chunk_tiles(n, width)

    def send_mod():
        swap(4, dp, dp_got).wait()
        total = (dp[...] + dp_got[...]).astype(low).astype(f32)
        own = jnp.where(c == 0, total[0:3], total[3:6])
        for r in range(3):
            msg[r] = own[r : r + 1]
        msg_got[me] = msg[...]
        chunk[...] = jnp.zeros_like(chunk)
        for t in range(5 * tiles):
            chunk[t // per, t % per] = vec[t // tiles : t // tiles + 1, t % tiles * 128 : t % tiles * 128 + 128]
        vec_got[me] = chunk[me]
        msg_start()
        vec_start()

    keep_mod = pltpu.make_async_copy(d_mod, d_mod_all.at[c], mod_sem.at[0])
    keep_cond = pltpu.make_async_copy(d_cond, cond_all.at[me], mod_sem.at[2])

    def mod_grad():
        msg_wait()
        vec_wait()

        @pl.loop(0, n)
        def _(s):
            for r in range(3):
                d_mod[pl.ds(s, 1), r * width : (r + 1) * width] = msg_got[s, r]

        bias_sum[c] = jnp.zeros((8, 128), f32)
        for r in range(per):
            bias_sum[c, r : r + 1] = jnp.sum(vec_got[:, r], axis=0)
        d_silu[...] = dot(d_mod[...].astype(low), modulation[...], 1, 1)
        swap(5, d_silu, d_silu_got).start()
        swap(6, d_mod, d_mod_all.at[c]).start()
        swap(7, bias_sum.at[c], bias_sum.at[c]).start()
        keep_mod.start()

    cond_start, cond_wait = all_peers(n, d_cond, cond_all, cond_send, cond_recv, False)
    bias_start, bias_wait = all_peers(n, bias_sum, bias_all, bias_send, bias_recv, False)
    square_start, square_wait = all_peers(n, squares, squares_got, square_send, square_recv, False)

    def cond_grad():
        swap(5, d_silu, d_silu_got).wait()
        swap(6, d_mod, d_mod_all.at[c]).wait()
        swap(7, bias_sum.at[c], bias_sum.at[c]).wait()
        keep_mod.wait()
        gate = 1.0 / (1.0 + jnp.exp(-cond[...]))
        d_cond[...] = (d_silu[...] + d_silu_got[...]) * (gate + cond[...] * gate * (1.0 - gate))
        keep_cond.start()
        bias_all[me] = bias_sum[...]
        cond_start()
        bias_start()
        d_low = d_mod[...].astype(low)
        grad = dot(silu[...], d_low, 0, 0)[: out.shape[1]]
        sums = jnp.sum(d_mod[...], axis=0, keepdims=True)
        tile = per * me + lax.broadcasted_iota(jnp.int32, (8, 128), 0)
        counted = (tile < 3 * tiles) | (c == 0)
        total = jnp.sum(grad * grad) + jnp.where(me == 0, jnp.sum(sums * sums), 0.0)
        total = total + jnp.sum(jnp.where(counted, bias_sum[c] * bias_sum[c], 0.0))
        squares[...] = jnp.full((8, 128), total, f32)

    def table_norm():
        cond_wait()
        bias_wait()
        keep_cond.wait()
        table_squares[...] = jnp.zeros((8, 128), f32)
        size = cond_some.shape[0]

        @pl.loop(0, n // size)
        def _(j):
            some = pltpu.make_async_copy(cond_all.at[pl.ds(j * size, size)], cond_some, mod_sem.at[1])
            some.start()
            some.wait()
            gram = jnp.zeros((n, n), f32)
            for i in range(size):
                part = cond_some[i]
                gram = gram + lax.dot_general(
                    part, part, (((1,), (1,)), ((), ())), preferred_element_type=f32, precision=lax.Precision.HIGHEST)
            table_squares[...] = table_squares[...] + jnp.sum(gram * same[...])

    def share(m):
        return swap(8 + m, out_contract.at[0] if m == 0 else out.at[m - 1], both.at[c, m])

    def reduced(m):
        value = out_contract[0] if m == 0 else out[m - 1]
        both[c, m] = value
        share(m).start()
        value = value.astype(f32)
        squares[...] = squares[...] + jnp.sum(value * value)

    parts = (hidden_back, middle_back, mixed_back) + (None,) * heads
    parts += (attention_grads, input_back, first_back, branch_out, send_mod, mod_grad, cond_grad, table_norm)
    first_head = parts.index(None)
    begun, carried = ([places[u // line * 4 + u % line * 4 // line] for u in range(red.units)] for places in UNIT_PLACES)

    def upto(places, s):
        total = jnp.int32(0)
        for place in places:
            total = total + (place <= s).astype(jnp.int32)
        return total

    @pl.loop(0, len(parts) + 1)
    def _(s):
        @pl.loop(upto(begun, s - 1), upto(begun, s))
        def _(v):
            red.begin(v)

        @pl.loop(upto(carried, s - 1), upto(carried, s))
        def _(u):
            red.unit(u)

        when((s >= first_head) & (s < first_head + heads), lambda: head(s - first_head))
        for i, part in enumerate(parts):
            if part is not None:
                when(s == i, part)

    reduced(0)
    reduced(1)
    red.final(1)
    reduced(2)
    squares_got[me] = squares[...]
    square_start()
    red.drain()
    square_wait()
    squares[...] = jnp.sum(squares_got[...], axis=0)
    swap(11, squares, squares_pair).start()
    for m in range(3):
        share(m).wait()
    swap(11, squares, squares_pair).wait()
    norm = jnp.sqrt(squares[...] + squares_pair[...] + table_squares[...])
    norm_out[...] = norm
    factor_out[...] = jnp.minimum(1.0, CLIP_LIMIT / (norm + 1e-06))


def chunk_tiles(n, width):
    return -(-5 * (width // 128) // n)


def backward(hbm_args, vmem_args, n, collective_id):
    line = n // 4
    grad = hbm_args[1]
    rows, cols = grad.shape[-2:]
    heads = vmem_args[5].shape
    own, width = vmem_args[10].shape
    all_rows = 2 * own
    low, f32 = jnp.bfloat16, jnp.float32
    dma = pltpu.SemaphoreType.DMA
    vmem, hbm = pl.BlockSpec(memory_space=pltpu.VMEM), pl.BlockSpec(memory_space=pltpu.HBM)
    per = chunk_tiles(n, width)
    return pl.pallas_call(
        functools.partial(backward_kernel, line),
        out_shape=[
            jax.ShapeDtypeStruct(grad.shape, low),
            jax.ShapeDtypeStruct((2, n, 3 * width), f32),
            jax.ShapeDtypeStruct((n, n, 128), f32),
            jax.ShapeDtypeStruct((2, 3, rows, cols), low),
            jax.ShapeDtypeStruct((own, width), low),
            jax.ShapeDtypeStruct((own, width), low),
            jax.ShapeDtypeStruct((n, 2, 8, 128), f32),
            jax.ShapeDtypeStruct((8, 128), f32),
            jax.ShapeDtypeStruct((8, 128), f32),
        ],
        in_specs=[hbm] * len(hbm_args) + [vmem] * len(vmem_args),
        out_specs=[hbm] * 3 + [vmem] * 6,
        scratch_shapes=[
            pltpu.VMEM((width, cols), low),
            pltpu.VMEM((2 * all_rows, cols), low),
            pltpu.VMEM(heads, low),
            pltpu.VMEM(heads, f32),
            pltpu.VMEM(heads, f32),
            pltpu.VMEM(heads, f32),
            pltpu.VMEM((2, own, width), f32),
            pltpu.VMEM((own, width), f32),
            pltpu.VMEM((own, width), f32),
            pltpu.VMEM((own, width), f32),
            pltpu.VMEM((2, own, width), low),
            pltpu.VMEM((n, rows, all_rows), low),
            pltpu.VMEM((2, rows, cols), low),
            pltpu.VMEM((8, width), f32),
            pltpu.VMEM((8, width), f32),
            pltpu.VMEM((3, 1, width), f32),
            pltpu.VMEM((n, 3, 1, width), f32),
            pltpu.VMEM((n, 3 * width), f32),
            pltpu.VMEM((8, width), f32),
            pltpu.VMEM((n, per, 1, 128), f32),
            pltpu.VMEM((n, 128), f32),
            pltpu.VMEM((n, 128), f32),
            pltpu.VMEM((n, per, 1, 128), f32),
            pltpu.VMEM((2, rows, cols), low),
            pltpu.VMEM((2, 8, 128), f32),
            pltpu.VMEM((n, 128), f32),
            pltpu.VMEM((8, 128), f32),
            pltpu.VMEM((n, 8, 128), f32),
            pltpu.VMEM((8, 128), f32),
            pltpu.VMEM((8, 128), f32),
            pltpu.VMEM((min(n, 16), n, 128), f32),
            dma((3,)),
            dma((3,)),
            dma((2,)),
            dma((12,)),
            dma((12,)),
        ]
        + [dma((n,))] * 10
        + reducer_scratch(2, line, rows, low),
        compiler_params=pltpu.CompilerParams(
            collective_id=collective_id, has_side_effects=True, vmem_limit_bytes=63 * 2**20),
        name="backward",
    )(*hbm_args, *vmem_args)


def adam_step(grad, master, first, second, rate):
    first_new = BETA_FIRST * first + (1.0 - BETA_FIRST) * grad
    second_new = BETA_SECOND * second + (1.0 - BETA_SECOND) * grad * grad
    first_hat = first_new / (1.0 - BETA_FIRST**STEP)
    second_hat = second_new / (1.0 - BETA_SECOND**STEP)
    master_new = master - rate * (
        first_hat / (jnp.sqrt(second_hat) + ADAM_EPS) + WEIGHT_DECAY * master
    )
    return (first_new, second_new, master_new)


def chunk_rows(rows):
    sizes = [d for d in range(8, 257, 8) if rows % d == 0]
    return sizes[-1] if sizes else rows


def adam_kernel(n, rates, *refs):
    kinds = len(rates)
    factor_ref, both, silu, d_mod, cond_all, onehot = refs[:6]
    at = 6
    states = [refs[at + 3 * a : at + 3 * a + 3] for a in range(kinds)]
    at += 3 * kinds
    news = [refs[at + 3 * a : at + 3 * a + 3] for a in range(kinds)]
    at += 3 * kinds
    held, flat = refs[at : at + kinds], refs[at + kinds : at + 2 * kinds]
    wide, in_sem, out_sem = refs[at + 2 * kinds :]
    rows, half = both.shape[2:]
    head = half // 4
    order = (3, 4, 0, 1, 2, 5)

    def loads(a):
        return [pltpu.make_async_copy(states[a][k], held[a].at[k], in_sem.at[a, k]) for k in range(3)]

    for a in order:
        for copy in loads(a):
            copy.start()

    def spread(a, width, count=rows):
        tiles = width // 128
        for t in range(tiles):
            flat[a][pl.ds(t, count, stride=tiles), :] = wide[:count, 128 * t : 128 * t + 128]

    def gradient(a):
        if a == 0:
            part = d_mod.shape[2]
            for core in range(2):
                grad = dot(silu[...], d_mod[core].astype(silu.dtype), 0, 0)
                wide[:, core * part : (core + 1) * part] = grad[:rows]
            spread(a, 2 * part)
        elif a == 1:
            for core in range(2):
                for part in range(3):
                    lo = (2 * part + core) * head
                    wide[:, lo : lo + head] = both[core, 2, :, part * head : (part + 1) * head].astype(jnp.float32)
            spread(a, 6 * head)
        elif a == 2:
            for core in range(2):
                wide[:, core * head : (core + 1) * head] = both[core, 2, :, 3 * head :].astype(jnp.float32)
            spread(a, 2 * head)
        elif a == 5:
            count = onehot.shape[1]
            for i in range(n):
                wide[:count, i * rows : (i + 1) * rows] = lax.dot_general(
                    onehot[...], cond_all[i], (((0,), (0,)), ((), ())), preferred_element_type=jnp.float32,
                    precision=lax.Precision.HIGHEST)[:, :rows]
            spread(a, n * rows, count)
        else:
            for core in range(2):
                wide[:, core * half : (core + 1) * half] = both[core, 4 - a].astype(jnp.float32)
            spread(a, 2 * half)

    factor = factor_ref[:1, :]
    for a in order:
        gradient(a)
        for copy in loads(a):
            copy.wait()
        size = chunk_rows(flat[a].shape[0])

        @pl.loop(0, flat[a].shape[0] // size)
        def _(i, a=a, size=size):
            part = pl.ds(pl.multiple_of(i * size, size), size)
            grad = flat[a][part] * factor
            master, first, second = held[a][0, part], held[a][1, part], held[a][2, part]
            first, second, master = adam_step(grad, master, first, second, rates[a])
            held[a][0, part], held[a][1, part], held[a][2, part] = master, first, second
            for k in range(3):
                pltpu.make_async_copy(held[a].at[k, part], news[a][k].at[part], out_sem.at[a, k]).start()

    for a in range(kinds):
        for k in range(3):
            pltpu.make_async_copy(held[a].at[k], news[a][k], out_sem.at[a, k]).wait()


def adam(factor, both, silu, d_mod, cond_all, onehot, states, rates, n):
    vmem, hbm = pl.BlockSpec(memory_space=pltpu.VMEM), pl.BlockSpec(memory_space=pltpu.HBM)
    dma = pltpu.SemaphoreType.DMA
    kinds = len(states)
    flats = [jax.ShapeDtypeStruct(s[0].shape, jnp.float32) for s in states]
    news = pl.pallas_call(
        functools.partial(adam_kernel, n, rates),
        out_shape=[f for f in flats for _ in range(3)],
        in_specs=[vmem] * 6 + [hbm] * (3 * kinds),
        out_specs=[hbm] * (3 * kinds),
        scratch_shapes=[pltpu.VMEM((3,) + f.shape, jnp.float32) for f in flats]
        + [pltpu.VMEM(f.shape, jnp.float32) for f in flats]
        + [pltpu.VMEM((both.shape[2], 2 * d_mod.shape[2]), jnp.float32), dma((kinds, 3)), dma((kinds, 3))],
        compiler_params=pltpu.CompilerParams(vmem_limit_bytes=56 * 2**20),
        name="adam",
    )(factor, both, silu, d_mod, cond_all, onehot, *[item for s in states for item in s])
    order = [3 * a + k for a in range(kinds) for k in (1, 2, 0)]
    return [news[i] for i in order]


def per_device(
    tokens,
    cotangent,
    time_vec,
    labels,
    kept,
    keep_index,
    modulation_master,
    modulation_first,
    modulation_second,
    attention_in_master,
    attention_in_first,
    attention_in_second,
    attention_out_master,
    attention_out_first,
    attention_out_second,
    expand_master,
    expand_first,
    expand_second,
    contract_master,
    contract_first,
    contract_second,
    class_table_master,
    class_table_first,
    class_table_second,
    biases_master,
    biases_first,
    biases_second,
):
    rows, width = tokens.shape[1:]
    n, pairs = lax.axis_size("dp"), lax.axis_size("seq")
    me = lax.axis_index("dp")
    half_width = width // pairs
    low = jnp.bfloat16

    bias_share = biases_master.shape[0]
    bias_block = jnp.pad(biases_master.astype(low).astype(jnp.float32), (0, 1024 - bias_share)).reshape(8, 128)
    label_block = jnp.broadcast_to(labels.astype(jnp.float32)[:, None], (8, 128))
    place = keep_index[0]
    cells = jnp.stack([place // SIDE, place % SIDE], axis=1).astype(jnp.float32)
    quarter = width // 4
    freqs = 10000.0 ** (-jnp.arange(quarter).astype(jnp.float32) / quarter)
    (weights, _, grad_expand, _, normed_in, queries, keys, values, mixed, attended, middle, activated, d_hidden, sums, contract_sum,
     pieces, cond_own, silu_own, own_modulation, inputs, key_ok, row_ok, onehot, same, biases) = forward(
        [
            item.reshape(-1, 128)
            for item in (
                attention_in_master,
                attention_out_master,
                expand_master,
                contract_master,
                class_table_master,
                modulation_master,
            )
        ],
        [
            jnp.concatenate([bias_block, label_block]),
            time_vec,
            tokens[0],
            cells,
            freqs[None],
            kept.astype(jnp.float32)[None],
            cotangent[0],
        ],
        bias_share * n,
        n,
        1,
    )
    _, d_mod_all, cond_all, reduced, block_out, tokens_grad, bias_parts, norm, clip = backward(
        [weights.reshape(3, width, 4 * half_width), grad_expand],
        [
            normed_in,
            activated,
            d_hidden,
            sums,
            contract_sum,
            queries,
            keys,
            values,
            mixed,
            key_ok,
            inputs,
            middle,
            attended,
            cotangent[0],
            row_ok,
            pieces,
            biases[:, 9 * width + FF :],
            own_modulation,
            cond_own,
            silu_own,
            same,
        ],
        n,
        2,
    )
    block_out, tokens_grad, grad_norm = block_out[None], tokens_grad[None], norm[0, 0]
    rates = (
        width ** (-0.5),
        width ** (-0.5),
        (width // 4) ** (-0.5),
        width ** (-0.5),
        FF ** (-0.5),
        0.5,
        0.2,
    )
    masters = (
        modulation_master,
        attention_in_master,
        attention_out_master,
        expand_master,
        contract_master,
        class_table_master,
        biases_master,
    )
    firsts = (
        modulation_first,
        attention_in_first,
        attention_out_first,
        expand_first,
        contract_first,
        class_table_first,
        biases_first,
    )
    seconds = (
        modulation_second,
        attention_in_second,
        attention_out_second,
        expand_second,
        contract_second,
        class_table_second,
        biases_second,
    )
    states = list(zip(masters, firsts, seconds))
    updated = adam(
        clip,
        reduced,
        silu_own,
        d_mod_all,
        cond_all,
        onehot,
        [tuple(item.reshape(-1, 128) for item in state) for state in states[:-1]],
        rates[:-1],
        n,
    )
    bias_parts = bias_parts.reshape(n, pairs, 8, 128)[:, :, : chunk_tiles(n, width)].transpose(1, 0, 2, 3)
    bias_parts = bias_parts.reshape(pairs, -1)[:, : 5 * width].reshape(pairs, 5, width)
    grad_biases = jnp.concatenate(
        [
            jnp.sum(d_mod_all, axis=1).reshape(-1),
            bias_parts[:, 0, :half_width].reshape(-1),
            bias_parts[:, 0, half_width:].reshape(-1),
            bias_parts[0, 3],
            bias_parts[:, 1:3].reshape(-1),
            bias_parts[0, 4],
        ]
    )
    bias_grad = lax.dynamic_slice_in_dim(grad_biases, me * bias_share, bias_share, 0) * clip[0, 0]
    updated = [item.reshape(-1) for item in updated] + list(adam_step(bias_grad, *states[-1], rates[-1]))
    return (block_out, tokens_grad, grad_norm) + tuple(updated)


def solution(mesh):
    return jax.shard_map(
        per_device,
        mesh=mesh,
        in_specs=(
            P("dp", "seq", None),
            P("dp", "seq", None),
            P("dp", None),
            P("dp"),
            P("dp"),
            P("dp", "seq"),
            P("dp"),
            P("dp"),
            P("dp"),
            P("dp"),
            P("dp"),
            P("dp"),
            P("dp"),
            P("dp"),
            P("dp"),
            P("dp"),
            P("dp"),
            P("dp"),
            P("dp"),
            P("dp"),
            P("dp"),
            P("dp"),
            P("dp"),
            P("dp"),
            P("dp"),
            P("dp"),
            P("dp"),
        ),
        out_specs=(
            P("dp", "seq", None),
            P("dp", "seq", None),
            P(),
            P("dp"),
            P("dp"),
            P("dp"),
            P("dp"),
            P("dp"),
            P("dp"),
            P("dp"),
            P("dp"),
            P("dp"),
            P("dp"),
            P("dp"),
            P("dp"),
            P("dp"),
            P("dp"),
            P("dp"),
            P("dp"),
            P("dp"),
            P("dp"),
            P("dp"),
            P("dp"),
            P("dp"),
        ),
        check_vma=False,
    )
```

```python
import functools
import jax
import jax.numpy as jnp
from jax import lax
from jax.experimental import pallas as pl
from jax.experimental.pallas import tpu as pltpu
import numpy as np
from jax.sharding import PartitionSpec as P

HEAD_DIM = 72
FF = 4608
SIDE = 16
CLASSES = 1024
STEP = 10
LAYER_EPS = 1e-06
MASK_FILL = -1e30
BETA_FIRST = 0.5
BETA_SECOND = 0.5
ADAM_EPS = 1e-08
WEIGHT_DECAY = 0.1
CLIP_LIMIT = 1.0

MESH = pl.DeviceIdType.MESH
GELU_A = (2.0 / 3.141592653589793) ** 0.5
GELU_B = 0.044715
UNIT_PLACES = ((0, 0, 2, 10, 12, 13, 13, 15), (1, 3, 11, 12, 13, 14, 15, 18))
GROUPS = ((0, 640, 0, "x"), (640, 640, 0, "y"), (1280, 512, 1, "x"), (1792, 512, 1, "y"))


def when(cond, fn):
    pl.when(cond)(fn)


class Place:
    def __init__(self, line):
        self.line = line
        i = lax.axis_index("dp")
        self.c = lax.axis_index("seq")
        self.x, self.y, self.z = i % 2, (i // 2) % 2, i // 4

    def dev(self, z=None, y=None, x=None):
        z = self.z if z is None else z
        y = self.y if y is None else y
        x = self.x if x is None else x
        return (z * 4 + y * 2 + x, self.c)

    def peer(self, axis):
        return self.dev(x=1 - self.x) if axis == "x" else self.dev(y=1 - self.y)

    def barrier(self):
        bar = pltpu.get_barrier_semaphore()

        def sig(dev):
            pl.semaphore_signal(bar, inc=1, device_id=dev, device_id_type=MESH)

        sig(self.peer("x"))
        sig(self.peer("y"))
        when(self.z > 0, lambda: sig(self.dev(z=self.z - 1)))
        when(self.z < self.line - 1, lambda: sig(self.dev(z=self.z + 1)))
        pl.semaphore_wait(bar, 2 + (self.z > 0).astype(jnp.int32) + (self.z < self.line - 1).astype(jnp.int32))


class Gatherer:
    def __init__(self, line, own, out, keep_sem, sems):
        self.line, self.own, self.out, self.keep_sem = line, own, out, keep_sem
        self.send_a, self.send_z, self.send_b, self.recv_a, self.recv_z, self.recv_b = sems
        self.me = Place(line)
        self.up, self.down = self.me.z < line - 1, self.me.z > 0

    def single(self, m, g, zz):
        lo, width = GROUPS[g][:2]
        return self.out.at[m, zz, self.me.y, self.me.x, :, pl.ds(lo, width)]

    def pair(self, m, g, zz):
        lo, width, _, first = GROUPS[g]
        if first == "x":
            return self.out.at[m, zz, self.me.y, :, :, pl.ds(lo, width)]
        return self.out.at[m, zz, :, self.me.x, :, pl.ds(lo, width)]

    def remote(self, ref, send, recv, dev, source):
        return pltpu.make_async_remote_copy(
            src_ref=ref if source is None else source, dst_ref=ref, send_sem=send, recv_sem=recv,
            device_id=dev, device_id_type=MESH)

    def source(self, m, g):
        lo, width = GROUPS[g][:2]
        return self.own.at[m, :, pl.ds(lo, width)]

    def a_copy(self, m, g, zz, source=None):
        return self.remote(
            self.single(m, g, zz), self.send_a.at[m, g, zz], self.recv_a.at[m, g, zz], self.me.peer(GROUPS[g][3]), source)

    def z_ref(self, m, g, zz):
        return self.pair(m, g, zz) if GROUPS[g][2] == 0 else self.single(m, g, zz)

    def u_copy(self, m, g, zz, source=None):
        dev = self.me.dev(z=jnp.minimum(self.me.z + 1, self.line - 1))
        return self.remote(self.z_ref(m, g, zz), self.send_z.at[m, g, zz], self.recv_z.at[m, g, zz], dev, source)

    def d_copy(self, m, g, zz, source=None):
        dev = self.me.dev(z=jnp.maximum(self.me.z - 1, 0))
        sem = self.send_z.at[m, g, jnp.where(zz == self.me.z, self.line, zz)]
        return self.remote(self.z_ref(m, g, zz), sem, self.recv_z.at[m, g, zz], dev, source)

    def b_copy(self, m, g, zz):
        last = "y" if GROUPS[g][3] == "x" else "x"
        return self.remote(self.pair(m, g, zz), self.send_b.at[m, g, zz], self.recv_b.at[m, g, zz], self.me.peer(last), None)

    def keep(self, m):
        me = self.me
        return pltpu.make_async_copy(self.own.at[m], self.out.at[m, me.z, me.y, me.x], self.keep_sem.at[m])

    def begin(self, m):
        z = self.me.z
        self.keep(m).start()
        for g in range(4):
            self.a_copy(m, g, z, self.source(m, g)).start()
        for g in (2, 3):
            when(self.up, lambda g=g: self.u_copy(m, g, z, self.source(m, g)).start())
            when(self.down, lambda g=g: self.d_copy(m, g, z, self.source(m, g)).start())

    def paired(self, m):
        z = self.me.z
        self.keep(m).wait()
        for g in (0, 1):
            self.a_copy(m, g, z).wait_recv()
            when(self.up, lambda g=g: self.u_copy(m, g, z).start())
            when(self.down, lambda g=g: self.d_copy(m, g, z).start())
            self.b_copy(m, g, z).start()

    def arrive(self, m, zz, upward):
        for g in range(4):
            copy = self.u_copy if upward else self.d_copy
            copy(m, g, zz).wait_recv()
            when(self.up if upward else self.down, lambda g=g: copy(m, g, zz).start())
            if GROUPS[g][2] == 0:
                self.b_copy(m, g, zz).start()
            else:
                self.a_copy(m, g, zz).start()

    def crossed(self, m, zz):
        for g in (2, 3):
            self.a_copy(m, g, zz).wait_recv()
            self.b_copy(m, g, zz).start()

    def step(self, m, k):
        z, line = self.me.z, self.line
        when(k <= z, lambda: self.arrive(m, jnp.maximum(z - k, 0), True))
        when(z + k < line, lambda: self.arrive(m, jnp.minimum(z + k, line - 1), False))
        when(k - 1 <= z, lambda: self.crossed(m, jnp.maximum(z - k + 1, 0)))
        when((k > 1) & (z + k - 1 < line), lambda: self.crossed(m, jnp.minimum(z + k - 1, line - 1)))

    def steps(self, m, first, last):
        @pl.loop(first, last + 1)
        def _(k):
            self.step(m, k)

    def complete(self, m):
        @pl.loop(0, self.line)
        def _(zz):
            for g in range(4):
                self.b_copy(m, g, zz).wait_recv()

    def drain(self, m):
        z = self.me.z

        @pl.loop(0, self.line)
        def _(zz):
            for g in range(4):
                self.b_copy(m, g, zz).wait_send()
                if GROUPS[g][2] == 1:
                    self.a_copy(m, g, zz).wait_send()
                when(self.up & (zz <= z), lambda g=g: self.u_copy(m, g, zz).wait_send())
                when(self.down & (zz >= z), lambda g=g: self.d_copy(m, g, zz).wait_send())

        for g in (0, 1):
            self.a_copy(m, g, z).wait_send()


def dot(left, right, a=1, b=0):
    return lax.dot_general(left, right, (((a,), (b,)), ((), ())), preferred_element_type=jnp.float32)


def normal(values):
    centre = values - jnp.mean(values, axis=-1, keepdims=True)
    return centre * lax.rsqrt(jnp.mean(centre * centre, axis=-1, keepdims=True) + LAYER_EPS)


def all_peers(n, src, dst, send, recv, spread):
    me, c = lax.axis_index("dp"), lax.axis_index("seq")

    def copy(j, there, slot):
        return pltpu.make_async_remote_copy(
            src_ref=src.at[there] if spread else src, dst_ref=dst.at[slot], send_sem=send.at[j], recv_sem=recv.at[slot],
            device_id=(there, c), device_id_type=MESH)

    def start():
        @pl.loop(1, n)
        def _(j):
            copy(j, (me + j) % n, me).start()

    def wait():
        @pl.loop(1, n)
        def _(j):
            copy(j, (me + j) % n, (me + n - j) % n).wait()

    return start, wait


def greet_all(n):
    me, c = lax.axis_index("dp"), lax.axis_index("seq")
    bar = pltpu.get_barrier_semaphore()
    pl.semaphore_signal(bar, inc=1, device_id=(me, 1 - c), device_id_type=MESH)

    @pl.loop(1, n)
    def _(j):
        pl.semaphore_signal(bar, inc=1, device_id=((me + j) % n, c), device_id_type=MESH)

    return bar


def head_window(h):
    lo = pl.multiple_of(h * HEAD_DIM // 128 * 128, 128)
    lane = lax.broadcasted_iota(jnp.int32, (1, 256), 1) + lo - h * HEAD_DIM
    return pl.ds(lo, 256), ((lane >= 0) & (lane < HEAD_DIM)).astype(jnp.bfloat16)


def head_probs(qh, kh, seen):
    logits = jnp.where(seen, dot(qh, kh, 1, 1) * HEAD_DIM ** (-0.5), MASK_FILL)
    expo = jnp.exp(logits - jnp.max(logits, axis=-1, keepdims=True))
    return expo / jnp.sum(expo, axis=-1, keepdims=True)


def to_blocks(values, ref):
    count, size = ref.shape[:2]
    turned = values.T
    for i in range(count):
        ref[i] = turned[i * size : (i + 1) * size]


def write_blocks(n, target, stage, sem, block):
    def copy(i):
        return pltpu.make_async_copy(stage.at[i % 2], target.at[i // 4, i // 2 % 2, i % 2], sem.at[i % 2])

    @pl.loop(0, n)
    def _(i):
        when(i >= 2, lambda: copy(i).wait())
        stage[i % 2] = block(i).astype(stage.dtype)
        copy(i).start()

    copy(0).wait()
    copy(1).wait()


def forward_kernel(line, *refs):
    (m_in, m_out, m_expand, m_contract, m_table, m_mod, own_bias, meta, time_vec, tokens, cells, freqs, cot) = refs[:13]
    (weights, g_contract, g_expand, cond_got, h1_t, q, k, v, o, attended, middle, act, d_z, sums, out, pieces, cond, silu,
     mod_half, x, key_ok, row_ok, onehot, same, biases) = refs[13:38]
    (f_in, f_out, f_expand, f_contract, f_table, f_mod, own, table, cond_part, cond_some, mods, mod_part, mod_got, blocks, w,
     proj, mix, wide, partial, partial_got, h1, h2, h2_t, slope, d_branch, d_branch_t, stage, block, block_got, wide_bias, in_sem,
     w_sem, pair_send, pair_recv, peer_send, block_recv, cond_recv, mod_recv, keep_sem, stage_sem, cond_sem) = refs[38:79]
    n = line * 4
    low, f32 = jnp.bfloat16, jnp.float32
    me, c = lax.axis_index("dp"), lax.axis_index("seq")
    gat = Gatherer(line, own, weights, keep_sem, refs[79:85])
    red = make_reducer(line, (g_contract,), out, refs[85:])
    rows, width = x.shape
    own_rows, half = own.shape[1], own.shape[2] // 4
    edge = 3 * half // 128 * 128
    tiles = width // 128
    sources, flats = (m_in, m_out, m_table, m_mod, m_expand, m_contract), (f_in, f_out, f_table, f_mod, f_expand, f_contract)

    def load(i):
        return pltpu.make_async_copy(sources[i], flats[i], in_sem.at[i])

    for i in range(6):
        load(i).start()
    bar = greet_all(n)

    def swap(i, src, dst):
        return pltpu.make_async_remote_copy(
            src_ref=src, dst_ref=dst, send_sem=pair_send.at[i], recv_sem=pair_recv.at[i], device_id=(me, 1 - c),
            device_id_type=MESH)

    def tile(flat, t, count, per_row):
        return flat[pl.ds(t, count, stride=per_row), :]

    def cut_heads(flat, part, per_row):
        start = part * tiles + c * (tiles // 2)
        found = jnp.concatenate([tile(flat, start + j, own_rows, per_row) for j in range(tiles // 2 + 1)], axis=1)
        return jnp.where(c == 0, found[:, :half], found[:, found.shape[1] - half :]).astype(low)

    def cut(flat, target, count):
        for j in range(count):
            target[:own_rows, 128 * j : 128 * j + 128] = tile(flat, c * count + j, own_rows, 2 * count).astype(low)

    block_start, block_wait = all_peers(n, block, block_got, peer_send, block_recv, False)
    cond_start, cond_wait = all_peers(n, cond_part, cond_got, peer_send, cond_recv, True)
    mod_start, mod_wait = all_peers(n, mod_part, mod_got, peer_send, mod_recv, True)
    share = own_bias.shape[1]
    for r in range(-(-share // 128)):
        size = min(128, share - 128 * r)
        block[r : r + 1, :size] = own_bias[:, 128 * r : 128 * r + size].astype(low).astype(f32)
    block[8:] = jnp.broadcast_to(meta[:, :1].astype(f32), (8, 128))
    block_got[me] = block[...]
    load(0).wait()
    load(1).wait()
    for part in range(3):
        own[0, :, part * half : (part + 1) * half] = cut_heads(f_in, part, 3 * tiles)
    own[0, :, 3 * half :] = cut_heads(f_out, 0, tiles)
    pl.semaphore_wait(bar, n)
    block_start()
    gat.begin(0)
    load(5).wait()
    cut(f_contract, own.at[2], 4 * half // 128)
    load(2).wait()
    class_rows = table.shape[0]
    for t in range(tiles):
        table[:, 128 * t : 128 * t + 128] = tile(f_table, t, class_rows, tiles).astype(low)

    block_wait()
    labels = block_got[:, 8, :]
    hot = (labels[:, :class_rows] - (me * class_rows).astype(f32)
           == lax.broadcasted_iota(jnp.int32, (n, class_rows), 1).astype(f32)).astype(f32)
    onehot[...] = hot
    row = jnp.concatenate([block_got[s, 8:9, :1] for s in range(n)], axis=1)
    same[...] = (labels[:, :1] == row).astype(f32)
    found = dot(hot.astype(low), table[...])
    mine = lax.broadcasted_iota(jnp.int32, (n, width), 0) == me
    found = found + jnp.where(mine, jnp.broadcast_to(time_vec[...].astype(f32), (n, width)), 0.0)
    cond_part[...] = jnp.zeros_like(cond_part)
    for i in range(n):
        cond_part[i, :, :own_rows] = found[:, i * own_rows : (i + 1) * own_rows]
    keep_cond = pltpu.make_async_copy(cond_part.at[me], cond_got.at[me], cond_sem.at[0])
    keep_cond.start()
    cond_start()
    gat.begin(2)
    gat.paired(0)
    load(3).wait()
    mod_half[own_rows:] = jnp.zeros((mod_half.shape[0] - own_rows, mod_half.shape[1]), low)
    cut(f_mod, mod_half, 3 * tiles)
    load(4).wait()
    cut(f_expand, own.at[1], 4 * half // 128)
    gat.begin(1)

    for i in range(n):
        for r in range(-(-share // 128)):
            size = min(128, share - 128 * r)
            biases[:, i * share + 128 * r : i * share + 128 * r + size] = block_got[i, r : r + 1, :size]

    def bias(start, size):
        return biases[:, start : start + size]

    def bias_half(start, size):
        return jnp.where(c == 0, bias(start, size // 2), bias(start + size // 2, size // 2))

    half_kept = jnp.floor(meta[:, 1:2].astype(f32) * 0.5)
    rows_at = lax.broadcasted_iota(jnp.int32, (rows, 1), 0).astype(f32)
    row_ok[...] = (rows_at < half_kept).astype(f32)
    lanes_at = lax.broadcasted_iota(jnp.int32, (1, 2 * rows), 1)
    lanes_at = jnp.where(lanes_at < rows, lanes_at, lanes_at - rows).astype(f32)
    key_ok[...] = (lanes_at < half_kept).astype(f32)
    quarter = width // 4
    at = lax.broadcasted_iota(jnp.int32, (rows, rows), 0) == lax.broadcasted_iota(jnp.int32, (rows, rows), 1)
    cell = jnp.broadcast_to(cells[...].astype(f32), (rows, rows))
    cell = jnp.sum(jnp.where(at, cell, 0.0), axis=1, keepdims=True)
    across = jnp.floor(cell * (1.0 / SIDE))
    for i, place in enumerate((across, cell - SIDE * across)):
        angle = place * freqs[...]
        for j, wave in enumerate((jnp.sin(angle), jnp.cos(angle))):
            cols = slice((2 * i + j) * quarter, (2 * i + j + 1) * quarter)
            x[:, cols] = tokens[:, cols].astype(f32) + wave

    gat.steps(0, 1, 2)
    cond_wait()
    keep_cond.wait()
    cond[...] = jnp.zeros_like(cond)
    some = cond_some.shape[0]

    @pl.loop(0, n // some)
    def _(j):
        copy = pltpu.make_async_copy(cond_got.at[pl.ds(j * some, some)], cond_some, cond_sem.at[1])
        copy.start()
        copy.wait()
        cond[...] = cond[...] + jnp.sum(cond_some[...], axis=0)

    value = cond[...]
    silu[...] = (value / (1.0 + jnp.exp(-value))).astype(low)
    mods[...] = dot(silu[...], mod_half[...])

    @pl.loop(0, n)
    def _(s):
        mod_part[s] = mods[pl.ds(s, 1), :]

    mod_got[me] = mod_part[me]
    mod_start()
    gat.paired(1)
    gat.steps(0, 3, line)
    gat.steps(1, 1, 1)
    gat.steps(1, 2, 2)
    def fetch(m):
        return pltpu.make_async_copy(weights.at[m], blocks, w_sem.at[m])

    def unpack():
        for i in range(n):
            w[i * own_rows : (i + 1) * own_rows, :] = blocks[i // 4, i // 2 % 2, i % 2]

    gat.complete(0)
    fetch(0).start()
    mod_wait()
    pieces[c] = jnp.sum(mod_got[...], axis=0) + bias_half(0, 6 * width)
    swap(0, pieces.at[c], pieces.at[c]).start()
    swap(0, pieces.at[c], pieces.at[c]).wait()
    shift, scale, gate = (pieces[0, :, i * width : (i + 1) * width] for i in range(3))
    h1[c] = (normal(x[...]) * (1.0 + scale) + shift).astype(low)
    swap(1, h1.at[c], h1.at[c]).start()
    d_branch[c] = (pieces[1, :, 2 * width :] * (cot[...].astype(f32) * row_ok[...])).astype(low)
    swap(4, d_branch.at[c], d_branch.at[c]).start()
    fetch(0).wait()
    unpack()
    swap(1, h1.at[c], h1.at[c]).wait()
    both = jnp.concatenate([h1[0], h1[1]], axis=0)
    to_blocks(both, h1_t)
    gat.paired(2)

    @pl.loop(0, proj.shape[1] // 256)
    def _(t):
        cols = pl.ds(pl.multiple_of(t * 256, 256), 256)
        proj[:, cols] = dot(both, w[:, cols])

    spare = q.shape[1] - half
    for item, value in (
        (q, proj[:, :half] + bias_half(6 * width, width)),
        (k, proj[:, half : 2 * half]),
        (v, proj[:, 2 * half : 3 * half] + bias_half(7 * width, width)),
    ):
        item[:, :half] = value.astype(low)
        item[:, half:] = jnp.zeros((2 * rows, spare), low)
    mix[...] = jnp.zeros_like(mix)
    seen = jnp.broadcast_to(key_ok[...], (2 * rows, 2 * rows)) > 0.0
    heads = half // HEAD_DIM

    def head(h):
        win, lanes = head_window(h)
        probs = head_probs(q[:, win] * lanes, k[:, win], seen)
        mix[:, win] = mix[:, win] + dot(probs.astype(low), v[:, win] * lanes)

    @pl.loop(0, heads)
    def _(t):
        head(t)
        when(t == 0, lambda: gat.steps(1, 3, 3))
        when(t == heads - 1, lambda: gat.steps(1, 4, line))

    o[...] = mix[...].astype(low)
    wide[:, : 3 * half - edge] = jnp.zeros((2 * rows, 3 * half - edge), low)
    wide[:, 3 * half - edge :] = mix[:, :half].astype(low)

    @pl.loop(0, tiles)
    def _(t):
        cols = pl.ds(pl.multiple_of(t * 128, 128), 128)
        part = dot(wide[...], w[cols, edge:], 1, 1)
        partial[0, :, cols] = part[:rows]
        partial[1, :, cols] = part[rows:]

    swap(2, partial.at[1 - c], partial_got).start()
    gat.steps(2, 1, 1)
    swap(2, partial.at[1 - c], partial_got).wait()
    attended[...] = partial[c] + partial_got[...] + bias(8 * width, width)
    middle[...] = x[...] + gate * attended[...]
    shift, scale = (pieces[1, :, i * width : (i + 1) * width] for i in range(2))
    h2[c] = (normal(middle[...]) * (1.0 + scale) + shift).astype(low)
    swap(3, h2.at[c], h2.at[c]).start()
    gat.complete(1)
    fetch(1).start()
    swap(4, d_branch.at[c], d_branch.at[c]).wait()
    to_blocks(jnp.concatenate([d_branch[0], d_branch[1]], axis=0), d_branch_t)
    swap(3, h2.at[c], h2.at[c]).wait()
    both = jnp.concatenate([h2[0], h2[1]], axis=0)
    to_blocks(both, h2_t)
    fetch(1).wait()
    unpack()
    gat.steps(2, 2, 2)

    wide_bias[...] = bias_half(9 * width, 8 * half)

    @pl.loop(0, act.shape[1] // 256)
    def _(t):
        cols = pl.ds(pl.multiple_of(t * 256, 256), 256)
        z = dot(both, w[:, cols]) + wide_bias[:, cols]
        bend = jnp.tanh(GELU_A * (z + GELU_B * z * z * z))
        act[:, cols] = (0.5 * z * (1.0 + bend)).astype(low)
        slope[:, cols] = 0.5 * (1.0 + bend) + 0.5 * z * (1.0 - bend * bend) * (GELU_A * (1.0 + 3.0 * GELU_B * z * z))

    def contract_block(i):
        when(i == 0, lambda: gat.steps(2, 3, 3))
        when(i == n // 2, lambda: gat.steps(2, 4, line))
        return dot(d_branch_t[i], act[...])

    write_blocks(n, g_contract, stage, stage_sem, contract_block)
    quarter = line // 4
    red.begin_some(0, 2 * quarter)
    gat.complete(2)
    fetch(2).start()
    sums[...] = jnp.zeros_like(sums)
    sums[4:5] = jnp.sum(d_branch[...].astype(f32), axis=(0, 1))[None]
    fetch(2).wait()
    unpack()
    red.unit_some(0, quarter)
    d_out = jnp.concatenate([d_branch[0], d_branch[1]], axis=0)

    @pl.loop(0, act.shape[1] // 256)
    def _(t):
        cols = pl.ds(pl.multiple_of(t * 256, 256), 256)
        d_z[:, cols] = (dot(d_out, w[:, cols]) * slope[:, cols]).astype(low)

    red.begin_some(2 * quarter, 3 * quarter)
    red.unit_some(quarter, 2 * quarter)
    totals = jnp.sum(d_z[...].astype(f32), axis=0, keepdims=True)
    sums[1:2] = totals[:, :width]
    sums[2:3] = totals[:, width:]

    def expand_block(i):
        when(i == n // 4, lambda: red.begin_some(3 * quarter, line))
        when(i == n // 2, lambda: red.unit_some(2 * quarter, 3 * quarter))
        return dot(h2_t[i], d_z[...])

    write_blocks(n, g_expand, stage, stage_sem, expand_block)
    red.unit_some(3 * quarter, line)
    red.final(0)
    red.drain()

    @pl.loop(0, 3)
    def _(m):
        gat.drain(m)


def forward(hbm_args, vmem_args, bias_size, n, collective_id):
    line = n // 4
    tokens = vmem_args[3]
    rows, width = tokens.shape
    class_rows = hbm_args[4].size // width
    own_rows, half = width // n, width // 2
    low, f32 = jnp.bfloat16, jnp.float32
    dma = pltpu.SemaphoreType.DMA
    vmem, hbm = pl.BlockSpec(memory_space=pltpu.VMEM), pl.BlockSpec(memory_space=pltpu.HBM)
    heads = (2 * rows, -(-half // 128) * 128)
    edge = 3 * half // 128 * 128

    def shape(dims, kind):
        return jax.ShapeDtypeStruct(dims, kind)

    def scratch(dims, kind):
        return pltpu.VMEM(dims, kind)

    return pl.pallas_call(
        functools.partial(forward_kernel, line),
        out_shape=[
            shape((3, line, 2, 2, own_rows, 4 * half), low),
            shape((line, 2, 2, own_rows, 4 * half), low),
            shape((line, 2, 2, own_rows, 4 * half), low),
            shape((n, n, 128), f32),
            shape((n, own_rows, 2 * rows), low),
            shape(heads, low),
            shape(heads, low),
            shape(heads, low),
            shape(heads, low),
            shape((rows, width), f32),
            shape((rows, width), f32),
            shape((2 * rows, 4 * half), low),
            shape((2 * rows, 4 * half), low),
            shape((8, width), f32),
            shape((1, own_rows, 4 * half), low),
            shape((2, 1, 3 * width), f32),
            shape((n, 128), f32),
            shape((n, 128), low),
            shape((128, 3 * width), low),
            shape((rows, width), f32),
            shape((1, 2 * rows), f32),
            shape((rows, 1), f32),
            shape((n, class_rows), f32),
            shape((n, n), f32),
            shape((1, bias_size), f32),
        ],
        in_specs=[hbm] * len(hbm_args) + [vmem] * len(vmem_args),
        out_specs=[hbm] * 4 + [vmem] * 21,
        scratch_shapes=[scratch(item.shape, f32) for item in hbm_args]
        + [
            scratch((3, own_rows, 4 * half), low),
            scratch((class_rows, width), low),
            scratch((n, n, 128), f32),
            scratch((min(n, 16), n, 128), f32),
            scratch((n, 3 * width), f32),
            scratch((n, 1, 3 * width), f32),
            scratch((n, 1, 3 * width), f32),
            scratch((line, 2, 2, own_rows, 4 * half), low),
            scratch((width, 4 * half), low),
            scratch((2 * rows, edge + 128), f32),
            scratch(heads, f32),
            scratch(heads, low),
            scratch((2, rows, width), f32),
            scratch((rows, width), f32),
            scratch((2, rows, width), low),
            scratch((2, rows, width), low),
            scratch((n, own_rows, 2 * rows), low),
            scratch((2 * rows, 4 * half), f32),
            scratch((2, rows, width), low),
            scratch((n, own_rows, 2 * rows), low),
            scratch((2, own_rows, 4 * half), low),
            scratch((16, 128), f32),
            scratch((n, 16, 128), f32),
            scratch((1, 4 * half), f32),
            dma((6,)),
            dma((3,)),
            dma((5,)),
            dma((5,)),
            dma((n,)),
            dma((n,)),
            dma((n,)),
            dma((n,)),
            dma((3,)),
            dma((2,)),
            dma((2,)),
        ]
        + [dma((3, 4, line)), dma((3, 4, line + 1))] + [dma((3, 4, line))] * 4
        + reducer_scratch(1, line, own_rows, low),
        compiler_params=pltpu.CompilerParams(
            collective_id=collective_id, has_side_effects=True, vmem_limit_bytes=63 * 2**20),
        name="forward",
    )(*hbm_args, *vmem_args)


class Reducer:
    def __init__(self, line, grads, out, own, got_b, got_z, got_a, sems):
        self.line, self.grads, self.out = line, grads, out
        self.own, self.acc, self.got_z, self.got_a = own, got_b, got_z, got_a
        self.load, self.send_b, self.send_z, self.send_a, self.recv_b, self.recv_z, self.recv_a = sems
        self.me = me = Place(line)
        self.up, self.down = me.z < line - 1, me.z > 0
        self.above, self.below = me.dev(z=jnp.minimum(me.z + 1, line - 1)), me.dev(z=jnp.maximum(me.z - 1, 0))
        self.units = len(grads) * line

    def last(self, g):
        return "y" if GROUPS[g][3] == "x" else "x"

    def first(self, g):
        return self.me.x if GROUPS[g][3] == "x" else self.me.y

    def half(self, grad, g, zz, mine):
        cols = pl.ds(GROUPS[g][0], GROUPS[g][1])
        if self.last(g) == "y":
            return grad.at[zz, self.me.y if mine else 1 - self.me.y, :, :, cols]
        return grad.at[zz, :, self.me.x if mine else 1 - self.me.x, :, cols]

    def loading(self, u, g, zz, side, grad=None):
        grad = self.grads[0] if grad is None else grad
        return pltpu.make_async_copy(
            self.half(grad, g, zz, True), self.own[g].at[u % 3, side], self.load.at[u % 3, g, side])

    def remote(self, src, dst, send, recv, dev):
        return pltpu.make_async_remote_copy(
            src_ref=src, dst_ref=dst, send_sem=send, recv_sem=recv, device_id=dev, device_id_type=MESH)

    def b_copy(self, m, g, zz, grad=None):
        grad = self.grads[0] if grad is None else grad
        return self.remote(
            self.half(grad, g, zz, False), self.acc[g].at[m, zz], self.send_b.at[m, g, zz], self.recv_b.at[m, g, zz],
            self.me.peer(self.last(g)))

    def slot_a(self, g, zz):
        return zz if GROUPS[g][2] == 1 else 0

    def a_copy(self, m, g, zz):
        return self.remote(
            self.acc[g].at[m, zz, 1 - self.first(g)], self.got_a[g].at[m, self.slot_a(g, zz)], self.send_a.at[m, g, zz],
            self.recv_a.at[m, g, zz], self.me.peer(GROUPS[g][3]))

    def z_copy(self, m, g, zz, slot, dev):
        part = self.acc[g].at[m, zz] if GROUPS[g][2] == 0 else self.acc[g].at[m, zz, self.first(g)]
        return self.remote(part, self.got_z[g].at[m, slot], self.send_z.at[m, g, zz], self.recv_z.at[m, g, slot], dev)

    def add_b(self, m, g, zz, u, side):
        self.loading(u, g, zz, side).wait()
        self.b_copy(m, g, zz).wait_recv()
        self.acc[g][m, zz] = self.acc[g][m, zz] + self.own[g][u % 3, side]

    def add_z(self, m, g, zz, slot):
        acc, got = self.acc[g], self.got_z[g]
        self.z_copy(m, g, self.me.z, slot, self.below).wait_recv()
        if GROUPS[g][2] == 0:
            acc[m, zz] = acc[m, zz] + got[m, slot]
        else:
            acc[m, zz, self.first(g)] = acc[m, zz, self.first(g)] + got[m, slot]

    def add_a(self, m, g, zz):
        self.a_copy(m, g, zz).wait_recv()
        acc, first = self.acc[g], self.first(g)
        acc[m, zz, first] = acc[m, zz, first] + self.got_a[g][m, self.slot_a(g, zz)]

    def planes(self, k, fn):
        z, line = self.me.z, self.line
        when(z + k < line, lambda: fn(jnp.minimum(z + k, line - 1), True))
        when((z >= k) & (k > 0), lambda: fn(jnp.maximum(z - k, 0), False))

    def begin(self, v):
        m, j = v // self.line, v % self.line

        def one(grad, zz, upward):
            for g in range(4):
                self.b_copy(m, g, zz, grad).start()
                self.loading(v, g, zz, 0 if upward else 1, grad).start()

        for index, grad in enumerate(self.grads):
            when(m == index, lambda: self.planes(self.line - 1 - j, lambda zz, upward: one(grad, zz, upward)))

    def onward(self, m, g, zz, k, upward):
        if upward:
            when(self.down, lambda: self.add_z(m, g, zz, zz))
            self.z_copy(m, g, zz, zz, self.above).start()
        else:
            when(self.up, lambda: self.add_z(m, g, zz, zz))
            self.z_copy(m, g, zz, jnp.where(k == 1, self.line, zz), self.below).start()

    def near(self, u, m, j):
        k = self.line - 1 - j

        def one(zz, upward):
            for g in range(4):
                self.add_b(m, g, zz, u, 0 if upward else 1)
                if GROUPS[g][2] == 1:
                    self.a_copy(m, g, zz).start()
                else:
                    when(k > 0, lambda g=g: self.onward(m, g, zz, k, upward))

        self.planes(k, one)

    def far(self, m, j):
        k = self.line - j

        def one(zz, upward):
            for g in (2, 3):
                self.add_a(m, g, zz)
                self.onward(m, g, zz, k, upward)

        when((k > 0) & (k < self.line), lambda: self.planes(k, one))

    def close(self, m):
        z = self.me.z
        for g in (0, 1):
            when(self.down, lambda g=g: self.add_z(m, g, z, z))
            when(self.up, lambda g=g: self.add_z(m, g, z, self.line))
            self.a_copy(m, g, z).start()

    def final(self, m):
        z = self.me.z
        for g in range(4):
            cols = pl.ds(GROUPS[g][0], GROUPS[g][1])
            self.add_a(m, g, z)
            if GROUPS[g][2] == 1:
                when(self.down, lambda g=g: self.add_z(m, g, z, z))
                when(self.up, lambda g=g: self.add_z(m, g, z, self.line))
            self.out[m, :, cols] = self.acc[g][m, z, self.first(g)]

    def unit(self, u):
        line = self.line
        m, j = u // line, u % line
        self.near(u, m, j)
        self.far(m, j)
        when(j == line - 1, lambda: self.close(m))
        if len(self.grads) > 1:
            when((j == 0) & (m > 0), lambda: self.final(jnp.maximum(m - 1, 0)))

    def begin_some(self, first, last):
        @pl.loop(first, last)
        def _(v):
            self.begin(v)

    def unit_some(self, first, last):
        @pl.loop(first, last)
        def _(u):
            self.unit(u)

    def drain(self):
        z = self.me.z

        @pl.loop(0, len(self.grads))
        def _(m):
            @pl.loop(0, self.line)
            def _(zz):
                for g in range(4):
                    self.b_copy(m, g, zz).wait_send()
                    if GROUPS[g][2] == 1:
                        self.a_copy(m, g, zz).wait_send()
                    when(zz != z, lambda g=g: self.z_copy(m, g, zz, zz, self.above).wait_send())
            for g in (0, 1):
                self.a_copy(m, g, z).wait_send()


def reducer_scratch(count, line, rows, dt):
    dma = pltpu.SemaphoreType.DMA
    own = [pltpu.VMEM((3, 2, 2, rows, GROUPS[g][1]), dt) for g in range(4)]
    got_b = [pltpu.VMEM((count, line, 2, rows, GROUPS[g][1]), dt) for g in range(4)]
    got_z = [pltpu.VMEM((count, line + 1) + ((2,) if GROUPS[g][2] == 0 else ()) + (rows, GROUPS[g][1]), dt) for g in range(4)]
    got_a = [pltpu.VMEM((count, line if GROUPS[g][2] == 1 else 1, rows, GROUPS[g][1]), dt) for g in range(4)]
    sems = [dma((3, 4, 2))] + [dma((count, 4, line))] * 4 + [dma((count, 4, line + 1))] + [dma((count, 4, line))]
    return own + got_b + got_z + got_a + sems


def make_reducer(line, grads, out, refs):
    return Reducer(line, grads, out, refs[:4], refs[4:8], refs[8:12], refs[12:16], refs[16:])


def backward_kernel(line, *refs):
    (weights, g_expand, h1_t, act, d_z, sums, out_contract, q, k, v, o, key_ok, x, middle, attended, cot, row_ok, pieces,
     biases, modulation, cond, silu, same) = refs[:23]
    (g_attn, d_mod_all, cond_all, both, block_out, tokens_grad, bias_grad, norm_out, factor_out) = refs[23:32]
    (w, rhs, d_o, d_q, d_k, d_v, d_h, d_h_got, branch_got, d_mid, d_att, d_att_t, stage, dp, dp_got, msg, msg_got, d_mod, vec,
     vec_got, d_silu, d_silu_got, chunk, out, bias_sum, d_cond, squares, squares_got, table_squares, squares_pair, cond_some, bias_all,
     mod_sums, vec_all, w_sem,
     mod_sem, stage_sem, pair_send, pair_recv, msg_send, msg_recv, vec_send, vec_recv, cond_send, cond_recv, bias_send, bias_recv, square_send,
     square_recv) = refs[32:81]
    n = line * 4
    low, f32 = jnp.bfloat16, jnp.float32
    me, c = lax.axis_index("dp"), lax.axis_index("seq")
    red = make_reducer(line, (g_expand, g_attn), out, refs[81:])
    rows, width = x.shape
    half = weights.shape[2] // 4
    heads = half // HEAD_DIM
    edge = 3 * half // 128 * 128
    tiles = width // 128

    def swap(i, src, dst):
        return pltpu.make_async_remote_copy(
            src_ref=src, dst_ref=dst, send_sem=pair_send.at[i], recv_sem=pair_recv.at[i], device_id=(me, 1 - c),
            device_id_type=MESH)

    def fetch(i):
        return pltpu.make_async_copy(weights.at[(1, 0, 2)[i]], w, w_sem.at[i])

    def back(values, lanes):
        @pl.loop(0, tiles)
        def _(t):
            cols = pl.ds(pl.multiple_of(t * 128, 128), 128)
            part = dot(values[...], w[cols, :lanes], 1, 1)
            d_h[0, :, cols] = part[:rows]
            d_h[1, :, cols] = part[rows:]

    def column_sums(values):
        return jnp.sum(values.astype(f32), axis=0, keepdims=True)

    def norm_back(values, scale, d_n):
        centre = values - jnp.mean(values, axis=-1, keepdims=True)
        inv = lax.rsqrt(jnp.mean(centre * centre, axis=-1, keepdims=True) + LAYER_EPS)
        normed = centre * inv
        e = d_n * (1.0 + scale)
        d_x = (e - jnp.mean(e, axis=-1, keepdims=True) - normed * jnp.mean(e * normed, axis=-1, keepdims=True)) * inv
        return d_x, jnp.sum(d_n, axis=0, keepdims=True), jnp.sum(d_n * normed, axis=0, keepdims=True)

    def piece(i):
        return pieces[i // 3, :, i % 3 * width : (i % 3 + 1) * width]

    fetch(0).start()
    bar = greet_all(n)
    for item in (d_q, d_k, d_v):
        item[...] = jnp.zeros_like(item)
    dp[...] = jnp.zeros_like(dp)
    vec[...] = sums[...]
    pl.semaphore_wait(bar, n)

    def hidden_back():
        fetch(0).wait()
        back(d_z, 4 * half)
        swap(0, d_h.at[1 - c], d_h_got).start()
        fetch(1).start()

    def middle_back():
        swap(0, d_h.at[1 - c], d_h_got).wait()
        d_x, shift, scale = norm_back(middle[...], piece(4), d_h[c] + d_h_got[...])
        d_mid[...] = d_x + cot[...].astype(f32) * row_ok[...]
        dp[2:3] = jnp.sum(d_mid[...] * attended[...], axis=0, keepdims=True)
        dp[3:4] = shift
        dp[4:5] = scale
        d_att[c] = (piece(2) * d_mid[...]).astype(low)
        swap(1, d_att.at[c], d_att.at[c]).start()

    def mixed_back():
        swap(1, d_att.at[c], d_att.at[c]).wait()
        d_all = jnp.concatenate([d_att[0], d_att[1]], axis=0)
        to_blocks(d_all, d_att_t)
        vec[3:4] = column_sums(d_att[0]) + column_sums(d_att[1])
        fetch(1).wait()
        d_o[:, :half] = dot(d_all, w[:, edge:])[:, 3 * half - edge :].astype(low)
        d_o[:, half:] = jnp.zeros((2 * rows, d_o.shape[1] - half), low)

    seen = jnp.broadcast_to(key_ok[...], (2 * rows, 2 * rows)) > 0.0

    def head(h):
        win, lanes = head_window(h)
        qh, kh, doh = q[:, win] * lanes, k[:, win] * lanes, d_o[:, win] * lanes
        probs = head_probs(qh, kh, seen)
        d_probs = dot(doh, v[:, win], 1, 1)
        inner = jnp.sum(probs * d_probs, axis=-1, keepdims=True)
        d_logits = (probs * (d_probs - inner)).astype(low)
        d_q[:, win] = d_q[:, win] + dot(d_logits, kh) * HEAD_DIM ** (-0.5)
        d_k[:, win] = d_k[:, win] + dot(d_logits, qh, 0, 0) * HEAD_DIM ** (-0.5)
        d_v[:, win] = d_v[:, win] + dot(probs.astype(low), doh, 0, 0)

    def attention_grads():
        for i, item in enumerate((d_q, d_k, d_v)):
            rhs[: 2 * rows, i * half : (i + 1) * half] = item[:, :half].astype(low)
        rhs[: 2 * rows, 3 * half :] = jnp.zeros((2 * rows, half), low)
        rhs[2 * rows :, edge : 3 * half] = jnp.zeros((2 * rows, 3 * half - edge), low)
        rhs[2 * rows :, 3 * half :] = o[:, :half]
        sums = column_sums(rhs[: 2 * rows, : 3 * half])
        vec[0:1, :half] = sums[:, :half]
        vec[0:1, half:] = sums[:, 2 * half :]

        def block(i):
            left = dot(h1_t[i], rhs[: 2 * rows, :edge])
            right = dot(h1_t[i], rhs[: 2 * rows, edge:]) + dot(d_att_t[i], rhs[2 * rows :, edge:])
            return jnp.concatenate([left, right], axis=1)

        write_blocks(n, g_attn, stage, stage_sem, block)

    def input_back():
        back(rhs.at[: 2 * rows, : edge + 128], edge + 128)
        swap(2, d_h.at[1 - c], d_h_got).start()
        fetch(2).start()

    def first_back():
        swap(2, d_h.at[1 - c], d_h_got).wait()
        d_x, shift, scale = norm_back(x[...], piece(1), d_h[c] + d_h_got[...])
        tokens_grad[...] = (d_x + d_mid[...]).astype(low)
        dp[0:1] = shift
        dp[1:2] = scale
        fetch(2).wait()
        back(act, 4 * half)
        swap(3, d_h.at[1 - c], branch_got).start()

    def branch_out():
        swap(3, d_h.at[1 - c], branch_got).wait()
        branch = d_h[c] + branch_got[...] + biases[:, 9 * width + 8 * half :]
        result = middle[...] + piece(5) * branch
        block_out[...] = jnp.where(jnp.broadcast_to(row_ok[...], result.shape) > 0.0, result, 0.0).astype(low)
        dp[5:6] = jnp.sum(cot[...].astype(f32) * row_ok[...] * branch, axis=0, keepdims=True)
        swap(4, dp, dp_got).start()

    msg_start, msg_wait = all_peers(n, msg, msg_got, msg_send, msg_recv, False)
    vec_start, vec_wait = all_peers(n, chunk, vec_got, vec_send, vec_recv, True)
    per = chunk_tiles(n, width)

    def send_mod():
        swap(4, dp, dp_got).wait()
        total = (dp[...] + dp_got[...]).astype(low).astype(f32)
        own = jnp.where(c == 0, total[0:3], total[3:6])
        for r in range(3):
            msg[r] = own[r : r + 1]
        msg_got[me] = msg[...]
        chunk[...] = jnp.zeros_like(chunk)
        for t in range(5 * tiles):
            chunk[t // per, t % per] = vec[t // tiles : t // tiles + 1, t % tiles * 128 : t % tiles * 128 + 128]
        vec_got[me] = chunk[me]
        msg_start()
        vec_start()

    keep_mod = pltpu.make_async_copy(d_mod, d_mod_all.at[c], mod_sem.at[0])
    keep_cond = pltpu.make_async_copy(d_cond, cond_all.at[me], mod_sem.at[2])

    def mod_grad():
        msg_wait()
        vec_wait()

        @pl.loop(0, n)
        def _(s):
            for r in range(3):
                d_mod[pl.ds(s, 1), r * width : (r + 1) * width] = msg_got[s, r]

        bias_sum[c] = jnp.zeros((8, 128), f32)
        for r in range(per):
            bias_sum[c, r : r + 1] = jnp.sum(vec_got[:, r], axis=0)
        d_silu[...] = dot(d_mod[...].astype(low), modulation[...], 1, 1)
        swap(5, d_silu, d_silu_got).start()
        swap(6, d_mod, d_mod_all.at[c]).start()
        swap(7, bias_sum.at[c], bias_sum.at[c]).start()
        keep_mod.start()

    cond_start, cond_wait = all_peers(n, d_cond, cond_all, cond_send, cond_recv, False)
    bias_start, bias_wait = all_peers(n, bias_sum, bias_all, bias_send, bias_recv, False)
    square_start, square_wait = all_peers(n, squares, squares_got, square_send, square_recv, False)

    def cond_grad():
        swap(5, d_silu, d_silu_got).wait()
        swap(6, d_mod, d_mod_all.at[c]).wait()
        swap(7, bias_sum.at[c], bias_sum.at[c]).wait()
        keep_mod.wait()
        gate = 1.0 / (1.0 + jnp.exp(-cond[...]))
        d_cond[...] = (d_silu[...] + d_silu_got[...]) * (gate + cond[...] * gate * (1.0 - gate))
        keep_cond.start()
        bias_all[me] = bias_sum[...]
        cond_start()
        bias_start()
        d_low = d_mod[...].astype(low)
        grad = dot(silu[...], d_low, 0, 0)[: out.shape[1]]
        sums = jnp.sum(d_mod[...], axis=0, keepdims=True)
        mod_sums[c] = sums
        swap(12, mod_sums.at[c], mod_sums.at[c]).start()
        tile = per * me + lax.broadcasted_iota(jnp.int32, (8, 128), 0)
        counted = (tile < 3 * tiles) | (c == 0)
        total = jnp.sum(grad * grad) + jnp.where(me == 0, jnp.sum(sums * sums), 0.0)
        total = total + jnp.sum(jnp.where(counted, bias_sum[c] * bias_sum[c], 0.0))
        squares[...] = jnp.full((8, 128), total, f32)

    def table_norm():
        cond_wait()
        bias_wait()
        keep_cond.wait()
        swap(12, mod_sums.at[c], mod_sums.at[c]).wait()
        for core in range(2):
            bias_grad[:, 3 * core * width : 3 * (core + 1) * width] = mod_sums[core]
            for t in range(5 * tiles):
                vec_all[core, :, 128 * t : 128 * t + 128] = bias_all[t // per, core, t % per : t % per + 1]
            start = 6 * width + core * half
            bias_grad[:, start : start + half] = vec_all[core, :, :half]
            bias_grad[:, start + width : start + width + half] = vec_all[core, :, half:width]
            start = 9 * width + core * 4 * half
            bias_grad[:, start : start + 4 * half] = vec_all[core, :, width : 3 * width]
        bias_grad[:, 8 * width : 9 * width] = vec_all[0, :, 3 * width : 4 * width]
        bias_grad[:, 9 * width + 8 * half :] = vec_all[0, :, 4 * width :]
        table_squares[...] = jnp.zeros((8, 128), f32)
        size = cond_some.shape[0]

        @pl.loop(0, n // size)
        def _(j):
            some = pltpu.make_async_copy(cond_all.at[pl.ds(j * size, size)], cond_some, mod_sem.at[1])
            some.start()
            some.wait()
            gram = jnp.zeros((n, n), f32)
            for i in range(size):
                part = cond_some[i]
                gram = gram + lax.dot_general(
                    part, part, (((1,), (1,)), ((), ())), preferred_element_type=f32, precision=lax.Precision.HIGHEST)
            table_squares[...] = table_squares[...] + jnp.sum(gram * same[...])

    def share(m):
        return swap(8 + m, out_contract.at[0] if m == 0 else out.at[m - 1], both.at[c, m])

    def reduced(m):
        value = out_contract[0] if m == 0 else out[m - 1]
        both[c, m] = value
        share(m).start()
        value = value.astype(f32)
        squares[...] = squares[...] + jnp.sum(value * value)

    parts = (hidden_back, middle_back, mixed_back) + (None,) * heads
    parts += (attention_grads, input_back, first_back, branch_out, send_mod, mod_grad, cond_grad, table_norm)
    first_head = parts.index(None)
    begun, carried = ([places[u // line * 4 + u % line * 4 // line] for u in range(red.units)] for places in UNIT_PLACES)

    def upto(places, s):
        total = jnp.int32(0)
        for place in places:
            total = total + (place <= s).astype(jnp.int32)
        return total

    @pl.loop(0, len(parts) + 1)
    def _(s):
        @pl.loop(upto(begun, s - 1), upto(begun, s))
        def _(v):
            red.begin(v)

        @pl.loop(upto(carried, s - 1), upto(carried, s))
        def _(u):
            red.unit(u)

        when((s >= first_head) & (s < first_head + heads), lambda: head(s - first_head))
        for i, part in enumerate(parts):
            if part is not None:
                when(s == i, part)

    reduced(0)
    reduced(1)
    red.final(1)
    reduced(2)
    squares_got[me] = squares[...]
    square_start()
    red.drain()
    square_wait()
    squares[...] = jnp.sum(squares_got[...], axis=0)
    swap(11, squares, squares_pair).start()
    for m in range(3):
        share(m).wait()
    swap(11, squares, squares_pair).wait()
    norm = jnp.sqrt(squares[...] + squares_pair[...] + table_squares[...])
    norm_out[...] = norm[:1, :1]
    factor_out[...] = jnp.minimum(1.0, CLIP_LIMIT / (norm + 1e-06))


def chunk_tiles(n, width):
    return -(-5 * (width // 128) // n)


def backward(hbm_args, vmem_args, n, collective_id):
    line = n // 4
    grad = hbm_args[1]
    rows, cols = grad.shape[-2:]
    heads = vmem_args[5].shape
    own, width = vmem_args[10].shape
    all_rows = 2 * own
    low, f32 = jnp.bfloat16, jnp.float32
    dma = pltpu.SemaphoreType.DMA
    vmem, hbm = pl.BlockSpec(memory_space=pltpu.VMEM), pl.BlockSpec(memory_space=pltpu.HBM)
    per = chunk_tiles(n, width)
    return pl.pallas_call(
        functools.partial(backward_kernel, line),
        out_shape=[
            jax.ShapeDtypeStruct(grad.shape, low),
            jax.ShapeDtypeStruct((2, n, 3 * width), f32),
            jax.ShapeDtypeStruct((n, n, 128), f32),
            jax.ShapeDtypeStruct((2, 3, rows, cols), low),
            jax.ShapeDtypeStruct((own, width), low),
            jax.ShapeDtypeStruct((own, width), low),
            jax.ShapeDtypeStruct(vmem_args[16].shape, f32),
            jax.ShapeDtypeStruct((1, 1), f32),
            jax.ShapeDtypeStruct((8, 128), f32),
        ],
        in_specs=[hbm] * len(hbm_args) + [vmem] * len(vmem_args),
        out_specs=[hbm] * 3 + [vmem] * 6,
        scratch_shapes=[
            pltpu.VMEM((width, cols), low),
            pltpu.VMEM((2 * all_rows, cols), low),
            pltpu.VMEM(heads, low),
            pltpu.VMEM(heads, f32),
            pltpu.VMEM(heads, f32),
            pltpu.VMEM(heads, f32),
            pltpu.VMEM((2, own, width), f32),
            pltpu.VMEM((own, width), f32),
            pltpu.VMEM((own, width), f32),
            pltpu.VMEM((own, width), f32),
            pltpu.VMEM((2, own, width), low),
            pltpu.VMEM((n, rows, all_rows), low),
            pltpu.VMEM((2, rows, cols), low),
            pltpu.VMEM((8, width), f32),
            pltpu.VMEM((8, width), f32),
            pltpu.VMEM((3, 1, width), f32),
            pltpu.VMEM((n, 3, 1, width), f32),
            pltpu.VMEM((n, 3 * width), f32),
            pltpu.VMEM((8, width), f32),
            pltpu.VMEM((n, per, 1, 128), f32),
            pltpu.VMEM((n, 128), f32),
            pltpu.VMEM((n, 128), f32),
            pltpu.VMEM((n, per, 1, 128), f32),
            pltpu.VMEM((2, rows, cols), low),
            pltpu.VMEM((2, 8, 128), f32),
            pltpu.VMEM((n, 128), f32),
            pltpu.VMEM((8, 128), f32),
            pltpu.VMEM((n, 8, 128), f32),
            pltpu.VMEM((8, 128), f32),
            pltpu.VMEM((8, 128), f32),
            pltpu.VMEM((min(n, 16), n, 128), f32),
            pltpu.VMEM((n, 2, 8, 128), f32),
            pltpu.VMEM((2, 1, 3 * width), f32),
            pltpu.VMEM((2, 1, 5 * width), f32),
            dma((3,)),
            dma((3,)),
            dma((2,)),
            dma((13,)),
            dma((13,)),
        ]
        + [dma((n,))] * 10
        + reducer_scratch(2, line, rows, low),
        compiler_params=pltpu.CompilerParams(
            collective_id=collective_id, has_side_effects=True, vmem_limit_bytes=63 * 2**20),
        name="backward",
    )(*hbm_args, *vmem_args)


def adam_step(grad, master, first, second, rate):
    first_new = BETA_FIRST * first + (1.0 - BETA_FIRST) * grad
    second_new = BETA_SECOND * second + (1.0 - BETA_SECOND) * grad * grad
    first_hat = first_new / (1.0 - BETA_FIRST**STEP)
    second_hat = second_new / (1.0 - BETA_SECOND**STEP)
    master_new = master - rate * (
        first_hat / (jnp.sqrt(second_hat) + ADAM_EPS) + WEIGHT_DECAY * master
    )
    return (first_new, second_new, master_new)


def chunk_rows(rows):
    sizes = [d for d in range(8, 257, 8) if rows % d == 0]
    return sizes[-1] if sizes else rows


def adam_kernel(n, rates, *refs):
    kinds = len(rates)
    factor_ref, both, silu, d_mod, cond_all, onehot = refs[:6]
    at = 6
    states = [refs[at + 3 * a : at + 3 * a + 3] for a in range(kinds)]
    at += 3 * kinds
    news = [refs[at + 3 * a : at + 3 * a + 3] for a in range(kinds)]
    at += 3 * kinds
    held, flat = refs[at : at + kinds], refs[at + kinds : at + 2 * kinds]
    wide, in_sem, out_sem = refs[at + 2 * kinds :]
    rows, half = both.shape[2:]
    head = half // 4
    order = (3, 4, 0, 1, 2, 5)

    def loads(a):
        return [pltpu.make_async_copy(states[a][k], held[a].at[k], in_sem.at[a, k]) for k in range(3)]

    for a in order:
        for copy in loads(a):
            copy.start()

    def spread(a, width, count=rows):
        tiles = width // 128
        for t in range(tiles):
            flat[a][pl.ds(t, count, stride=tiles), :] = wide[:count, 128 * t : 128 * t + 128]

    def gradient(a):
        if a == 0:
            part = d_mod.shape[2]
            for core in range(2):
                grad = dot(silu[...], d_mod[core].astype(silu.dtype), 0, 0)
                wide[:, core * part : (core + 1) * part] = grad[:rows]
            spread(a, 2 * part)
        elif a == 1:
            for core in range(2):
                for part in range(3):
                    lo = (2 * part + core) * head
                    wide[:, lo : lo + head] = both[core, 2, :, part * head : (part + 1) * head].astype(jnp.float32)
            spread(a, 6 * head)
        elif a == 2:
            for core in range(2):
                wide[:, core * head : (core + 1) * head] = both[core, 2, :, 3 * head :].astype(jnp.float32)
            spread(a, 2 * head)
        elif a == 5:
            count = onehot.shape[1]
            for i in range(n):
                wide[:count, i * rows : (i + 1) * rows] = lax.dot_general(
                    onehot[...], cond_all[i], (((0,), (0,)), ((), ())), preferred_element_type=jnp.float32,
                    precision=lax.Precision.HIGHEST)[:, :rows]
            spread(a, n * rows, count)
        else:
            for core in range(2):
                wide[:, core * half : (core + 1) * half] = both[core, 4 - a].astype(jnp.float32)
            spread(a, 2 * half)

    factor = factor_ref[:1, :]
    for a in order:
        gradient(a)
        for copy in loads(a):
            copy.wait()
        size = chunk_rows(flat[a].shape[0])

        @pl.loop(0, flat[a].shape[0] // size)
        def _(i, a=a, size=size):
            part = pl.ds(pl.multiple_of(i * size, size), size)
            grad = flat[a][part] * factor
            master, first, second = held[a][0, part], held[a][1, part], held[a][2, part]
            first, second, master = adam_step(grad, master, first, second, rates[a])
            held[a][0, part], held[a][1, part], held[a][2, part] = master, first, second
            for k in range(3):
                pltpu.make_async_copy(held[a].at[k, part], news[a][k].at[part], out_sem.at[a, k]).start()

    for a in range(kinds):
        for k in range(3):
            pltpu.make_async_copy(held[a].at[k], news[a][k], out_sem.at[a, k]).wait()


def adam(factor, both, silu, d_mod, cond_all, onehot, states, rates, n):
    vmem, hbm = pl.BlockSpec(memory_space=pltpu.VMEM), pl.BlockSpec(memory_space=pltpu.HBM)
    dma = pltpu.SemaphoreType.DMA
    kinds = len(states)
    flats = [jax.ShapeDtypeStruct(s[0].shape, jnp.float32) for s in states]
    news = pl.pallas_call(
        functools.partial(adam_kernel, n, rates),
        out_shape=[f for f in flats for _ in range(3)],
        in_specs=[vmem] * 6 + [hbm] * (3 * kinds),
        out_specs=[hbm] * (3 * kinds),
        scratch_shapes=[pltpu.VMEM((3,) + f.shape, jnp.float32) for f in flats]
        + [pltpu.VMEM(f.shape, jnp.float32) for f in flats]
        + [pltpu.VMEM((both.shape[2], 2 * d_mod.shape[2]), jnp.float32), dma((kinds, 3)), dma((kinds, 3))],
        compiler_params=pltpu.CompilerParams(vmem_limit_bytes=56 * 2**20),
        name="adam",
    )(factor, both, silu, d_mod, cond_all, onehot, *[item for s in states for item in s])
    order = [3 * a + k for a in range(kinds) for k in (1, 2, 0)]
    return [news[i] for i in order]


def per_device(
    tokens,
    cotangent,
    time_vec,
    labels,
    kept,
    keep_index,
    modulation_master,
    modulation_first,
    modulation_second,
    attention_in_master,
    attention_in_first,
    attention_in_second,
    attention_out_master,
    attention_out_first,
    attention_out_second,
    expand_master,
    expand_first,
    expand_second,
    contract_master,
    contract_first,
    contract_second,
    class_table_master,
    class_table_first,
    class_table_second,
    biases_master,
    biases_first,
    biases_second,
):
    rows, width = tokens.shape[1:]
    n, pairs = lax.axis_size("dp"), lax.axis_size("seq")
    me = lax.axis_index("dp")
    half_width = width // pairs
    low = jnp.bfloat16

    bias_share = biases_master.shape[0]
    quarter = width // 4
    freqs = np.float32(10000.0) ** (-np.arange(quarter, dtype=np.float32) / np.float32(quarter))
    (weights, _, grad_expand, _, normed_in, queries, keys, values, mixed, attended, middle, activated, d_hidden, sums, contract_sum,
     pieces, cond_own, silu_own, own_modulation, inputs, key_ok, row_ok, onehot, same, biases) = forward(
        [
            item.reshape(-1, 128)
            for item in (
                attention_in_master,
                attention_out_master,
                expand_master,
                contract_master,
                class_table_master,
                modulation_master,
            )
        ],
        [
            biases_master[None],
            jnp.stack([labels, kept], axis=1),
            time_vec,
            tokens[0],
            keep_index,
            jnp.asarray(freqs)[None],
            cotangent[0],
        ],
        bias_share * n,
        n,
        1,
    )
    _, d_mod_all, cond_all, reduced, block_out, tokens_grad, grad_biases, norm, clip = backward(
        [weights.reshape(3, width, 4 * half_width), grad_expand],
        [
            normed_in,
            activated,
            d_hidden,
            sums,
            contract_sum,
            queries,
            keys,
            values,
            mixed,
            key_ok,
            inputs,
            middle,
            attended,
            cotangent[0],
            row_ok,
            pieces,
            biases,
            own_modulation,
            cond_own,
            silu_own,
            same,
        ],
        n,
        2,
    )
    block_out, tokens_grad, grad_norm = block_out[None], tokens_grad[None], norm.reshape(())
    rates = (
        width ** (-0.5),
        width ** (-0.5),
        (width // 4) ** (-0.5),
        width ** (-0.5),
        FF ** (-0.5),
        0.5,
        0.2,
    )
    masters = (
        modulation_master,
        attention_in_master,
        attention_out_master,
        expand_master,
        contract_master,
        class_table_master,
        biases_master,
    )
    firsts = (
        modulation_first,
        attention_in_first,
        attention_out_first,
        expand_first,
        contract_first,
        class_table_first,
        biases_first,
    )
    seconds = (
        modulation_second,
        attention_in_second,
        attention_out_second,
        expand_second,
        contract_second,
        class_table_second,
        biases_second,
    )
    states = list(zip(masters, firsts, seconds))
    updated = adam(
        clip,
        reduced,
        silu_own,
        d_mod_all,
        cond_all,
        onehot,
        [tuple(item.reshape(-1, 128) for item in state) for state in states[:-1]],
        rates[:-1],
        n,
    )
    bias_grad = lax.dynamic_slice_in_dim(grad_biases[0], me * bias_share, bias_share, 0) * clip.reshape(-1)[:bias_share]
    updated = [item.reshape(-1) for item in updated] + list(adam_step(bias_grad, *states[-1], rates[-1]))
    return (block_out, tokens_grad, grad_norm) + tuple(updated)


def solution(mesh):
    return jax.shard_map(
        per_device,
        mesh=mesh,
        in_specs=(
            P("dp", "seq", None),
            P("dp", "seq", None),
            P("dp", None),
            P("dp"),
            P("dp"),
            P("dp", "seq"),
            P("dp"),
            P("dp"),
            P("dp"),
            P("dp"),
            P("dp"),
            P("dp"),
            P("dp"),
            P("dp"),
            P("dp"),
            P("dp"),
            P("dp"),
            P("dp"),
            P("dp"),
            P("dp"),
            P("dp"),
            P("dp"),
            P("dp"),
            P("dp"),
            P("dp"),
            P("dp"),
            P("dp"),
        ),
        out_specs=(
            P("dp", "seq", None),
            P("dp", "seq", None),
            P(),
            P("dp"),
            P("dp"),
            P("dp"),
            P("dp"),
            P("dp"),
            P("dp"),
            P("dp"),
            P("dp"),
            P("dp"),
            P("dp"),
            P("dp"),
            P("dp"),
            P("dp"),
            P("dp"),
            P("dp"),
            P("dp"),
            P("dp"),
            P("dp"),
            P("dp"),
            P("dp"),
            P("dp"),
        ),
        check_vma=False,
    )
```

```python
import functools
import jax
import jax.numpy as jnp
from jax import lax
from jax.experimental import pallas as pl
from jax.experimental.pallas import tpu as pltpu
import numpy as np
from jax.sharding import PartitionSpec as P

HEAD_DIM = 72
FF = 4608
SIDE = 16
CLASSES = 1024
STEP = 10
LAYER_EPS = 1e-06
MASK_FILL = -1e30
BETA_FIRST = 0.5
BETA_SECOND = 0.5
ADAM_EPS = 1e-08
WEIGHT_DECAY = 0.1
CLIP_LIMIT = 1.0

MESH = pl.DeviceIdType.MESH
GELU_A = (2.0 / 3.141592653589793) ** 0.5
GELU_B = 0.044715
UNIT_PLACES = ((0, 0, 2, 10, 12, 13, 14, 15), (1, 3, 11, 12, 14, 15, 16, 18))
GROUPS = ((0, 640, 0, "x"), (640, 640, 0, "y"), (1280, 512, 1, "x"), (1792, 512, 1, "y"))


def when(cond, fn):
    pl.when(cond)(fn)


class Place:
    def __init__(self, line):
        self.line = line
        i = lax.axis_index("dp")
        self.c = lax.axis_index("seq")
        self.x, self.y, self.z = i % 2, (i // 2) % 2, i // 4

    def dev(self, z=None, y=None, x=None):
        z = self.z if z is None else z
        y = self.y if y is None else y
        x = self.x if x is None else x
        return (z * 4 + y * 2 + x, self.c)

    def peer(self, axis):
        return self.dev(x=1 - self.x) if axis == "x" else self.dev(y=1 - self.y)

    def barrier(self):
        bar = pltpu.get_barrier_semaphore()

        def sig(dev):
            pl.semaphore_signal(bar, inc=1, device_id=dev, device_id_type=MESH)

        sig(self.peer("x"))
        sig(self.peer("y"))
        when(self.z > 0, lambda: sig(self.dev(z=self.z - 1)))
        when(self.z < self.line - 1, lambda: sig(self.dev(z=self.z + 1)))
        pl.semaphore_wait(bar, 2 + (self.z > 0).astype(jnp.int32) + (self.z < self.line - 1).astype(jnp.int32))


class Gatherer:
    def __init__(self, line, own, out, keep_sem, sems):
        self.line, self.own, self.out, self.keep_sem = line, own, out, keep_sem
        self.send_a, self.send_z, self.send_b, self.recv_a, self.recv_z, self.recv_b = sems
        self.me = Place(line)
        self.up, self.down = self.me.z < line - 1, self.me.z > 0

    def single(self, m, g, zz):
        lo, width = GROUPS[g][:2]
        return self.out.at[m, zz, self.me.y, self.me.x, :, pl.ds(lo, width)]

    def pair(self, m, g, zz):
        lo, width, _, first = GROUPS[g]
        if first == "x":
            return self.out.at[m, zz, self.me.y, :, :, pl.ds(lo, width)]
        return self.out.at[m, zz, :, self.me.x, :, pl.ds(lo, width)]

    def remote(self, ref, send, recv, dev, source):
        return pltpu.make_async_remote_copy(
            src_ref=ref if source is None else source, dst_ref=ref, send_sem=send, recv_sem=recv,
            device_id=dev, device_id_type=MESH)

    def source(self, m, g):
        lo, width = GROUPS[g][:2]
        return self.own.at[m, :, pl.ds(lo, width)]

    def a_copy(self, m, g, zz, source=None):
        return self.remote(
            self.single(m, g, zz), self.send_a.at[m, g, zz], self.recv_a.at[m, g, zz], self.me.peer(GROUPS[g][3]), source)

    def z_ref(self, m, g, zz):
        return self.pair(m, g, zz) if GROUPS[g][2] == 0 else self.single(m, g, zz)

    def u_copy(self, m, g, zz, source=None):
        dev = self.me.dev(z=jnp.minimum(self.me.z + 1, self.line - 1))
        return self.remote(self.z_ref(m, g, zz), self.send_z.at[m, g, zz], self.recv_z.at[m, g, zz], dev, source)

    def d_copy(self, m, g, zz, source=None):
        dev = self.me.dev(z=jnp.maximum(self.me.z - 1, 0))
        sem = self.send_z.at[m, g, jnp.where(zz == self.me.z, self.line, zz)]
        return self.remote(self.z_ref(m, g, zz), sem, self.recv_z.at[m, g, zz], dev, source)

    def b_copy(self, m, g, zz):
        last = "y" if GROUPS[g][3] == "x" else "x"
        return self.remote(self.pair(m, g, zz), self.send_b.at[m, g, zz], self.recv_b.at[m, g, zz], self.me.peer(last), None)

    def keep(self, m):
        me = self.me
        return pltpu.make_async_copy(self.own.at[m], self.out.at[m, me.z, me.y, me.x], self.keep_sem.at[m])

    def begin(self, m):
        z = self.me.z
        self.keep(m).start()
        for g in range(4):
            self.a_copy(m, g, z, self.source(m, g)).start()
        for g in (2, 3):
            when(self.up, lambda g=g: self.u_copy(m, g, z, self.source(m, g)).start())
            when(self.down, lambda g=g: self.d_copy(m, g, z, self.source(m, g)).start())

    def paired(self, m):
        z = self.me.z
        self.keep(m).wait()
        for g in (0, 1):
            self.a_copy(m, g, z).wait_recv()
            when(self.up, lambda g=g: self.u_copy(m, g, z).start())
            when(self.down, lambda g=g: self.d_copy(m, g, z).start())
            self.b_copy(m, g, z).start()

    def arrive(self, m, zz, upward):
        for g in range(4):
            copy = self.u_copy if upward else self.d_copy
            copy(m, g, zz).wait_recv()
            when(self.up if upward else self.down, lambda g=g: copy(m, g, zz).start())
            if GROUPS[g][2] == 0:
                self.b_copy(m, g, zz).start()
            else:
                self.a_copy(m, g, zz).start()

    def crossed(self, m, zz):
        for g in (2, 3):
            self.a_copy(m, g, zz).wait_recv()
            self.b_copy(m, g, zz).start()

    def step(self, m, k):
        z, line = self.me.z, self.line
        when(k <= z, lambda: self.arrive(m, jnp.maximum(z - k, 0), True))
        when(z + k < line, lambda: self.arrive(m, jnp.minimum(z + k, line - 1), False))
        when(k - 1 <= z, lambda: self.crossed(m, jnp.maximum(z - k + 1, 0)))
        when((k > 1) & (z + k - 1 < line), lambda: self.crossed(m, jnp.minimum(z + k - 1, line - 1)))

    def steps(self, m, first, last):
        @pl.loop(first, last + 1)
        def _(k):
            self.step(m, k)

    def complete(self, m):
        @pl.loop(0, self.line)
        def _(zz):
            for g in range(4):
                self.b_copy(m, g, zz).wait_recv()

    def drain(self, m):
        z = self.me.z

        @pl.loop(0, self.line)
        def _(zz):
            for g in range(4):
                self.b_copy(m, g, zz).wait_send()
                if GROUPS[g][2] == 1:
                    self.a_copy(m, g, zz).wait_send()
                when(self.up & (zz <= z), lambda g=g: self.u_copy(m, g, zz).wait_send())
                when(self.down & (zz >= z), lambda g=g: self.d_copy(m, g, zz).wait_send())

        for g in (0, 1):
            self.a_copy(m, g, z).wait_send()


def dot(left, right, a=1, b=0):
    return lax.dot_general(left, right, (((a,), (b,)), ((), ())), preferred_element_type=jnp.float32)


def normal(values):
    centre = values - jnp.mean(values, axis=-1, keepdims=True)
    return centre * lax.rsqrt(jnp.mean(centre * centre, axis=-1, keepdims=True) + LAYER_EPS)


def all_peers(n, src, dst, send, recv, spread):
    me, c = lax.axis_index("dp"), lax.axis_index("seq")

    def copy(j, there, slot):
        return pltpu.make_async_remote_copy(
            src_ref=src.at[there] if spread else src, dst_ref=dst.at[slot], send_sem=send.at[j], recv_sem=recv.at[slot],
            device_id=(there, c), device_id_type=MESH)

    def start():
        @pl.loop(1, n)
        def _(j):
            copy(j, (me + j) % n, me).start()

    def wait():
        @pl.loop(1, n)
        def _(j):
            copy(j, (me + j) % n, (me + n - j) % n).wait()

    return start, wait


def greet_all(n):
    me, c = lax.axis_index("dp"), lax.axis_index("seq")
    bar = pltpu.get_barrier_semaphore()
    pl.semaphore_signal(bar, inc=1, device_id=(me, 1 - c), device_id_type=MESH)

    @pl.loop(1, n)
    def _(j):
        pl.semaphore_signal(bar, inc=1, device_id=((me + j) % n, c), device_id_type=MESH)

    return bar


def head_window(h):
    lo = pl.multiple_of(h * HEAD_DIM // 128 * 128, 128)
    lane = lax.broadcasted_iota(jnp.int32, (1, 256), 1) + lo - h * HEAD_DIM
    return pl.ds(lo, 256), ((lane >= 0) & (lane < HEAD_DIM)).astype(jnp.bfloat16)


def head_probs(qh, kh, seen):
    logits = jnp.where(seen, dot(qh, kh, 1, 1) * HEAD_DIM ** (-0.5), MASK_FILL)
    expo = jnp.exp(logits - jnp.max(logits, axis=-1, keepdims=True))
    return expo / jnp.sum(expo, axis=-1, keepdims=True)


def to_blocks(values, ref):
    count, size = ref.shape[:2]
    turned = values.T
    for i in range(count):
        ref[i] = turned[i * size : (i + 1) * size]


def write_blocks(n, target, stage, sem, block):
    def copy(i):
        return pltpu.make_async_copy(stage.at[i % 2], target.at[i // 4, i // 2 % 2, i % 2], sem.at[i % 2])

    @pl.loop(0, n)
    def _(i):
        when(i >= 2, lambda: copy(i).wait())
        stage[i % 2] = block(i).astype(stage.dtype)
        copy(i).start()

    copy(0).wait()
    copy(1).wait()


def forward_kernel(line, *refs):
    (m_in, m_out, m_expand, m_contract, m_table, m_mod, own_bias, meta, time_vec, tokens, cells, freqs, cot) = refs[:13]
    (weights, g_contract, g_expand, cond_got, h1_t, q, k, v, o, attended, middle, act, d_z, sums, out, pieces, cond, silu,
     mod_half, x, key_ok, row_ok, onehot, same, biases) = refs[13:38]
    (f_in, f_out, f_expand, f_contract, f_table, f_mod, own, table, cond_part, cond_some, mods, mod_part, mod_got, blocks, w,
     proj, mix, wide, partial, partial_got, h1, h2, h2_t, slope, d_branch, d_branch_t, stage, block, block_got, wide_bias, in_sem,
     w_sem, pair_send, pair_recv, peer_send, block_recv, cond_recv, mod_recv, keep_sem, stage_sem, cond_sem) = refs[38:79]
    n = line * 4
    low, f32 = jnp.bfloat16, jnp.float32
    me, c = lax.axis_index("dp"), lax.axis_index("seq")
    gat = Gatherer(line, own, weights, keep_sem, refs[79:85])
    red = make_reducer(line, (g_contract,), out, refs[85:])
    rows, width = x.shape
    own_rows, half = own.shape[1], own.shape[2] // 4
    edge = 3 * half // 128 * 128
    tiles = width // 128
    sources, flats = (m_in, m_out, m_table, m_mod, m_expand, m_contract), (f_in, f_out, f_table, f_mod, f_expand, f_contract)

    def load(i):
        return pltpu.make_async_copy(sources[i], flats[i], in_sem.at[i])

    for i in range(6):
        load(i).start()
    bar = greet_all(n)

    def swap(i, src, dst):
        return pltpu.make_async_remote_copy(
            src_ref=src, dst_ref=dst, send_sem=pair_send.at[i], recv_sem=pair_recv.at[i], device_id=(me, 1 - c),
            device_id_type=MESH)

    def tile(flat, t, count, per_row):
        return flat[pl.ds(t, count, stride=per_row), :]

    def cut_heads(flat, part, per_row):
        start = part * tiles + c * (tiles // 2)
        found = jnp.concatenate([tile(flat, start + j, own_rows, per_row) for j in range(tiles // 2 + 1)], axis=1)
        return jnp.where(c == 0, found[:, :half], found[:, found.shape[1] - half :]).astype(low)

    def cut(flat, target, count):
        for j in range(count):
            target[:own_rows, 128 * j : 128 * j + 128] = tile(flat, c * count + j, own_rows, 2 * count).astype(low)

    block_start, block_wait = all_peers(n, block, block_got, peer_send, block_recv, False)
    cond_start, cond_wait = all_peers(n, cond_part, cond_got, peer_send, cond_recv, True)
    mod_start, mod_wait = all_peers(n, mod_part, mod_got, peer_send, mod_recv, True)
    share = own_bias.shape[1]
    for r in range(-(-share // 128)):
        size = min(128, share - 128 * r)
        block[r : r + 1, :size] = own_bias[:, 128 * r : 128 * r + size].astype(low).astype(f32)
    block[8:] = jnp.broadcast_to(meta[:, :1].astype(f32), (8, 128))
    block_got[me] = block[...]
    load(0).wait()
    load(1).wait()
    for part in range(3):
        own[0, :, part * half : (part + 1) * half] = cut_heads(f_in, part, 3 * tiles)
    own[0, :, 3 * half :] = cut_heads(f_out, 0, tiles)
    pl.semaphore_wait(bar, n)
    block_start()
    gat.begin(0)
    load(5).wait()
    cut(f_contract, own.at[2], 4 * half // 128)
    load(2).wait()
    class_rows = table.shape[0]
    for t in range(tiles):
        table[:, 128 * t : 128 * t + 128] = tile(f_table, t, class_rows, tiles).astype(low)

    block_wait()
    labels = block_got[:, 8, :]
    hot = (labels[:, :class_rows] - (me * class_rows).astype(f32)
           == lax.broadcasted_iota(jnp.int32, (n, class_rows), 1).astype(f32)).astype(f32)
    onehot[...] = hot
    row = jnp.concatenate([block_got[s, 8:9, :1] for s in range(n)], axis=1)
    same[...] = (labels[:, :1] == row).astype(f32)
    found = dot(hot.astype(low), table[...])
    mine = lax.broadcasted_iota(jnp.int32, (n, width), 0) == me
    found = found + jnp.where(mine, jnp.broadcast_to(time_vec[...].astype(f32), (n, width)), 0.0)
    cond_part[...] = jnp.zeros_like(cond_part)
    for i in range(n):
        cond_part[i, :, :own_rows] = found[:, i * own_rows : (i + 1) * own_rows]
    keep_cond = pltpu.make_async_copy(cond_part.at[me], cond_got.at[me], cond_sem.at[0])
    keep_cond.start()
    cond_start()
    gat.begin(2)
    gat.paired(0)
    load(3).wait()
    mod_half[own_rows:] = jnp.zeros((mod_half.shape[0] - own_rows, mod_half.shape[1]), low)
    cut(f_mod, mod_half, 3 * tiles)
    load(4).wait()
    cut(f_expand, own.at[1], 4 * half // 128)
    gat.begin(1)

    for i in range(n):
        for r in range(-(-share // 128)):
            size = min(128, share - 128 * r)
            biases[:, i * share + 128 * r : i * share + 128 * r + size] = block_got[i, r : r + 1, :size]

    def bias(start, size):
        return biases[:, start : start + size]

    def bias_half(start, size):
        return jnp.where(c == 0, bias(start, size // 2), bias(start + size // 2, size // 2))

    half_kept = jnp.floor(meta[:, 1:2].astype(f32) * 0.5)
    rows_at = lax.broadcasted_iota(jnp.int32, (rows, 1), 0).astype(f32)
    row_ok[...] = (rows_at < half_kept).astype(f32)
    lanes_at = lax.broadcasted_iota(jnp.int32, (1, 2 * rows), 1)
    lanes_at = jnp.where(lanes_at < rows, lanes_at, lanes_at - rows).astype(f32)
    key_ok[...] = (lanes_at < half_kept).astype(f32)
    quarter = width // 4
    at = lax.broadcasted_iota(jnp.int32, (rows, rows), 0) == lax.broadcasted_iota(jnp.int32, (rows, rows), 1)
    cell = jnp.broadcast_to(cells[...].astype(f32), (rows, rows))
    cell = jnp.sum(jnp.where(at, cell, 0.0), axis=1, keepdims=True)
    across = jnp.floor(cell * (1.0 / SIDE))
    for i, place in enumerate((across, cell - SIDE * across)):
        angle = place * freqs[...]
        for j, wave in enumerate((jnp.sin(angle), jnp.cos(angle))):
            cols = slice((2 * i + j) * quarter, (2 * i + j + 1) * quarter)
            x[:, cols] = tokens[:, cols].astype(f32) + wave

    gat.steps(0, 1, 2)
    cond_wait()
    keep_cond.wait()
    cond[...] = jnp.zeros_like(cond)
    some = cond_some.shape[0]

    @pl.loop(0, n // some)
    def _(j):
        copy = pltpu.make_async_copy(cond_got.at[pl.ds(j * some, some)], cond_some, cond_sem.at[1])
        copy.start()
        copy.wait()
        cond[...] = cond[...] + jnp.sum(cond_some[...], axis=0)

    value = cond[...]
    silu[...] = (value / (1.0 + jnp.exp(-value))).astype(low)
    mods[...] = dot(silu[...], mod_half[...])

    @pl.loop(0, n)
    def _(s):
        mod_part[s] = mods[pl.ds(s, 1), :]

    mod_got[me] = mod_part[me]
    mod_start()
    gat.paired(1)
    gat.steps(0, 3, line)
    gat.steps(1, 1, 1)
    gat.steps(1, 2, 2)
    def fetch(m):
        return pltpu.make_async_copy(weights.at[m], blocks, w_sem.at[m])

    def unpack():
        for i in range(n):
            w[i * own_rows : (i + 1) * own_rows, :] = blocks[i // 4, i // 2 % 2, i % 2]

    gat.complete(0)
    fetch(0).start()
    mod_wait()
    pieces[c] = jnp.sum(mod_got[...], axis=0) + bias_half(0, 6 * width)
    swap(0, pieces.at[c], pieces.at[c]).start()
    swap(0, pieces.at[c], pieces.at[c]).wait()
    shift, scale, gate = (pieces[0, :, i * width : (i + 1) * width] for i in range(3))
    h1[c] = (normal(x[...]) * (1.0 + scale) + shift).astype(low)
    swap(1, h1.at[c], h1.at[c]).start()
    d_branch[c] = (pieces[1, :, 2 * width :] * (cot[...].astype(f32) * row_ok[...])).astype(low)
    swap(4, d_branch.at[c], d_branch.at[c]).start()
    fetch(0).wait()
    unpack()
    swap(1, h1.at[c], h1.at[c]).wait()
    both = jnp.concatenate([h1[0], h1[1]], axis=0)
    to_blocks(both, h1_t)
    gat.paired(2)

    @pl.loop(0, proj.shape[1] // 256)
    def _(t):
        cols = pl.ds(pl.multiple_of(t * 256, 256), 256)
        proj[:, cols] = dot(both, w[:, cols])

    spare = q.shape[1] - half
    for item, value in (
        (q, proj[:, :half] + bias_half(6 * width, width)),
        (k, proj[:, half : 2 * half]),
        (v, proj[:, 2 * half : 3 * half] + bias_half(7 * width, width)),
    ):
        item[:, :half] = value.astype(low)
        item[:, half:] = jnp.zeros((2 * rows, spare), low)
    mix[...] = jnp.zeros_like(mix)
    seen = jnp.broadcast_to(key_ok[...], (2 * rows, 2 * rows)) > 0.0
    heads = half // HEAD_DIM

    def head(h):
        win, lanes = head_window(h)
        probs = head_probs(q[:, win] * lanes, k[:, win], seen)
        mix[:, win] = mix[:, win] + dot(probs.astype(low), v[:, win] * lanes)

    @pl.loop(0, heads)
    def _(t):
        head(t)
        when(t == 0, lambda: gat.steps(1, 3, 3))
        when(t == heads - 1, lambda: gat.steps(1, 4, line))

    o[...] = mix[...].astype(low)
    wide[:, : 3 * half - edge] = jnp.zeros((2 * rows, 3 * half - edge), low)
    wide[:, 3 * half - edge :] = mix[:, :half].astype(low)

    @pl.loop(0, tiles)
    def _(t):
        cols = pl.ds(pl.multiple_of(t * 128, 128), 128)
        part = dot(wide[...], w[cols, edge:], 1, 1)
        partial[0, :, cols] = part[:rows]
        partial[1, :, cols] = part[rows:]

    swap(2, partial.at[1 - c], partial_got).start()
    gat.steps(2, 1, 1)
    swap(2, partial.at[1 - c], partial_got).wait()
    attended[...] = partial[c] + partial_got[...] + bias(8 * width, width)
    middle[...] = x[...] + gate * attended[...]
    shift, scale = (pieces[1, :, i * width : (i + 1) * width] for i in range(2))
    h2[c] = (normal(middle[...]) * (1.0 + scale) + shift).astype(low)
    swap(3, h2.at[c], h2.at[c]).start()
    gat.complete(1)
    fetch(1).start()
    swap(4, d_branch.at[c], d_branch.at[c]).wait()
    to_blocks(jnp.concatenate([d_branch[0], d_branch[1]], axis=0), d_branch_t)
    swap(3, h2.at[c], h2.at[c]).wait()
    both = jnp.concatenate([h2[0], h2[1]], axis=0)
    to_blocks(both, h2_t)
    fetch(1).wait()
    unpack()
    gat.steps(2, 2, 2)

    wide_bias[...] = bias_half(9 * width, 8 * half)

    @pl.loop(0, act.shape[1] // 256)
    def _(t):
        cols = pl.ds(pl.multiple_of(t * 256, 256), 256)
        z = dot(both, w[:, cols]) + wide_bias[:, cols]
        bend = jnp.tanh(GELU_A * (z + GELU_B * z * z * z))
        act[:, cols] = (0.5 * z * (1.0 + bend)).astype(low)
        slope[:, cols] = 0.5 * (1.0 + bend) + 0.5 * z * (1.0 - bend * bend) * (GELU_A * (1.0 + 3.0 * GELU_B * z * z))

    def contract_block(i):
        when(i == 0, lambda: gat.steps(2, 3, 3))
        when(i == n // 2, lambda: gat.steps(2, 4, line))
        return dot(d_branch_t[i], act[...])

    write_blocks(n, g_contract, stage, stage_sem, contract_block)
    quarter = line // 4
    red.begin_some(0, 2 * quarter)
    gat.complete(2)
    fetch(2).start()
    sums[...] = jnp.zeros_like(sums)
    sums[4:5] = jnp.sum(d_branch[...].astype(f32), axis=(0, 1))[None]
    fetch(2).wait()
    unpack()
    red.unit_some(0, quarter)
    d_out = jnp.concatenate([d_branch[0], d_branch[1]], axis=0)

    @pl.loop(0, act.shape[1] // 256)
    def _(t):
        cols = pl.ds(pl.multiple_of(t * 256, 256), 256)
        d_z[:, cols] = (dot(d_out, w[:, cols]) * slope[:, cols]).astype(low)

    red.begin_some(2 * quarter, 3 * quarter)
    red.unit_some(quarter, 2 * quarter)
    totals = jnp.sum(d_z[...].astype(f32), axis=0, keepdims=True)
    sums[1:2] = totals[:, :width]
    sums[2:3] = totals[:, width:]

    def expand_block(i):
        when(i == n // 4, lambda: red.begin_some(3 * quarter, line))
        when(i == n // 2, lambda: red.unit_some(2 * quarter, 3 * quarter))
        return dot(h2_t[i], d_z[...])

    write_blocks(n, g_expand, stage, stage_sem, expand_block)
    red.unit_some(3 * quarter, line)
    red.final(0)
    red.drain()

    @pl.loop(0, 3)
    def _(m):
        gat.drain(m)


def forward(hbm_args, vmem_args, bias_size, n, collective_id):
    line = n // 4
    tokens = vmem_args[3]
    rows, width = tokens.shape
    class_rows = hbm_args[4].size // width
    own_rows, half = width // n, width // 2
    low, f32 = jnp.bfloat16, jnp.float32
    dma = pltpu.SemaphoreType.DMA
    vmem, hbm = pl.BlockSpec(memory_space=pltpu.VMEM), pl.BlockSpec(memory_space=pltpu.HBM)
    heads = (2 * rows, -(-half // 128) * 128)
    edge = 3 * half // 128 * 128

    def shape(dims, kind):
        return jax.ShapeDtypeStruct(dims, kind)

    def scratch(dims, kind):
        return pltpu.VMEM(dims, kind)

    return pl.pallas_call(
        functools.partial(forward_kernel, line),
        out_shape=[
            shape((3, line, 2, 2, own_rows, 4 * half), low),
            shape((line, 2, 2, own_rows, 4 * half), low),
            shape((line, 2, 2, own_rows, 4 * half), low),
            shape((n, n, 128), f32),
            shape((n, own_rows, 2 * rows), low),
            shape(heads, low),
            shape(heads, low),
            shape(heads, low),
            shape(heads, low),
            shape((rows, width), f32),
            shape((rows, width), f32),
            shape((2 * rows, 4 * half), low),
            shape((2 * rows, 4 * half), low),
            shape((8, width), f32),
            shape((1, own_rows, 4 * half), low),
            shape((2, 1, 3 * width), f32),
            shape((n, 128), f32),
            shape((n, 128), low),
            shape((128, 3 * width), low),
            shape((rows, width), f32),
            shape((1, 2 * rows), f32),
            shape((rows, 1), f32),
            shape((n, class_rows), f32),
            shape((n, n), f32),
            shape((1, bias_size), f32),
        ],
        in_specs=[hbm] * len(hbm_args) + [vmem] * len(vmem_args),
        out_specs=[hbm] * 4 + [vmem] * 21,
        scratch_shapes=[scratch(item.shape, f32) for item in hbm_args]
        + [
            scratch((3, own_rows, 4 * half), low),
            scratch((class_rows, width), low),
            scratch((n, n, 128), f32),
            scratch((min(n, 16), n, 128), f32),
            scratch((n, 3 * width), f32),
            scratch((n, 1, 3 * width), f32),
            scratch((n, 1, 3 * width), f32),
            scratch((line, 2, 2, own_rows, 4 * half), low),
            scratch((width, 4 * half), low),
            scratch((2 * rows, edge + 128), f32),
            scratch(heads, f32),
            scratch(heads, low),
            scratch((2, rows, width), f32),
            scratch((rows, width), f32),
            scratch((2, rows, width), low),
            scratch((2, rows, width), low),
            scratch((n, own_rows, 2 * rows), low),
            scratch((2 * rows, 4 * half), f32),
            scratch((2, rows, width), low),
            scratch((n, own_rows, 2 * rows), low),
            scratch((2, own_rows, 4 * half), low),
            scratch((16, 128), f32),
            scratch((n, 16, 128), f32),
            scratch((1, 4 * half), f32),
            dma((6,)),
            dma((3,)),
            dma((5,)),
            dma((5,)),
            dma((n,)),
            dma((n,)),
            dma((n,)),
            dma((n,)),
            dma((3,)),
            dma((2,)),
            dma((2,)),
        ]
        + [dma((3, 4, line)), dma((3, 4, line + 1))] + [dma((3, 4, line))] * 4
        + reducer_scratch(1, line, own_rows, low),
        compiler_params=pltpu.CompilerParams(
            collective_id=collective_id, has_side_effects=True, vmem_limit_bytes=63 * 2**20),
        name="forward",
    )(*hbm_args, *vmem_args)


class Reducer:
    def __init__(self, line, grads, out, own, got_b, got_z, got_a, sems):
        self.line, self.grads, self.out = line, grads, out
        self.own, self.acc, self.got_z, self.got_a = own, got_b, got_z, got_a
        self.load, self.send_b, self.send_z, self.send_a, self.recv_b, self.recv_z, self.recv_a = sems
        self.me = me = Place(line)
        self.up, self.down = me.z < line - 1, me.z > 0
        self.above, self.below = me.dev(z=jnp.minimum(me.z + 1, line - 1)), me.dev(z=jnp.maximum(me.z - 1, 0))
        self.units = len(grads) * line

    def last(self, g):
        return "y" if GROUPS[g][3] == "x" else "x"

    def first(self, g):
        return self.me.x if GROUPS[g][3] == "x" else self.me.y

    def half(self, grad, g, zz, mine):
        cols = pl.ds(GROUPS[g][0], GROUPS[g][1])
        if self.last(g) == "y":
            return grad.at[zz, self.me.y if mine else 1 - self.me.y, :, :, cols]
        return grad.at[zz, :, self.me.x if mine else 1 - self.me.x, :, cols]

    def loading(self, u, g, zz, side, grad=None):
        grad = self.grads[0] if grad is None else grad
        return pltpu.make_async_copy(
            self.half(grad, g, zz, True), self.own[g].at[u % 3, side], self.load.at[u % 3, g, side])

    def remote(self, src, dst, send, recv, dev):
        return pltpu.make_async_remote_copy(
            src_ref=src, dst_ref=dst, send_sem=send, recv_sem=recv, device_id=dev, device_id_type=MESH)

    def b_copy(self, m, g, zz, grad=None):
        grad = self.grads[0] if grad is None else grad
        return self.remote(
            self.half(grad, g, zz, False), self.acc[g].at[m, zz], self.send_b.at[m, g, zz], self.recv_b.at[m, g, zz],
            self.me.peer(self.last(g)))

    def slot_a(self, g, zz):
        return zz if GROUPS[g][2] == 1 else 0

    def a_copy(self, m, g, zz):
        return self.remote(
            self.acc[g].at[m, zz, 1 - self.first(g)], self.got_a[g].at[m, self.slot_a(g, zz)], self.send_a.at[m, g, zz],
            self.recv_a.at[m, g, zz], self.me.peer(GROUPS[g][3]))

    def z_copy(self, m, g, zz, slot, dev):
        part = self.acc[g].at[m, zz] if GROUPS[g][2] == 0 else self.acc[g].at[m, zz, self.first(g)]
        return self.remote(part, self.got_z[g].at[m, slot], self.send_z.at[m, g, zz], self.recv_z.at[m, g, slot], dev)

    def add_b(self, m, g, zz, u, side):
        self.loading(u, g, zz, side).wait()
        self.b_copy(m, g, zz).wait_recv()
        self.acc[g][m, zz] = self.acc[g][m, zz] + self.own[g][u % 3, side]

    def add_z(self, m, g, zz, slot):
        acc, got = self.acc[g], self.got_z[g]
        self.z_copy(m, g, self.me.z, slot, self.below).wait_recv()
        if GROUPS[g][2] == 0:
            acc[m, zz] = acc[m, zz] + got[m, slot]
        else:
            acc[m, zz, self.first(g)] = acc[m, zz, self.first(g)] + got[m, slot]

    def add_a(self, m, g, zz):
        self.a_copy(m, g, zz).wait_recv()
        acc, first = self.acc[g], self.first(g)
        acc[m, zz, first] = acc[m, zz, first] + self.got_a[g][m, self.slot_a(g, zz)]

    def planes(self, k, fn):
        z, line = self.me.z, self.line
        when(z + k < line, lambda: fn(jnp.minimum(z + k, line - 1), True))
        when((z >= k) & (k > 0), lambda: fn(jnp.maximum(z - k, 0), False))

    def begin(self, v):
        m, j = v // self.line, v % self.line

        def one(grad, zz, upward):
            for g in range(4):
                self.b_copy(m, g, zz, grad).start()
                self.loading(v, g, zz, 0 if upward else 1, grad).start()

        for index, grad in enumerate(self.grads):
            when(m == index, lambda: self.planes(self.line - 1 - j, lambda zz, upward: one(grad, zz, upward)))

    def onward(self, m, g, zz, k, upward):
        if upward:
            when(self.down, lambda: self.add_z(m, g, zz, zz))
            self.z_copy(m, g, zz, zz, self.above).start()
        else:
            when(self.up, lambda: self.add_z(m, g, zz, zz))
            self.z_copy(m, g, zz, jnp.where(k == 1, self.line, zz), self.below).start()

    def near(self, u, m, j):
        k = self.line - 1 - j

        def one(zz, upward):
            for g in range(4):
                self.add_b(m, g, zz, u, 0 if upward else 1)
                if GROUPS[g][2] == 1:
                    self.a_copy(m, g, zz).start()
                else:
                    when(k > 0, lambda g=g: self.onward(m, g, zz, k, upward))

        self.planes(k, one)

    def far(self, m, j):
        k = self.line - j

        def one(zz, upward):
            for g in (2, 3):
                self.add_a(m, g, zz)
                self.onward(m, g, zz, k, upward)

        when((k > 0) & (k < self.line), lambda: self.planes(k, one))

    def close(self, m):
        z = self.me.z
        for g in (0, 1):
            when(self.down, lambda g=g: self.add_z(m, g, z, z))
            when(self.up, lambda g=g: self.add_z(m, g, z, self.line))
            self.a_copy(m, g, z).start()

    def final(self, m):
        z = self.me.z
        for g in range(4):
            cols = pl.ds(GROUPS[g][0], GROUPS[g][1])
            self.add_a(m, g, z)
            if GROUPS[g][2] == 1:
                when(self.down, lambda g=g: self.add_z(m, g, z, z))
                when(self.up, lambda g=g: self.add_z(m, g, z, self.line))
            self.out[m, :, cols] = self.acc[g][m, z, self.first(g)]

    def unit(self, u):
        line = self.line
        m, j = u // line, u % line
        self.near(u, m, j)
        self.far(m, j)
        when(j == line - 1, lambda: self.close(m))
        if len(self.grads) > 1:
            when((j == 0) & (m > 0), lambda: self.final(jnp.maximum(m - 1, 0)))

    def begin_some(self, first, last):
        @pl.loop(first, last)
        def _(v):
            self.begin(v)

    def unit_some(self, first, last):
        @pl.loop(first, last)
        def _(u):
            self.unit(u)

    def drain(self):
        z = self.me.z

        @pl.loop(0, len(self.grads))
        def _(m):
            @pl.loop(0, self.line)
            def _(zz):
                for g in range(4):
                    self.b_copy(m, g, zz).wait_send()
                    if GROUPS[g][2] == 1:
                        self.a_copy(m, g, zz).wait_send()
                    when(zz != z, lambda g=g: self.z_copy(m, g, zz, zz, self.above).wait_send())
            for g in (0, 1):
                self.a_copy(m, g, z).wait_send()


def reducer_scratch(count, line, rows, dt):
    dma = pltpu.SemaphoreType.DMA
    own = [pltpu.VMEM((3, 2, 2, rows, GROUPS[g][1]), dt) for g in range(4)]
    got_b = [pltpu.VMEM((count, line, 2, rows, GROUPS[g][1]), dt) for g in range(4)]
    got_z = [pltpu.VMEM((count, line + 1) + ((2,) if GROUPS[g][2] == 0 else ()) + (rows, GROUPS[g][1]), dt) for g in range(4)]
    got_a = [pltpu.VMEM((count, line if GROUPS[g][2] == 1 else 1, rows, GROUPS[g][1]), dt) for g in range(4)]
    sems = [dma((3, 4, 2))] + [dma((count, 4, line))] * 4 + [dma((count, 4, line + 1))] + [dma((count, 4, line))]
    return own + got_b + got_z + got_a + sems


def make_reducer(line, grads, out, refs):
    return Reducer(line, grads, out, refs[:4], refs[4:8], refs[8:12], refs[12:16], refs[16:])


def backward_kernel(line, *refs):
    (weights, g_expand, h1_t, act, d_z, sums, out_contract, q, k, v, o, key_ok, x, middle, attended, cot, row_ok, pieces,
     biases, modulation, cond, silu, same) = refs[:23]
    (g_attn, d_mod_all, cond_all, both, block_out, tokens_grad, bias_grad, norm_out, factor_out) = refs[23:32]
    (w, rhs, d_o, d_q, d_k, d_v, d_h, d_h_got, branch_got, d_mid, d_att, d_att_t, stage, dp, dp_got, msg, msg_got, d_mod, vec,
     vec_got, d_silu, d_silu_got, chunk, out, bias_sum, d_cond, squares, squares_got, table_squares, squares_pair, cond_some, bias_all,
     mod_sums, vec_all, w_sem,
     mod_sem, stage_sem, pair_send, pair_recv, msg_send, msg_recv, vec_send, vec_recv, cond_send, cond_recv, bias_send, bias_recv, square_send,
     square_recv) = refs[32:81]
    n = line * 4
    low, f32 = jnp.bfloat16, jnp.float32
    me, c = lax.axis_index("dp"), lax.axis_index("seq")
    red = make_reducer(line, (g_expand, g_attn), out, refs[81:])
    rows, width = x.shape
    half = weights.shape[2] // 4
    heads = half // HEAD_DIM
    edge = 3 * half // 128 * 128
    tiles = width // 128

    def swap(i, src, dst):
        return pltpu.make_async_remote_copy(
            src_ref=src, dst_ref=dst, send_sem=pair_send.at[i], recv_sem=pair_recv.at[i], device_id=(me, 1 - c),
            device_id_type=MESH)

    def fetch(i):
        return pltpu.make_async_copy(weights.at[(1, 0, 2)[i]], w, w_sem.at[i])

    def back(values, lanes):
        @pl.loop(0, tiles)
        def _(t):
            cols = pl.ds(pl.multiple_of(t * 128, 128), 128)
            part = dot(values[...], w[cols, :lanes], 1, 1)
            d_h[0, :, cols] = part[:rows]
            d_h[1, :, cols] = part[rows:]

    def column_sums(values):
        return jnp.sum(values.astype(f32), axis=0, keepdims=True)

    def norm_back(values, scale, d_n):
        centre = values - jnp.mean(values, axis=-1, keepdims=True)
        inv = lax.rsqrt(jnp.mean(centre * centre, axis=-1, keepdims=True) + LAYER_EPS)
        normed = centre * inv
        e = d_n * (1.0 + scale)
        d_x = (e - jnp.mean(e, axis=-1, keepdims=True) - normed * jnp.mean(e * normed, axis=-1, keepdims=True)) * inv
        return d_x, jnp.sum(d_n, axis=0, keepdims=True), jnp.sum(d_n * normed, axis=0, keepdims=True)

    def piece(i):
        return pieces[i // 3, :, i % 3 * width : (i % 3 + 1) * width]

    fetch(0).start()
    bar = greet_all(n)
    for item in (d_q, d_k, d_v):
        item[...] = jnp.zeros_like(item)
    dp[...] = jnp.zeros_like(dp)
    vec[...] = sums[...]
    pl.semaphore_wait(bar, n)

    def hidden_back():
        fetch(0).wait()
        back(d_z, 4 * half)
        swap(0, d_h.at[1 - c], d_h_got).start()
        fetch(1).start()

    def middle_back():
        swap(0, d_h.at[1 - c], d_h_got).wait()
        d_x, shift, scale = norm_back(middle[...], piece(4), d_h[c] + d_h_got[...])
        d_mid[...] = d_x + cot[...].astype(f32) * row_ok[...]
        dp[2:3] = jnp.sum(d_mid[...] * attended[...], axis=0, keepdims=True)
        dp[3:4] = shift
        dp[4:5] = scale
        d_att[c] = (piece(2) * d_mid[...]).astype(low)
        swap(1, d_att.at[c], d_att.at[c]).start()

    def mixed_back():
        swap(1, d_att.at[c], d_att.at[c]).wait()
        d_all = jnp.concatenate([d_att[0], d_att[1]], axis=0)
        to_blocks(d_all, d_att_t)
        vec[3:4] = column_sums(d_att[0]) + column_sums(d_att[1])
        fetch(1).wait()
        d_o[:, :half] = dot(d_all, w[:, edge:])[:, 3 * half - edge :].astype(low)
        d_o[:, half:] = jnp.zeros((2 * rows, d_o.shape[1] - half), low)

    seen = jnp.broadcast_to(key_ok[...], (2 * rows, 2 * rows)) > 0.0

    def head(h):
        win, lanes = head_window(h)
        qh, kh, doh = q[:, win] * lanes, k[:, win] * lanes, d_o[:, win] * lanes
        probs = head_probs(qh, kh, seen)
        d_probs = dot(doh, v[:, win], 1, 1)
        inner = jnp.sum(probs * d_probs, axis=-1, keepdims=True)
        d_logits = (probs * (d_probs - inner)).astype(low)
        d_q[:, win] = d_q[:, win] + dot(d_logits, kh) * HEAD_DIM ** (-0.5)
        d_k[:, win] = d_k[:, win] + dot(d_logits, qh, 0, 0) * HEAD_DIM ** (-0.5)
        d_v[:, win] = d_v[:, win] + dot(probs.astype(low), doh, 0, 0)

    def attention_grads():
        for i, item in enumerate((d_q, d_k, d_v)):
            rhs[: 2 * rows, i * half : (i + 1) * half] = item[:, :half].astype(low)
        rhs[: 2 * rows, 3 * half :] = jnp.zeros((2 * rows, half), low)
        rhs[2 * rows :, edge : 3 * half] = jnp.zeros((2 * rows, 3 * half - edge), low)
        rhs[2 * rows :, 3 * half :] = o[:, :half]
        sums = column_sums(rhs[: 2 * rows, : 3 * half])
        vec[0:1, :half] = sums[:, :half]
        vec[0:1, half:] = sums[:, 2 * half :]

        def block(i):
            left = dot(h1_t[i], rhs[: 2 * rows, :edge])
            right = dot(h1_t[i], rhs[: 2 * rows, edge:]) + dot(d_att_t[i], rhs[2 * rows :, edge:])
            return jnp.concatenate([left, right], axis=1)

        write_blocks(n, g_attn, stage, stage_sem, block)

    def input_back():
        back(rhs.at[: 2 * rows, : edge + 128], edge + 128)
        swap(2, d_h.at[1 - c], d_h_got).start()
        fetch(2).start()

    def first_back():
        swap(2, d_h.at[1 - c], d_h_got).wait()
        d_x, shift, scale = norm_back(x[...], piece(1), d_h[c] + d_h_got[...])
        tokens_grad[...] = (d_x + d_mid[...]).astype(low)
        dp[0:1] = shift
        dp[1:2] = scale
        fetch(2).wait()
        back(act, 4 * half)
        swap(3, d_h.at[1 - c], branch_got).start()

    def branch_out():
        swap(3, d_h.at[1 - c], branch_got).wait()
        branch = d_h[c] + branch_got[...] + biases[:, 9 * width + 8 * half :]
        result = middle[...] + piece(5) * branch
        block_out[...] = jnp.where(jnp.broadcast_to(row_ok[...], result.shape) > 0.0, result, 0.0).astype(low)
        dp[5:6] = jnp.sum(cot[...].astype(f32) * row_ok[...] * branch, axis=0, keepdims=True)
        swap(4, dp, dp_got).start()

    msg_start, msg_wait = all_peers(n, msg, msg_got, msg_send, msg_recv, False)
    vec_start, vec_wait = all_peers(n, chunk, vec_got, vec_send, vec_recv, True)
    per = chunk_tiles(n, width)

    def send_mod():
        swap(4, dp, dp_got).wait()
        total = (dp[...] + dp_got[...]).astype(low).astype(f32)
        own = jnp.where(c == 0, total[0:3], total[3:6])
        for r in range(3):
            msg[r] = own[r : r + 1]
        msg_got[me] = msg[...]
        chunk[...] = jnp.zeros_like(chunk)
        for t in range(5 * tiles):
            chunk[t // per, t % per] = vec[t // tiles : t // tiles + 1, t % tiles * 128 : t % tiles * 128 + 128]
        vec_got[me] = chunk[me]
        msg_start()
        vec_start()

    keep_mod = pltpu.make_async_copy(d_mod, d_mod_all.at[c], mod_sem.at[0])
    keep_cond = pltpu.make_async_copy(d_cond, cond_all.at[me], mod_sem.at[2])

    def mod_grad():
        msg_wait()
        vec_wait()

        @pl.loop(0, n)
        def _(s):
            for r in range(3):
                d_mod[pl.ds(s, 1), r * width : (r + 1) * width] = msg_got[s, r]

        for r in range(per):
            bias_sum[c, r] = jnp.sum(vec_got[:, r], axis=0)
        d_silu[...] = dot(d_mod[...].astype(low), modulation[...], 1, 1)
        swap(5, d_silu, d_silu_got).start()
        swap(6, d_mod, d_mod_all.at[c]).start()
        swap(7, bias_sum.at[c], bias_sum.at[c]).start()
        keep_mod.start()

    cond_start, cond_wait = all_peers(n, d_cond, cond_all, cond_send, cond_recv, False)
    bias_start, bias_wait = all_peers(n, bias_sum, bias_all, bias_send, bias_recv, False)
    square_start, square_wait = all_peers(n, squares, squares_got, square_send, square_recv, False)

    def cond_grad():
        swap(5, d_silu, d_silu_got).wait()
        swap(6, d_mod, d_mod_all.at[c]).wait()
        swap(7, bias_sum.at[c], bias_sum.at[c]).wait()
        keep_mod.wait()
        gate = 1.0 / (1.0 + jnp.exp(-cond[...]))
        d_cond[...] = (d_silu[...] + d_silu_got[...]) * (gate + cond[...] * gate * (1.0 - gate))
        keep_cond.start()
        bias_all[me] = bias_sum[...]
        cond_start()
        bias_start()
        d_low = d_mod[...].astype(low)
        grad = dot(silu[...], d_low, 0, 0)[: out.shape[1]]
        sums = jnp.sum(d_mod[...], axis=0, keepdims=True)
        mod_sums[c] = sums
        swap(12, mod_sums.at[c], mod_sums.at[c]).start()
        counted = [(per * me + r < 3 * tiles) | (c == 0) for r in range(per)]
        total = jnp.sum(grad * grad) + jnp.where(me == 0, jnp.sum(sums * sums), 0.0)
        for r in range(per):
            total = total + jnp.where(counted[r], jnp.sum(bias_sum[c, r] * bias_sum[c, r]), 0.0)
        squares[...] = jnp.full((1, 128), total, f32)

    def table_norm():
        cond_wait()
        bias_wait()
        keep_cond.wait()
        swap(12, mod_sums.at[c], mod_sums.at[c]).wait()
        for core in range(2):
            bias_grad[:, 3 * core * width : 3 * (core + 1) * width] = mod_sums[core]
            for t in range(5 * tiles):
                vec_all[core, :, 128 * t : 128 * t + 128] = bias_all[t // per, core, t % per]
            start = 6 * width + core * half
            bias_grad[:, start : start + half] = vec_all[core, :, :half]
            bias_grad[:, start + width : start + width + half] = vec_all[core, :, half:width]
            start = 9 * width + core * 4 * half
            bias_grad[:, start : start + 4 * half] = vec_all[core, :, width : 3 * width]
        bias_grad[:, 8 * width : 9 * width] = vec_all[0, :, 3 * width : 4 * width]
        bias_grad[:, 9 * width + 8 * half :] = vec_all[0, :, 4 * width :]
        table_squares[...] = jnp.zeros((1, 128), f32)
        size = cond_some.shape[0]

        @pl.loop(0, n // size)
        def _(j):
            some = pltpu.make_async_copy(cond_all.at[pl.ds(j * size, size)], cond_some, mod_sem.at[1])
            some.start()
            some.wait()
            gram = jnp.zeros((n, n), f32)
            for i in range(size):
                part = cond_some[i]
                gram = gram + lax.dot_general(
                    part, part, (((1,), (1,)), ((), ())), preferred_element_type=f32, precision=lax.Precision.HIGHEST)
            table_squares[...] = table_squares[...] + jnp.sum(gram * same[...])

    def share(m):
        return swap(8 + m, out_contract.at[0] if m == 0 else out.at[m - 1], both.at[c, m])

    def reduced(m):
        value = out_contract[0] if m == 0 else out[m - 1]
        both[c, m] = value
        share(m).start()
        value = value.astype(f32)
        squares[...] = squares[...] + jnp.sum(value * value)

    parts = (hidden_back, middle_back, mixed_back) + (None,) * heads
    parts += (attention_grads, input_back, first_back, branch_out, send_mod, mod_grad, cond_grad, table_norm)
    first_head = parts.index(None)
    begun, carried = ([places[u // line * 4 + u % line * 4 // line] for u in range(red.units)] for places in UNIT_PLACES)

    def upto(places, s):
        total = jnp.int32(0)
        for place in places:
            total = total + (place <= s).astype(jnp.int32)
        return total

    @pl.loop(0, len(parts) + 1)
    def _(s):
        @pl.loop(upto(begun, s - 1), upto(begun, s))
        def _(v):
            red.begin(v)

        @pl.loop(upto(carried, s - 1), upto(carried, s))
        def _(u):
            red.unit(u)

        when((s >= first_head) & (s < first_head + heads), lambda: head(s - first_head))
        for i, part in enumerate(parts):
            if part is not None:
                when(s == i, part)

    reduced(0)
    reduced(1)
    red.final(1)
    reduced(2)
    squares_got[me] = squares[...]
    square_start()
    red.drain()
    square_wait()
    squares[...] = jnp.sum(squares_got[...], axis=0)
    swap(11, squares, squares_pair).start()
    for m in range(3):
        share(m).wait()
    swap(11, squares, squares_pair).wait()
    norm = jnp.sqrt(squares[...] + squares_pair[...] + table_squares[...])
    norm_out[...] = norm[:, :1]
    factor_out[...] = jnp.broadcast_to(jnp.minimum(1.0, CLIP_LIMIT / (norm + 1e-06)), (8, 128))


def chunk_tiles(n, width):
    return -(-5 * (width // 128) // n)


def backward(hbm_args, vmem_args, n, collective_id):
    line = n // 4
    grad = hbm_args[1]
    rows, cols = grad.shape[-2:]
    heads = vmem_args[5].shape
    own, width = vmem_args[10].shape
    all_rows = 2 * own
    low, f32 = jnp.bfloat16, jnp.float32
    dma = pltpu.SemaphoreType.DMA
    vmem, hbm = pl.BlockSpec(memory_space=pltpu.VMEM), pl.BlockSpec(memory_space=pltpu.HBM)
    per = chunk_tiles(n, width)
    return pl.pallas_call(
        functools.partial(backward_kernel, line),
        out_shape=[
            jax.ShapeDtypeStruct(grad.shape, low),
            jax.ShapeDtypeStruct((2, n, 3 * width), f32),
            jax.ShapeDtypeStruct((n, n, 128), f32),
            jax.ShapeDtypeStruct((2, 3, rows, cols), low),
            jax.ShapeDtypeStruct((own, width), low),
            jax.ShapeDtypeStruct((own, width), low),
            jax.ShapeDtypeStruct(vmem_args[16].shape, f32),
            jax.ShapeDtypeStruct((1, 1), f32),
            jax.ShapeDtypeStruct((8, 128), f32),
        ],
        in_specs=[hbm] * len(hbm_args) + [vmem] * len(vmem_args),
        out_specs=[hbm] * 3 + [vmem] * 6,
        scratch_shapes=[
            pltpu.VMEM((width, cols), low),
            pltpu.VMEM((2 * all_rows, cols), low),
            pltpu.VMEM(heads, low),
            pltpu.VMEM(heads, f32),
            pltpu.VMEM(heads, f32),
            pltpu.VMEM(heads, f32),
            pltpu.VMEM((2, own, width), f32),
            pltpu.VMEM((own, width), f32),
            pltpu.VMEM((own, width), f32),
            pltpu.VMEM((own, width), f32),
            pltpu.VMEM((2, own, width), low),
            pltpu.VMEM((n, rows, all_rows), low),
            pltpu.VMEM((2, rows, cols), low),
            pltpu.VMEM((8, width), f32),
            pltpu.VMEM((8, width), f32),
            pltpu.VMEM((3, 1, width), f32),
            pltpu.VMEM((n, 3, 1, width), f32),
            pltpu.VMEM((n, 3 * width), f32),
            pltpu.VMEM((8, width), f32),
            pltpu.VMEM((n, per, 1, 128), f32),
            pltpu.VMEM((n, 128), f32),
            pltpu.VMEM((n, 128), f32),
            pltpu.VMEM((n, per, 1, 128), f32),
            pltpu.VMEM((2, rows, cols), low),
            pltpu.VMEM((2, per, 1, 128), f32),
            pltpu.VMEM((n, 128), f32),
            pltpu.VMEM((1, 128), f32),
            pltpu.VMEM((n, 1, 128), f32),
            pltpu.VMEM((1, 128), f32),
            pltpu.VMEM((1, 128), f32),
            pltpu.VMEM((min(n, 16), n, 128), f32),
            pltpu.VMEM((n, 2, per, 1, 128), f32),
            pltpu.VMEM((2, 1, 3 * width), f32),
            pltpu.VMEM((2, 1, 5 * width), f32),
            dma((3,)),
            dma((3,)),
            dma((2,)),
            dma((13,)),
            dma((13,)),
        ]
        + [dma((n,))] * 10
        + reducer_scratch(2, line, rows, low),
        compiler_params=pltpu.CompilerParams(
            collective_id=collective_id, has_side_effects=True, vmem_limit_bytes=63 * 2**20),
        name="backward",
    )(*hbm_args, *vmem_args)


def adam_step(grad, master, first, second, rate):
    first_new = BETA_FIRST * first + (1.0 - BETA_FIRST) * grad
    second_new = BETA_SECOND * second + (1.0 - BETA_SECOND) * grad * grad
    first_hat = first_new / (1.0 - BETA_FIRST**STEP)
    second_hat = second_new / (1.0 - BETA_SECOND**STEP)
    master_new = master - rate * (
        first_hat / (jnp.sqrt(second_hat) + ADAM_EPS) + WEIGHT_DECAY * master
    )
    return (first_new, second_new, master_new)


def chunk_rows(rows):
    sizes = [d for d in range(8, 257, 8) if rows % d == 0]
    return sizes[-1] if sizes else rows


def adam_kernel(n, rates, *refs):
    kinds = len(rates)
    factor_ref, both, silu, d_mod, cond_all, onehot = refs[:6]
    at = 6
    states = [refs[at + 3 * a : at + 3 * a + 3] for a in range(kinds)]
    at += 3 * kinds
    news = [refs[at + 3 * a : at + 3 * a + 3] for a in range(kinds)]
    at += 3 * kinds
    held, flat = refs[at : at + kinds], refs[at + kinds : at + 2 * kinds]
    wide, in_sem, out_sem = refs[at + 2 * kinds :]
    rows, half = both.shape[2:]
    head = half // 4
    order = (3, 4, 0, 1, 2, 5)

    def loads(a):
        return [pltpu.make_async_copy(states[a][k], held[a].at[k], in_sem.at[a, k]) for k in range(3)]

    for a in order:
        for copy in loads(a):
            copy.start()

    def spread(a, width, count=rows):
        tiles = width // 128
        for t in range(tiles):
            flat[a][pl.ds(t, count, stride=tiles), :] = wide[:count, 128 * t : 128 * t + 128]

    def gradient(a):
        if a == 0:
            part = d_mod.shape[2]
            for core in range(2):
                grad = dot(silu[...], d_mod[core].astype(silu.dtype), 0, 0)
                wide[:, core * part : (core + 1) * part] = grad[:rows]
            spread(a, 2 * part)
        elif a == 1:
            for core in range(2):
                for part in range(3):
                    lo = (2 * part + core) * head
                    wide[:, lo : lo + head] = both[core, 2, :, part * head : (part + 1) * head].astype(jnp.float32)
            spread(a, 6 * head)
        elif a == 2:
            for core in range(2):
                wide[:, core * head : (core + 1) * head] = both[core, 2, :, 3 * head :].astype(jnp.float32)
            spread(a, 2 * head)
        elif a == 5:
            count = onehot.shape[1]
            for i in range(n):
                wide[:count, i * rows : (i + 1) * rows] = lax.dot_general(
                    onehot[...], cond_all[i], (((0,), (0,)), ((), ())), preferred_element_type=jnp.float32,
                    precision=lax.Precision.HIGHEST)[:, :rows]
            spread(a, n * rows, count)
        else:
            for core in range(2):
                wide[:, core * half : (core + 1) * half] = both[core, 4 - a].astype(jnp.float32)
            spread(a, 2 * half)

    factor = factor_ref[:1, :]
    for a in order:
        gradient(a)
        for copy in loads(a):
            copy.wait()
        size = chunk_rows(flat[a].shape[0])

        @pl.loop(0, flat[a].shape[0] // size)
        def _(i, a=a, size=size):
            part = pl.ds(pl.multiple_of(i * size, size), size)
            grad = flat[a][part] * factor
            master, first, second = held[a][0, part], held[a][1, part], held[a][2, part]
            first, second, master = adam_step(grad, master, first, second, rates[a])
            held[a][0, part], held[a][1, part], held[a][2, part] = master, first, second
            for k in range(3):
                pltpu.make_async_copy(held[a].at[k, part], news[a][k].at[part], out_sem.at[a, k]).start()

    for a in range(kinds):
        for k in range(3):
            pltpu.make_async_copy(held[a].at[k], news[a][k], out_sem.at[a, k]).wait()


def adam(factor, both, silu, d_mod, cond_all, onehot, states, rates, n):
    vmem, hbm = pl.BlockSpec(memory_space=pltpu.VMEM), pl.BlockSpec(memory_space=pltpu.HBM)
    dma = pltpu.SemaphoreType.DMA
    kinds = len(states)
    flats = [jax.ShapeDtypeStruct(s[0].shape, jnp.float32) for s in states]
    news = pl.pallas_call(
        functools.partial(adam_kernel, n, rates),
        out_shape=[f for f in flats for _ in range(3)],
        in_specs=[vmem] * 6 + [hbm] * (3 * kinds),
        out_specs=[hbm] * (3 * kinds),
        scratch_shapes=[pltpu.VMEM((3,) + f.shape, jnp.float32) for f in flats]
        + [pltpu.VMEM(f.shape, jnp.float32) for f in flats]
        + [pltpu.VMEM((both.shape[2], 2 * d_mod.shape[2]), jnp.float32), dma((kinds, 3)), dma((kinds, 3))],
        compiler_params=pltpu.CompilerParams(vmem_limit_bytes=56 * 2**20),
        name="adam",
    )(factor, both, silu, d_mod, cond_all, onehot, *[item for s in states for item in s])
    order = [3 * a + k for a in range(kinds) for k in (1, 2, 0)]
    return [news[i] for i in order]


def per_device(
    tokens,
    cotangent,
    time_vec,
    labels,
    kept,
    keep_index,
    modulation_master,
    modulation_first,
    modulation_second,
    attention_in_master,
    attention_in_first,
    attention_in_second,
    attention_out_master,
    attention_out_first,
    attention_out_second,
    expand_master,
    expand_first,
    expand_second,
    contract_master,
    contract_first,
    contract_second,
    class_table_master,
    class_table_first,
    class_table_second,
    biases_master,
    biases_first,
    biases_second,
):
    rows, width = tokens.shape[1:]
    n, pairs = lax.axis_size("dp"), lax.axis_size("seq")
    me = lax.axis_index("dp")
    half_width = width // pairs
    low = jnp.bfloat16

    bias_share = biases_master.shape[0]
    quarter = width // 4
    freqs = np.float32(10000.0) ** (-np.arange(quarter, dtype=np.float32) / np.float32(quarter))
    (weights, _, grad_expand, _, normed_in, queries, keys, values, mixed, attended, middle, activated, d_hidden, sums, contract_sum,
     pieces, cond_own, silu_own, own_modulation, inputs, key_ok, row_ok, onehot, same, biases) = forward(
        [
            item.reshape(-1, 128)
            for item in (
                attention_in_master,
                attention_out_master,
                expand_master,
                contract_master,
                class_table_master,
                modulation_master,
            )
        ],
        [
            biases_master[None],
            jnp.stack([labels, kept], axis=1),
            time_vec,
            tokens[0],
            keep_index,
            jnp.asarray(freqs)[None],
            cotangent[0],
        ],
        bias_share * n,
        n,
        1,
    )
    _, d_mod_all, cond_all, reduced, block_out, tokens_grad, grad_biases, norm, clip = backward(
        [weights.reshape(3, width, 4 * half_width), grad_expand],
        [
            normed_in,
            activated,
            d_hidden,
            sums,
            contract_sum,
            queries,
            keys,
            values,
            mixed,
            key_ok,
            inputs,
            middle,
            attended,
            cotangent[0],
            row_ok,
            pieces,
            biases,
            own_modulation,
            cond_own,
            silu_own,
            same,
        ],
        n,
        2,
    )
    block_out, tokens_grad, grad_norm = block_out[None], tokens_grad[None], norm.reshape(())
    rates = (
        width ** (-0.5),
        width ** (-0.5),
        (width // 4) ** (-0.5),
        width ** (-0.5),
        FF ** (-0.5),
        0.5,
        0.2,
    )
    masters = (
        modulation_master,
        attention_in_master,
        attention_out_master,
        expand_master,
        contract_master,
        class_table_master,
        biases_master,
    )
    firsts = (
        modulation_first,
        attention_in_first,
        attention_out_first,
        expand_first,
        contract_first,
        class_table_first,
        biases_first,
    )
    seconds = (
        modulation_second,
        attention_in_second,
        attention_out_second,
        expand_second,
        contract_second,
        class_table_second,
        biases_second,
    )
    states = list(zip(masters, firsts, seconds))
    updated = adam(
        clip,
        reduced,
        silu_own,
        d_mod_all,
        cond_all,
        onehot,
        [tuple(item.reshape(-1, 128) for item in state) for state in states[:-1]],
        rates[:-1],
        n,
    )
    bias_grad = lax.dynamic_slice_in_dim(grad_biases[0], me * bias_share, bias_share, 0) * clip.reshape(-1)[:bias_share]
    updated = [item.reshape(-1) for item in updated] + list(adam_step(bias_grad, *states[-1], rates[-1]))
    return (block_out, tokens_grad, grad_norm) + tuple(updated)


def solution(mesh):
    return jax.shard_map(
        per_device,
        mesh=mesh,
        in_specs=(
            P("dp", "seq", None),
            P("dp", "seq", None),
            P("dp", None),
            P("dp"),
            P("dp"),
            P("dp", "seq"),
            P("dp"),
            P("dp"),
            P("dp"),
            P("dp"),
            P("dp"),
            P("dp"),
            P("dp"),
            P("dp"),
            P("dp"),
            P("dp"),
            P("dp"),
            P("dp"),
            P("dp"),
            P("dp"),
            P("dp"),
            P("dp"),
            P("dp"),
            P("dp"),
            P("dp"),
            P("dp"),
            P("dp"),
        ),
        out_specs=(
            P("dp", "seq", None),
            P("dp", "seq", None),
            P(),
            P("dp"),
            P("dp"),
            P("dp"),
            P("dp"),
            P("dp"),
            P("dp"),
            P("dp"),
            P("dp"),
            P("dp"),
            P("dp"),
            P("dp"),
            P("dp"),
            P("dp"),
            P("dp"),
            P("dp"),
            P("dp"),
            P("dp"),
            P("dp"),
            P("dp"),
            P("dp"),
            P("dp"),
        ),
        check_vma=False,
    )
```
